128 devices in a mesh: ctx: 32 (over z_hi, x, y), fsdp: 4 (over z_lo, core).
Axes of the slice: x: 4, y: 4, z: 4 (z_hi: 2, z_lo: 2; z = z_hi * 2 + z_lo), core: 2. Of those that a mesh axis runs over, the one named last changes fastest.
Arguments:
- layer_input: bfloat16 [4, 4096, 2048], P('fsdp', 'ctx'), may hold values from -6 to 6
- w_qkv: bfloat16 [2048, 2304], P(('ctx', 'fsdp')), may hold values from -0.125 to 0.125
- w_out: bfloat16 [2048, 1536], P(('ctx', 'fsdp')), may hold values from -6 to 6
- w_gate_up: bfloat16 [2048, 8704], P(('ctx', 'fsdp')), may hold values from -0.125 to 0.125
- w_down: bfloat16 [2048, 4352], P(('ctx', 'fsdp')), may hold values from -0.09375 to 0.09375
- norm_gains: bfloat16 [4224], P(('ctx', 'fsdp')), may hold values from 0.5 to 1.5
- span_map: int32 [4, 32], replicated, may hold values from 0 to 31, each once within a row
- cotangent: bfloat16 [4, 4096, 2048], P('fsdp', 'ctx'), may hold values from -6 to 6
Outputs:
- layer_out: bfloat16 [4, 4096, 2048], P('fsdp', 'ctx')
- input_grad: bfloat16 [4, 4096, 2048], P('fsdp', 'ctx')
- grad_qkv: float32 [2048, 2304], P(('ctx', 'fsdp'))
- grad_out: float32 [2048, 1536], P(('ctx', 'fsdp'))
- grad_gate_up: float32 [2048, 8704], P(('ctx', 'fsdp'))
- grad_down: float32 [2048, 4352], P(('ctx', 'fsdp'))
- grad_gains: float32 [4224], P(('ctx', 'fsdp'))
- stream_rms: float32 [4], replicated
The draws below stay inside these ranges and needn't reach their ends.
Inputs may be any that keep to these rules, and one draw needn't show every extreme that they name: `span_map`: each row is a permutation of 0 to 31.
All inputs are finite; a program needn't handle non-finite values.
Results may differ from the reference program's by a relative error of at most 0.02.
Values may be sent and summed in bfloat16 or wider, within the bound.
A program may use at most 512 MiB of HBM per device.

```python
import jax
import jax.numpy as jnp
from jax import lax

D = 2048
HQ = 24
HK = 6
HD = 64
FF = 4352
TOK_DEV = 128
LENGTH = 4096
SEQS = 4
GAINS = 4224
QKVW = 2304
N_CTX = 32


def level_of(stream_key, extent, pieces, least, largest):
    def one(axis_at, blocks):
        heights = jax.random.uniform(jax.random.fold_in(jax.random.fold_in(stream_key, 6), axis_at), (blocks,), jnp.float32, least / len(pieces), largest / len(pieces))
        return jnp.repeat(jnp.exp(heights), extent[axis_at] // blocks).reshape((-1,) + (1,) * (len(extent) - axis_at - 1))

    level = one(*pieces[0])
    for cut in pieces[1:]:
        level = level * one(*cut)
    return level


def scatter_about(stream_key, dims, spread, most, pieces=(), kind=jnp.bfloat16):
    array = spread * jax.random.normal(stream_key, dims, jnp.float32)
    if pieces:
        array = array * level_of(stream_key, dims, pieces, -0.22, 0.18)
    return jnp.clip(array, -most, most).astype(kind)


def setup_inputs(seed: int = 0) -> dict:
    key_list = jax.random.split(jax.random.key(seed), 9)
    layer_input = scatter_about(key_list[0], (SEQS, LENGTH, D), 1.0, 6.0, ((0, 4), (1, 32)))
    w_qkv = scatter_about(key_list[1], (D, QKVW), D ** -0.5, 0.125, ((0, 128),))
    w_out = scatter_about(key_list[2], (D, HQ * HD), (max(1, HQ * HD // LENGTH)) ** -0.5, 6.0, ((0, 128),))
    w_gate_up = scatter_about(key_list[3], (D, 2 * FF), D ** -0.5, 0.125, ((0, 128),))
    w_down = scatter_about(key_list[4], (D, FF), FF ** -0.5, 0.09375, ((0, 128),))
    norm_gains = jnp.clip(1.0 + 0.1 * jax.random.normal(key_list[5], (GAINS,), jnp.float32), 0.5, 1.5).astype(jnp.bfloat16)
    span_map = jax.vmap(lambda own: jax.random.permutation(own, N_CTX))(jax.random.split(key_list[6], SEQS)).reshape((SEQS, N_CTX)).astype(jnp.int32)
    cotangent = scatter_about(key_list[7], (SEQS, LENGTH, D), 1.0, 6.0, ((0, 4), (1, 32)))
    return dict(layer_input=layer_input, w_qkv=w_qkv, w_out=w_out, w_gate_up=w_gate_up, w_down=w_down, norm_gains=norm_gains, span_map=span_map, cotangent=cotangent)


EPSILON = 1e-06
ROPE_BASE = 10000.0
NEGATIVE = -1e+30
PRECISION = lax.Precision.HIGHEST

@jax.custom_vjp
def low(v):
    return lax.optimization_barrier(v.astype(jnp.bfloat16)).astype(jnp.float32)

@jax.custom_vjp
def low_back(v):
    return v

def low_keep(v):
    return (low(v), None)

def low_pass(kept, grad):
    return (grad,)

def back_keep(v):
    return (v, None)

def back_low(kept, grad):
    return (low(grad),)
low.defvjp(low_keep, low_pass)
low_back.defvjp(back_keep, back_low)

def row_positions(span_row, row_ids, rows_dev, n_ctx):
    span_rows = rows_dev // 2
    slot_index = row_ids // rows_dev
    half_index = row_ids % rows_dev // span_rows
    compare = slot_index[:, None] == jnp.arange(n_ctx, dtype=jnp.int32)[None, :]
    first_span = lax.optimization_barrier(jnp.sum(jnp.where(compare, span_row[None, :], 0), axis=1)).astype(jnp.int32)
    span_index = jnp.where(half_index == 0, first_span, 2 * n_ctx - 1 - first_span)
    return (span_index * span_rows + row_ids % span_rows).astype(jnp.int32)

def rope_tables(positions, head_dim):
    half_dim = head_dim // 2
    frequencies = ROPE_BASE ** (-(jnp.arange(half_dim, dtype=jnp.float32) * 2.0 / head_dim))
    angles = positions.astype(jnp.float32)[:, None] * frequencies[None, :]
    cosine = jnp.cos(angles)
    sine_rows = jnp.sin(angles)
    return (jnp.concatenate([cosine, cosine], axis=1), jnp.concatenate([sine_rows, sine_rows], axis=1))

def rotate(value_in, cosine, sine_rows):
    half_dim = value_in.shape[-1] // 2
    turned = jnp.concatenate([-value_in[..., half_dim:], value_in[..., :half_dim]], axis=-1)
    return value_in * cosine + turned * sine_rows

def norm_rows(value_in, gain_row):
    inverse = lax.rsqrt(lax.optimization_barrier(jnp.mean(value_in * value_in, axis=-1, keepdims=True)) + EPSILON)
    return value_in * inverse * gain_row

def seq_forward(stream_in, span_row, w_qkv, w_out, w_gate_up, w_down, gain_vec):
    length = stream_in.shape[0]
    q_group = HQ // HK
    q_width = HQ * HD
    k_width = HK * HD
    score_scale = HD ** (-0.5)
    gain_one = gain_vec[:D]
    gain_two = gain_vec[D:2 * D]
    gain_query = gain_vec[2 * D:2 * D + HD]
    gain_key = gain_vec[2 * D + HD:]
    normed_one = low(norm_rows(stream_in, gain_one))
    joined_rows = low_back(jnp.dot(normed_one, w_qkv, precision=PRECISION))
    queries = joined_rows[:, :q_width].reshape(length, HQ, HD)
    keys_raw = joined_rows[:, q_width:q_width + k_width].reshape(length, HK, HD)
    values_raw = joined_rows[:, q_width + k_width:].reshape(length, HK, HD)
    positions = row_positions(span_row, jnp.arange(length, dtype=jnp.int32), TOK_DEV, N_CTX)
    cosine, sine_rows = rope_tables(positions, HD)
    cosine = cosine[:, None, :]
    sine_rows = sine_rows[:, None, :]
    query_rot = low(rotate(norm_rows(queries, gain_query), cosine, sine_rows))
    key_rot = low(rotate(norm_rows(keys_raw, gain_key), cosine, sine_rows))
    value_low = low(values_raw)
    query_heads = query_rot.reshape(length, HK, q_group, HD).transpose(1, 2, 0, 3)
    key_heads = key_rot.transpose(1, 0, 2)
    value_heads = value_low.transpose(1, 0, 2)
    q_block = min(512, length)
    n_blocks = length // q_block
    query_blocks = query_heads.reshape(HK, q_group, n_blocks, q_block, HD).transpose(2, 0, 1, 3, 4)
    pos_blocks = positions.reshape(n_blocks, q_block)

    @jax.checkpoint
    def attend(block_item):
        query_block, pos_block = block_item
        raw_scores = jnp.einsum('hgqd,hkd->hgqk', query_block, key_heads, precision=PRECISION) * score_scale
        allowed = positions[None, None, None, :] <= pos_block[None, None, :, None]
        scores = low_back(jnp.where(allowed, raw_scores, NEGATIVE))
        row_max = lax.optimization_barrier(jnp.max(scores, axis=-1, keepdims=True))
        exp_terms = jnp.where(allowed, jnp.exp(scores - row_max), 0.0)
        prob_rows = exp_terms / lax.optimization_barrier(jnp.sum(exp_terms, axis=-1, keepdims=True))
        return jnp.einsum('hgqk,hkd->hgqd', low(prob_rows), value_heads, precision=PRECISION)
    attn_blocks = lax.map(attend, (query_blocks, pos_blocks))
    attended = attn_blocks.transpose(0, 3, 1, 2, 4).reshape(length, q_width)
    attn_low = low(low_back(attended))
    branch_a = low_back(jnp.dot(attn_low, w_out.T, precision=PRECISION))
    middle = stream_in + branch_a
    normed_two = low(norm_rows(middle, gain_two))
    gate_up = low_back(jnp.dot(normed_two, w_gate_up, precision=PRECISION))
    gate_part = gate_up[:, :FF]
    up_part = gate_up[:, FF:]
    hidden = low(jax.nn.silu(gate_part) * up_part)
    branch_f = low_back(jnp.dot(hidden, w_down.T, precision=PRECISION))
    result = middle + branch_f
    stat_rows = jnp.stack([jnp.sum(jnp.sqrt(lax.optimization_barrier(jnp.mean(stream * stream, axis=-1)))) for stream in (stream_in, branch_a, middle, branch_f)])
    return (result, stat_rows)

def reference(layer_input, w_qkv, w_out, w_gate_up, w_down, norm_gains, span_map, cotangent):

    def forward(stream_all, w_joined, w_proj, w_mlp, w_back, gain_vec):

        def one_seq(seq_item):
            stream_in, span_row = seq_item
            return seq_forward(stream_in, span_row, w_joined, w_proj, w_mlp, w_back, gain_vec)
        outputs, stat_rows = lax.map(one_seq, (stream_all, span_map))
        return (outputs, lax.optimization_barrier(jnp.sum(stat_rows, axis=0)) / (stream_all.shape[0] * stream_all.shape[1]))
    outputs, pullback, stat_rows = jax.vjp(forward, layer_input.astype(jnp.float32), w_qkv.astype(jnp.float32), w_out.astype(jnp.float32), w_gate_up.astype(jnp.float32), w_down.astype(jnp.float32), norm_gains.astype(jnp.float32), has_aux=True)
    grad_x, grad_joined, grad_proj, grad_mlp, grad_back, grad_gain = pullback(cotangent.astype(jnp.float32))
    return (outputs.astype(jnp.bfloat16), grad_x.astype(jnp.bfloat16), grad_joined, grad_proj, grad_mlp, grad_back, grad_gain, stat_rows)
```

```python
import functools

import jax
import jax.numpy as jnp
from jax import lax
from jax.experimental import pallas as pl
from jax.experimental.pallas import tpu as pltpu
from jax.sharding import PartitionSpec as P

D = 2048
HQ = 24
HK = 6
HD = 64
FF = 4352
TOK = 128
SPAN = 64
N_CTX = 32

HH = HK // 2
GROUP = HQ // HK
QH = HQ // 2
QW = QH * HD
KVW = HH * 2 * HD
FH = FF // 2
KEYS = 512
SPANS_STEP = KEYS // SPAN
FULL_STEPS = 7
QROWS = GROUP * SPAN

EPSILON = 1e-06
ROPE_BASE = 10000.0
LOG2E = 1.4426950408889634
MESH = pl.DeviceIdType.MESH
BF = jnp.bfloat16
F32 = jnp.float32
NT = (((1,), (1,)), ((), ()))
NN = (((1,), (0,)), ((), ()))
TN = (((0,), (0,)), ((), ()))
W_DIMS = ("h", "x", "y", "l")
KV_DIMS = ("h", "x", "y")
ORDERS = (("x", "y", "z"), ("y", "z", "x"), ("z", "x", "y"))
KV_ORDERS = (("h", "x", "y"), ("x", "y", "h"), ("y", "h", "x"))
SIZES = {"x": 4, "y": 4, "z": 4, "h": 2}


def here():
    c = lax.axis_index("ctx")
    f = lax.axis_index("fsdp")
    return {
        "x": lax.rem(lax.div(c, 4), 4),
        "y": lax.rem(c, 4),
        "z": lax.div(c, 16) * 2 + lax.div(f, 2),
        "h": lax.div(c, 16),
        "l": lax.rem(f, 2) * 0 + lax.div(f, 2),
        "core": lax.rem(f, 2),
    }


def device_of(x, y, z, core):
    return (lax.div(z, 2) * 16 + x * 4 + y, lax.rem(z, 2) * 2 + core)


def moved(at, axis, by):
    if axis == "core":
        return device_of(at["x"], at["y"], at["z"], 1 - at["core"])
    place = {k: at[k] for k in ("x", "y", "z")}
    if axis == "h":
        place["z"] = lax.rem(at["z"] + 2, 4)
    else:
        place[axis] = lax.rem(at[axis] + by + 4, 4)
    return device_of(place["x"], place["y"], place["z"], at["core"])


def labels(axis, value):
    if axis == "z":
        return {"h": lax.div(value, 2), "l": lax.rem(value, 2)}
    return {axis: value}


def pick(ref, dims, values, tail):
    return ref.at[tuple(values[d] if d in values else slice(None) for d in dims) + tail]


def greet(devices):
    barrier = pltpu.get_barrier_semaphore()
    for d in devices:
        pl.semaphore_signal(barrier, inc=1, device_id=d, device_id_type=MESH)
    pl.semaphore_wait(barrier, len(devices))


def send(src, dst, ssem, rsem, device):
    copy = pltpu.make_async_remote_copy(
        src_ref=src, dst_ref=dst, send_sem=ssem, recv_sem=rsem, device_id=device, device_id_type=MESH
    )
    copy.start()
    return copy


def ring_gather(streams, dims, at, ssem, rsem):
    sent = []
    for phase in range(3):
        first = []
        for k, (ref, order, rows, cols) in enumerate(streams):
            axis = order[phase]
            later = {}
            for a in order[phase + 1 :]:
                later.update(labels(a, at[a]))
            mine = pick(ref, dims, {**later, **labels(axis, at[axis])}, (slice(None), cols))
            if SIZES[axis] == 2:
                first.append((send(mine, mine, ssem.at[k, phase, 0], rsem.at[k, phase, 0], moved(at, axis, 1)),))
            else:
                up = send(mine, mine, ssem.at[k, phase, 0], rsem.at[k, phase, 0], moved(at, axis, 1))
                down = send(mine, mine, ssem.at[k, phase, 1], rsem.at[k, phase, 1], moved(at, axis, 3))
                first.append((up, down))
        second = []
        for k, (ref, order, rows, cols) in enumerate(streams):
            axis = order[phase]
            for c in first[k]:
                c.wait_recv()
                sent.append(c)
            if SIZES[axis] == 2:
                continue
            later = {}
            for a in order[phase + 1 :]:
                later.update(labels(a, at[a]))
            below = lax.rem(at[axis] + 3, 4)
            above = lax.rem(at[axis] + 1, 4)
            low = pick(ref, dims, {**later, **labels(axis, below)}, (pl.ds(0, rows // 2), cols))
            high = pick(ref, dims, {**later, **labels(axis, above)}, (pl.ds(rows // 2, rows // 2), cols))
            second.append(send(low, low, ssem.at[k, phase, 2], rsem.at[k, phase, 2], moved(at, axis, 1)))
            second.append(send(high, high, ssem.at[k, phase, 3], rsem.at[k, phase, 3], moved(at, axis, 3)))
        for c in second:
            c.wait_recv()
            sent.append(c)
    for c in sent:
        c.wait_send()


def neighbours(at, axes):
    out = []
    for a in axes:
        if a in ("core", "h"):
            out.append(moved(at, a, 1))
        else:
            out.append(moved(at, a, 1))
            out.append(moved(at, a, 3))
    return out


def weight_kernel(parts, n_pair, n_in, *refs):
    ins, outs = refs[:n_in], refs[n_in : 2 * n_in]
    psem, lsem, ssem, rsem = refs[2 * n_in :]
    at = here()
    core = at["core"]
    sibling = moved(at, "core", 1)
    greet([sibling] + neighbours(at, ("x", "y", "z")))
    own = {d: at[d] for d in W_DIMS}
    remote, local = [], []
    for i in range(n_in):
        if i < len(parts):
            dst = pick(outs[i], W_DIMS, own, (pl.ds(core * 16, 16), slice(None)))
            remote.append(send(ins[i].at[1 - core], dst, psem.at[i, 0], psem.at[i, 1], sibling))
            local.append(pltpu.make_async_copy(ins[i].at[core], dst, lsem.at[i]))
        else:
            dst = outs[i].at[core]
            remote.append(send(ins[i], dst, psem.at[i, 0], psem.at[i, 1], sibling))
            local.append(pltpu.make_async_copy(ins[i], dst, lsem.at[i]))
        local[-1].start()
    for i in range(len(parts)):
        remote[i].wait_recv()
        local[i].wait()
    streams = []
    for i, pieces in enumerate(parts):
        for start, length, order in pieces:
            streams.append((outs[i], order, 32, pl.ds(start, length)))
    ring_gather(streams, W_DIMS, at, ssem, rsem)
    for i in range(n_in):
        remote[i].wait_send()
        if i >= len(parts):
            remote[i].wait_recv()
            local[i].wait()


def gather_weights(shards, parts, pairs, cid):
    n_in = len(shards) + len(pairs)
    n_streams = sum(len(p) for p in parts)
    outs = [jax.ShapeDtypeStruct((2, 4, 4, 2, 32, s.shape[-1]), s.dtype) for s in shards]
    outs += [jax.ShapeDtypeStruct((2,) + p.shape, p.dtype) for p in pairs]
    anywhere = pl.BlockSpec(memory_space=pl.ANY)
    return pl.pallas_call(
        functools.partial(weight_kernel, parts, len(pairs), n_in),
        out_shape=outs,
        in_specs=[anywhere] * n_in,
        out_specs=[anywhere] * n_in,
        scratch_shapes=[
            pltpu.SemaphoreType.DMA((n_in, 2)),
            pltpu.SemaphoreType.DMA((n_in,)),
            pltpu.SemaphoreType.DMA((n_streams, 3, 4)),
            pltpu.SemaphoreType.DMA((n_streams, 3, 4)),
        ],
        compiler_params=pltpu.CompilerParams(collective_id=cid, has_side_effects=True),
        name=f"gather_weights_{cid}",
    )(*shards, *pairs)


def kv_gather_kernel(src, out, lsem, ssem, rsem):
    at = here()
    greet(neighbours(at, ("h", "x", "y")))
    local = pltpu.make_async_copy(src, pick(out, KV_DIMS, {d: at[d] for d in KV_DIMS}, ()), lsem)
    local.start()
    local.wait()
    streams = [(out, KV_ORDERS[h], 256, pl.ds(h * 2 * HD, 2 * HD)) for h in range(HH)]
    ring_gather(streams, KV_DIMS, at, ssem, rsem)


def gather_kv(kv_local, cid):
    anywhere = pl.BlockSpec(memory_space=pl.ANY)
    return pl.pallas_call(
        kv_gather_kernel,
        out_shape=jax.ShapeDtypeStruct((2, 4, 4, 2 * TOK, KVW), BF),
        in_specs=[anywhere],
        out_specs=anywhere,
        scratch_shapes=[
            pltpu.SemaphoreType.DMA,
            pltpu.SemaphoreType.DMA((HH, 3, 4)),
            pltpu.SemaphoreType.DMA((HH, 3, 4)),
        ],
        compiler_params=pltpu.CompilerParams(collective_id=cid, has_side_effects=True),
        name="gather_kv",
    )(kv_local)


def lead_shape(dims):
    full = {"h": 2, "x": 4, "y": 4, "l": 2}
    return tuple(full[d] for d in dims)


def without(dims, axis):
    gone = ("h", "l") if axis == "z" else (axis,)
    return tuple(d for d in dims if d not in gone)


def sum_streams(specs, dims, at, arrived, mine, ssem, rsem, lsem):
    state = [(s[0], dims, s[3]) for s in specs]
    sent = []
    for phase in range(3):
        flight = []
        for k, (unused, order, rows, cols0, width) in enumerate(specs):
            ref, now, cols = state[k]
            axis = order[phase]
            size = SIZES[axis]
            copies = []
            for i in (1, 3, 2) if size == 4 else (1,):
                target = lax.rem(at[axis] + i, size)
                src = pick(ref, now, labels(axis, target), (slice(None), cols))
                copies.append(
                    send(src, arrived[k][phase].at[i - 1], ssem.at[k, phase, i - 1], rsem.at[k, phase, i - 1], moved(at, axis, i))
                )
            local = None
            if phase == 0:
                src = pick(ref, now, labels(axis, at[axis]), (slice(None), cols))
                local = pltpu.make_async_copy(src, mine[k][0], lsem.at[k])
                local.start()
            flight.append((copies, local))
        for k, (unused, order, rows, cols0, width) in enumerate(specs):
            ref, now, cols = state[k]
            axis = order[phase]
            size = SIZES[axis]
            copies, local = flight[k]
            rest = without(now, axis)
            if local is not None:
                local.wait()
            for c in copies:
                c.wait_recv()
                sent.append(c)
            got = arrived[k][phase]
            lead = lead_shape(rest)
            out = mine[k][phase + 1]

            def add(idx):
                if phase == 0:
                    own = mine[k][0][idx]
                else:
                    own = pick(ref, now, labels(axis, at[axis]), ())[idx]
                total = own.astype(F32)
                for i in range(size - 1):
                    total = total + got[(i,) + idx].astype(F32)
                out[idx] = total.astype(out.dtype)

            spots = [()]
            for n in lead:
                spots = [s + (j,) for s in spots for j in range(n)]
            for s in spots:
                add(s + (slice(None), slice(None)))
            state[k] = (out, rest, slice(None))
    for c in sent:
        c.wait_send()


def sum_scratch(specs, dims, last):
    arrived, mine = [], []
    for order, rows, width in specs:
        now = dims
        a, m = [], []
        for phase in range(3):
            rest = without(now, order[phase])
            lead = lead_shape(rest)
            a.append(pltpu.VMEM((SIZES[order[phase]] - 1,) + lead + (rows, width), BF))
            if phase == 0:
                m.append(pltpu.VMEM(lead + (rows, width), BF))
            m.append(pltpu.VMEM(lead + (rows, width), BF if phase < 2 else last))
            now = rest
        arrived.append(a)
        mine.append(m)
    return arrived, mine


def sum_peers(at, axes):
    out = []
    for a in axes:
        for i in (1, 3, 2) if SIZES[a] == 4 else (1,):
            out.append(moved(at, a, i))
    return out


def kv_sum_kernel(src, out, arrived, mine, ssem, rsem, lsem):
    at = here()
    greet(sum_peers(at, ("h", "x", "y")))
    orders = KV_ORDERS
    specs = [(src, orders[h], 2 * TOK, pl.ds(h * 2 * HD, 2 * HD), 2 * HD) for h in range(HH)]
    sum_streams(specs, KV_DIMS, at, arrived, mine, ssem, rsem, lsem)
    for h in range(HH):
        out[:, h * 2 * HD : (h + 1) * 2 * HD] = mine[h][3][...]


def sum_kv(grads, cid):
    scratch = sum_scratch([(KV_ORDERS[h], 2 * TOK, 2 * HD) for h in range(HH)], KV_DIMS, F32)
    return pl.pallas_call(
        kv_sum_kernel,
        out_shape=jax.ShapeDtypeStruct((2 * TOK, KVW), F32),
        in_specs=[pl.BlockSpec(memory_space=pl.ANY)],
        out_specs=pl.BlockSpec(memory_space=pltpu.VMEM),
        scratch_shapes=[
            scratch[0],
            scratch[1],
            pltpu.SemaphoreType.DMA((HH, 3, 3)),
            pltpu.SemaphoreType.DMA((HH, 3, 3)),
            pltpu.SemaphoreType.DMA((HH,)),
        ],
        compiler_params=pltpu.CompilerParams(
            collective_id=cid, has_side_effects=True, vmem_limit_bytes=48 * 1024 * 1024
        ),
        name="sum_kv",
    )(grads)


SMALL = (("q", 0, 384), ("q", 384, 384), ("q", 768, 384), ("o", 0, 256), ("o", 256, 256), ("o", 512, 256))


def weight_sum_kernel(gq, go, oq, oo, arrived, mine, stage_q, stage_o, got_q, got_o, ssem, rsem, lsem, csem):
    at = here()
    core = at["core"]
    sibling = moved(at, "core", 1)
    greet([sibling] + sum_peers(at, ("x", "y", "z")))
    specs = []
    for k, (name, start, width) in enumerate(SMALL):
        specs.append((gq if name == "q" else go, ORDERS[k % 3], 32, pl.ds(start, width), width))
    sum_streams(specs, W_DIMS, at, arrived, mine, ssem, rsem, lsem)
    for k, (name, start, width) in enumerate(SMALL):
        stage = stage_q if name == "q" else stage_o
        stage[:, start : start + width] = mine[k][3][...]
    other = pl.ds(pl.multiple_of((1 - core) * 16, 16), 16)
    own = pl.ds(pl.multiple_of(core * 16, 16), 16)
    a = send(stage_q.at[other], got_q, csem.at[0], csem.at[1], sibling)
    b = send(stage_o.at[other], got_o, csem.at[2], csem.at[3], sibling)
    oq[core] = stage_q[own, :]
    oo[core] = stage_o[own, :]
    a.wait_recv()
    oq[1 - core] = got_q[...]
    b.wait_recv()
    oo[1 - core] = got_o[...]
    a.wait_send()
    b.wait_send()


def sum_weights(gq, go, cid):
    scratch = sum_scratch([(ORDERS[k % 3], 32, SMALL[k][2]) for k in range(6)], W_DIMS, F32)
    anywhere = pl.BlockSpec(memory_space=pl.ANY)
    vmem = pl.BlockSpec(memory_space=pltpu.VMEM)
    wq, wo = gq.shape[-1], go.shape[-1]
    return pl.pallas_call(
        weight_sum_kernel,
        out_shape=[jax.ShapeDtypeStruct((2, 16, wq), F32), jax.ShapeDtypeStruct((2, 16, wo), F32)],
        in_specs=[anywhere] * 2,
        out_specs=[vmem] * 2,
        scratch_shapes=[
            scratch[0],
            scratch[1],
            pltpu.VMEM((32, wq), F32),
            pltpu.VMEM((32, wo), F32),
            pltpu.VMEM((16, wq), F32),
            pltpu.VMEM((16, wo), F32),
            pltpu.SemaphoreType.DMA((6, 3, 3)),
            pltpu.SemaphoreType.DMA((6, 3, 3)),
            pltpu.SemaphoreType.DMA((6,)),
            pltpu.SemaphoreType.DMA((4,)),
        ],
        compiler_params=pltpu.CompilerParams(
            collective_id=cid, has_side_effects=True, vmem_limit_bytes=48 * 1024 * 1024
        ),
        name="sum_weights",
    )(gq, go)


def total_kernel(x_ref, o_ref, buf, ssem, rsem):
    at = here()
    greet([moved(at, "core", 1)] + sum_peers(at, ("x", "y", "z")))
    value = x_ref[...]
    sent = []
    for phase, axis in enumerate(("core", "z", "y", "x")):
        buf[phase, 0] = value
        copies = []
        for i in (1, 3, 2) if axis != "core" else (1,):
            copies.append(
                send(buf.at[phase, 0], buf.at[phase, i], ssem.at[phase, i], rsem.at[phase, i], moved(at, axis, i))
            )
        for c in copies:
            c.wait_recv()
            sent.append(c)
        if axis == "core":
            value = buf[phase, 0] + buf[phase, 1]
        else:
            value = (buf[phase, 0] + buf[phase, 2]) + (buf[phase, 1] + buf[phase, 3])
    o_ref[...] = value
    for c in sent:
        c.wait_send()


def total_everywhere(x, cid):
    return pl.pallas_call(
        total_kernel,
        out_shape=jax.ShapeDtypeStruct(x.shape, F32),
        in_specs=[pl.BlockSpec(memory_space=pltpu.VMEM)],
        out_specs=pl.BlockSpec(memory_space=pltpu.VMEM),
        scratch_shapes=[
            pltpu.VMEM((4, 4) + x.shape, F32),
            pltpu.SemaphoreType.DMA((4, 4)),
            pltpu.SemaphoreType.DMA((4, 4)),
        ],
        compiler_params=pltpu.CompilerParams(collective_id=cid, has_side_effects=True),
        name="total_everywhere",
    )(x)


def fetch_keys(tab, kvg, kv, sems):
    for s in range(2):

        def go(p, carry):
            slot = tab[s, p]
            row = lax.rem(slot, 2) * SPAN + s * TOK
            pltpu.make_async_copy(
                kvg.at[lax.div(slot, 2), pl.ds(pl.multiple_of(row, SPAN), SPAN)],
                kv.at[s, pl.ds(pl.multiple_of(p * SPAN, SPAN), SPAN)],
                sems.at[s],
            ).start()
            return carry

        lax.fori_loop(0, 2 * N_CTX, go, 0)


def step_of(t, low_steps):
    half = jnp.where(t < low_steps, 0, 1)
    return half, jnp.where(t < low_steps, t, t - low_steps)


def attend_kernel(tab, q_ref, kvg, o_ref, l_ref, kv, acc, total, sems):
    fetch_keys(tab, kvg, kv, sems)
    rate = LOG2E * HD**-0.5
    for s in range(2):
        pltpu.make_async_copy(kv.at[s], kv.at[s], sems.at[s]).wait()
        span = tab[s, 2 * N_CTX]
        low_steps = lax.div(span, SPANS_STEP)
        for h in range(HH):
            acc[...] = jnp.zeros_like(acc)
            total[...] = jnp.zeros_like(total)

            def step(half, block, limit):
                keys = kv[s, pl.ds(pl.multiple_of(block * KEYS, KEYS), KEYS), h * 2 * HD : (h + 1) * 2 * HD]
                scores = lax.dot_general(keys, q_ref[s, h, half], NT, preferred_element_type=F32)
                prob = jnp.exp2(scores * rate)
                if limit is not None:
                    row = lax.broadcasted_iota(jnp.int32, prob.shape, 0)
                    col = lax.rem(lax.broadcasted_iota(jnp.int32, prob.shape, 1), SPAN)
                    prob = jnp.where(row <= col + limit, prob, 0.0)
                total[half] += jnp.sum(prob, axis=0, keepdims=True)
                acc[half] += lax.dot_general(keys, prob.astype(BF), TN, preferred_element_type=F32)

            def full(t, carry):
                half, block = step_of(t, low_steps)
                step(half, block, None)
                return carry

            lax.fori_loop(0, FULL_STEPS, full, 0)
            for half, first in ((0, span), (1, 2 * N_CTX - 1 - span)):
                step(half, lax.div(first, SPANS_STEP), lax.rem(first, SPANS_STEP) * SPAN)
                out = acc[half, HD:, :] / total[half]
                o_ref[s, h, half] = out.T
                l_ref[s, h, half] = jnp.log2(total[half])


def attend(tab, q_pad, kvg):
    vmem = pl.BlockSpec(memory_space=pltpu.VMEM)
    return pl.pallas_call(
        attend_kernel,
        out_shape=[
            jax.ShapeDtypeStruct((2, HH, 2, QROWS, HD), F32),
            jax.ShapeDtypeStruct((2, HH, 2, 1, QROWS), F32),
        ],
        in_specs=[pl.BlockSpec(memory_space=pltpu.SMEM), vmem, pl.BlockSpec(memory_space=pl.ANY)],
        out_specs=[vmem, vmem],
        scratch_shapes=[
            pltpu.VMEM((2, N_CTX * TOK, KVW), BF),
            pltpu.VMEM((2, 2 * HD, QROWS), F32),
            pltpu.VMEM((2, 1, QROWS), F32),
            pltpu.SemaphoreType.DMA((2,)),
        ],
        compiler_params=pltpu.CompilerParams(vmem_limit_bytes=48 * 1024 * 1024),
        cost_estimate=pl.CostEstimate(flops=20_000_000_000, bytes_accessed=20_000_000, transcendentals=8_000_000),
        name="attend",
    )(tab, q_pad, kvg)


def attend_back_kernel(tab, qd_ref, l_ref, delta_ref, kvg, dq_ref, dkv_ref, kv, stage, acc, dq_acc, sems, osems):
    fetch_keys(tab, kvg, kv, sems)
    rate = LOG2E * HD**-0.5
    lanes = lax.broadcasted_iota(jnp.int32, (1, 2 * HD), 1)
    factor = jnp.where(lanes < HD, HD**-0.5, 1.0)
    for s in range(2):
        pltpu.make_async_copy(kv.at[s], kv.at[s], sems.at[s]).wait()
        span = tab[s, 2 * N_CTX]
        low_steps = lax.div(span, SPANS_STEP)
        for h in range(HH):
            dq_acc[...] = jnp.zeros_like(dq_acc)
            acc[...] = jnp.zeros_like(acc)

            def step(half, block, limit):
                rows = pl.ds(pl.multiple_of(block * KEYS, KEYS), KEYS)
                keys = kv[s, rows, h * 2 * HD : (h + 1) * 2 * HD]
                both = lax.dot_general(keys, qd_ref[s, h, half], NT, preferred_element_type=F32)
                prob = jnp.exp2(both[:, :QROWS] * rate - l_ref[s, h, half])
                if limit is not None:
                    row = lax.broadcasted_iota(jnp.int32, prob.shape, 0)
                    col = lax.rem(lax.broadcasted_iota(jnp.int32, prob.shape, 1), SPAN)
                    prob = jnp.where(row <= col + limit, prob, 0.0)
                grad = (prob * (both[:, QROWS:] - delta_ref[s, h, half])).astype(BF)
                pair = jnp.concatenate([grad, prob.astype(BF)], axis=1)
                acc[rows, :] += lax.dot_general(pair, qd_ref[s, h, half], NN, preferred_element_type=F32)
                dq_acc[half] += lax.dot_general(keys, grad, TN, preferred_element_type=F32)

            def full(t, carry):
                half, block = step_of(t, low_steps)
                step(half, block, None)
                return carry

            lax.fori_loop(0, FULL_STEPS, full, 0)
            for half, first in ((0, span), (1, 2 * N_CTX - 1 - span)):
                step(half, lax.div(first, SPANS_STEP), lax.rem(first, SPANS_STEP) * SPAN)
                dq_ref[s, h, half] = (dq_acc[half, :HD, :] * HD**-0.5).T

            def cast(b, carry):
                rows = pl.ds(pl.multiple_of(b * KEYS, KEYS), KEYS)
                stage[s, rows, h * 2 * HD : (h + 1) * 2 * HD] = (acc[rows, :] * factor).astype(BF)
                return carry

            lax.fori_loop(0, N_CTX * TOK // KEYS, cast, 0)

        def put(p, carry):
            slot = tab[s, p]
            row = lax.rem(slot, 2) * SPAN + s * TOK
            pltpu.make_async_copy(
                stage.at[s, pl.ds(pl.multiple_of(p * SPAN, SPAN), SPAN)],
                dkv_ref.at[lax.div(slot, 2), pl.ds(pl.multiple_of(row, SPAN), SPAN)],
                osems.at[s],
            ).start()
            return carry

        lax.fori_loop(0, 2 * N_CTX, put, 0)
    for s in range(2):
        pltpu.make_async_copy(stage.at[s], stage.at[s], osems.at[s]).wait()


def attend_back(tab, qd, log_sum, delta, kvg):
    vmem = pl.BlockSpec(memory_space=pltpu.VMEM)
    anywhere = pl.BlockSpec(memory_space=pl.ANY)
    return pl.pallas_call(
        attend_back_kernel,
        out_shape=[
            jax.ShapeDtypeStruct((2, HH, 2, QROWS, HD), F32),
            jax.ShapeDtypeStruct((N_CTX, 2 * TOK, KVW), BF),
        ],
        in_specs=[pl.BlockSpec(memory_space=pltpu.SMEM), vmem, vmem, vmem, anywhere],
        out_specs=[vmem, anywhere],
        scratch_shapes=[
            pltpu.VMEM((2, N_CTX * TOK, KVW), BF),
            pltpu.VMEM((2, N_CTX * TOK, KVW), BF),
            pltpu.VMEM((N_CTX * TOK, 2 * HD), F32),
            pltpu.VMEM((2, 2 * HD, QROWS), F32),
            pltpu.SemaphoreType.DMA((2,)),
            pltpu.SemaphoreType.DMA((2,)),
        ],
        compiler_params=pltpu.CompilerParams(vmem_limit_bytes=48 * 1024 * 1024),
        cost_estimate=pl.CostEstimate(flops=50_000_000_000, bytes_accessed=30_000_000, transcendentals=8_000_000),
        name="attend_back",
    )(tab, qd, log_sum, delta, kvg)


def permutation(axis, by):
    pairs = []
    for c in range(N_CTX):
        for f in range(4):
            h, x, y = c // 16, (c // 4) % 4, c % 4
            z, core = h * 2 + f // 2, f % 2
            if axis == "x":
                x = (x + by) % 4
            elif axis == "y":
                y = (y + by) % 4
            elif axis == "z":
                z = (z + by) % 4
            else:
                core = 1 - core
            pairs.append((c * 4 + f, ((z // 2) * 16 + x * 4 + y) * 4 + (z % 2) * 2 + core))
    return pairs


def shift(value, axis, by=1):
    return lax.ppermute(value, ("ctx", "fsdp"), permutation(axis, by))


def take(value, dims, axis, index, offset=0):
    for label, i in labels(axis, index).items():
        at = offset + dims.index(label)
        value = lax.dynamic_slice_in_dim(value, i, 1, axis=at)
    gone = tuple(offset + dims.index(d) for d in labels(axis, index))
    return lax.squeeze(value, gone)


def sum_at_owner(left, right, order, at):
    tokens = left.shape[0]
    blocks = left.reshape(tokens, 2, 4, 4, 2, 32)
    axis = order[0]
    dims = W_DIMS
    rest = without(dims, axis)

    def product(target):
        rows = take(blocks, dims, axis, target, 1).reshape(tokens, -1)
        out = lax.dot_general(rows, right, TN, preferred_element_type=F32).astype(BF)
        return out.reshape(lead_shape(rest) + (32, right.shape[1]))

    gathered = [shift(product(lax.rem(at[axis] + i, 4)), axis, i) for i in (1, 3, 2)]
    gathered.append(product(at[axis]))
    for phase in (1, 2):
        dims, axis = rest, order[phase]
        rest = without(dims, axis)

        def block(target, kind):
            total = sum(take(g, dims, axis, target).astype(F32) for g in gathered)
            return total.astype(kind)

        nxt = [shift(block(lax.rem(at[axis] + i, 4), BF), axis, i) for i in (1, 3, 2)]
        nxt.append(block(at[axis], F32))
        gathered = nxt
    return sum(g.astype(F32) for g in gathered)


def norm_rows(value_in, gain_row):
    inverse = lax.rsqrt(jnp.mean(value_in * value_in, axis=-1, keepdims=True) + EPSILON)
    return (value_in * inverse * gain_row, inverse)


def norm_back(value_in, inverse, gain_row, upstream):
    scaled = upstream * gain_row
    backward = inverse * scaled - value_in * inverse**3 * jnp.mean(scaled * value_in, axis=-1, keepdims=True)
    return (backward, upstream * value_in * inverse)


def rotate(value_in, cosine, sine_rows):
    half_dim = value_in.shape[-1] // 2
    turned = jnp.concatenate([-value_in[..., half_dim:], value_in[..., :half_dim]], axis=-1)
    return value_in * cosine + turned * sine_rows


def rotate_back(upstream, cosine, sine_rows):
    half_dim = upstream.shape[-1] // 2
    turned = jnp.concatenate([upstream[..., half_dim:], -upstream[..., :half_dim]], axis=-1)
    return upstream * cosine + turned * sine_rows


def by_head(rows):
    r = rows.reshape(2, 2, SPAN, HH, GROUP, HD)
    return r.transpose(0, 3, 1, 4, 2, 5).reshape(2, HH, 2, QROWS, HD)


def by_token(heads):
    r = heads.reshape(2, HH, 2, GROUP, SPAN, HD)
    return r.transpose(0, 2, 4, 1, 3, 5).reshape(2 * TOK, QH, HD)


def body(layer_input, w_qkv, w_out, w_gate_up, w_down, norm_gains, span_map, cotangent):
    at = here()
    core, low = at["core"], at["l"]
    w_q = w_qkv[:, : HQ * HD].reshape(16, 2, QW).transpose(1, 0, 2)
    w_k = w_qkv[:, HQ * HD : (HQ + HK) * HD].reshape(16, 2, HH, HD)
    w_v = w_qkv[:, (HQ + HK) * HD :].reshape(16, 2, HH, HD)
    w_kv = jnp.concatenate([w_k, w_v], axis=3).reshape(16, 2, KVW).transpose(1, 0, 2)
    gains_row = jnp.pad(norm_gains[None, None, :], ((0, 1), (0, 15), (0, 128 - norm_gains.shape[0])))
    gains_row = jnp.broadcast_to(gains_row[:1], (2, 16, 128))
    shard_one = jnp.concatenate([w_q, w_kv, gains_row], axis=2)
    shard_gate = w_gate_up[:, :FF].reshape(16, 2, FH).transpose(1, 0, 2)
    shard_up = w_gate_up[:, FF:].reshape(16, 2, FH).transpose(1, 0, 2)
    shard_down = w_down.reshape(16, 2, FH).transpose(1, 0, 2)
    shard_out = w_out.reshape(16, 2, QW).transpose(1, 0, 2)

    one_parts = (((0, 384, ORDERS[0]), (384, 384, ORDERS[1]), (768, 512, ORDERS[2])),)
    w_one, x_pair, dy_pair = gather_weights([shard_one], one_parts, [layer_input[0], cotangent[0]], 1)
    w_one = w_one.reshape(D, QW + KVW + 128)
    gain_full = w_one.reshape(128, 16, -1)[:, 0, QW + KVW : QW + KVW + 33].reshape(-1).astype(F32)
    gain_one, gain_two = gain_full[:D], gain_full[D : 2 * D]
    gain_query, gain_key = gain_full[2 * D : 2 * D + HD], gain_full[2 * D + HD :]
    w_joined = w_one[:, : QW + KVW]

    ctx_index = lax.axis_index("ctx")
    maps = lax.dynamic_slice_in_dim(span_map, low * 2, 2, 0)
    own_span = lax.dynamic_slice_in_dim(maps, ctx_index, 1, 1)
    spans = jnp.concatenate([own_span, 2 * N_CTX - 1 - own_span], axis=1)
    positions = (spans[:, :, None] * SPAN + jnp.arange(SPAN, dtype=jnp.int32)).reshape(2 * TOK)
    match = maps[:, None, :] == jnp.arange(N_CTX, dtype=jnp.int32)[None, :, None]
    inverse_map = jnp.sum(jnp.where(match, jnp.arange(N_CTX, dtype=jnp.int32), 0), axis=2)
    tab = jnp.concatenate([inverse_map * 2, inverse_map[:, ::-1] * 2 + 1, own_span], axis=1)
    half_dim = HD // 2
    frequencies = ROPE_BASE ** (-(jnp.arange(half_dim, dtype=F32) * 2.0 / HD))
    angles = positions.astype(F32)[:, None] * frequencies[None, :]
    cosine, sine_rows = jnp.cos(angles), jnp.sin(angles)
    cosine = jnp.concatenate([cosine, cosine], axis=1)[:, None, :]
    sine_rows = jnp.concatenate([sine_rows, sine_rows], axis=1)[:, None, :]

    stream_in = x_pair.reshape(2 * TOK, D).astype(F32)
    dy = dy_pair.reshape(2 * TOK, D)
    normed_one, inverse_one = norm_rows(stream_in, gain_one)
    normed_one = normed_one.astype(BF)
    joined = jnp.dot(normed_one, w_joined, preferred_element_type=F32)
    queries = joined[:, :QW].reshape(2 * TOK, QH, HD)
    kv_raw = joined[:, QW:].reshape(2 * TOK, HH, 2 * HD)
    keys_raw, values_raw = kv_raw[..., :HD], kv_raw[..., HD:]
    query_norm, inverse_query = norm_rows(queries, gain_query)
    key_norm, inverse_key = norm_rows(keys_raw, gain_key)
    query_rot = rotate(query_norm, cosine, sine_rows).astype(BF)
    key_rot = rotate(key_norm, cosine, sine_rows).astype(BF)
    kv_local = jnp.concatenate([key_rot, values_raw.astype(BF)], axis=2).reshape(2 * TOK, KVW)
    kvg = gather_kv(kv_local, 2).reshape(N_CTX, 2 * TOK, KVW)
    q_heads = by_head(query_rot)
    q_pad = jnp.pad(q_heads, ((0, 0),) * 4 + ((0, HD),))
    attn_f32, log_sum = attend(tab, q_pad, kvg)

    two_parts = (
        ((0, FH, ORDERS[0]),),
        ((0, FH, ORDERS[1]),),
        ((0, FH, ORDERS[2]),),
        ((0, 256, ORDERS[0]), (256, 256, ORDERS[1]), (512, 256, ORDERS[2])),
    )
    shards = [shard_gate, shard_up, shard_down, shard_out]
    w_gate, w_up, w_back, w_proj = (w.reshape(D, -1) for w in gather_weights(shards, two_parts, [], 3))

    attn_low = by_token(attn_f32.astype(BF)).reshape(2 * TOK, QW)
    partial_a = lax.dot_general(attn_low, w_proj, NT, preferred_element_type=F32)
    branch_a = partial_a + shift(partial_a, "core")
    middle = stream_in + branch_a
    normed_two, inverse_two = norm_rows(middle, gain_two)
    normed_two = normed_two.astype(BF)
    gate_part = jnp.dot(normed_two, w_gate, preferred_element_type=F32)
    up_part = jnp.dot(normed_two, w_up, preferred_element_type=F32)
    sigmoid_gate = jax.nn.sigmoid(gate_part)
    silu_gate = gate_part * sigmoid_gate
    hidden = (silu_gate * up_part).astype(BF)
    partial_f = lax.dot_general(hidden, w_back, NT, preferred_element_type=F32)
    grad_hidden = jnp.dot(dy, w_back, preferred_element_type=F32)
    grad_gate = (grad_hidden * up_part * sigmoid_gate * (1.0 + gate_part * (1.0 - sigmoid_gate))).astype(BF)
    grad_up = (grad_hidden * silu_gate).astype(BF)
    partial_n = lax.dot_general(grad_gate, w_gate, NT, preferred_element_type=F32)
    partial_n = partial_n + lax.dot_general(grad_up, w_up, NT, preferred_element_type=F32)

    def own_rows(value):
        return lax.dynamic_slice_in_dim(value, core * TOK, TOK, 0)

    def other_rows(value):
        return lax.dynamic_slice_in_dim(value, (1 - core) * TOK, TOK, 0)

    branch_f = own_rows(partial_f) + shift(other_rows(partial_f), "core")
    result = own_rows(middle) + branch_f
    grad_normed_two = partial_n + shift(partial_n, "core")
    back_two, gain_two_terms = norm_back(middle, inverse_two, gain_two, grad_normed_two)
    grad_middle = dy.astype(F32) + back_two
    grad_branch = grad_middle.astype(BF)

    row_gate = sum_at_owner(normed_two, grad_gate, ORDERS[0], at)
    row_up = sum_at_owner(normed_two, grad_up, ORDERS[1], at)
    row_down = sum_at_owner(dy, hidden, ORDERS[2], at)

    grad_attn = jnp.dot(grad_branch, w_proj, preferred_element_type=F32).astype(BF)
    d_heads = by_head(grad_attn.reshape(2 * TOK, QH, HD))
    delta = jnp.sum(d_heads.astype(F32) * attn_f32, axis=-1)[:, :, :, None, :]
    d_pad = jnp.pad(d_heads, ((0, 0),) * 4 + ((HD, 0),))
    qd = jnp.concatenate([q_pad, d_pad], axis=3)
    dq_heads, dkv = attend_back(tab, qd, log_sum, delta, kvg)
    grad_kv = sum_kv(dkv.reshape(2, 4, 4, 2 * TOK, KVW), 4).reshape(2 * TOK, HH, 2 * HD)

    grad_query_raw, query_gain_terms = norm_back(
        queries, inverse_query, gain_query, rotate_back(by_token(dq_heads), cosine, sine_rows)
    )
    grad_key_raw, key_gain_terms = norm_back(
        keys_raw, inverse_key, gain_key, rotate_back(grad_kv[..., :HD], cosine, sine_rows)
    )
    grad_kv_raw = jnp.concatenate([grad_key_raw, grad_kv[..., HD:]], axis=2).reshape(2 * TOK, KVW)
    grad_joined = jnp.concatenate([grad_query_raw.reshape(2 * TOK, QW), grad_kv_raw], axis=1).astype(BF)
    partial_one = lax.dot_general(grad_joined, w_joined, NT, preferred_element_type=F32)
    grad_normed_one = own_rows(partial_one) + shift(other_rows(partial_one), "core")
    back_one, gain_one_terms = norm_back(
        own_rows(stream_in), own_rows(inverse_one), gain_one, grad_normed_one
    )
    grad_input = own_rows(grad_middle) + back_one

    g_qkv = lax.dot_general(normed_one, grad_joined, TN, preferred_element_type=F32).astype(BF)
    g_out = lax.dot_general(grad_branch, attn_low, TN, preferred_element_type=F32).astype(BF)
    own_qkv, own_out = sum_weights(
        g_qkv.reshape(2, 4, 4, 2, 32, QW + KVW), g_out.reshape(2, 4, 4, 2, 32, QW), 5
    )

    def rows_of_half(value):
        mine = lax.dynamic_slice_in_dim(value, core * 16, 16, 0)
        theirs = shift(lax.dynamic_slice_in_dim(value, (1 - core) * 16, 16, 0), "core")
        first = core == 0
        return jnp.where(first, mine, theirs), jnp.where(first, theirs, mine)

    gate_halves = rows_of_half(row_gate)
    up_halves = rows_of_half(row_up)
    down_halves = rows_of_half(row_down)
    grad_mlp = jnp.concatenate([*gate_halves, *up_halves], axis=1)
    grad_down = jnp.concatenate(down_halves, axis=1)
    kv_cols = own_qkv[:, :, QW:].reshape(2, 16, HH, 2, HD)
    grad_qkv = jnp.concatenate(
        [
            own_qkv[0, :, :QW],
            own_qkv[1, :, :QW],
            *(kv_cols[half, :, :, kind].reshape(16, HH * HD) for kind in range(2) for half in range(2)),
        ],
        axis=1,
    )
    grad_proj = jnp.concatenate([own_out[0], own_out[1]], axis=1)

    def mean_root(stream):
        return jnp.sum(jnp.sqrt(jnp.mean(stream * stream, axis=-1)))

    stats = jnp.stack([mean_root(own_rows(s)) for s in (stream_in, branch_a, middle)] + [mean_root(branch_f)])
    sums = jnp.concatenate(
        [
            jnp.sum(gain_one_terms, axis=0),
            jnp.sum(own_rows(gain_two_terms), axis=0),
            jnp.sum(query_gain_terms, axis=(0, 1)),
            jnp.sum(key_gain_terms, axis=(0, 1)),
            stats,
        ]
    )
    sums = jnp.pad(sums, (0, 40 * 128 - sums.shape[0])).reshape(40, 128)
    sums = total_everywhere(sums, 6).reshape(-1)
    share = norm_gains.shape[0]
    own_gains = lax.dynamic_slice_in_dim(sums, lax.axis_index(("ctx", "fsdp")) * share, share, 0)
    stream_rms = sums[4224:4228] / (TOK * N_CTX * 4)
    return (
        result[None].astype(BF),
        grad_input[None].astype(BF),
        grad_qkv,
        grad_proj,
        grad_mlp,
        grad_down,
        own_gains,
        stream_rms,
    )


def solution(mesh):
    rows = P(("ctx", "fsdp"), None)
    tokens = P("fsdp", "ctx", None)
    return jax.shard_map(
        body,
        mesh=mesh,
        in_specs=(tokens, rows, rows, rows, rows, P(("ctx", "fsdp")), P(), tokens),
        out_specs=(tokens, tokens, rows, rows, rows, rows, P(("ctx", "fsdp")), P()),
        check_vma=False,
    )
```

```python
import functools

import jax
import jax.numpy as jnp
from jax import lax
from jax.experimental import pallas as pl
from jax.experimental.pallas import tpu as pltpu
from jax.sharding import PartitionSpec as P

D = 2048
HQ = 24
HK = 6
HD = 64
FF = 4352
TOK = 128
SPAN = 64
N_CTX = 32

HH = HK // 2
GROUP = HQ // HK
QH = HQ // 2
QW = QH * HD
KVW = HH * 2 * HD
FH = FF // 2
KEYS = 512
SPANS_STEP = KEYS // SPAN
FULL_STEPS = 7
QROWS = GROUP * SPAN

EPSILON = 1e-06
ROPE_BASE = 10000.0
LOG2E = 1.4426950408889634
MESH = pl.DeviceIdType.MESH
BF = jnp.bfloat16
F32 = jnp.float32
NT = (((1,), (1,)), ((), ()))
NN = (((1,), (0,)), ((), ()))
TN = (((0,), (0,)), ((), ()))
W_DIMS = ("h", "x", "y", "l")
KV_DIMS = ("h", "x", "y")
ORDERS = (("x", "y", "z"), ("y", "z", "x"), ("z", "x", "y"))
KV_ORDERS = (("h", "x", "y"), ("x", "y", "h"), ("y", "h", "x"))
KV_SUM_ORDERS = (("y", "x", "h"), ("h", "y", "x"), ("x", "h", "y"))
SUMS = (
    (0, 0, 1152, ORDERS[0]),
    (1, 0, 1152, ORDERS[1]),
    (2, 0, 1152, ORDERS[2]),
    (0, 1152, 1024, ORDERS[0]),
    (1, 1152, 1024, ORDERS[1]),
    (2, 1152, 1024, ORDERS[2]),
    (4, 0, 384, ORDERS[0]),
    (4, 384, 384, ORDERS[1]),
    (4, 768, 384, ORDERS[2]),
    (3, 0, 256, ORDERS[0]),
    (3, 256, 256, ORDERS[1]),
    (3, 512, 256, ORDERS[2]),
)
SIZES = {"x": 4, "y": 4, "z": 4, "h": 2}


def here():
    c = lax.axis_index("ctx")
    f = lax.axis_index("fsdp")
    return {
        "x": lax.rem(lax.div(c, 4), 4),
        "y": lax.rem(c, 4),
        "z": lax.div(c, 16) * 2 + lax.div(f, 2),
        "h": lax.div(c, 16),
        "l": lax.div(f, 2),
        "core": lax.rem(f, 2),
    }


def device_of(x, y, z, core):
    return (lax.div(z, 2) * 16 + x * 4 + y, lax.rem(z, 2) * 2 + core)


def moved(at, axis, by):
    if axis == "core":
        return device_of(at["x"], at["y"], at["z"], 1 - at["core"])
    place = {k: at[k] for k in ("x", "y", "z")}
    if axis == "h":
        place["z"] = lax.rem(at["z"] + 2, 4)
    else:
        place[axis] = lax.rem(at[axis] + by + 4, 4)
    return device_of(place["x"], place["y"], place["z"], at["core"])


def labels(axis, value):
    if axis == "z":
        return {"h": lax.div(value, 2), "l": lax.rem(value, 2)}
    return {axis: value}


def pick(ref, dims, values, tail):
    return ref.at[tuple(values[d] if d in values else slice(None) for d in dims) + tail]


def greet(devices):
    barrier = pltpu.get_barrier_semaphore()
    for d in devices:
        pl.semaphore_signal(barrier, inc=1, device_id=d, device_id_type=MESH)
    pl.semaphore_wait(barrier, len(devices))


def send(src, dst, ssem, rsem, device):
    copy = pltpu.make_async_remote_copy(
        src_ref=src, dst_ref=dst, send_sem=ssem, recv_sem=rsem, device_id=device, device_id_type=MESH
    )
    copy.start()
    return copy


class Gathering:
    def __init__(self, ref, dims, at, order, rows, cols, ssem, rsem):
        self.ref, self.dims, self.at, self.order, self.rows, self.cols = ref, dims, at, order, rows, cols
        self.ssem, self.rsem, self.phase, self.sent = ssem, rsem, 0, []

    def block(self, coordinate, rows):
        later = {}
        for a in self.order[self.phase + 1 :]:
            later.update(labels(a, self.at[a]))
        return pick(self.ref, self.dims, {**later, **labels(self.axis, coordinate)}, (rows, self.cols))

    def send(self, n, ref, by):
        c = send(ref, ref, self.ssem.at[self.phase, n], self.rsem.at[self.phase, n], moved(self.at, self.axis, by))
        self.sent.append(c)
        return c

    def start(self):
        self.axis = self.order[self.phase]
        mine = self.block(self.at[self.axis], slice(None))
        self.first = [self.send(0, mine, 1)]
        if SIZES[self.axis] == 4:
            self.first.append(self.send(1, mine, 3))

    def pass_on(self):
        for c in self.first:
            c.wait_recv()
        self.second = []
        if SIZES[self.axis] == 4:
            half = self.rows // 2
            me = self.at[self.axis]
            self.second.append(self.send(2, self.block(lax.rem(me + 3, 4), pl.ds(0, half)), 1))
            self.second.append(self.send(3, self.block(lax.rem(me + 1, 4), pl.ds(half, half)), 3))

    def finish(self):
        for c in self.second:
            c.wait_recv()
        self.phase += 1

    def wait_sent(self):
        for c in self.sent:
            c.wait_send()


def neighbours(at, axes):
    out = []
    for a in axes:
        if a in ("core", "h"):
            out.append(moved(at, a, 1))
        else:
            out.append(moved(at, a, 1))
            out.append(moved(at, a, 3))
    return out


GATHER = (
    (0, 0, 1152, ORDERS[0]),
    (1, 0, 1152, ORDERS[1]),
    (2, 0, 1152, ORDERS[2]),
    (0, 1152, 1024, ORDERS[0]),
    (1, 1152, 1024, ORDERS[1]),
    (2, 1152, 1024, ORDERS[2]),
    (3, 0, 256, ORDERS[0]),
    (3, 256, 256, ORDERS[1]),
    (3, 512, 256, ORDERS[2]),
)


def lane_of(shape):
    return lax.broadcasted_iota(jnp.int32, shape, len(shape) - 1)


def swap_halves(v):
    return jnp.where(lax.rem(lane_of(v.shape), HD) < HD // 2, pltpu.roll(v, 96, 1), pltpu.roll(v, 32, 1))


def head_sums(v):
    low = lane_of(v.shape) < HD
    a = jnp.sum(jnp.where(low, v, 0.0), axis=1, keepdims=True)
    b = jnp.sum(jnp.where(low, 0.0, v), axis=1, keepdims=True)
    return jnp.where(low, a, b)


def tile_gain(row, is_key):
    low = lane_of(row.shape) < HD
    turned = pltpu.roll(row, HD, 1)
    return jnp.where(low, turned, 1.0) if is_key else jnp.where(low, row, turned)


def front_kernel(
    shard_one, shard_gate, shard_up, shard_down, shard_out, x, dy, gains, cosine, sine,
    w_one, w_gate, w_up, w_down, w_out, x_pair, dy_pair, gain_all, joined, normed, query, kvg,
    one, kv_src, small_buf, psem, lsem, tssem, trsem, ossem, orsem, gssem, grsem, kssem, krsem, ksem,
):
    at = here()
    core = at["core"]
    sibling = moved(at, "core", 1)
    greet([sibling] + sum_peers(at, ("x", "y", "z")))
    own = {d: at[d] for d in W_DIMS}
    total = Total(gains[...], at, small_buf, tssem, trsem)
    remote, local = [], []
    pairs = [(shard_one, one), (shard_gate, w_gate), (shard_up, w_up), (shard_down, w_down), (shard_out, w_out)]
    for i, (src, ref) in enumerate(pairs):
        dst = pick(ref, W_DIMS, own, (pl.ds(core * 16, 16), slice(None)))
        remote.append(send(src.at[1 - core], dst, psem.at[i, 0], psem.at[i, 1], sibling))
        local.append(pltpu.make_async_copy(src.at[core], dst, lsem.at[i]))
        local[-1].start()
    for i, (src, ref) in ((5, (x, x_pair)), (6, (dy, dy_pair))):
        remote.append(send(src, ref.at[core], psem.at[i, 0], psem.at[i, 1], sibling))
        local.append(pltpu.make_async_copy(src, ref.at[core], lsem.at[i]))
        local[-1].start()

    def arrived(i):
        remote[i].wait_recv()
        local[i].wait()

    ones = [
        Gathering(one, W_DIMS, at, ORDERS[k], 32, pl.ds(k * 384, 384), ossem.at[k], orsem.at[k]) for k in range(3)
    ]
    rest = [
        Gathering(pairs[1 + a][1], W_DIMS, at, order, 32, pl.ds(start, width), gssem.at[k], grsem.at[k])
        for k, (a, start, width, order) in enumerate(GATHER)
    ]
    kvs = [
        Gathering(kvg.at[h], KV_DIMS, at, KV_ORDERS[h], 2 * TOK, slice(None), kssem.at[h], krsem.at[h]) for h in range(HH)
    ]

    def every(streams, *steps):
        for s in streams:
            for step in steps:
                getattr(s, step)()

    arrived(0)
    every(ones, "start")
    for i in range(1, 5):
        arrived(i)
    every(rest, "start")
    total.step()
    every(ones, "pass_on")
    every(rest, "pass_on")
    total.step()
    every(ones, "finish", "start")
    every(rest, "finish")
    total.step()
    every(ones, "pass_on")
    total.step()
    gain_all[...] = total.value
    every(ones, "finish", "start")
    every(rest, "start")
    arrived(5)
    gain_row = jnp.concatenate([total.value[j : j + 1] for j in range(D // 128)], axis=1)

    def norm(r, carry):
        rows = pl.ds(pl.multiple_of(r * 32, 32), 32)
        for s in range(2):
            v = x_pair[s, rows, :].astype(F32)
            inverse = lax.rsqrt(jnp.sum(v * v, axis=1, keepdims=True) * (1.0 / D) + EPSILON)
            normed[pl.ds(pl.multiple_of(s * TOK + r * 32, 32), 32), :] = (v * inverse * gain_row).astype(BF)
        return carry

    lax.fori_loop(0, TOK // 32, norm, 0)
    every(ones, "pass_on")
    every(ones, "finish")
    keep = pltpu.make_async_copy(one, w_one, lsem.at[7])
    keep.start()
    head_gains = total.value[32:33]

    def product(start, width):
        w = one[:, :, :, :, :, start : start + width].reshape(D, width)
        joined[:, start : start + width] = jnp.dot(normed[...], w, preferred_element_type=F32)

    def rope(tile, is_key):
        v = joined[:, tile * 128 : (tile + 1) * 128]
        low = lane_of(v.shape) < HD
        c, n = cosine[...], sine[...]
        inverse = lax.rsqrt(head_sums(v * v) * (1.0 / HD) + EPSILON)
        if is_key:
            inverse = jnp.where(low, inverse, 1.0)
            c, n = jnp.where(low, c, 1.0), jnp.where(low, n, 0.0)
        v = v * inverse * tile_gain(head_gains, is_key)
        return (v * c + swap_halves(v) * n).astype(BF)

    product(QW, KVW)
    for h in range(HH):
        kv_src[h] = rope(QW // 128 + h, True)
    kv_own = {d: at[d] for d in KV_DIMS}
    puts = [pltpu.make_async_copy(kv_src.at[h], pick(kvg.at[h], KV_DIMS, kv_own, ()), ksem.at[h]) for h in range(HH)]
    for c in puts:
        c.start()
    for c in puts:
        c.wait()
    every(kvs, "start")
    every(rest, "pass_on")
    product(0, 384)
    every(kvs, "pass_on")
    every(rest, "finish", "start")
    product(384, 384)
    every(kvs, "finish", "start")
    for t in range(QW // 128):
        query[:, t * 128 : (t + 1) * 128] = rope(t, False)
    every(kvs, "pass_on")
    every(kvs, "finish", "start")
    every(rest[:3], "pass_on")
    every(kvs, "pass_on")
    every(rest[3:], "pass_on")
    every(kvs, "finish")
    every(rest, "finish")
    arrived(6)
    keep.wait()
    for c in remote + total.sent:
        c.wait_send()
    for s in ones + rest + kvs:
        s.wait_sent()


def front(shards, x, dy, gains, cosine, sine, cid):
    anywhere = pl.BlockSpec(memory_space=pl.ANY)
    vmem = pl.BlockSpec(memory_space=pltpu.VMEM)
    full = [jax.ShapeDtypeStruct((2, 4, 4, 2, 32, s.shape[-1]), BF) for s in shards]
    n = len(GATHER)
    return pl.pallas_call(
        front_kernel,
        out_shape=full
        + [
            jax.ShapeDtypeStruct((2,) + x.shape, BF),
            jax.ShapeDtypeStruct((2,) + dy.shape, BF),
            jax.ShapeDtypeStruct(gains.shape, F32),
            jax.ShapeDtypeStruct((2 * TOK, QW + KVW), F32),
            jax.ShapeDtypeStruct((2 * TOK, D), BF),
            jax.ShapeDtypeStruct((2 * TOK, QW), BF),
            jax.ShapeDtypeStruct((HH, 2, 4, 4, 2 * TOK, 2 * HD), BF),
        ],
        in_specs=[anywhere] * 7 + [vmem] * 3,
        out_specs=[anywhere] * 5 + [vmem, anywhere] + [vmem] * 4 + [anywhere],
        scratch_shapes=[
            pltpu.VMEM((2, 4, 4, 2, 32, QW + KVW), BF),
            pltpu.VMEM((HH, 2 * TOK, 2 * HD), BF),
            pltpu.VMEM((4, 4) + gains.shape, F32),
            pltpu.SemaphoreType.DMA((7, 2)),
            pltpu.SemaphoreType.DMA((8,)),
            pltpu.SemaphoreType.DMA((4, 4)),
            pltpu.SemaphoreType.DMA((4, 4)),
            pltpu.SemaphoreType.DMA((3, 3, 4)),
            pltpu.SemaphoreType.DMA((3, 3, 4)),
            pltpu.SemaphoreType.DMA((n, 3, 4)),
            pltpu.SemaphoreType.DMA((n, 3, 4)),
            pltpu.SemaphoreType.DMA((HH, 3, 4)),
            pltpu.SemaphoreType.DMA((HH, 3, 4)),
            pltpu.SemaphoreType.DMA((HH,)),
        ],
        compiler_params=pltpu.CompilerParams(
            collective_id=cid, has_side_effects=True, vmem_limit_bytes=32 * 1024 * 1024
        ),
        name="front",
    )(*shards, x, dy, gains, cosine, sine)


def rope_back_kernel(joined, dq, dkv, gains, cosine, sine, out, terms):
    head_gains = gains[32:33]

    def tile(t, is_key, grad):
        v = joined[:, t * 128 : (t + 1) * 128]
        low = lane_of(v.shape) < HD
        back = grad * cosine[...] - swap_halves(grad) * sine[...]
        inverse = lax.rsqrt(head_sums(v * v) * (1.0 / HD) + EPSILON)
        scaled = back * tile_gain(head_gains, is_key)
        inner = head_sums(scaled * v) * (1.0 / HD)
        result = inverse * scaled - v * (inverse * inverse * inverse) * inner
        if is_key:
            result = jnp.where(low, result, grad)
        out[:, t * 128 : (t + 1) * 128] = result.astype(BF)
        return jnp.sum(back * v * inverse, axis=0, keepdims=True)

    q_terms = sum(tile(t, False, dq[:, t * 128 : (t + 1) * 128]) for t in range(QW // 128))
    k_terms = sum(tile(QW // 128 + h, True, dkv[h]) for h in range(HH))
    low = lane_of(q_terms.shape) < HD
    q_terms = q_terms + pltpu.roll(q_terms, HD, 1)
    terms[...] = jnp.where(low, q_terms, pltpu.roll(k_terms, HD, 1))


def rope_back(joined, dq, dkv, gains, cosine, sine):
    vmem = pl.BlockSpec(memory_space=pltpu.VMEM)
    return pl.pallas_call(
        rope_back_kernel,
        out_shape=[jax.ShapeDtypeStruct((2 * TOK, QW + KVW), BF), jax.ShapeDtypeStruct((1, 128), F32)],
        in_specs=[vmem] * 6,
        out_specs=[vmem] * 2,
        compiler_params=pltpu.CompilerParams(vmem_limit_bytes=32 * 1024 * 1024),
        name="rope_back",
    )(joined, dq, dkv, gains, cosine, sine)


def lead_shape(dims):
    full = {"h": 2, "x": 4, "y": 4, "l": 2}
    return tuple(full[d] for d in dims)


def without(dims, axis):
    gone = ("h", "l") if axis == "z" else (axis,)
    return tuple(d for d in dims if d not in gone)


class Summing:
    def __init__(self, source, dims, at, order, rows, cols, buffers, ssem, rsem, lsem):
        self.ref, self.dims, self.at, self.order = source, dims, at, order
        self.cols, self.buffers, self.rows = cols, buffers, rows
        self.ssem, self.rsem, self.lsem = ssem, rsem, lsem
        self.phase, self.sent = 0, []

    def part(self, coordinate, rows):
        return pick(self.ref, self.dims, labels(self.axis, coordinate), (rows, self.cols))

    def send(self, n, src, dst, by):
        c = send(src, dst, self.ssem.at[self.phase, n], self.rsem.at[self.phase, n], moved(self.at, self.axis, by))
        self.sent.append(c)
        return c

    def start(self):
        self.axis = self.order[self.phase]
        self.rest = without(self.dims, self.axis)
        self.lead = lead_shape(self.rest)
        half = self.rows // 2
        first, second, every = pl.ds(0, half), pl.ds(half, half), pl.ds(0, self.rows)
        i = self.at[self.axis]
        buf = self.buffers[self.phase]
        self.local = []
        if SIZES[self.axis] == 2:
            self.direct = (self.send(0, self.part(1 - i, every), buf["got"].at[0], 1),)
        else:
            up, down, far = lax.rem(i + 1, 4), lax.rem(i + 3, 4), lax.rem(i + 2, 4)
            self.relay = (
                self.send(0, self.part(far, first), buf["relay"].at[0], 1),
                self.send(1, self.part(far, second), buf["relay"].at[1], 3),
            )
            self.direct = (
                self.send(2, self.part(up, second), buf["got"].at[1, 1], 1),
                self.send(3, self.part(down, first), buf["got"].at[0, 1], 3),
            )
            self.near = (up, down)
        if self.phase == 0:
            todo = [(self.part(i, every), buf["mine"])]
            if SIZES[self.axis] == 4:
                todo.append((self.part(up, first), buf["own"].at[0]))
                todo.append((self.part(down, second), buf["own"].at[1]))
            for n, (src, dst) in enumerate(todo):
                c = pltpu.make_async_copy(src, dst, self.lsem.at[n])
                c.start()
                self.local.append(c)

    def over_lead(self, add):
        rest = self.lead[1:]
        spots = [()]
        for n in rest:
            spots = [s + (j,) for s in spots for j in range(n)]
        if not self.lead:
            add(())
            return

        def go(j, carry):
            for s in spots:
                add((j,) + s)
            return carry

        lax.fori_loop(0, self.lead[0], go, 0)

    def pass_on(self):
        if SIZES[self.axis] == 2:
            return
        buf = self.buffers[self.phase]
        half = self.rows // 2
        for n, by in ((0, 1), (1, 3)):
            self.relay[n].wait_recv()
            if self.phase == 0:
                self.local[1 + n].wait()
                own = buf["own"].at[n]
            else:
                own = self.part(self.near[n], pl.ds(n * half, half))

            def add(spot):
                here_ = spot + (slice(None), slice(None))
                both = buf["relay"][(n,) + here_].astype(F32) + own[here_].astype(F32)
                buf["relay"][(n,) + here_] = both.astype(BF)

            self.over_lead(add)
            c = self.send(4 + n, buf["relay"].at[n], buf["got"].at[n, 0], by)
            self.direct = self.direct + (c,)

    def finish(self):
        buf = self.buffers[self.phase]
        half = self.rows // 2
        if self.local:
            self.local[0].wait()
        for c in self.direct:
            c.wait_recv()
        own = buf["mine"] if self.phase == 0 else self.part(self.at[self.axis], pl.ds(0, self.rows))
        out = buf["mine"] if self.phase == 0 else buf["sum"]

        def add(spot):
            if SIZES[self.axis] == 2:
                here_ = spot + (slice(None), slice(None))
                out[here_] = (own[here_].astype(F32) + buf["got"][(0,) + here_].astype(F32)).astype(out.dtype)
                return
            for n in range(2):
                rows = spot + (pl.ds(n * half, half), slice(None))
                all_ = spot + (slice(None), slice(None))
                total = own[rows].astype(F32) + buf["got"][(n, 0) + all_].astype(F32)
                total = total + buf["got"][(n, 1) + all_].astype(F32)
                out[rows] = total.astype(out.dtype)

        self.over_lead(add)
        self.ref, self.dims, self.cols = out, self.rest, slice(None)
        self.phase += 1


class Total:
    def __init__(self, value, at, buf, ssem, rsem):
        self.value, self.at, self.buf, self.ssem, self.rsem = value, at, buf, ssem, rsem
        self.phase, self.sent = 0, []
        self.start()

    def start(self):
        n, axis = self.phase, ("core", "z", "y", "x")[self.phase]
        self.buf[n, 0] = self.value
        self.copies = []
        for i in (1, 3, 2) if axis != "core" else (1,):
            self.copies.append(
                send(self.buf.at[n, 0], self.buf.at[n, i], self.ssem.at[n, i], self.rsem.at[n, i], moved(self.at, axis, i))
            )

    def step(self):
        n, buf = self.phase, self.buf
        if n == 4:
            return
        for c in self.copies:
            c.wait_recv()
            self.sent.append(c)
        if n == 0:
            self.value = buf[n, 0] + buf[n, 1]
        else:
            self.value = (buf[n, 0] + buf[n, 2]) + (buf[n, 1] + buf[n, 3])
        self.phase += 1
        if self.phase < 4:
            self.start()


def run_sums(streams, total=None):
    for s in streams:
        s.start()
    for phase in range(3):
        for s in streams:
            s.pass_on()
        if total is not None:
            total.step()
        for s in streams:
            s.finish()
            if phase < 2:
                s.start()
        if total is not None:
            total.step()
    for s in streams:
        for c in s.sent:
            c.wait_send()


def sum_scratch(order, dims, rows, width):
    buffers = []
    for phase, axis in enumerate(order):
        rest = without(dims, axis)
        lead = lead_shape(rest)
        buf = {}
        if SIZES[axis] == 2:
            buf["got"] = pltpu.VMEM((1,) + lead + (rows, width), BF)
        else:
            buf["got"] = pltpu.VMEM((2, 2) + lead + (rows // 2, width), BF)
            buf["relay"] = pltpu.VMEM((2,) + lead + (rows // 2, width), BF)
        if phase == 0:
            buf["mine"] = pltpu.VMEM(lead + (rows, width), BF)
            if SIZES[axis] == 4:
                buf["own"] = pltpu.VMEM((2,) + lead + (rows // 2, width), BF)
        else:
            buf["sum"] = pltpu.VMEM(lead + (rows, width), BF if phase < 2 else F32)
        buffers.append(buf)
        dims = rest
    return buffers


def kv_sum_kernel(src, out, buffers, ssem, rsem, lsem):
    at = here()
    greet(neighbours(at, ("h", "x", "y")))
    streams = [
        Summing(src.at[h], KV_DIMS, at, KV_SUM_ORDERS[h], 2 * TOK, slice(None), buffers[h], ssem.at[h], rsem.at[h], lsem.at[h])
        for h in range(HH)
    ]
    run_sums(streams)
    for h in range(HH):
        out[h] = buffers[h][2]["sum"][...]


def sum_kv(grads, cid):
    return pl.pallas_call(
        kv_sum_kernel,
        out_shape=jax.ShapeDtypeStruct((HH, 2 * TOK, 2 * HD), F32),
        in_specs=[pl.BlockSpec(memory_space=pl.ANY)],
        out_specs=pl.BlockSpec(memory_space=pltpu.VMEM),
        scratch_shapes=[
            [sum_scratch(KV_SUM_ORDERS[h], KV_DIMS, 2 * TOK, 2 * HD) for h in range(HH)],
            pltpu.SemaphoreType.DMA((HH, 3, 6)),
            pltpu.SemaphoreType.DMA((HH, 3, 6)),
            pltpu.SemaphoreType.DMA((HH, 3)),
        ],
        compiler_params=pltpu.CompilerParams(
            collective_id=cid, has_side_effects=True, vmem_limit_bytes=48 * 1024 * 1024
        ),
        name="sum_kv",
    )(grads)


def weight_sum_kernel(pieces, n, *refs):
    ins, small, outs, small_out = refs[:n], refs[n], refs[n + 1 : 2 * n + 1], refs[2 * n + 1]
    buffers, stages, swapped, small_buf, ssem, rsem, lsem, csem, tssem, trsem = refs[2 * n + 2 :]
    at = here()
    core = at["core"]
    sibling = moved(at, "core", 1)
    greet([sibling] + sum_peers(at, ("x", "y", "z")))
    streams = [
        Summing(ins[a], W_DIMS, at, order, 32, pl.ds(start, width), buffers[k], ssem.at[k], rsem.at[k], lsem.at[k])
        for k, (a, start, width, order) in enumerate(pieces)
    ]
    total = Total(small[...], at, small_buf, tssem, trsem)
    run_sums(streams, total)
    small_out[...] = total.value
    for k, (a, start, width, order) in enumerate(pieces):
        stages[a][:, start : start + width] = buffers[k][2]["sum"][...]
    other = pl.ds(pl.multiple_of((1 - core) * 16, 16), 16)
    own = pl.ds(pl.multiple_of(core * 16, 16), 16)
    copies = [send(stages[a].at[other], swapped[a], csem.at[a, 0], csem.at[a, 1], sibling) for a in range(n)]
    for a in range(n):
        outs[a][core] = stages[a][own, :]
        copies[a].wait_recv()
        outs[a][1 - core] = swapped[a][...]
    for c in copies + total.sent:
        c.wait_send()


def sum_weights(grads, small, pieces, cid, limit):
    n, k = len(grads), len(pieces)
    anywhere = pl.BlockSpec(memory_space=pl.ANY)
    vmem = pl.BlockSpec(memory_space=pltpu.VMEM)
    widths = [g.shape[-1] for g in grads]
    return pl.pallas_call(
        functools.partial(weight_sum_kernel, pieces, n),
        out_shape=[jax.ShapeDtypeStruct((2, 16, w), F32) for w in widths] + [jax.ShapeDtypeStruct(small.shape, F32)],
        in_specs=[anywhere] * n + [vmem],
        out_specs=[vmem] * (n + 1),
        scratch_shapes=[
            [sum_scratch(order, W_DIMS, 32, width) for a, start, width, order in pieces],
            [pltpu.VMEM((32, w), F32) for w in widths],
            [pltpu.VMEM((16, w), F32) for w in widths],
            pltpu.VMEM((4, 4) + small.shape, F32),
            pltpu.SemaphoreType.DMA((k, 3, 6)),
            pltpu.SemaphoreType.DMA((k, 3, 6)),
            pltpu.SemaphoreType.DMA((k, 3)),
            pltpu.SemaphoreType.DMA((n, 2)),
            pltpu.SemaphoreType.DMA((4, 4)),
            pltpu.SemaphoreType.DMA((4, 4)),
        ],
        compiler_params=pltpu.CompilerParams(collective_id=cid, has_side_effects=True, vmem_limit_bytes=limit),
        name="sum_weights",
    )(*[g.reshape(2, 4, 4, 2, 32, g.shape[-1]) for g in grads], small)


def sum_peers(at, axes):
    out = []
    for a in axes:
        for i in (1, 3, 2) if SIZES[a] == 4 else (1,):
            out.append(moved(at, a, i))
    return out


def fetch_keys(tab, kvg, kv, sems):
    for s in range(2):
        for h in range(HH):

            def go(p, carry):
                slot = tab[s, p]
                row = lax.rem(slot, 2) * SPAN + s * TOK
                pltpu.make_async_copy(
                    kvg.at[h, lax.div(slot, 2), pl.ds(pl.multiple_of(row, SPAN), SPAN)],
                    kv.at[s, h, pl.ds(pl.multiple_of(p * SPAN, SPAN), SPAN)],
                    sems.at[s, h],
                ).start()
                return carry

            lax.fori_loop(0, 2 * N_CTX, go, 0)


def step_of(t, low_steps):
    half = jnp.where(t < low_steps, 0, 1)
    return half, jnp.where(t < low_steps, t, t - low_steps)


def heads_at(ref, s, h, half, width=HD):
    rows = slice(s * TOK + half * SPAN, s * TOK + (half + 1) * SPAN)
    return jnp.concatenate([ref[rows, (h * GROUP + g) * HD : (h * GROUP + g + 1) * HD] for g in range(GROUP)], axis=0)


def put_heads(ref, s, h, half, value):
    rows = slice(s * TOK + half * SPAN, s * TOK + (half + 1) * SPAN)
    for g in range(0, GROUP, 2):
        both = jnp.concatenate([value[g * SPAN : (g + 1) * SPAN], value[(g + 1) * SPAN : (g + 2) * SPAN]], axis=1)
        ref[rows, (h * GROUP + g) * HD : (h * GROUP + g + 2) * HD] = both.astype(ref.dtype)


def attend_kernel(tab, qr, kvg, o_ref, low_ref, l_ref, kv, q_ref, acc, total, sems):
    fetch_keys(tab, kvg, kv, sems)
    rate = LOG2E * HD**-0.5
    blank = jnp.zeros((QROWS, HD), BF)
    for s in range(2):
        for h in range(HH):
            for half in range(2):
                q_ref[s, h, half] = jnp.concatenate([heads_at(qr, s, h, half), blank], axis=1)
    for s in range(2):
        span = tab[s, 2 * N_CTX]
        low_steps = lax.div(span, SPANS_STEP)
        for h in range(HH):
            pltpu.make_async_copy(kv.at[s, h], kv.at[s, h], sems.at[s, h]).wait()
            acc[...] = jnp.zeros_like(acc)
            total[...] = jnp.zeros_like(total)

            def step(half, block, limit):
                keys = kv[s, h, pl.ds(pl.multiple_of(block * KEYS, KEYS), KEYS), :]
                scores = lax.dot_general(keys, q_ref[s, h, half], NT, preferred_element_type=F32)
                prob = jnp.exp2(scores * rate)
                if limit is not None:
                    row = lax.broadcasted_iota(jnp.int32, prob.shape, 0)
                    col = lax.rem(lax.broadcasted_iota(jnp.int32, prob.shape, 1), SPAN)
                    prob = jnp.where(row <= col + limit, prob, 0.0)
                total[half] += jnp.sum(prob, axis=0, keepdims=True)
                acc[half] += lax.dot_general(keys, prob.astype(BF), TN, preferred_element_type=F32)

            def full(t, carry):
                half, block = step_of(t, low_steps)
                step(half, block, None)
                return carry

            lax.fori_loop(0, FULL_STEPS, full, 0)
            for half, first in ((0, span), (1, 2 * N_CTX - 1 - span)):
                step(half, lax.div(first, SPANS_STEP), lax.rem(first, SPANS_STEP) * SPAN)
                out = (acc[half, HD:, :] / total[half]).T
                put_heads(o_ref, s, h, half, out)
                put_heads(low_ref, s, h, half, out)
                l_ref[s, h, half] = jnp.log2(total[half])


def attend(tab, query, kvg):
    vmem = pl.BlockSpec(memory_space=pltpu.VMEM)
    return pl.pallas_call(
        attend_kernel,
        out_shape=[
            jax.ShapeDtypeStruct((2 * TOK, QW), F32),
            jax.ShapeDtypeStruct((2 * TOK, QW), BF),
            jax.ShapeDtypeStruct((2, HH, 2, 1, QROWS), F32),
        ],
        in_specs=[pl.BlockSpec(memory_space=pltpu.SMEM), vmem, pl.BlockSpec(memory_space=pl.ANY)],
        out_specs=[vmem, vmem, vmem],
        scratch_shapes=[
            pltpu.VMEM((2, HH, N_CTX * TOK, 2 * HD), BF),
            pltpu.VMEM((2, HH, 2, QROWS, 2 * HD), BF),
            pltpu.VMEM((2, 2 * HD, QROWS), F32),
            pltpu.VMEM((2, 1, QROWS), F32),
            pltpu.SemaphoreType.DMA((2, HH)),
        ],
        compiler_params=pltpu.CompilerParams(vmem_limit_bytes=32 * 1024 * 1024),
        name="attend",
    )(tab, query, kvg)


def attend_back_kernel(
    tab, qr, da, attn, l_ref, kvg, dq_ref, dkv_ref, kv, qd_ref, delta_ref, stage, acc, dq_acc, sems, osems
):
    fetch_keys(tab, kvg, kv, sems)
    blank = jnp.zeros((QROWS, HD), BF)
    for s in range(2):
        for h in range(HH):
            for half in range(2):
                grads = heads_at(da, s, h, half)
                qd_ref[s, h, half, :QROWS] = jnp.concatenate([heads_at(qr, s, h, half), blank], axis=1)
                qd_ref[s, h, half, QROWS:] = jnp.concatenate([blank, grads], axis=1)
                inner = (grads.astype(F32) * heads_at(attn, s, h, half)).T
                delta_ref[s, h, half] = jnp.sum(inner, axis=0, keepdims=True)
    rate = LOG2E * HD**-0.5
    lanes = lax.broadcasted_iota(jnp.int32, (1, 2 * HD), 1)
    factor = jnp.where(lanes < HD, HD**-0.5, 1.0)
    for s in range(2):
        span = tab[s, 2 * N_CTX]
        low_steps = lax.div(span, SPANS_STEP)
        for h in range(HH):
            pltpu.make_async_copy(kv.at[s, h], kv.at[s, h], sems.at[s, h]).wait()
            dq_acc[...] = jnp.zeros_like(dq_acc)
            acc[...] = jnp.zeros_like(acc)

            def step(half, block, limit):
                rows = pl.ds(pl.multiple_of(block * KEYS, KEYS), KEYS)
                keys = kv[s, h, rows, :]
                both = lax.dot_general(keys, qd_ref[s, h, half], NT, preferred_element_type=F32)
                prob = jnp.exp2(both[:, :QROWS] * rate - l_ref[s, h, half])
                if limit is not None:
                    row = lax.broadcasted_iota(jnp.int32, prob.shape, 0)
                    col = lax.rem(lax.broadcasted_iota(jnp.int32, prob.shape, 1), SPAN)
                    prob = jnp.where(row <= col + limit, prob, 0.0)
                grad = (prob * (both[:, QROWS:] - delta_ref[s, h, half])).astype(BF)
                pair = jnp.concatenate([grad, prob.astype(BF)], axis=1)
                acc[rows, :] += lax.dot_general(pair, qd_ref[s, h, half], NN, preferred_element_type=F32)
                dq_acc[half] += lax.dot_general(keys, grad, TN, preferred_element_type=F32)

            def full(t, carry):
                half, block = step_of(t, low_steps)
                step(half, block, None)
                return carry

            lax.fori_loop(0, FULL_STEPS, full, 0)
            for half, first in ((0, span), (1, 2 * N_CTX - 1 - span)):
                step(half, lax.div(first, SPANS_STEP), lax.rem(first, SPANS_STEP) * SPAN)
                put_heads(dq_ref, s, h, half, (dq_acc[half, :HD, :] * HD**-0.5).T)

            def cast(b, carry):
                rows = pl.ds(pl.multiple_of(b * KEYS, KEYS), KEYS)
                stage[s, h, rows, :] = (acc[rows, :] * factor).astype(BF)
                return carry

            lax.fori_loop(0, N_CTX * TOK // KEYS, cast, 0)

            def put(p, carry):
                slot = tab[s, p]
                row = lax.rem(slot, 2) * SPAN + s * TOK
                pltpu.make_async_copy(
                    stage.at[s, h, pl.ds(pl.multiple_of(p * SPAN, SPAN), SPAN)],
                    dkv_ref.at[h, lax.div(slot, 2), pl.ds(pl.multiple_of(row, SPAN), SPAN)],
                    osems.at[s, h],
                ).start()
                return carry

            lax.fori_loop(0, 2 * N_CTX, put, 0)
    for s in range(2):
        for h in range(HH):
            pltpu.make_async_copy(stage.at[s, h], stage.at[s, h], osems.at[s, h]).wait()


def attend_back(tab, query, grad_attn, attn, log_sum, kvg):
    vmem = pl.BlockSpec(memory_space=pltpu.VMEM)
    anywhere = pl.BlockSpec(memory_space=pl.ANY)
    return pl.pallas_call(
        attend_back_kernel,
        out_shape=[
            jax.ShapeDtypeStruct((2 * TOK, QW), F32),
            jax.ShapeDtypeStruct((HH, N_CTX, 2 * TOK, 2 * HD), BF),
        ],
        in_specs=[pl.BlockSpec(memory_space=pltpu.SMEM), vmem, vmem, vmem, vmem, anywhere],
        out_specs=[vmem, anywhere],
        scratch_shapes=[
            pltpu.VMEM((2, HH, N_CTX * TOK, 2 * HD), BF),
            pltpu.VMEM((2, HH, 2, 2 * QROWS, 2 * HD), BF),
            pltpu.VMEM((2, HH, 2, 1, QROWS), F32),
            pltpu.VMEM((2, HH, N_CTX * TOK, 2 * HD), BF),
            pltpu.VMEM((N_CTX * TOK, 2 * HD), F32),
            pltpu.VMEM((2, 2 * HD, QROWS), F32),
            pltpu.SemaphoreType.DMA((2, HH)),
            pltpu.SemaphoreType.DMA((2, HH)),
        ],
        compiler_params=pltpu.CompilerParams(vmem_limit_bytes=40 * 1024 * 1024),
        name="attend_back",
    )(tab, query, grad_attn, attn, log_sum, kvg)


def permutation(axis, by):
    pairs = []
    for c in range(N_CTX):
        for f in range(4):
            h, x, y = c // 16, (c // 4) % 4, c % 4
            z, core = h * 2 + f // 2, f % 2
            if axis == "x":
                x = (x + by) % 4
            elif axis == "y":
                y = (y + by) % 4
            elif axis == "z":
                z = (z + by) % 4
            else:
                core = 1 - core
            pairs.append((c * 4 + f, ((z // 2) * 16 + x * 4 + y) * 4 + (z % 2) * 2 + core))
    return pairs


def shift(value, axis, by=1):
    return lax.ppermute(value, ("ctx", "fsdp"), permutation(axis, by))


def norm_rows(value_in, gain_row):
    inverse = lax.rsqrt(jnp.mean(value_in * value_in, axis=-1, keepdims=True) + EPSILON)
    return (value_in * inverse * gain_row, inverse)


def norm_back(value_in, inverse, gain_row, upstream):
    scaled = upstream * gain_row
    backward = inverse * scaled - value_in * inverse**3 * jnp.mean(scaled * value_in, axis=-1, keepdims=True)
    return (backward, upstream * value_in * inverse)


def body(layer_input, w_qkv, w_out, w_gate_up, w_down, norm_gains, span_map, cotangent):
    at = here()
    core, low = at["core"], at["l"]
    w_q = w_qkv[:, : HQ * HD].reshape(16, 2, QW).transpose(1, 0, 2)
    w_k = w_qkv[:, HQ * HD : (HQ + HK) * HD].reshape(16, 2, HH, HD)
    w_v = w_qkv[:, (HQ + HK) * HD :].reshape(16, 2, HH, HD)
    w_kv = jnp.concatenate([w_k, w_v], axis=3).reshape(16, 2, KVW).transpose(1, 0, 2)
    shard_one = jnp.concatenate([w_q, w_kv], axis=2)
    shard_gate = w_gate_up[:, :FF].reshape(16, 2, FH).transpose(1, 0, 2)
    shard_up = w_gate_up[:, FF:].reshape(16, 2, FH).transpose(1, 0, 2)
    shard_down = w_down.reshape(16, 2, FH).transpose(1, 0, 2)
    shard_out = w_out.reshape(16, 2, QW).transpose(1, 0, 2)
    share = norm_gains.shape[0]
    device = lax.axis_index(("ctx", "fsdp"))
    own_gain = lax.dynamic_update_slice_in_dim(jnp.zeros((40 * 128,), F32), norm_gains.astype(F32), device * share, 0)

    ctx_index = lax.axis_index("ctx")
    maps = lax.dynamic_slice_in_dim(span_map, low * 2, 2, 0)
    own_span = lax.dynamic_slice_in_dim(maps, ctx_index, 1, 1)
    spans = jnp.concatenate([own_span, 2 * N_CTX - 1 - own_span], axis=1)
    positions = (spans[:, :, None] * SPAN + jnp.arange(SPAN, dtype=jnp.int32)).reshape(2 * TOK)
    match = maps[:, None, :] == jnp.arange(N_CTX, dtype=jnp.int32)[None, :, None]
    inverse_map = jnp.sum(jnp.where(match, jnp.arange(N_CTX, dtype=jnp.int32), 0), axis=2)
    tab = jnp.concatenate([inverse_map * 2, inverse_map[:, ::-1] * 2 + 1, own_span], axis=1)
    half_dim = HD // 2
    frequencies = ROPE_BASE ** (-(jnp.arange(half_dim, dtype=F32) * 2.0 / HD))
    angles = positions.astype(F32)[:, None] * frequencies[None, :]
    cosine, sine = jnp.cos(angles), jnp.sin(angles)
    cosine = jnp.concatenate([cosine] * 4, axis=1)
    sine = jnp.concatenate([-sine, sine] * 2, axis=1)

    weights = [shard_one, shard_gate, shard_up, shard_down, shard_out]
    (w_joined, w_gate, w_up, w_back, w_proj, x_pair, dy_pair, gains, joined, normed_one, query, kvg) = front(
        weights, layer_input[0], cotangent[0], own_gain.reshape(40, 128), cosine, sine, 1
    )
    w_joined, w_gate, w_up, w_back, w_proj = (w.reshape(D, -1) for w in (w_joined, w_gate, w_up, w_back, w_proj))
    kvg = kvg.reshape(HH, N_CTX, 2 * TOK, 2 * HD)
    gain_one, gain_two = gains[:16].reshape(D), gains[16:32].reshape(D)
    stream_in = x_pair.reshape(2 * TOK, D).astype(F32)
    dy = dy_pair.reshape(2 * TOK, D)
    attn_f32, attn_low, log_sum = attend(tab, query, kvg)

    partial_a = lax.dot_general(attn_low, w_proj, NT, preferred_element_type=F32)
    branch_a = partial_a + shift(partial_a, "core")
    middle = stream_in + branch_a
    normed_two, inverse_two = norm_rows(middle, gain_two)
    normed_two = normed_two.astype(BF)
    gate_part = jnp.dot(normed_two, w_gate, preferred_element_type=F32)
    up_part = jnp.dot(normed_two, w_up, preferred_element_type=F32)
    sigmoid_gate = jax.nn.sigmoid(gate_part)
    silu_gate = gate_part * sigmoid_gate
    hidden = (silu_gate * up_part).astype(BF)
    partial_f = lax.dot_general(hidden, w_back, NT, preferred_element_type=F32)
    grad_hidden = jnp.dot(dy, w_back, preferred_element_type=F32)
    grad_gate = (grad_hidden * up_part * sigmoid_gate * (1.0 + gate_part * (1.0 - sigmoid_gate))).astype(BF)
    grad_up = (grad_hidden * silu_gate).astype(BF)
    partial_n = lax.dot_general(grad_gate, w_gate, NT, preferred_element_type=F32)
    partial_n = partial_n + lax.dot_general(grad_up, w_up, NT, preferred_element_type=F32)

    def own_rows(value):
        return lax.dynamic_slice_in_dim(value, core * TOK, TOK, 0)

    def other_rows(value):
        return lax.dynamic_slice_in_dim(value, (1 - core) * TOK, TOK, 0)

    branch_f = own_rows(partial_f) + shift(other_rows(partial_f), "core")
    result = own_rows(middle) + branch_f
    grad_normed_two = partial_n + shift(partial_n, "core")
    back_two, gain_two_terms = norm_back(middle, inverse_two, gain_two, grad_normed_two)
    grad_middle = dy.astype(F32) + back_two
    grad_branch = grad_middle.astype(BF)

    def outer(left, right):
        return lax.dot_general(left, right, TN, preferred_element_type=F32).astype(BF)

    early = [outer(normed_two, grad_gate), outer(normed_two, grad_up), outer(dy, hidden), outer(grad_branch, attn_low)]

    grad_attn = jnp.dot(grad_branch, w_proj, preferred_element_type=F32).astype(BF)
    dq, dkv = attend_back(tab, query, grad_attn, attn_f32, log_sum, kvg)
    grad_kv = sum_kv(dkv.reshape(HH, 2, 4, 4, 2 * TOK, 2 * HD), 4)
    grad_joined, head_terms = rope_back(joined, dq, grad_kv, gains, cosine, sine)
    partial_one = lax.dot_general(grad_joined, w_joined, NT, preferred_element_type=F32)
    grad_normed_one = own_rows(partial_one) + shift(other_rows(partial_one), "core")
    own_in = layer_input[0].astype(F32)
    inverse_one = lax.rsqrt(jnp.mean(own_in * own_in, axis=-1, keepdims=True) + EPSILON)
    back_one, gain_one_terms = norm_back(own_in, inverse_one, gain_one, grad_normed_one)
    grad_input = own_rows(grad_middle) + back_one

    def mean_root(stream):
        return jnp.sum(jnp.sqrt(jnp.mean(stream * stream, axis=-1)))

    stats = jnp.stack([mean_root(s) for s in (own_in, own_rows(branch_a), own_rows(middle))] + [mean_root(branch_f)])
    sums = jnp.concatenate(
        [
            jnp.sum(gain_one_terms, axis=0),
            jnp.sum(own_rows(gain_two_terms), axis=0),
            head_terms[0],
            stats,
        ]
    )
    sums = jnp.pad(sums, (0, 40 * 128 - sums.shape[0])).reshape(40, 128)
    own_gate, own_up, own_down, own_out, own_qkv, sums = sum_weights(
        early + [outer(normed_one, grad_joined)], sums, SUMS, 5, 62 * 1024 * 1024
    )
    sums = sums.reshape(-1)
    grad_mlp = jnp.concatenate([own_gate[0], own_gate[1], own_up[0], own_up[1]], axis=1)
    grad_down = jnp.concatenate([own_down[0], own_down[1]], axis=1)
    kv_cols = own_qkv[:, :, QW:].reshape(2, 16, HH, 2, HD)
    grad_qkv = jnp.concatenate(
        [
            own_qkv[0, :, :QW],
            own_qkv[1, :, :QW],
            *(kv_cols[half, :, :, kind].reshape(16, HH * HD) for kind in range(2) for half in range(2)),
        ],
        axis=1,
    )
    grad_proj = jnp.concatenate([own_out[0], own_out[1]], axis=1)

    own_gains = lax.dynamic_slice_in_dim(sums, device * share, share, 0)
    stream_rms = sums[4224:4228] / (TOK * N_CTX * 4)
    return (
        result[None].astype(BF),
        grad_input[None].astype(BF),
        grad_qkv,
        grad_proj,
        grad_mlp,
        grad_down,
        own_gains,
        stream_rms,
    )


def solution(mesh):
    rows = P(("ctx", "fsdp"), None)
    tokens = P("fsdp", "ctx", None)
    return jax.shard_map(
        body,
        mesh=mesh,
        in_specs=(tokens, rows, rows, rows, rows, P(("ctx", "fsdp")), P(), tokens),
        out_specs=(tokens, tokens, rows, rows, rows, rows, P(("ctx", "fsdp")), P()),
        check_vma=False,
    )
```

```python
import functools

import jax
import jax.numpy as jnp
from jax import lax
from jax.experimental import pallas as pl
from jax.experimental.pallas import tpu as pltpu
from jax.sharding import PartitionSpec as P

D = 2048
HQ = 24
HK = 6
HD = 64
FF = 4352
TOK = 128
SPAN = 64
N_CTX = 32

HH = HK // 2
GROUP = HQ // HK
QH = HQ // 2
QW = QH * HD
KVW = HH * 2 * HD
FH = FF // 2
KEYS = 512
SPANS_STEP = KEYS // SPAN
KEY_BLOCKS = 8
QROWS = GROUP * SPAN

EPSILON = 1e-06
ROPE_BASE = 10000.0
LOG2E = 1.4426950408889634
AT_H, AT_X, AT_Y, AT_HALF = 0, 64, 128, 192
AT_STEP_HALF, AT_STEP_BLOCK, AT_MARK, AT_EDGE, AT_LIMIT, AT_MAP = 256, 259, 262, 266, 268, 270
MESH = pl.DeviceIdType.MESH
BF = jnp.bfloat16
F32 = jnp.float32
NT = (((1,), (1,)), ((), ()))
NN = (((1,), (0,)), ((), ()))
TN = (((0,), (0,)), ((), ()))
W_DIMS = ("h", "x", "y", "l")
KV_DIMS = ("h", "x", "y")
ORDERS = (("x", "y", "z"), ("y", "z", "x"), ("z", "x", "y"))
KV_ORDERS = (("h", "x", "y"), ("x", "y", "h"), ("y", "h", "x"))
KV_SUM_ORDERS = (("y", "x", "h"), ("h", "y", "x"), ("x", "h", "y"))
SUMS = (
    (0, 0, 1152, ORDERS[0]),
    (1, 0, 1152, ORDERS[1]),
    (2, 0, 1152, ORDERS[2]),
    (0, 1152, 1024, ORDERS[0]),
    (1, 1152, 1024, ORDERS[1]),
    (2, 1152, 1024, ORDERS[2]),
    (3, 0, 256, ORDERS[0]),
    (3, 256, 256, ORDERS[1]),
    (3, 512, 256, ORDERS[2]),
    (4, 0, 384, ORDERS[0]),
    (4, 384, 384, ORDERS[1]),
    (4, 768, 384, ORDERS[2]),
)
N_EARLY = 9
SIZES = {"x": 4, "y": 4, "z": 4, "h": 2}


def here():
    c = lax.axis_index("ctx")
    f = lax.axis_index("fsdp")
    return {
        "x": lax.rem(lax.div(c, 4), 4),
        "y": lax.rem(c, 4),
        "z": lax.div(c, 16) * 2 + lax.div(f, 2),
        "h": lax.div(c, 16),
        "l": lax.div(f, 2),
        "core": lax.rem(f, 2),
    }


def device_of(x, y, z, core):
    return (lax.div(z, 2) * 16 + x * 4 + y, lax.rem(z, 2) * 2 + core)


def moved(at, axis, by):
    if axis == "core":
        return device_of(at["x"], at["y"], at["z"], 1 - at["core"])
    place = {k: at[k] for k in ("x", "y", "z")}
    if axis == "h":
        place["z"] = lax.rem(at["z"] + 2, 4)
    else:
        place[axis] = lax.rem(at[axis] + by + 4, 4)
    return device_of(place["x"], place["y"], place["z"], at["core"])


def labels(axis, value):
    if axis == "z":
        return {"h": lax.div(value, 2), "l": lax.rem(value, 2)}
    return {axis: value}


def pick(ref, dims, values, tail):
    return ref.at[tuple(values[d] if d in values else slice(None) for d in dims) + tail]


def greet(devices):
    barrier = pltpu.get_barrier_semaphore()
    for d in devices:
        pl.semaphore_signal(barrier, inc=1, device_id=d, device_id_type=MESH)
    pl.semaphore_wait(barrier, len(devices))


def send(src, dst, ssem, rsem, device):
    copy = pltpu.make_async_remote_copy(
        src_ref=src, dst_ref=dst, send_sem=ssem, recv_sem=rsem, device_id=device, device_id_type=MESH
    )
    copy.start()
    return copy


class Gathering:
    def __init__(self, ref, dims, at, order, rows, cols, ssem, rsem):
        self.ref, self.dims, self.at, self.order, self.rows, self.cols = ref, dims, at, order, rows, cols
        self.ssem, self.rsem, self.phase, self.sent = ssem, rsem, 0, []

    def block(self, coordinate, rows):
        later = {}
        for a in self.order[self.phase + 1 :]:
            later.update(labels(a, self.at[a]))
        return pick(self.ref, self.dims, {**later, **labels(self.axis, coordinate)}, (rows, self.cols))

    def send(self, n, ref, by):
        c = send(ref, ref, self.ssem.at[self.phase, n], self.rsem.at[self.phase, n], moved(self.at, self.axis, by))
        self.sent.append(c)
        return c

    def start(self):
        self.axis = self.order[self.phase]
        mine = self.block(self.at[self.axis], slice(None))
        self.first = [self.send(0, mine, 1)]
        if SIZES[self.axis] == 4:
            self.first.append(self.send(1, mine, 3))

    def pass_on(self):
        for c in self.first:
            c.wait_recv()
        self.second = []
        if SIZES[self.axis] == 4:
            half = self.rows // 2
            me = self.at[self.axis]
            self.second.append(self.send(2, self.block(lax.rem(me + 3, 4), pl.ds(0, half)), 1))
            self.second.append(self.send(3, self.block(lax.rem(me + 1, 4), pl.ds(half, half)), 3))

    def finish(self):
        for c in self.second:
            c.wait_recv()
        self.phase += 1

    def wait_sent(self):
        for c in self.sent:
            c.wait_send()


def neighbours(at, axes):
    out = []
    for a in axes:
        if a in ("core", "h"):
            out.append(moved(at, a, 1))
        else:
            out.append(moved(at, a, 1))
            out.append(moved(at, a, 3))
    return out


GATHER = (
    (0, 0, 1152, ORDERS[0]),
    (1, 0, 1152, ORDERS[1]),
    (2, 0, 1152, ORDERS[2]),
    (0, 1152, 1024, ORDERS[0]),
    (1, 1152, 1024, ORDERS[1]),
    (2, 1152, 1024, ORDERS[2]),
    (3, 0, 256, ORDERS[0]),
    (3, 256, 256, ORDERS[1]),
    (3, 512, 256, ORDERS[2]),
)


def lane_of(shape):
    return lax.broadcasted_iota(jnp.int32, shape, len(shape) - 1)


def swap_halves(v):
    return jnp.where(lax.rem(lane_of(v.shape), HD) < HD // 2, pltpu.roll(v, 96, 1), pltpu.roll(v, 32, 1))


def head_sums(v):
    low = lane_of(v.shape) < HD
    a = jnp.sum(jnp.where(low, v, 0.0), axis=1, keepdims=True)
    b = jnp.sum(jnp.where(low, 0.0, v), axis=1, keepdims=True)
    return jnp.where(low, a, b)


def tile_gain(row, is_key):
    low = lane_of(row.shape) < HD
    turned = pltpu.roll(row, HD, 1)
    return jnp.where(low, turned, 1.0) if is_key else jnp.where(low, row, turned)


def front_kernel(
    tab, shard_one, shard_gate, shard_up, shard_down, shard_out, x, dy, gains, cosine, sine,
    w_one, w_gate, w_up, w_down, w_out, x_pair, dy_pair, gain_all, joined, normed, query, kv_out, o_ref, low_ref, l_ref,
    one, kv_src, kvg, kvs, q_ref, acc, sum_ref, small_buf, psem, lsem, tssem, trsem, ossem, orsem, gssem, grsem, kssem, krsem, ksem,
):
    at = here()
    core = at["core"]
    sibling = moved(at, "core", 1)
    greet([sibling] + sum_peers(at, ("x", "y", "z")))
    own = {d: at[d] for d in W_DIMS}
    total = Total(gains[...], at, small_buf, tssem, trsem)
    remote, local = [], []
    pairs = [(shard_one, one), (shard_gate, w_gate), (shard_up, w_up), (shard_down, w_down), (shard_out, w_out)]
    for i, (src, ref) in enumerate(pairs):
        dst = pick(ref, W_DIMS, own, (pl.ds(core * 16, 16), slice(None)))
        remote.append(send(src.at[1 - core], dst, psem.at[i, 0], psem.at[i, 1], sibling))
        local.append(pltpu.make_async_copy(src.at[core], dst, lsem.at[i]))
        local[-1].start()
    for i, (src, ref) in ((5, (x, x_pair)), (6, (dy, dy_pair))):
        remote.append(send(src, ref.at[core], psem.at[i, 0], psem.at[i, 1], sibling))
        local.append(pltpu.make_async_copy(src, ref.at[core], lsem.at[i]))
        local[-1].start()

    def arrived(i):
        remote[i].wait_recv()
        local[i].wait()

    ones = [
        Gathering(one, W_DIMS, at, ORDERS[k], 32, pl.ds(k * 384, 384), ossem.at[k], orsem.at[k]) for k in range(3)
    ]
    rest = [
        Gathering(pairs[1 + a][1], W_DIMS, at, order, 32, pl.ds(start, width), gssem.at[k], grsem.at[k])
        for k, (a, start, width, order) in enumerate(GATHER)
    ]
    keys = [
        Gathering(kvg.at[h], KV_DIMS, at, KV_ORDERS[h], 4, slice(None), kssem.at[h], krsem.at[h]) for h in range(HH)
    ]

    def every(streams, *steps):
        for s in streams:
            for step in steps:
                getattr(s, step)()

    arrived(0)
    every(ones, "start")
    for i in range(1, 5):
        arrived(i)
    every(rest, "start")
    total.step()
    every(ones, "pass_on")
    every(rest, "pass_on")
    total.step()
    every(ones, "finish", "start")
    every(rest, "finish")
    total.step()
    every(ones, "pass_on")
    total.step()
    gain_all[...] = total.value
    every(ones, "finish", "start")
    every(rest, "start")
    arrived(5)
    gain_row = jnp.concatenate([total.value[j : j + 1] for j in range(D // 128)], axis=1)

    def norm(r, carry):
        rows = pl.ds(pl.multiple_of(r * 32, 32), 32)
        for s in range(2):
            v = x_pair[s, rows, :].astype(F32)
            inverse = lax.rsqrt(jnp.sum(v * v, axis=1, keepdims=True) * (1.0 / D) + EPSILON)
            normed[pl.ds(pl.multiple_of(s * TOK + r * 32, 32), 32), :] = (v * inverse * gain_row).astype(BF)
        return carry

    lax.fori_loop(0, TOK // 32, norm, 0)
    every(ones, "pass_on")
    every(ones, "finish")
    keep = pltpu.make_async_copy(one, w_one, lsem.at[7])
    keep.start()
    head_gains = total.value[32:33]

    def product(start, width):
        w = one[:, :, :, :, :, start : start + width].reshape(D, width)
        joined[:, start : start + width] = jnp.dot(normed[...], w, preferred_element_type=F32)

    def rope(tile, is_key):
        v = joined[:, tile * 128 : (tile + 1) * 128]
        low = lane_of(v.shape) < HD
        c, n = cosine[...], sine[...]
        inverse = lax.rsqrt(head_sums(v * v) * (1.0 / HD) + EPSILON)
        if is_key:
            inverse = jnp.where(low, inverse, 1.0)
            c, n = jnp.where(low, c, 1.0), jnp.where(low, n, 0.0)
        v = v * inverse * tile_gain(head_gains, is_key)
        return (v * c + swap_halves(v) * n).astype(BF)

    product(QW, KVW)
    for h in range(HH):
        kv_src[h] = rope(QW // 128 + h, True).reshape(4, SPAN, 2 * HD)
    kv_own = {d: at[d] for d in KV_DIMS}
    puts = [pltpu.make_async_copy(kv_src.at[h], pick(kvg.at[h], KV_DIMS, kv_own, ()), ksem.at[h]) for h in range(HH)]
    for c in puts:
        c.start()
    for c in puts:
        c.wait()
    every(keys, "start")
    every(rest, "pass_on")
    product(0, 384)
    every(keys, "pass_on")
    every(rest, "finish")
    every(keys, "finish", "start")
    product(384, 384)
    every(keys, "pass_on")
    for t in range(QW // 128):
        query[:, t * 128 : (t + 1) * 128] = rope(t, False)
    every(keys, "finish", "start")
    every(rest[:3], "start")
    blank = jnp.zeros((QROWS, HD), BF)
    for s in range(2):
        for h in range(HH):
            for half in range(2):
                q_ref[s, h, half] = jnp.concatenate([heads_at(query, s, h, half), blank], axis=1)
    every(keys, "pass_on")
    every(rest[3:], "start")
    every(keys, "finish")

    def sort(p, carry):
        for s in range(2):
            place = tuple(tab[s, column + p] for column in (AT_H, AT_X, AT_Y))
            half = tab[s, AT_HALF + p]
            for h in range(HH):
                kvs[s, h, lax.div(p, SPANS_STEP), lax.rem(p, SPANS_STEP)] = kvg[(h,) + place + (s * 2 + half,)]
        return carry

    lax.fori_loop(0, 2 * N_CTX, sort, 0)
    keep_keys = pltpu.make_async_copy(kvs, kv_out, ksem.at[HH])
    keep_keys.start()
    attend_heads(tab, 0, q_ref, kvs, o_ref, low_ref, l_ref, acc, sum_ref)
    every(rest[:3], "pass_on")
    attend_heads(tab, 1, q_ref, kvs, o_ref, low_ref, l_ref, acc, sum_ref)
    every(rest[3:], "pass_on")
    every(rest, "finish")
    keep_keys.wait()
    arrived(6)
    keep.wait()
    for c in remote + total.sent:
        c.wait_send()
    for s in ones + rest + keys:
        s.wait_sent()


def front(tab, shards, x, dy, gains, cosine, sine, cid):
    anywhere = pl.BlockSpec(memory_space=pl.ANY)
    vmem = pl.BlockSpec(memory_space=pltpu.VMEM)
    full = [jax.ShapeDtypeStruct((2, 4, 4, 2, 32, s.shape[-1]), BF) for s in shards]
    n = len(GATHER)
    return pl.pallas_call(
        front_kernel,
        out_shape=full
        + [
            jax.ShapeDtypeStruct((2,) + x.shape, BF),
            jax.ShapeDtypeStruct((2,) + dy.shape, BF),
            jax.ShapeDtypeStruct(gains.shape, F32),
            jax.ShapeDtypeStruct((2 * TOK, QW + KVW), F32),
            jax.ShapeDtypeStruct((2 * TOK, D), BF),
            jax.ShapeDtypeStruct((2 * TOK, QW), BF),
            jax.ShapeDtypeStruct((2, HH, KEY_BLOCKS, SPANS_STEP, SPAN, 2 * HD), BF),
            jax.ShapeDtypeStruct((2 * TOK, QW), F32),
            jax.ShapeDtypeStruct((2 * TOK, QW), BF),
            jax.ShapeDtypeStruct((2, HH, 2, 1, QROWS), F32),
        ],
        in_specs=[pl.BlockSpec(memory_space=pltpu.SMEM)] + [anywhere] * 7 + [vmem] * 3,
        out_specs=[anywhere] * 5 + [vmem, anywhere] + [vmem] * 4 + [anywhere] + [vmem] * 3,
        scratch_shapes=[
            pltpu.VMEM((2, 4, 4, 2, 32, QW + KVW), BF),
            pltpu.VMEM((HH, 4, SPAN, 2 * HD), BF),
            pltpu.VMEM((HH, 2, 4, 4, 4, SPAN, 2 * HD), BF),
            pltpu.VMEM((2, HH, KEY_BLOCKS, SPANS_STEP, SPAN, 2 * HD), BF),
            pltpu.VMEM((2, HH, 2, QROWS, 2 * HD), BF),
            pltpu.VMEM((2, 2 * HD, QROWS), F32),
            pltpu.VMEM((2, 1, QROWS), F32),
            pltpu.VMEM((4, 4) + gains.shape, F32),
            pltpu.SemaphoreType.DMA((7, 2)),
            pltpu.SemaphoreType.DMA((8,)),
            pltpu.SemaphoreType.DMA((4, 4)),
            pltpu.SemaphoreType.DMA((4, 4)),
            pltpu.SemaphoreType.DMA((3, 3, 4)),
            pltpu.SemaphoreType.DMA((3, 3, 4)),
            pltpu.SemaphoreType.DMA((n, 3, 4)),
            pltpu.SemaphoreType.DMA((n, 3, 4)),
            pltpu.SemaphoreType.DMA((HH, 3, 4)),
            pltpu.SemaphoreType.DMA((HH, 3, 4)),
            pltpu.SemaphoreType.DMA((HH + 1,)),
        ],
        compiler_params=pltpu.CompilerParams(
            collective_id=cid, has_side_effects=True, vmem_limit_bytes=48 * 1024 * 1024
        ),
        name="front",
    )(tab, *shards, x, dy, gains, cosine, sine)


def rope_back_kernel(joined, dq, dkv, gains, cosine, sine, out, terms):
    head_gains = gains[32:33]

    def tile(t, is_key, grad):
        v = joined[:, t * 128 : (t + 1) * 128]
        low = lane_of(v.shape) < HD
        back = grad * cosine[...] - swap_halves(grad) * sine[...]
        inverse = lax.rsqrt(head_sums(v * v) * (1.0 / HD) + EPSILON)
        scaled = back * tile_gain(head_gains, is_key)
        inner = head_sums(scaled * v) * (1.0 / HD)
        result = inverse * scaled - v * (inverse * inverse * inverse) * inner
        if is_key:
            result = jnp.where(low, result, grad)
        out[:, t * 128 : (t + 1) * 128] = result.astype(BF)
        return jnp.sum(back * v * inverse, axis=0, keepdims=True)

    q_terms = sum(tile(t, False, dq[:, t * 128 : (t + 1) * 128]) for t in range(QW // 128))
    k_terms = sum(tile(QW // 128 + h, True, dkv[h]) for h in range(HH))
    low = lane_of(q_terms.shape) < HD
    q_terms = q_terms + pltpu.roll(q_terms, HD, 1)
    terms[...] = jnp.where(low, q_terms, pltpu.roll(k_terms, HD, 1))


def rope_back(joined, dq, dkv, gains, cosine, sine):
    vmem = pl.BlockSpec(memory_space=pltpu.VMEM)
    return pl.pallas_call(
        rope_back_kernel,
        out_shape=[jax.ShapeDtypeStruct((2 * TOK, QW + KVW), BF), jax.ShapeDtypeStruct((1, 128), F32)],
        in_specs=[vmem] * 6,
        out_specs=[vmem] * 2,
        compiler_params=pltpu.CompilerParams(vmem_limit_bytes=32 * 1024 * 1024),
        name="rope_back",
    )(joined, dq, dkv, gains, cosine, sine)


def lead_shape(dims):
    full = {"h": 2, "x": 4, "y": 4, "l": 2}
    return tuple(full[d] for d in dims)


def without(dims, axis):
    gone = ("h", "l") if axis == "z" else (axis,)
    return tuple(d for d in dims if d not in gone)


class Summing:
    def __init__(self, source, dims, at, order, rows, cols, buffers, ssem, rsem, lsem, begun=None):
        self.ref, self.dims, self.at, self.order, self.begun = source, dims, at, order, begun
        self.cols, self.buffers, self.rows = cols, buffers, rows
        self.ssem, self.rsem, self.lsem = ssem, rsem, lsem
        self.phase, self.sent = 0, []

    def part(self, coordinate, rows):
        return pick(self.ref, self.dims, labels(self.axis, coordinate), (rows, self.cols))

    def send(self, n, src, dst, by):
        c = send(src, dst, self.ssem.at[self.phase, n], self.rsem.at[self.phase, n], moved(self.at, self.axis, by))
        self.sent.append(c)
        return c

    def start(self):
        self.axis = self.order[self.phase]
        self.rest = without(self.dims, self.axis)
        self.lead = lead_shape(self.rest)
        half = self.rows // 2
        first, second, every = pl.ds(0, half), pl.ds(half, half), pl.ds(0, self.rows)
        i = self.at[self.axis]
        buf = self.buffers[self.phase]
        self.local = []
        if SIZES[self.axis] == 2:
            self.direct = (self.send(0, self.part(1 - i, every), buf["got"].at[0], 1),)
        else:
            up, down, far = lax.rem(i + 1, 4), lax.rem(i + 3, 4), lax.rem(i + 2, 4)
            self.near = (up, down)
        if self.phase == 0 and self.begun is not None:
            self.relay, self.direct = (), ()
        elif SIZES[self.axis] == 4:
            self.relay = (
                self.send(0, self.part(far, first), buf["relay"].at[0], 1),
                self.send(1, self.part(far, second), buf["relay"].at[1], 3),
            )
            self.direct = (
                self.send(2, self.part(up, second), buf["got"].at[1, 1], 1),
                self.send(3, self.part(down, first), buf["got"].at[0, 1], 3),
            )
        if self.phase == 0:
            todo = [(self.part(i, every), buf["mine"])]
            if SIZES[self.axis] == 4:
                todo.append((self.part(up, first), buf["own"].at[0]))
                todo.append((self.part(down, second), buf["own"].at[1]))
            if self.begun is not None:
                todo.append((self.begun[0], buf["relay"]))
                todo.append((self.begun[1].at[0], buf["got"].at[0, 1]))
                todo.append((self.begun[1].at[1], buf["got"].at[1, 1]))
            for n, (src, dst) in enumerate(todo):
                c = pltpu.make_async_copy(src, dst, self.lsem.at[n])
                c.start()
                self.local.append(c)

    def over_lead(self, add):
        rest = self.lead[1:]
        spots = [()]
        for n in rest:
            spots = [s + (j,) for s in spots for j in range(n)]
        if not self.lead:
            add(())
            return

        def go(j, carry):
            for s in spots:
                add((j,) + s)
            return carry

        lax.fori_loop(0, self.lead[0], go, 0)

    def pass_on(self):
        if SIZES[self.axis] == 2:
            return
        buf = self.buffers[self.phase]
        half = self.rows // 2
        for n, by in ((0, 1), (1, 3)):
            if self.relay:
                self.relay[n].wait_recv()
            elif n == 0:
                self.local[3].wait()
            if self.phase == 0:
                self.local[1 + n].wait()
                own = buf["own"].at[n]
            else:
                own = self.part(self.near[n], pl.ds(n * half, half))

            def add(spot):
                here_ = spot + (slice(None), slice(None))
                both = buf["relay"][(n,) + here_].astype(F32) + own[here_].astype(F32)
                buf["relay"][(n,) + here_] = both.astype(BF)

            self.over_lead(add)
            c = self.send(4 + n, buf["relay"].at[n], buf["got"].at[n, 0], by)
            self.direct = self.direct + (c,)

    def finish(self):
        buf = self.buffers[self.phase]
        half = self.rows // 2
        if self.local:
            self.local[0].wait()
        for c in self.local[4:]:
            c.wait()
        for c in self.direct:
            c.wait_recv()
        own = buf["mine"] if self.phase == 0 else self.part(self.at[self.axis], pl.ds(0, self.rows))
        out = buf["mine"] if self.phase == 0 else buf["sum"]

        def add(spot):
            if SIZES[self.axis] == 2:
                here_ = spot + (slice(None), slice(None))
                out[here_] = (own[here_].astype(F32) + buf["got"][(0,) + here_].astype(F32)).astype(out.dtype)
                return
            for n in range(2):
                rows = spot + (pl.ds(n * half, half), slice(None))
                all_ = spot + (slice(None), slice(None))
                total = own[rows].astype(F32) + buf["got"][(n, 0) + all_].astype(F32)
                total = total + buf["got"][(n, 1) + all_].astype(F32)
                out[rows] = total.astype(out.dtype)

        self.over_lead(add)
        self.ref, self.dims, self.cols = out, self.rest, slice(None)
        self.phase += 1


class Total:
    def __init__(self, value, at, buf, ssem, rsem):
        self.value, self.at, self.buf, self.ssem, self.rsem = value, at, buf, ssem, rsem
        self.phase, self.sent = 0, []
        self.start()

    def start(self):
        n, axis = self.phase, ("core", "z", "y", "x")[self.phase]
        self.buf[n, 0] = self.value
        self.copies = []
        for i in (1, 3, 2) if axis != "core" else (1,):
            self.copies.append(
                send(self.buf.at[n, 0], self.buf.at[n, i], self.ssem.at[n, i], self.rsem.at[n, i], moved(self.at, axis, i))
            )

    def step(self):
        n, buf = self.phase, self.buf
        if n == 4:
            return
        for c in self.copies:
            c.wait_recv()
            self.sent.append(c)
        if n == 0:
            self.value = buf[n, 0] + buf[n, 1]
        else:
            self.value = (buf[n, 0] + buf[n, 2]) + (buf[n, 1] + buf[n, 3])
        self.phase += 1
        if self.phase < 4:
            self.start()


def run_sums(streams, total=None):
    for s in streams:
        s.start()
    for phase in range(3):
        for s in streams:
            s.pass_on()
        if total is not None:
            total.step()
        for s in streams:
            s.finish()
            if phase < 2:
                s.start()
        if total is not None:
            total.step()
    for s in streams:
        for c in s.sent:
            c.wait_send()


def sum_scratch(order, dims, rows, width):
    buffers = []
    for phase, axis in enumerate(order):
        rest = without(dims, axis)
        lead = lead_shape(rest)
        buf = {}
        if SIZES[axis] == 2:
            buf["got"] = pltpu.VMEM((1,) + lead + (rows, width), BF)
        else:
            buf["got"] = pltpu.VMEM((2, 2) + lead + (rows // 2, width), BF)
            buf["relay"] = pltpu.VMEM((2,) + lead + (rows // 2, width), BF)
        if phase == 0:
            buf["mine"] = pltpu.VMEM(lead + (rows, width), BF)
            if SIZES[axis] == 4:
                buf["own"] = pltpu.VMEM((2,) + lead + (rows // 2, width), BF)
        else:
            buf["sum"] = pltpu.VMEM(lead + (rows, width), BF if phase < 2 else F32)
        buffers.append(buf)
        dims = rest
    return buffers


def weight_sum_kernel(pieces, n, *refs):
    ins, small, begun, refs = refs[:n], refs[n], refs[n + 1 : n + 1 + 2 * N_EARLY], refs[n + 1 + 2 * N_EARLY :]
    outs, small_out = refs[:n], refs[n]
    buffers, stages, swapped, small_buf, ssem, rsem, lsem, csem, tssem, trsem = refs[n + 1 :]
    at = here()
    core = at["core"]
    sibling = moved(at, "core", 1)
    greet([sibling] + sum_peers(at, ("x", "y", "z")))
    streams = [
        Summing(
            ins[a], W_DIMS, at, order, 32, pl.ds(start, width), buffers[k], ssem.at[k], rsem.at[k], lsem.at[k],
            (begun[2 * k], begun[2 * k + 1]) if k < N_EARLY else None,
        )
        for k, (a, start, width, order) in enumerate(pieces)
    ]
    total = Total(small[...], at, small_buf, tssem, trsem)
    run_sums(streams, total)
    small_out[...] = total.value
    for k, (a, start, width, order) in enumerate(pieces):
        stages[a][:, start : start + width] = buffers[k][2]["sum"][...]
    other = pl.ds(pl.multiple_of((1 - core) * 16, 16), 16)
    own = pl.ds(pl.multiple_of(core * 16, 16), 16)
    copies = [send(stages[a].at[other], swapped[a], csem.at[a, 0], csem.at[a, 1], sibling) for a in range(n)]
    for a in range(n):
        outs[a][core] = stages[a][own, :]
        copies[a].wait_recv()
        outs[a][1 - core] = swapped[a][...]
    for c in copies + total.sent:
        c.wait_send()


def sum_weights(grads, small, begun, pieces, cid, limit):
    n, k = len(grads), len(pieces)
    anywhere = pl.BlockSpec(memory_space=pl.ANY)
    vmem = pl.BlockSpec(memory_space=pltpu.VMEM)
    widths = [g.shape[-1] for g in grads]
    return pl.pallas_call(
        functools.partial(weight_sum_kernel, pieces, n),
        out_shape=[jax.ShapeDtypeStruct((2, 16, w), F32) for w in widths] + [jax.ShapeDtypeStruct(small.shape, F32)],
        in_specs=[anywhere] * n + [vmem] + [anywhere] * len(begun),
        out_specs=[vmem] * (n + 1),
        scratch_shapes=[
            [sum_scratch(order, W_DIMS, 32, width) for a, start, width, order in pieces],
            [pltpu.VMEM((32, w), F32) for w in widths],
            [pltpu.VMEM((16, w), F32) for w in widths],
            pltpu.VMEM((4, 4) + small.shape, F32),
            pltpu.SemaphoreType.DMA((k, 3, 6)),
            pltpu.SemaphoreType.DMA((k, 3, 6)),
            pltpu.SemaphoreType.DMA((k, 6)),
            pltpu.SemaphoreType.DMA((n, 2)),
            pltpu.SemaphoreType.DMA((4, 4)),
            pltpu.SemaphoreType.DMA((4, 4)),
        ],
        compiler_params=pltpu.CompilerParams(collective_id=cid, has_side_effects=True, vmem_limit_bytes=limit),
        name="sum_weights",
    )(*[g.reshape(2, 4, 4, 2, 32, g.shape[-1]) for g in grads], small, *begun)


def sum_peers(at, axes):
    out = []
    for a in axes:
        for i in (1, 3, 2) if SIZES[a] == 4 else (1,):
            out.append(moved(at, a, i))
    return out


def heads_at(ref, s, h, half):
    rows = slice(s * TOK + half * SPAN, s * TOK + (half + 1) * SPAN)
    return jnp.concatenate([ref[rows, (h * GROUP + g) * HD : (h * GROUP + g + 1) * HD] for g in range(GROUP)], axis=0)


def put_heads(ref, s, h, half, value):
    rows = pl.ds(pl.multiple_of(s * TOK + half * SPAN, SPAN), SPAN)
    for g in range(0, GROUP, 2):
        both = jnp.concatenate([value[g * SPAN : (g + 1) * SPAN], value[(g + 1) * SPAN : (g + 2) * SPAN]], axis=1)
        ref[rows, pl.ds(pl.multiple_of((h * GROUP + g) * HD, 2 * HD), 2 * HD)] = both.astype(ref.dtype)


def masked(prob, limit):
    if limit is None:
        return prob
    row = lax.broadcasted_iota(jnp.int32, prob.shape, 0)
    col = lax.rem(lax.broadcasted_iota(jnp.int32, prob.shape, 1), SPAN)
    return jnp.where(row <= col + limit, prob, 0.0)


def attend_heads(tab, s, q_ref, kvs, o_ref, low_ref, l_ref, acc, total):
    rate = LOG2E * HD**-0.5

    def head(h, carry):
        acc[...] = jnp.zeros_like(acc)
        total[...] = jnp.zeros_like(total)

        def scored(half, block, limit):
            keys = kvs[s, h, block].reshape(KEYS, 2 * HD)
            scores = lax.dot_general(keys, q_ref[s, h, half], NT, preferred_element_type=F32)
            prob = masked(jnp.exp2(scores * rate), limit)
            return (
                jnp.sum(prob, axis=0, keepdims=True),
                lax.dot_general(keys, prob.astype(BF), TN, preferred_element_type=F32),
            )

        def high(k, c):
            t, o = scored(1, k, None)
            total[1] += t
            acc[1] += o
            return c

        def either(k, c):
            half = tab[s, AT_STEP_HALF + k]
            t, o = scored(half, tab[s, AT_STEP_BLOCK + k], None)
            up = half.astype(F32)
            total[0] += t * (1.0 - up)
            total[1] += t * up
            acc[0] += o * (1.0 - up)
            acc[1] += o * up
            return c

        lax.fori_loop(0, 4, high, 0)
        lax.fori_loop(0, 3, either, 0)
        for half in range(2):
            t, o = scored(half, tab[s, AT_EDGE + half], tab[s, AT_LIMIT + half])
            t, o = total[half] + t, acc[half] + o
            out = (o[HD:, :] / t).T
            put_heads(o_ref, s, h, half, out)
            put_heads(low_ref, s, h, half, out)
            l_ref[s, h, half] = jnp.log2(t)
        return carry

    lax.fori_loop(0, HH, head, 0)


class Early:
    def __init__(self, source, at, order, cols, relay, direct, ssem, rsem):
        axis = order[0]
        i = at[axis]
        up, down, far = lax.rem(i + 1, 4), lax.rem(i + 3, 4), lax.rem(i + 2, 4)
        self.copies = []
        plan = ((far, 0, relay, 0, 1), (far, 1, relay, 1, 3), (up, 1, direct, 1, 1), (down, 0, direct, 0, 3))
        for n, (coordinate, half, dst, slot, by) in enumerate(plan):
            src = pick(source, W_DIMS, labels(axis, coordinate), (pl.ds(half * 16, 16), cols))
            self.copies.append(send(src, dst.at[slot], ssem.at[n], rsem.at[n], moved(at, axis, by)))

    def wait(self):
        for c in self.copies:
            c.wait_recv()
        for c in self.copies:
            c.wait_send()


def early_shapes():
    shapes = []
    for a, start, width, order in SUMS[:N_EARLY]:
        lead = lead_shape(without(W_DIMS, order[0]))
        shapes += [jax.ShapeDtypeStruct((2,) + lead + (16, width), BF)] * 2
    return shapes


def attend_back_kernel(*refs):
    tab, qr, da, attn, l_ref, kv_sorted = refs[:6]
    grads, refs = refs[6:10], refs[10:]
    dq_ref, dkv_out = refs[:2]
    begun, refs = refs[2 : 2 + 2 * N_EARLY], refs[2 + 2 * N_EARLY :]
    kvs, qd_ref, delta_ref, stage, acc, dq_acc, buffers, essem, ersem, ssem, rsem, lsem, sems = refs
    at = here()
    greet(neighbours(at, ("x", "y", "z", "h")))
    early = [
        Early(grads[a], at, order, pl.ds(start, width), begun[2 * k], begun[2 * k + 1], essem.at[k], ersem.at[k])
        for k, (a, start, width, order) in enumerate(SUMS[:N_EARLY])
    ]
    loads = []
    for h in range(HH):
        for s in range(2):
            loads.append(pltpu.make_async_copy(kv_sorted.at[s, h], kvs.at[s, h], sems.at[s, h]))
            loads[-1].start()
    rate = LOG2E * HD**-0.5
    factor = jnp.where(lax.broadcasted_iota(jnp.int32, (1, 2 * HD), 1) < HD, HD**-0.5, 1.0)
    blank = jnp.zeros((QROWS, HD), BF)
    for s in range(2):
        for h in range(HH):
            for half in range(2):
                up = heads_at(da, s, h, half)
                qd_ref[s, h, half, :QROWS] = jnp.concatenate([heads_at(qr, s, h, half), blank], axis=1)
                qd_ref[s, h, half, QROWS:] = jnp.concatenate([blank, up], axis=1)
                inner = (up.astype(F32) * heads_at(attn, s, h, half)).T
                delta_ref[s, h, half] = jnp.sum(inner, axis=0, keepdims=True)
    for c in loads:
        c.wait()
    streams = [
        Summing(stage.at[h], KV_DIMS, at, KV_SUM_ORDERS[h], 2 * TOK, slice(None), buffers[h], ssem.at[h], rsem.at[h], lsem.at[h])
        for h in range(HH)
    ]
    todo = [["pass_on", "finish", "start", "pass_on", "finish", "start", "pass_on", "finish"] for h in range(HH)]
    for h in range(HH):

        def sequence(s, carry):
            dq_acc[...] = jnp.zeros_like(dq_acc)
            acc[...] = jnp.zeros_like(acc)

            def backward(half, block, limit):
                keys = kvs[s, h, block].reshape(KEYS, 2 * HD)
                both = lax.dot_general(keys, qd_ref[s, h, half], NT, preferred_element_type=F32)
                prob = masked(jnp.exp2(both[:, :QROWS] * rate - l_ref[s, h, half]), limit)
                grad = (prob * (both[:, QROWS:] - delta_ref[s, h, half])).astype(BF)
                pair = jnp.concatenate([grad, prob.astype(BF)], axis=1)
                kv = lax.dot_general(pair, qd_ref[s, h, half], NN, preferred_element_type=F32)
                return (
                    kv.reshape(SPANS_STEP, SPAN, 2 * HD),
                    lax.dot_general(keys, grad, TN, preferred_element_type=F32),
                )

            def spans(block):
                return pl.ds(block * SPANS_STEP, SPANS_STEP)

            def high(k, c):
                kv, q = backward(1, k, None)
                acc[spans(k)] += kv
                dq_acc[1] += q
                return c

            def either(k, c):
                half = tab[s, AT_STEP_HALF + k]
                kv, q = backward(half, tab[s, AT_STEP_BLOCK + k], None)
                up = half.astype(F32)
                acc[spans(k)] += kv * (1.0 - up)
                acc[spans(6 - k)] += kv * up
                dq_acc[0] += q * (1.0 - up)
                dq_acc[1] += q * up
                return c

            lax.fori_loop(0, 4, high, 0)
            lax.fori_loop(0, 3, either, 0)
            for half in range(2):
                kv, q = backward(half, tab[s, AT_EDGE + half], tab[s, AT_LIMIT + half])
                for k in range(4):
                    acc[spans(k if half == 0 else 7 - k)] += kv * tab[s, AT_MARK + k].astype(F32)
                q = dq_acc[half] + q
                put_heads(dq_ref, s, h, half, (q[:HD, :] * HD**-0.5).T)

            def put(j, c):
                for half in range(2):
                    v = acc[tab[s, AT_MAP + half * N_CTX + j]] * factor
                    rows = pl.ds(pl.multiple_of(s * TOK + half * SPAN, SPAN), SPAN)
                    stage[h, lax.div(j, 16), lax.rem(lax.div(j, 4), 4), lax.rem(j, 4), rows, :] = v.astype(BF)
                return c

            lax.fori_loop(0, N_CTX, put, 0)
            return carry

        lax.fori_loop(0, 2, sequence, 0)
        for k in range(h):
            for step in range(1 if k == h - 1 else 2):
                getattr(streams[k], todo[k].pop(0))()
        streams[h].start()
    while any(todo):
        for k in range(HH):
            if todo[k]:
                name = todo[k].pop(0)
                getattr(streams[k], name)()
                if name == "finish" and todo[k]:
                    getattr(streams[k], todo[k].pop(0))()
    for h in range(HH):
        dkv_out[h] = buffers[h][2]["sum"][...]
    for e in early:
        e.wait()
    for st in streams:
        for c in st.sent:
            c.wait_send()


def attend_back(tab, query, grad_attn, attn, log_sum, kv_sorted, grads, cid):
    vmem = pl.BlockSpec(memory_space=pltpu.VMEM)
    anywhere = pl.BlockSpec(memory_space=pl.ANY)
    out = pl.pallas_call(
        attend_back_kernel,
        out_shape=[
            jax.ShapeDtypeStruct((2 * TOK, QW), F32),
            jax.ShapeDtypeStruct((HH, 2 * TOK, 2 * HD), F32),
        ]
        + early_shapes(),
        in_specs=[pl.BlockSpec(memory_space=pltpu.SMEM)] + [vmem] * 4 + [anywhere] * 5,
        out_specs=[vmem, vmem] + [anywhere] * (2 * N_EARLY),
        scratch_shapes=[
            pltpu.VMEM((2, HH, KEY_BLOCKS, SPANS_STEP, SPAN, 2 * HD), BF),
            pltpu.VMEM((2, HH, 2, 2 * QROWS, 2 * HD), BF),
            pltpu.VMEM((2, HH, 2, 1, QROWS), F32),
            pltpu.VMEM((HH, 2, 4, 4, 2 * TOK, 2 * HD), BF),
            pltpu.VMEM((2 * N_CTX, SPAN, 2 * HD), F32),
            pltpu.VMEM((2, 2 * HD, QROWS), F32),
            [sum_scratch(KV_SUM_ORDERS[h], KV_DIMS, 2 * TOK, 2 * HD) for h in range(HH)],
            pltpu.SemaphoreType.DMA((N_EARLY, 4)),
            pltpu.SemaphoreType.DMA((N_EARLY, 4)),
            pltpu.SemaphoreType.DMA((HH, 3, 6)),
            pltpu.SemaphoreType.DMA((HH, 3, 6)),
            pltpu.SemaphoreType.DMA((HH, 3)),
            pltpu.SemaphoreType.DMA((2, HH)),
        ],
        compiler_params=pltpu.CompilerParams(
            collective_id=cid, has_side_effects=True, vmem_limit_bytes=48 * 1024 * 1024
        ),
        name="attend_back",
    )(tab, query, grad_attn, attn, log_sum, kv_sorted, *[g.reshape(2, 4, 4, 2, 32, g.shape[-1]) for g in grads])
    return out[0], out[1], out[2:]


def permutation(axis, by):
    pairs = []
    for c in range(N_CTX):
        for f in range(4):
            h, x, y = c // 16, (c // 4) % 4, c % 4
            z, core = h * 2 + f // 2, f % 2
            if axis == "x":
                x = (x + by) % 4
            elif axis == "y":
                y = (y + by) % 4
            elif axis == "z":
                z = (z + by) % 4
            else:
                core = 1 - core
            pairs.append((c * 4 + f, ((z // 2) * 16 + x * 4 + y) * 4 + (z % 2) * 2 + core))
    return pairs


def shift(value, axis, by=1):
    return lax.ppermute(value, ("ctx", "fsdp"), permutation(axis, by))


def norm_rows(value_in, gain_row):
    inverse = lax.rsqrt(jnp.mean(value_in * value_in, axis=-1, keepdims=True) + EPSILON)
    return (value_in * inverse * gain_row, inverse)


def norm_back(value_in, inverse, gain_row, upstream):
    scaled = upstream * gain_row
    backward = inverse * scaled - value_in * inverse**3 * jnp.mean(scaled * value_in, axis=-1, keepdims=True)
    return (backward, upstream * value_in * inverse)


def body(layer_input, w_qkv, w_out, w_gate_up, w_down, norm_gains, span_map, cotangent):
    at = here()
    core, low = at["core"], at["l"]
    w_q = w_qkv[:, : HQ * HD].reshape(16, 2, QW).transpose(1, 0, 2)
    w_k = w_qkv[:, HQ * HD : (HQ + HK) * HD].reshape(16, 2, HH, HD)
    w_v = w_qkv[:, (HQ + HK) * HD :].reshape(16, 2, HH, HD)
    w_kv = jnp.concatenate([w_k, w_v], axis=3).reshape(16, 2, KVW).transpose(1, 0, 2)
    shard_one = jnp.concatenate([w_q, w_kv], axis=2)
    shard_gate = w_gate_up[:, :FF].reshape(16, 2, FH).transpose(1, 0, 2)
    shard_up = w_gate_up[:, FF:].reshape(16, 2, FH).transpose(1, 0, 2)
    shard_down = w_down.reshape(16, 2, FH).transpose(1, 0, 2)
    shard_out = w_out.reshape(16, 2, QW).transpose(1, 0, 2)
    share = norm_gains.shape[0]
    device = lax.axis_index(("ctx", "fsdp"))
    own_gain = lax.dynamic_update_slice_in_dim(jnp.zeros((40 * 128,), F32), norm_gains.astype(F32), device * share, 0)

    ctx_index = lax.axis_index("ctx")
    maps = lax.dynamic_slice_in_dim(span_map, low * 2, 2, 0)
    own_span = lax.dynamic_slice_in_dim(maps, ctx_index, 1, 1)
    spans = jnp.concatenate([own_span, 2 * N_CTX - 1 - own_span], axis=1)
    positions = (spans[:, :, None] * SPAN + jnp.arange(SPAN, dtype=jnp.int32)).reshape(2 * TOK)
    match = maps[:, None, :] == jnp.arange(N_CTX, dtype=jnp.int32)[None, :, None]
    inverse_map = jnp.sum(jnp.where(match, jnp.arange(N_CTX, dtype=jnp.int32), 0), axis=2)
    holder = jnp.concatenate([inverse_map, inverse_map[:, ::-1]], axis=1)
    upper = (jnp.arange(2 * N_CTX, dtype=jnp.int32) >= N_CTX).astype(jnp.int32)[None, :] + jnp.zeros_like(holder)
    low_block = own_span // SPANS_STEP
    low_limit = own_span % SPANS_STEP * SPAN
    three = jnp.arange(3, dtype=jnp.int32)[None, :]
    step_half = (three >= low_block).astype(jnp.int32)
    tab = jnp.concatenate(
        [
            holder // 16,
            holder // 4 % 4,
            holder % 4,
            upper,
            step_half,
            jnp.where(step_half == 0, three, 6 - three),
            (jnp.arange(4, dtype=jnp.int32)[None, :] == low_block).astype(jnp.int32),
            low_block,
            KEY_BLOCKS - 1 - low_block,
            low_limit,
            KEYS - SPAN - low_limit,
            maps,
            2 * N_CTX - 1 - maps,
        ],
        axis=1,
    )
    half_dim = HD // 2
    frequencies = ROPE_BASE ** (-(jnp.arange(half_dim, dtype=F32) * 2.0 / HD))
    angles = positions.astype(F32)[:, None] * frequencies[None, :]
    cosine, sine = jnp.cos(angles), jnp.sin(angles)
    cosine = jnp.concatenate([cosine] * 4, axis=1)
    sine = jnp.concatenate([-sine, sine] * 2, axis=1)

    weights = [shard_one, shard_gate, shard_up, shard_down, shard_out]
    (w_joined, w_gate, w_up, w_back, w_proj, x_pair, dy_pair, gains, joined, normed_one, query, keys, attn_f32, attn_low, log_sum) = front(
        tab, weights, layer_input[0], cotangent[0], own_gain.reshape(40, 128), cosine, sine, 1
    )
    w_joined, w_gate, w_up, w_back, w_proj = (w.reshape(D, -1) for w in (w_joined, w_gate, w_up, w_back, w_proj))
    gain_one, gain_two = gains[:16].reshape(D), gains[16:32].reshape(D)
    stream_in = x_pair.reshape(2 * TOK, D).astype(F32)
    dy = dy_pair.reshape(2 * TOK, D)

    partial_a = lax.dot_general(attn_low, w_proj, NT, preferred_element_type=F32)
    branch_a = partial_a + shift(partial_a, "core")
    middle = stream_in + branch_a
    normed_two, inverse_two = norm_rows(middle, gain_two)
    normed_two = normed_two.astype(BF)
    gate_part = jnp.dot(normed_two, w_gate, preferred_element_type=F32)
    up_part = jnp.dot(normed_two, w_up, preferred_element_type=F32)
    sigmoid_gate = jax.nn.sigmoid(gate_part)
    silu_gate = gate_part * sigmoid_gate
    hidden = (silu_gate * up_part).astype(BF)
    partial_f = lax.dot_general(hidden, w_back, NT, preferred_element_type=F32)
    grad_hidden = jnp.dot(dy, w_back, preferred_element_type=F32)
    grad_gate = (grad_hidden * up_part * sigmoid_gate * (1.0 + gate_part * (1.0 - sigmoid_gate))).astype(BF)
    grad_up = (grad_hidden * silu_gate).astype(BF)
    partial_n = lax.dot_general(grad_gate, w_gate, NT, preferred_element_type=F32)
    partial_n = partial_n + lax.dot_general(grad_up, w_up, NT, preferred_element_type=F32)

    def own_rows(value):
        return lax.dynamic_slice_in_dim(value, core * TOK, TOK, 0)

    def other_rows(value):
        return lax.dynamic_slice_in_dim(value, (1 - core) * TOK, TOK, 0)

    branch_f = own_rows(partial_f) + shift(other_rows(partial_f), "core")
    result = own_rows(middle) + branch_f
    grad_normed_two = partial_n + shift(partial_n, "core")
    back_two, gain_two_terms = norm_back(middle, inverse_two, gain_two, grad_normed_two)
    grad_middle = dy.astype(F32) + back_two
    grad_branch = grad_middle.astype(BF)

    def outer(left, right):
        return lax.dot_general(left, right, TN, preferred_element_type=F32).astype(BF)

    early = [outer(normed_two, grad_gate), outer(normed_two, grad_up), outer(dy, hidden), outer(grad_branch, attn_low)]

    grad_attn = jnp.dot(grad_branch, w_proj, preferred_element_type=F32).astype(BF)
    dq, grad_kv, begun = attend_back(tab, query, grad_attn, attn_f32, log_sum, keys, early, 4)
    grad_joined, head_terms = rope_back(joined, dq, grad_kv, gains, cosine, sine)
    partial_one = lax.dot_general(grad_joined, w_joined, NT, preferred_element_type=F32)
    grad_normed_one = own_rows(partial_one) + shift(other_rows(partial_one), "core")
    own_in = layer_input[0].astype(F32)
    inverse_one = lax.rsqrt(jnp.mean(own_in * own_in, axis=-1, keepdims=True) + EPSILON)
    back_one, gain_one_terms = norm_back(own_in, inverse_one, gain_one, grad_normed_one)
    grad_input = own_rows(grad_middle) + back_one

    def mean_root(stream):
        return jnp.sum(jnp.sqrt(jnp.mean(stream * stream, axis=-1)))

    stats = jnp.stack([mean_root(s) for s in (own_in, own_rows(branch_a), own_rows(middle))] + [mean_root(branch_f)])
    sums = jnp.concatenate(
        [
            jnp.sum(gain_one_terms, axis=0),
            jnp.sum(own_rows(gain_two_terms), axis=0),
            head_terms[0],
            stats,
        ]
    )
    sums = jnp.pad(sums, (0, 40 * 128 - sums.shape[0])).reshape(40, 128)
    own_gate, own_up, own_down, own_out, own_qkv, sums = sum_weights(
        early + [outer(normed_one, grad_joined)], sums, begun, SUMS, 5, 62 * 1024 * 1024
    )
    sums = sums.reshape(-1)
    grad_mlp = jnp.concatenate([own_gate[0], own_gate[1], own_up[0], own_up[1]], axis=1)
    grad_down = jnp.concatenate([own_down[0], own_down[1]], axis=1)
    kv_cols = own_qkv[:, :, QW:].reshape(2, 16, HH, 2, HD)
    grad_qkv = jnp.concatenate(
        [
            own_qkv[0, :, :QW],
            own_qkv[1, :, :QW],
            *(kv_cols[half, :, :, kind].reshape(16, HH * HD) for kind in range(2) for half in range(2)),
        ],
        axis=1,
    )
    grad_proj = jnp.concatenate([own_out[0], own_out[1]], axis=1)

    own_gains = lax.dynamic_slice_in_dim(sums, device * share, share, 0)
    stream_rms = sums[4224:4228] / (TOK * N_CTX * 4)
    return (
        result[None].astype(BF),
        grad_input[None].astype(BF),
        grad_qkv,
        grad_proj,
        grad_mlp,
        grad_down,
        own_gains,
        stream_rms,
    )


def solution(mesh):
    rows = P(("ctx", "fsdp"), None)
    tokens = P("fsdp", "ctx", None)
    return jax.shard_map(
        body,
        mesh=mesh,
        in_specs=(tokens, rows, rows, rows, rows, P(("ctx", "fsdp")), P(), tokens),
        out_specs=(tokens, tokens, rows, rows, rows, rows, P(("ctx", "fsdp")), P()),
        check_vma=False,
    )
```

```python
import functools

import jax
import jax.numpy as jnp
from jax import lax
from jax.experimental import pallas as pl
from jax.experimental.pallas import tpu as pltpu
from jax.sharding import PartitionSpec as P

D = 2048
HQ = 24
HK = 6
HD = 64
FF = 4352
TOK = 128
SPAN = 64
N_CTX = 32

HH = HK // 2
GROUP = HQ // HK
QH = HQ // 2
QW = QH * HD
KVW = HH * 2 * HD
FH = FF // 2
KEYS = 512
SPANS_STEP = KEYS // SPAN
KEY_BLOCKS = 8
QROWS = GROUP * SPAN

EPSILON = 1e-06
ROPE_BASE = 10000.0
LOG2E = 1.4426950408889634
AT_H, AT_X, AT_Y, AT_HALF = 0, 64, 128, 192
AT_STEP_HALF, AT_STEP_BLOCK, AT_MARK, AT_EDGE, AT_LIMIT, AT_MAP = 256, 259, 262, 266, 268, 270
MESH = pl.DeviceIdType.MESH
BF = jnp.bfloat16
F32 = jnp.float32
NT = (((1,), (1,)), ((), ()))
NN = (((1,), (0,)), ((), ()))
TN = (((0,), (0,)), ((), ()))
W_DIMS = ("h", "x", "y", "l")
KV_DIMS = ("h", "x", "y")
ORDERS = (("x", "y", "z"), ("y", "z", "x"), ("z", "x", "y"))
KV_ORDERS = (("h", "x", "y"), ("x", "y", "h"), ("y", "h", "x"))
KV_PARTS = ((0, 96, ("y", "x", "h")), (96, 96, ("x", "y", "h")), (192, 64, ("h", "x", "y")))
SUMS = (
    (0, 0, 1152, ORDERS[0]),
    (1, 0, 1152, ORDERS[1]),
    (2, 0, 1152, ORDERS[2]),
    (0, 1152, 1024, ORDERS[0]),
    (1, 1152, 1024, ORDERS[1]),
    (2, 1152, 1024, ORDERS[2]),
    (3, 0, 256, ORDERS[0]),
    (3, 256, 256, ORDERS[1]),
    (3, 512, 256, ORDERS[2]),
    (4, 0, 384, ORDERS[0]),
    (4, 384, 384, ORDERS[1]),
    (4, 768, 384, ORDERS[2]),
)
N_EARLY = 9
SIZES = {"x": 4, "y": 4, "z": 4, "h": 2}


def here():
    c = lax.axis_index("ctx")
    f = lax.axis_index("fsdp")
    return {
        "x": lax.rem(lax.div(c, 4), 4),
        "y": lax.rem(c, 4),
        "z": lax.div(c, 16) * 2 + lax.div(f, 2),
        "h": lax.div(c, 16),
        "l": lax.div(f, 2),
        "core": lax.rem(f, 2),
    }


def device_of(x, y, z, core):
    return (lax.div(z, 2) * 16 + x * 4 + y, lax.rem(z, 2) * 2 + core)


def moved(at, axis, by):
    if axis == "core":
        return device_of(at["x"], at["y"], at["z"], 1 - at["core"])
    place = {k: at[k] for k in ("x", "y", "z")}
    if axis == "h":
        place["z"] = lax.rem(at["z"] + 2, 4)
    else:
        place[axis] = lax.rem(at[axis] + by + 4, 4)
    return device_of(place["x"], place["y"], place["z"], at["core"])


def labels(axis, value):
    if axis == "z":
        return {"h": lax.div(value, 2), "l": lax.rem(value, 2)}
    return {axis: value}


def pick(ref, dims, values, tail):
    return ref.at[tuple(values[d] if d in values else slice(None) for d in dims) + tail]


def greet(devices):
    barrier = pltpu.get_barrier_semaphore()
    for d in devices:
        pl.semaphore_signal(barrier, inc=1, device_id=d, device_id_type=MESH)
    pl.semaphore_wait(barrier, len(devices))


def send(src, dst, ssem, rsem, device):
    copy = pltpu.make_async_remote_copy(
        src_ref=src, dst_ref=dst, send_sem=ssem, recv_sem=rsem, device_id=device, device_id_type=MESH
    )
    copy.start()
    return copy


class Gathering:
    def __init__(self, ref, dims, at, order, rows, cols, ssem, rsem):
        self.ref, self.dims, self.at, self.order, self.rows, self.cols = ref, dims, at, order, rows, cols
        self.ssem, self.rsem, self.phase, self.sent = ssem, rsem, 0, []

    def block(self, coordinate, rows):
        later = {}
        for a in self.order[self.phase + 1 :]:
            later.update(labels(a, self.at[a]))
        return pick(self.ref, self.dims, {**later, **labels(self.axis, coordinate)}, (rows, self.cols))

    def send(self, n, ref, by):
        c = send(ref, ref, self.ssem.at[self.phase, n], self.rsem.at[self.phase, n], moved(self.at, self.axis, by))
        self.sent.append(c)
        return c

    def start(self):
        self.axis = self.order[self.phase]
        mine = self.block(self.at[self.axis], slice(None))
        self.first = [self.send(0, mine, 1)]
        if SIZES[self.axis] == 4:
            self.first.append(self.send(1, mine, 3))

    def pass_on(self):
        for c in self.first:
            c.wait_recv()
        self.second = []
        if SIZES[self.axis] == 4:
            half = self.rows // 2
            me = self.at[self.axis]
            self.second.append(self.send(2, self.block(lax.rem(me + 3, 4), pl.ds(0, half)), 1))
            self.second.append(self.send(3, self.block(lax.rem(me + 1, 4), pl.ds(half, half)), 3))

    def finish(self):
        for c in self.second:
            c.wait_recv()
        self.phase += 1

    def wait_sent(self):
        for c in self.sent:
            c.wait_send()


def neighbours(at, axes):
    out = []
    for a in axes:
        if a in ("core", "h"):
            out.append(moved(at, a, 1))
        else:
            out.append(moved(at, a, 1))
            out.append(moved(at, a, 3))
    return out


GATHER = (
    (0, 0, 1152, ORDERS[0]),
    (1, 0, 1152, ORDERS[1]),
    (2, 0, 1152, ORDERS[2]),
    (0, 1152, 1024, ORDERS[0]),
    (1, 1152, 1024, ORDERS[1]),
    (2, 1152, 1024, ORDERS[2]),
    (3, 0, 256, ORDERS[0]),
    (3, 256, 256, ORDERS[1]),
    (3, 512, 256, ORDERS[2]),
)


def lane_of(shape):
    return lax.broadcasted_iota(jnp.int32, shape, len(shape) - 1)


def swap_halves(v):
    return jnp.where(lax.rem(lane_of(v.shape), HD) < HD // 2, pltpu.roll(v, 96, 1), pltpu.roll(v, 32, 1))


def head_sums(v):
    low = lane_of(v.shape) < HD
    a = jnp.sum(jnp.where(low, v, 0.0), axis=1, keepdims=True)
    b = jnp.sum(jnp.where(low, 0.0, v), axis=1, keepdims=True)
    return jnp.where(low, a, b)


def tile_gain(row, is_key):
    low = lane_of(row.shape) < HD
    turned = pltpu.roll(row, HD, 1)
    return jnp.where(low, turned, 1.0) if is_key else jnp.where(low, row, turned)


def front_kernel(
    tab, shard_one, gate_up, down, out, x, dy, gains, cosine, sine,
    w_one, w_gate, w_up, w_down, w_out, x_pair, dy_pair, gain_all, joined, normed, query, kv_out, o_ref, low_ref, l_ref,
    one, kv_src, kvg, kvs, q_ref, acc, sum_ref, small_buf, psem, lsem, tssem, trsem, ossem, orsem, gssem, grsem, kssem, krsem, ksem,
):
    at = here()
    core = at["core"]
    sibling = moved(at, "core", 1)
    greet([sibling] + sum_peers(at, ("x", "y", "z")))
    own = {d: at[d] for d in W_DIMS}
    total = Total(gains[...], at, small_buf, tssem, trsem)
    remote, local = [], []

    def half_of(src, start, width, which):
        return src.at[:, pl.ds(pl.multiple_of(start + which * width, 128), width)]

    pairs = [
        (lambda c: shard_one.at[c], one),
        (lambda c: half_of(gate_up, 0, FH, c), w_gate),
        (lambda c: half_of(gate_up, FF, FH, c), w_up),
        (lambda c: half_of(down, 0, FH, c), w_down),
        (lambda c: half_of(out, 0, QW, c), w_out),
    ]
    for i, (src, ref) in enumerate(pairs):
        dst = pick(ref, W_DIMS, own, (pl.ds(core * 16, 16), slice(None)))
        remote.append(send(src(1 - core), dst, psem.at[i, 0], psem.at[i, 1], sibling))
        local.append(pltpu.make_async_copy(src(core), dst, lsem.at[i]))
        local[-1].start()
    for i, (src, ref) in ((5, (x, x_pair)), (6, (dy, dy_pair))):
        remote.append(send(src, ref.at[core], psem.at[i, 0], psem.at[i, 1], sibling))
        local.append(pltpu.make_async_copy(src, ref.at[core], lsem.at[i]))
        local[-1].start()

    def arrived(i):
        remote[i].wait_recv()
        local[i].wait()

    ones = [
        Gathering(one, W_DIMS, at, ORDERS[k], 32, pl.ds(k * 384, 384), ossem.at[k], orsem.at[k]) for k in range(3)
    ]
    rest = [
        Gathering(pairs[1 + a][1], W_DIMS, at, order, 32, pl.ds(start, width), gssem.at[k], grsem.at[k])
        for k, (a, start, width, order) in enumerate(GATHER)
    ]
    keys = [
        Gathering(kvg.at[h], KV_DIMS, at, KV_ORDERS[h], 4, slice(None), kssem.at[h], krsem.at[h]) for h in range(HH)
    ]

    def every(streams, *steps):
        for s in streams:
            for step in steps:
                getattr(s, step)()

    arrived(0)
    every(ones, "start")
    for i in range(1, 5):
        arrived(i)
    every(rest, "start")
    total.step()
    every(ones, "pass_on")
    every(rest, "pass_on")
    total.step()
    every(ones, "finish", "start")
    every(rest, "finish")
    total.step()
    every(ones, "pass_on")
    total.step()
    gain_all[...] = total.value
    every(ones, "finish", "start")
    every(rest, "start")
    arrived(5)
    gain_row = jnp.concatenate([total.value[j : j + 1] for j in range(D // 128)], axis=1)

    def norm(r, carry):
        rows = pl.ds(pl.multiple_of(r * 32, 32), 32)
        for s in range(2):
            v = x_pair[s, rows, :].astype(F32)
            inverse = lax.rsqrt(jnp.sum(v * v, axis=1, keepdims=True) * (1.0 / D) + EPSILON)
            normed[pl.ds(pl.multiple_of(s * TOK + r * 32, 32), 32), :] = (v * inverse * gain_row).astype(BF)
        return carry

    lax.fori_loop(0, TOK // 32, norm, 0)
    every(ones, "pass_on")
    every(ones, "finish")
    keep = pltpu.make_async_copy(one, w_one, lsem.at[7])
    keep.start()
    head_gains = total.value[32:33]

    def product(start, width):
        w = one[:, :, :, :, :, start : start + width].reshape(D, width)
        joined[:, start : start + width] = jnp.dot(normed[...], w, preferred_element_type=F32)

    def rope(tile, is_key):
        v = joined[:, tile * 128 : (tile + 1) * 128]
        low = lane_of(v.shape) < HD
        c, n = cosine[...], sine[...]
        inverse = lax.rsqrt(head_sums(v * v) * (1.0 / HD) + EPSILON)
        if is_key:
            inverse = jnp.where(low, inverse, 1.0)
            c, n = jnp.where(low, c, 1.0), jnp.where(low, n, 0.0)
        v = v * inverse * tile_gain(head_gains, is_key)
        return (v * c + swap_halves(v) * n).astype(BF)

    product(QW, KVW)
    for h in range(HH):
        kv_src[h] = rope(QW // 128 + h, True).reshape(4, SPAN, 2 * HD)
    kv_own = {d: at[d] for d in KV_DIMS}
    puts = [pltpu.make_async_copy(kv_src.at[h], pick(kvg.at[h], KV_DIMS, kv_own, ()), ksem.at[h]) for h in range(HH)]
    for c in puts:
        c.start()
    for c in puts:
        c.wait()
    every(keys, "start")
    every(rest, "pass_on")
    product(0, 384)
    every(keys, "pass_on")
    every(rest[:3], "finish", "start")
    every(keys, "finish", "start")
    product(384, 384)
    every(keys, "pass_on")
    for t in range(QW // 128):
        query[:, t * 128 : (t + 1) * 128] = rope(t, False)
    every(keys, "finish", "start")
    every(rest[3:], "finish")
    blank = jnp.zeros((QROWS, HD), BF)
    for s in range(2):
        for h in range(HH):
            for half in range(2):
                q_ref[s, h, half] = jnp.concatenate([heads_at(query, s, h, half), blank], axis=1)
    every(keys, "pass_on")
    every(rest[3:], "start")
    every(keys, "finish")

    def sort(p, carry):
        for s in range(2):
            place = tuple(tab[s, column + p] for column in (AT_H, AT_X, AT_Y))
            half = tab[s, AT_HALF + p]
            for h in range(HH):
                kvs[s, h, lax.div(p, SPANS_STEP), lax.rem(p, SPANS_STEP)] = kvg[(h,) + place + (s * 2 + half,)]
        return carry

    lax.fori_loop(0, 2 * N_CTX, sort, 0)
    keep_keys = pltpu.make_async_copy(kvs, kv_out, ksem.at[HH])
    keep_keys.start()
    attend_heads(tab, 0, q_ref, kvs, o_ref, low_ref, l_ref, acc, sum_ref)
    every(rest[:3], "pass_on")
    attend_heads(tab, 1, q_ref, kvs, o_ref, low_ref, l_ref, acc, sum_ref)
    every(rest[3:], "pass_on")
    every(rest, "finish")
    keep_keys.wait()
    arrived(6)
    keep.wait()
    for c in remote + total.sent:
        c.wait_send()
    for s in ones + rest + keys:
        s.wait_sent()


def front(tab, shards, x, dy, gains, cosine, sine, cid):
    anywhere = pl.BlockSpec(memory_space=pl.ANY)
    vmem = pl.BlockSpec(memory_space=pltpu.VMEM)
    full = [jax.ShapeDtypeStruct((2, 4, 4, 2, 32, w), BF) for w in (QW + KVW, FH, FH, FH, QW)]
    n = len(GATHER)
    return pl.pallas_call(
        front_kernel,
        out_shape=full
        + [
            jax.ShapeDtypeStruct((2,) + x.shape, BF),
            jax.ShapeDtypeStruct((2,) + dy.shape, BF),
            jax.ShapeDtypeStruct(gains.shape, F32),
            jax.ShapeDtypeStruct((2 * TOK, QW + KVW), F32),
            jax.ShapeDtypeStruct((2 * TOK, D), BF),
            jax.ShapeDtypeStruct((2 * TOK, QW), BF),
            jax.ShapeDtypeStruct((2, HH, KEY_BLOCKS, SPANS_STEP, SPAN, 2 * HD), BF),
            jax.ShapeDtypeStruct((2 * TOK, QW), F32),
            jax.ShapeDtypeStruct((2 * TOK, QW), BF),
            jax.ShapeDtypeStruct((2, HH, 2, 1, QROWS), F32),
        ],
        in_specs=[pl.BlockSpec(memory_space=pltpu.SMEM)] + [anywhere] * 6 + [vmem] * 3,
        out_specs=[anywhere] * 5 + [vmem, anywhere] + [vmem] * 4 + [anywhere] + [vmem] * 3,
        scratch_shapes=[
            pltpu.VMEM((2, 4, 4, 2, 32, QW + KVW), BF),
            pltpu.VMEM((HH, 4, SPAN, 2 * HD), BF),
            pltpu.VMEM((HH, 2, 4, 4, 4, SPAN, 2 * HD), BF),
            pltpu.VMEM((2, HH, KEY_BLOCKS, SPANS_STEP, SPAN, 2 * HD), BF),
            pltpu.VMEM((2, HH, 2, QROWS, 2 * HD), BF),
            pltpu.VMEM((2, 2 * HD, QROWS), F32),
            pltpu.VMEM((2, 1, QROWS), F32),
            pltpu.VMEM((4, 4) + gains.shape, F32),
            pltpu.SemaphoreType.DMA((7, 2)),
            pltpu.SemaphoreType.DMA((8,)),
            pltpu.SemaphoreType.DMA((4, 4)),
            pltpu.SemaphoreType.DMA((4, 4)),
            pltpu.SemaphoreType.DMA((3, 3, 4)),
            pltpu.SemaphoreType.DMA((3, 3, 4)),
            pltpu.SemaphoreType.DMA((n, 3, 4)),
            pltpu.SemaphoreType.DMA((n, 3, 4)),
            pltpu.SemaphoreType.DMA((HH, 3, 4)),
            pltpu.SemaphoreType.DMA((HH, 3, 4)),
            pltpu.SemaphoreType.DMA((HH + 1,)),
        ],
        compiler_params=pltpu.CompilerParams(
            collective_id=cid, has_side_effects=True, vmem_limit_bytes=48 * 1024 * 1024
        ),
        name="front",
    )(tab, *shards, x, dy, gains, cosine, sine)


def lead_shape(dims):
    full = {"h": 2, "x": 4, "y": 4, "l": 2}
    return tuple(full[d] for d in dims)


def without(dims, axis):
    gone = ("h", "l") if axis == "z" else (axis,)
    return tuple(d for d in dims if d not in gone)


class Summing:
    def __init__(self, source, dims, at, order, rows, cols, buffers, ssem, rsem, lsem, begun=None, base=None):
        self.ref, self.dims, self.at, self.order, self.begun = source, dims, at, order, begun
        self.cols, self.buffers, self.rows = cols, buffers, rows
        self.ssem, self.rsem, self.lsem = ssem, rsem, lsem
        self.phase, self.sent, self.base = 0, [], base
        self.resident = base is not None

    def part(self, coordinate, start, length):
        rows = pl.ds(start + (self.base or 0), length)
        return pick(self.ref, self.dims, labels(self.axis, coordinate), (rows, self.cols))

    def send(self, n, src, dst, by):
        c = send(src, dst, self.ssem.at[self.phase, n], self.rsem.at[self.phase, n], moved(self.at, self.axis, by))
        self.sent.append(c)
        return c

    def start(self):
        self.axis = self.order[self.phase]
        self.rest = without(self.dims, self.axis)
        self.lead = lead_shape(self.rest)
        half = self.rows // 2
        first, second, every = (0, half), (half, half), (0, self.rows)
        i = self.at[self.axis]
        buf = self.buffers[self.phase]
        self.local = []
        if SIZES[self.axis] == 2:
            self.direct = (self.send(0, self.part(1 - i, *every), buf["got"].at[0], 1),)
        else:
            up, down, far = lax.rem(i + 1, 4), lax.rem(i + 3, 4), lax.rem(i + 2, 4)
            self.near = (up, down)
        if self.phase == 0 and self.begun is not None:
            self.relay, self.direct = (), ()
        elif SIZES[self.axis] == 4:
            self.relay = (
                self.send(0, self.part(far, *first), buf["relay"].at[0], 1),
                self.send(1, self.part(far, *second), buf["relay"].at[1], 3),
            )
            self.direct = (
                self.send(2, self.part(up, *second), buf["got"].at[1, 1], 1),
                self.send(3, self.part(down, *first), buf["got"].at[0, 1], 3),
            )
        if self.phase == 0 and not self.resident:
            todo = [(self.part(i, *every), buf["mine"])]
            if self.begun is not None:
                passed, direct = self.begun[1], self.begun[0]
                todo += [(passed.at[n], buf["got"].at[n, 0]) for n in range(2)]
                todo += [(direct.at[n], buf["got"].at[n, 1]) for n in range(2)]
            elif SIZES[self.axis] == 4:
                todo.append((self.part(up, *first), buf["own"].at[0]))
                todo.append((self.part(down, *second), buf["own"].at[1]))
            for n, (src, dst) in enumerate(todo):
                c = pltpu.make_async_copy(src, dst, self.lsem.at[n])
                c.start()
                self.local.append(c)

    def over_lead(self, add):
        rest = self.lead[1:]
        spots = [()]
        for n in rest:
            spots = [s + (j,) for s in spots for j in range(n)]
        if not self.lead:
            add(())
            return

        def go(j, carry):
            for s in spots:
                add((j,) + s)
            return carry

        lax.fori_loop(0, self.lead[0], go, 0)

    def pass_on(self):
        if SIZES[self.axis] == 2 or (self.phase == 0 and self.begun is not None):
            return
        buf = self.buffers[self.phase]
        half = self.rows // 2
        for n, by in ((0, 1), (1, 3)):
            self.relay[n].wait_recv()
            if self.phase == 0 and not self.resident:
                self.local[1 + n].wait()
                own = buf["own"].at[n]
            else:
                own = self.part(self.near[n], n * half, half)

            def add(spot):
                here_ = spot + (slice(None), slice(None))
                both = buf["relay"][(n,) + here_].astype(F32) + own[here_].astype(F32)
                buf["relay"][(n,) + here_] = both.astype(BF)

            self.over_lead(add)
            c = self.send(4 + n, buf["relay"].at[n], buf["got"].at[n, 0], by)
            self.direct = self.direct + (c,)

    def finish(self):
        buf = self.buffers[self.phase]
        half = self.rows // 2
        if self.local:
            self.local[0].wait()
        if self.begun is not None:
            for c in self.local[1:]:
                c.wait()
        for c in self.direct:
            c.wait_recv()
        copied = self.phase == 0 and not self.resident
        own = buf["mine"] if copied else self.part(self.at[self.axis], 0, self.rows)
        out = buf["mine"] if copied else buf["sum"]

        def add(spot):
            if SIZES[self.axis] == 2:
                here_ = spot + (slice(None), slice(None))
                out[here_] = (own[here_].astype(F32) + buf["got"][(0,) + here_].astype(F32)).astype(out.dtype)
                return
            for n in range(2):
                rows = spot + (pl.ds(n * half, half), slice(None))
                all_ = spot + (slice(None), slice(None))
                total = own[rows].astype(F32) + buf["got"][(n, 0) + all_].astype(F32)
                total = total + buf["got"][(n, 1) + all_].astype(F32)
                out[rows] = total.astype(out.dtype)

        self.over_lead(add)
        self.ref, self.dims, self.cols = out, self.rest, slice(None)
        self.phase += 1
        self.base = 0


class Total:
    def __init__(self, value, at, buf, ssem, rsem):
        self.value, self.at, self.buf, self.ssem, self.rsem = value, at, buf, ssem, rsem
        self.phase, self.sent = 0, []
        self.start()

    def start(self):
        n, axis = self.phase, ("core", "z", "y", "x")[self.phase]
        self.buf[n, 0] = self.value
        self.copies = []
        for i in (1, 3, 2) if axis != "core" else (1,):
            self.copies.append(
                send(self.buf.at[n, 0], self.buf.at[n, i], self.ssem.at[n, i], self.rsem.at[n, i], moved(self.at, axis, i))
            )

    def step(self):
        n, buf = self.phase, self.buf
        if n == 4:
            return
        for c in self.copies:
            c.wait_recv()
            self.sent.append(c)
        if n == 0:
            self.value = buf[n, 0] + buf[n, 1]
        else:
            self.value = (buf[n, 0] + buf[n, 2]) + (buf[n, 1] + buf[n, 3])
        self.phase += 1
        if self.phase < 4:
            self.start()


def run_sums(streams, total):
    todo = []
    for s in streams:
        s.start()
        steps = [("pass_on",), ("finish", "start"), ("pass_on",), ("finish", "start"), ("pass_on",), ("finish",)]
        todo.append(steps[1:] if s.begun is not None else steps)
    while any(todo):
        for s, steps in zip(streams, todo):
            if steps:
                for name in steps.pop(0):
                    getattr(s, name)()
        total.step()
    for s in streams:
        for c in s.sent:
            c.wait_send()


def sum_scratch(order, dims, rows, width, begun=False, resident=False):
    buffers = []
    for phase, axis in enumerate(order):
        rest = without(dims, axis)
        lead = lead_shape(rest)
        buf = {}
        if SIZES[axis] == 2:
            buf["got"] = pltpu.VMEM((1,) + lead + (rows, width), BF)
        else:
            buf["got"] = pltpu.VMEM((2, 2) + lead + (rows // 2, width), BF)
            if phase or not begun:
                buf["relay"] = pltpu.VMEM((2,) + lead + (rows // 2, width), BF)
        if phase == 0 and not resident:
            buf["mine"] = pltpu.VMEM(lead + (rows, width), BF)
            if SIZES[axis] == 4 and not begun:
                buf["own"] = pltpu.VMEM((2,) + lead + (rows // 2, width), BF)
        else:
            buf["sum"] = pltpu.VMEM(lead + (rows, width), BF if phase < 2 else F32)
        buffers.append(buf)
        dims = rest
    return buffers


def weight_sum_kernel(pieces, n, *refs):
    ins, small, begun, refs = refs[:n], refs[n], refs[n + 1 : n + 1 + 2 * N_EARLY], refs[n + 1 + 2 * N_EARLY :]
    outs, small_out = refs[: n - 1], refs[n - 1]
    buffers, stages, swapped, small_buf, ssem, rsem, lsem, csem, tssem, trsem = refs[n:]
    at = here()
    core = at["core"]
    sibling = moved(at, "core", 1)
    greet([sibling] + sum_peers(at, ("x", "y", "z")))
    streams = [
        Summing(
            ins[a], W_DIMS, at, order, 32, pl.ds(start, width), buffers[k], ssem.at[k], rsem.at[k], lsem.at[k],
            (begun[2 * k], begun[2 * k + 1]) if k < N_EARLY else None,
        )
        for k, (a, start, width, order) in enumerate(pieces)
    ]
    total = Total(small[...], at, small_buf, tssem, trsem)
    run_sums(streams, total)
    small_out[...] = total.value
    for k, (a, start, width, order) in enumerate(pieces):
        stages[a][:, start : start + width] = buffers[k][2]["sum"][...]
    other = pl.ds(pl.multiple_of((1 - core) * 16, 16), 16)
    own = pl.ds(pl.multiple_of(core * 16, 16), 16)
    copies = [send(stages[a].at[other], swapped[a], csem.at[a, 0], csem.at[a, 1], sibling) for a in range(n)]

    def put(a, half, value):
        width = value.shape[1]
        ref, start = ((outs[0], 0), (outs[0], FF), (outs[1], 0), (outs[2], 0), (outs[3], 0))[a]
        ref[:, pl.ds(pl.multiple_of(start + half * width, 128), width)] = value

    for a in range(n):
        put(a, core, stages[a][own, :])
    for a in range(n):
        copies[a].wait_recv()
        put(a, 1 - core, swapped[a][...])
    for c in copies + total.sent:
        c.wait_send()


def sum_weights(grads, small, begun, pieces, cid, limit):
    n, count = len(grads), len(pieces)
    anywhere = pl.BlockSpec(memory_space=pl.ANY)
    vmem = pl.BlockSpec(memory_space=pltpu.VMEM)
    widths = [g.shape[-1] for g in grads]
    return pl.pallas_call(
        functools.partial(weight_sum_kernel, pieces, n),
        out_shape=[jax.ShapeDtypeStruct((16, w), F32) for w in (2 * FF, FF, HQ * HD, 2 * (QW + KVW))]
        + [jax.ShapeDtypeStruct(small.shape, F32)],
        in_specs=[anywhere] * n + [vmem] + [anywhere] * len(begun),
        out_specs=[vmem] * n,
        scratch_shapes=[
            [sum_scratch(order, W_DIMS, 32, width, k < N_EARLY) for k, (a, start, width, order) in enumerate(pieces)],
            [pltpu.VMEM((32, w), F32) for w in widths],
            [pltpu.VMEM((16, w), F32) for w in widths],
            pltpu.VMEM((4, 4) + small.shape, F32),
            pltpu.SemaphoreType.DMA((count, 3, 6)),
            pltpu.SemaphoreType.DMA((count, 3, 6)),
            pltpu.SemaphoreType.DMA((count, 6)),
            pltpu.SemaphoreType.DMA((n, 2)),
            pltpu.SemaphoreType.DMA((4, 4)),
            pltpu.SemaphoreType.DMA((4, 4)),
        ],
        compiler_params=pltpu.CompilerParams(collective_id=cid, has_side_effects=True, vmem_limit_bytes=limit),
        name="sum_weights",
    )(*grads, small, *begun)


def sum_peers(at, axes):
    out = []
    for a in axes:
        for i in (1, 3, 2) if SIZES[a] == 4 else (1,):
            out.append(moved(at, a, i))
    return out


def heads_at(ref, s, h, half):
    rows = slice(s * TOK + half * SPAN, s * TOK + (half + 1) * SPAN)
    return jnp.concatenate([ref[rows, (h * GROUP + g) * HD : (h * GROUP + g + 1) * HD] for g in range(GROUP)], axis=0)


def put_heads(ref, s, h, half, value):
    rows = pl.ds(pl.multiple_of(s * TOK + half * SPAN, SPAN), SPAN)
    for g in range(0, GROUP, 2):
        both = jnp.concatenate([value[g * SPAN : (g + 1) * SPAN], value[(g + 1) * SPAN : (g + 2) * SPAN]], axis=1)
        ref[rows, pl.ds(pl.multiple_of((h * GROUP + g) * HD, 2 * HD), 2 * HD)] = both.astype(ref.dtype)


def masked(prob, limit):
    if limit is None:
        return prob
    row = lax.broadcasted_iota(jnp.int32, prob.shape, 0)
    col = lax.rem(lax.broadcasted_iota(jnp.int32, prob.shape, 1), SPAN)
    return jnp.where(row <= col + limit, prob, 0.0)


def attend_heads(tab, s, q_ref, kvs, o_ref, low_ref, l_ref, acc, total):
    rate = LOG2E * HD**-0.5

    def head(h, carry):
        acc[...] = jnp.zeros_like(acc)
        total[...] = jnp.zeros_like(total)

        def scored(half, block, limit):
            keys = kvs[s, h, block].reshape(KEYS, 2 * HD)
            scores = lax.dot_general(keys, q_ref[s, h, half], NT, preferred_element_type=F32)
            prob = masked(jnp.exp2(scores * rate), limit)
            return (
                jnp.sum(prob, axis=0, keepdims=True),
                lax.dot_general(keys, prob.astype(BF), TN, preferred_element_type=F32),
            )

        def high(k, c):
            t, o = scored(1, k, None)
            total[1] += t
            acc[1] += o
            return c

        def either(k, c):
            half = tab[s, AT_STEP_HALF + k]
            t, o = scored(half, tab[s, AT_STEP_BLOCK + k], None)
            up = half.astype(F32)
            total[0] += t * (1.0 - up)
            total[1] += t * up
            acc[0] += o * (1.0 - up)
            acc[1] += o * up
            return c

        lax.fori_loop(0, 4, high, 0)
        lax.fori_loop(0, 3, either, 0)
        for half in range(2):
            t, o = scored(half, tab[s, AT_EDGE + half], tab[s, AT_LIMIT + half])
            t, o = total[half] + t, acc[half] + o
            out = (o[HD:, :] / t).T
            put_heads(o_ref, s, h, half, out)
            put_heads(low_ref, s, h, half, out)
            l_ref[s, h, half] = jnp.log2(t)
        return carry

    lax.fori_loop(0, HH, head, 0)


class Early:
    def __init__(self, source, at, order, cols, width, relay, direct, passed, ssem, rsem):
        self.source, self.at, self.axis, self.cols, self.width = source, at, order[0], cols, width
        self.relay, self.passed, self.ssem, self.rsem, self.views = relay, passed, ssem, rsem, {}
        i = at[self.axis]
        self.near = (lax.rem(i + 1, 4), lax.rem(i + 3, 4))
        far = lax.rem(i + 2, 4)
        plan = (
            (far, 0, relay, 0, 1),
            (far, 1, relay, 1, 3),
            (self.near[0], 1, direct, 1, 1),
            (self.near[1], 0, direct, 0, 3),
        )
        self.copies = []
        for n, (coordinate, half, dst, slot, by) in enumerate(plan):
            self.copies.append(self.send(n, self.part(coordinate, half), dst.at[slot], by))

    def part(self, coordinate, half):
        return pick(self.source, W_DIMS, labels(self.axis, coordinate), (pl.ds(half * 16, 16), self.cols))

    def send(self, n, src, dst, by):
        return send(src, dst, self.ssem.at[n], self.rsem.at[n], moved(self.at, self.axis, by))

    def load(self, n, own, sem):
        lead = lead_shape(without(W_DIMS, self.axis))
        view = own.at[(slice(None),) * (len(lead) + 1) + (pl.ds(0, self.width),)]
        self.views[n] = view
        copy = pltpu.make_async_copy(self.part(self.near[n], n), view, sem)
        copy.start()
        return copy

    def add(self, n):
        self.copies[n].wait_recv()
        came, own = self.relay.at[n], self.views[n]
        lead = lead_shape(without(W_DIMS, self.axis))
        spots = [()]
        for size in lead[1:]:
            spots = [s + (j,) for s in spots for j in range(size)]

        def go(j, carry):
            for s in spots:
                at = (j,) + s + (slice(None), slice(None))
                came[at] = (came[at].astype(F32) + own[at].astype(F32)).astype(BF)
            return carry

        lax.fori_loop(0, lead[0], go, 0)
        self.copies.append(self.send(4 + n, came, self.passed.at[n], 1 if n == 0 else 3))

    def wait(self):
        for c in self.copies[2:]:
            c.wait_recv()


def early_shapes():
    shapes = []
    for a, start, width, order in SUMS[:N_EARLY]:
        lead = lead_shape(without(W_DIMS, order[0]))
        shapes += [jax.ShapeDtypeStruct((2,) + lead + (16, width), BF)] * 2
    return shapes


def attend_back_kernel(*refs):
    tab, qr, da, attn, attn_low, l_ref, kv_sorted, normed, dy, low_mid, hid, dgate, dup = refs[:13]
    joined, normed_one, w_one, gains, cosine, sine, grad_mid, own_x = refs[13:21]
    input_grad, terms, head_terms = refs[21:24]
    grads, refs = refs[24:29], refs[29:]
    begun, refs = refs[: 2 * N_EARLY], refs[2 * N_EARLY :]
    held, qd_ref, delta_ref, stage, acc, dq_acc, dq_ref, buffers, refs = refs[:8] + (refs[8:],)
    tiles, mix, mix_z, relays, w_ref, d_joined, part, got = refs[:8]
    essem, ersem, ssem, rsem, sems, tsem, msem, psem = refs[8:]
    at = here()
    core = at["core"]
    sibling = moved(at, "core", 1)
    def load_keys(h):
        return [pltpu.make_async_copy(kv_sorted.at[s, h], held[h % 2].at[s], sems.at[s, h]) for s in range(2)]

    for c in load_keys(0):
        c.start()

    def load_w(c):
        return pltpu.make_async_copy(w_one.at[c], w_ref, psem.at[0])

    load_w(0).start()
    greet([sibling] + neighbours(at, ("x", "y", "z", "h")))
    sides = ((normed, dgate), (normed, dup), (dy, hid), (low_mid, attn_low), (normed_one, d_joined))

    def tile_copy(n, i, slot, parity):
        a, start, width = n
        half = lax.rem(i, 2)
        return pltpu.make_async_copy(
            tiles.at[parity, slot, :, :, :, :, pl.ds(0, width)],
            grads[a].at[lax.div(i, 2), pl.ds(half * 2, 2), :, :, :, pl.ds(start, width)],
            tsem.at[parity, slot],
        )

    def outer(n, parity):
        a, start, width = n
        left, right = sides[a]

        def go(i, carry):
            slot = lax.rem(i, 2)

            @pl.when(i > 1)
            def _():
                tile_copy(n, i, slot, parity).wait()

            rows = pl.ds(pl.multiple_of(i * 512, 512), 512)
            value = lax.dot_general(left[:, rows], right[:, start : start + width], TN, preferred_element_type=F32)
            tiles[parity, slot, :, :, :, :, :width] = value.astype(BF).reshape(2, 4, 2, 32, width)
            tile_copy(n, i, slot, parity).start()
            return carry

        lax.fori_loop(0, 4, go, 0)

    def drain(n, parity):
        for slot in range(2):
            tile_copy(n, slot, slot, parity).wait()

    early = []

    def begin(k):
        a, start, width, order = SUMS[k]
        drain((a, start, width), k % 2)
        early.append(
            Early(
                grads[a], at, order, pl.ds(start, width), width, relays[k], begun[2 * k], begun[2 * k + 1],
                essem.at[k], ersem.at[k],
            )
        )

    for k in range(N_EARLY):
        outer(SUMS[k][:3], k % 2)
        if k:
            begin(k - 1)
    rate = LOG2E * HD**-0.5
    factor = jnp.where(lax.broadcasted_iota(jnp.int32, (1, 2 * HD), 1) < HD, HD**-0.5, 1.0)
    blank = jnp.zeros((QROWS, HD), BF)
    for s in range(2):
        for h in range(HH):
            for half in range(2):
                up = heads_at(da, s, h, half)
                qd_ref[s, h, half, :QROWS] = jnp.concatenate([heads_at(qr, s, h, half), blank], axis=1)
                qd_ref[s, h, half, QROWS:] = jnp.concatenate([blank, up], axis=1)
                inner = (up.astype(F32) * heads_at(attn, s, h, half)).T
                delta_ref[s, h, half] = jnp.sum(inner, axis=0, keepdims=True)
    begin(N_EARLY - 1)
    streams = [
        [
            Summing(
                stage.at[h], KV_DIMS, at, order, rows, slice(None), buffers[h][j],
                ssem.at[h, j], rsem.at[h, j], None, None, start,
            )
            for j, (start, rows, order) in enumerate(KV_PARTS)
        ]
        for h in range(HH)
    ]
    todo = [[("pass_on",), ("finish", "start"), ("pass_on",), ("finish", "start"), ("pass_on",), ("finish",)] for h in range(HH)]

    def move(h):
        for name_of in todo[h].pop(0) if todo[h] else ():
            for st in streams[h]:
                getattr(st, name_of)()

    units = [(k, n) for k in range(N_EARLY) for n in range(2)]
    used, flying, ahead = {}, [], [0]

    def fetch():
        k, n = units[ahead[0]]
        pool, slots, first = (mix_z, 2, 3) if early[k].axis == "z" else (mix, 3, 0)
        slot = used.get(slots, 0) % slots
        used[slots] = used.get(slots, 0) + 1
        flying.append((k, n, early[k].load(n, pool.at[slot], msem.at[first + slot])))
        ahead[0] += 1

    def advance(count):
        for _ in range(count):
            while ahead[0] < len(units) and len(flying) < 2:
                fetch()
            if flying:
                k, n, copy = flying.pop(0)
                copy.wait()
                early[k].add(n)

    for h in range(HH):
        for c in load_keys(h):
            c.wait()
        if h + 1 < HH:
            for c in load_keys(h + 1):
                c.start()
        kvs = held[h % 2]

        def sequence(s, carry, h=h, kvs=kvs):
            dq_acc[...] = jnp.zeros_like(dq_acc)
            acc[...] = jnp.zeros_like(acc)

            def backward(half, block, limit):
                keys = kvs[s, block].reshape(KEYS, 2 * HD)
                both = lax.dot_general(keys, qd_ref[s, h, half], NT, preferred_element_type=F32)
                prob = masked(jnp.exp2(both[:, :QROWS] * rate - l_ref[s, h, half]), limit)
                grad = (prob * (both[:, QROWS:] - delta_ref[s, h, half])).astype(BF)
                pair = jnp.concatenate([grad, prob.astype(BF)], axis=1)
                kv = lax.dot_general(pair, qd_ref[s, h, half], NN, preferred_element_type=F32)
                return (
                    kv.reshape(SPANS_STEP, SPAN, 2 * HD),
                    lax.dot_general(keys, grad, TN, preferred_element_type=F32),
                )

            def spans(block):
                return pl.ds(block * SPANS_STEP, SPANS_STEP)

            def high(k, c):
                kv, q = backward(1, k, None)
                acc[spans(k)] += kv
                dq_acc[1] += q
                return c

            def either(k, c):
                half = tab[s, AT_STEP_HALF + k]
                kv, q = backward(half, tab[s, AT_STEP_BLOCK + k], None)
                up = half.astype(F32)
                acc[spans(k)] += kv * (1.0 - up)
                acc[spans(6 - k)] += kv * up
                dq_acc[0] += q * (1.0 - up)
                dq_acc[1] += q * up
                return c

            lax.fori_loop(0, 4, high, 0)
            lax.fori_loop(0, 3, either, 0)
            for half in range(2):
                kv, q = backward(half, tab[s, AT_EDGE + half], tab[s, AT_LIMIT + half])
                for k in range(4):
                    acc[spans(k if half == 0 else 7 - k)] += kv * tab[s, AT_MARK + k].astype(F32)
                q = dq_acc[half] + q
                put_heads(dq_ref, s, h, half, (q[:HD, :] * HD**-0.5).T)

            def put(j, c):
                for half in range(2):
                    v = acc[tab[s, AT_MAP + half * N_CTX + j]] * factor
                    rows = pl.ds(pl.multiple_of(s * TOK + half * SPAN, SPAN), SPAN)
                    stage[h, lax.div(j, 16), lax.rem(lax.div(j, 4), 4), lax.rem(j, 4), rows, :] = v.astype(BF)
                return c

            lax.fori_loop(0, N_CTX, put, 0)
            return carry

        lax.fori_loop(0, 2, sequence, 0)
        for k in range(h):
            move(k)
        for st in streams[h]:
            st.start()
        advance((4, 6, 2)[h])
    while any(todo):
        for h in range(HH):
            move(h)
        advance(1)

    head_gains = gains[32:33]

    def tile(t, is_key, grad):
        v = joined[:, t * 128 : (t + 1) * 128]
        low = lane_of(v.shape) < HD
        back = grad * cosine[...] - swap_halves(grad) * sine[...]
        inverse = lax.rsqrt(head_sums(v * v) * (1.0 / HD) + EPSILON)
        scaled = back * tile_gain(head_gains, is_key)
        inner = head_sums(scaled * v) * (1.0 / HD)
        result = inverse * scaled - v * (inverse * inverse * inverse) * inner
        if is_key:
            result = jnp.where(low, result, grad)
        d_joined[:, t * 128 : (t + 1) * 128] = result.astype(BF)
        return jnp.sum(back * v * inverse, axis=0, keepdims=True)

    q_terms = sum(tile(t, False, dq_ref[:, t * 128 : (t + 1) * 128]) for t in range(QW // 128))
    k_terms = 0.0
    for h in range(HH):
        grad = jnp.concatenate([buffers[h][j][2]["sum"][...] for j in range(len(KV_PARTS))], axis=0)
        k_terms = k_terms + tile(QW // 128 + h, True, grad)
    q_terms = q_terms + pltpu.roll(q_terms, HD, 1)
    head_terms[...] = jnp.where(lane_of(q_terms.shape) < HD, q_terms, pltpu.roll(k_terms, HD, 1))
    other = pl.ds(pl.multiple_of((1 - core) * TOK, TOK), TOK)
    swaps = []
    for c in range(2):
        load_w(c).wait()
        w = w_ref[...].reshape(D // 2, QW + KVW)
        part[c] = lax.dot_general(d_joined[...], w, NT, preferred_element_type=F32)
        if c == 0:
            load_w(1).start()
        swaps.append(send(part.at[c, other], got.at[c], psem.at[1 + c], psem.at[3 + c], sibling))
    advance(4)
    outer((4, 0, QW + KVW), 0)
    advance(4)
    gain_row = jnp.concatenate([gains[j : j + 1] for j in range(D // 128)], axis=1)
    for c in swaps:
        c.wait_recv()

    def last(r, carry):
        rows = rows_at(r)
        own = pl.ds(pl.multiple_of(core * TOK + r * 32, 32), 32)
        e = jnp.concatenate([part[c, own, :] + got[c, rows, :] for c in range(2)], axis=1)
        v = own_x[rows, :].astype(F32)
        inverse = lax.rsqrt(jnp.sum(v * v, axis=1, keepdims=True) * (1.0 / D) + EPSILON)
        scaled = e * gain_row
        inner = jnp.sum(scaled * v, axis=1, keepdims=True) * (1.0 / D)
        total = grad_mid[rows, :] + inverse * scaled - v * (inverse * inverse * inverse) * inner
        input_grad[rows, :] = total.astype(BF)
        return carry + jnp.sum(e * v * inverse, axis=0, keepdims=True)

    terms[...] = lax.fori_loop(0, TOK // 32, last, jnp.zeros((1, D), F32))
    advance(len(units))
    drain((4, 0, QW + KVW), 0)
    for e in early:
        e.wait()
    pending = [c for e in early for c in e.copies] + swaps + [c for group in streams for st in group for c in st.sent]
    for c in pending:
        c.wait_send()


def attend_back(operands, cid):
    vmem = pl.BlockSpec(memory_space=pltpu.VMEM)
    anywhere = pl.BlockSpec(memory_space=pl.ANY)
    tokens = 2 * TOK
    widths = (FH, FH, FH, QW, QW + KVW)
    out = pl.pallas_call(
        attend_back_kernel,
        out_shape=[
            jax.ShapeDtypeStruct((TOK, D), BF),
            jax.ShapeDtypeStruct((1, D), F32),
            jax.ShapeDtypeStruct((1, 128), F32),
        ]
        + [jax.ShapeDtypeStruct((2, 4, 4, 2, 32, w), BF) for w in widths]
        + early_shapes(),
        in_specs=[pl.BlockSpec(memory_space=pltpu.SMEM)]
        + [vmem] * 5
        + [anywhere]
        + [vmem] * 8
        + [anywhere]
        + [vmem] * 5,
        out_specs=[vmem] * 3 + [anywhere] * (5 + 2 * N_EARLY),
        scratch_shapes=[
            [pltpu.VMEM((2, KEY_BLOCKS, SPANS_STEP, SPAN, 2 * HD), BF)] * 2,
            pltpu.VMEM((2, HH, 2, 2 * QROWS, 2 * HD), BF),
            pltpu.VMEM((2, HH, 2, 1, QROWS), F32),
            pltpu.VMEM((HH, 2, 4, 4, tokens, 2 * HD), BF),
            pltpu.VMEM((2 * N_CTX, SPAN, 2 * HD), F32),
            pltpu.VMEM((2, 2 * HD, QROWS), F32),
            pltpu.VMEM((tokens, QW), F32),
            [
                [sum_scratch(order, KV_DIMS, rows, 2 * HD, False, True) for start, rows, order in KV_PARTS]
                for h in range(HH)
            ],
            pltpu.VMEM((2, 2, 2, 4, 2, 32, 1152), BF),
            pltpu.VMEM((3, 2, 4, 2, 16, 1152), BF),
            pltpu.VMEM((2, 4, 4, 16, 1152), BF),
            [
                pltpu.VMEM((2,) + lead_shape(without(W_DIMS, order[0])) + (16, width), BF)
                for a, start, width, order in SUMS[:N_EARLY]
            ],
            pltpu.VMEM((4, 4, 2, 32, QW + KVW), BF),
            pltpu.VMEM((tokens, QW + KVW), BF),
            pltpu.VMEM((2, tokens, D // 2), F32),
            pltpu.VMEM((2, TOK, D // 2), F32),
            pltpu.SemaphoreType.DMA((N_EARLY, 6)),
            pltpu.SemaphoreType.DMA((N_EARLY, 6)),
            pltpu.SemaphoreType.DMA((HH, 3, 3, 6)),
            pltpu.SemaphoreType.DMA((HH, 3, 3, 6)),
            pltpu.SemaphoreType.DMA((2, HH)),
            pltpu.SemaphoreType.DMA((2, 2)),
            pltpu.SemaphoreType.DMA((5,)),
            pltpu.SemaphoreType.DMA((5,)),
        ],
        compiler_params=pltpu.CompilerParams(
            collective_id=cid, has_side_effects=True, vmem_limit_bytes=63 * 1024 * 1024
        ),
        name="attend_back",
    )(*operands)
    return out[0], out[1], out[2], out[3:8], out[8:]


CHUNKS = ((0, 768), (768, 768), (1536, 640))


def rows_at(r, n=32):
    return pl.ds(pl.multiple_of(r * n, n), n)


def feed_kernel(
    attn, x, dy, gains, wo_h, wg_h, wu_h, wd_h,
    result, grad_mid, grad_attn, normed, hid, dgate, dup, low_mid, stats, terms,
    wo, wg, wu, wd, mid, part, got, part_f, got_f, wsem, psem,
):
    at = here()
    core = at["core"]
    sibling = moved(at, "core", 1)
    loads = []
    for i, (src, dst) in enumerate(((wo_h, wo), (wg_h, wg), (wu_h, wu), (wd_h, wd))):
        loads.append(pltpu.make_async_copy(src, dst, wsem.at[i]))
        loads[-1].start()
    greet([sibling])
    gain_row = jnp.concatenate([gains[16 + j : 17 + j] for j in range(D // 128)], axis=1)
    sent = []
    loads[0].wait()
    for c in range(2):
        cols = slice(c * 1024, (c + 1) * 1024)
        part[0, c] = lax.dot_general(attn[...], wo[cols, :], NT, preferred_element_type=F32)
        sent.append(send(part.at[0, c], got.at[0, c], psem.at[c, 0], psem.at[c, 1], sibling))
    for c in sent:
        c.wait_recv()

    def root(v):
        return jnp.sum(jnp.sqrt(jnp.sum(v * v, axis=1, keepdims=True) * (1.0 / D)), axis=0, keepdims=True)

    def middle(r, carry):
        rows = rows_at(r)
        branch = jnp.concatenate([part[0, c, rows, :] + got[0, c, rows, :] for c in range(2)], axis=1)
        v = x[rows, :].astype(F32)
        m = v + branch
        mid[rows, :] = m
        inverse = lax.rsqrt(jnp.sum(m * m, axis=1, keepdims=True) * (1.0 / D) + EPSILON)
        normed[rows, :] = (m * inverse * gain_row).astype(BF)
        own = jnp.where(lax.div(r, TOK // 32) == core, 1.0, 0.0)
        return tuple(t + own * root(u) for t, u in zip(carry, (v, branch, m)))

    zero = jnp.zeros((1, 1), F32)
    roots = lax.fori_loop(0, 2 * TOK // 32, middle, (zero, zero, zero))
    for c in loads[1:]:
        c.wait()
    for start, width in CHUNKS:
        cols = slice(start, start + width)
        gate = jnp.dot(normed[...], wg[:, cols], preferred_element_type=F32)
        up = jnp.dot(normed[...], wu[:, cols], preferred_element_type=F32)
        back = jnp.dot(dy[...], wd[:, cols], preferred_element_type=F32)
        sigmoid = lax.logistic(gate)
        silu = gate * sigmoid
        hid[:, cols] = (silu * up).astype(BF)
        dup[:, cols] = (back * silu).astype(BF)
        dgate[:, cols] = (back * up * sigmoid * (1.0 + gate * (1.0 - sigmoid))).astype(BF)
    late = []
    for c in range(2):
        cols = slice(c * 1024, (c + 1) * 1024)
        one = lax.dot_general(dgate[...], wg[cols, :], NT, preferred_element_type=F32)
        part[1, c] = one + lax.dot_general(dup[...], wu[cols, :], NT, preferred_element_type=F32)
        late.append(send(part.at[1, c], got.at[1, c], psem.at[2 + c, 0], psem.at[2 + c, 1], sibling))
    part_f[...] = lax.dot_general(hid[...], wd[...], NT, preferred_element_type=F32)
    other = pl.ds(pl.multiple_of((1 - core) * TOK, TOK), TOK)
    last = send(part_f.at[other], got_f, psem.at[4, 0], psem.at[4, 1], sibling)

    for c in late:
        c.wait_recv()

    def backward(r, carry):
        rows = rows_at(r)
        e = jnp.concatenate([part[1, c, rows, :] + got[1, c, rows, :] for c in range(2)], axis=1)
        v = mid[rows, :]
        inverse = lax.rsqrt(jnp.sum(v * v, axis=1, keepdims=True) * (1.0 / D) + EPSILON)
        scaled = e * gain_row
        inner = jnp.sum(scaled * v, axis=1, keepdims=True) * (1.0 / D)
        total = dy[rows, :].astype(F32) + inverse * scaled - v * (inverse * inverse * inverse) * inner
        low_mid[rows, :] = total.astype(BF)
        mid[rows, :] = total
        own = jnp.where(lax.div(r, TOK // 32) == core, 1.0, 0.0)
        return carry + own * jnp.sum(e * v * inverse, axis=0, keepdims=True)

    def finish(r, carry):
        rows = rows_at(r)
        own = pl.ds(pl.multiple_of(core * TOK + r * 32, 32), 32)
        branch = part_f[own, :] + got_f[rows, :]
        result[rows, :] = (mid[own, :] + branch).astype(BF)
        return carry + root(branch)

    last.wait_recv()
    final = lax.fori_loop(0, TOK // 32, finish, zero)
    terms[...] = lax.fori_loop(0, 2 * TOK // 32, backward, jnp.zeros((1, D), F32))
    for i, v in enumerate(roots + (final,)):
        stats[i : i + 1, :] = jnp.broadcast_to(v, (1, 128))
    grad_attn[...] = jnp.dot(low_mid[...], wo[...], preferred_element_type=F32).astype(BF)
    grad_mid[...] = mid[pl.ds(pl.multiple_of(core * TOK, TOK), TOK), :]
    for c in sent + late + [last]:
        c.wait_send()


def feed(attn, x, dy, gains, w_out, w_gate, w_up, w_down, cid):
    vmem = pl.BlockSpec(memory_space=pltpu.VMEM)
    anywhere = pl.BlockSpec(memory_space=pl.ANY)
    tokens = 2 * TOK
    return pl.pallas_call(
        feed_kernel,
        out_shape=[
            jax.ShapeDtypeStruct((TOK, D), BF),
            jax.ShapeDtypeStruct((TOK, D), F32),
            jax.ShapeDtypeStruct((tokens, QW), BF),
            jax.ShapeDtypeStruct((tokens, D), BF),
            jax.ShapeDtypeStruct((tokens, FH), BF),
            jax.ShapeDtypeStruct((tokens, FH), BF),
            jax.ShapeDtypeStruct((tokens, FH), BF),
            jax.ShapeDtypeStruct((tokens, D), BF),
            jax.ShapeDtypeStruct((4, 128), F32),
            jax.ShapeDtypeStruct((1, D), F32),
        ],
        in_specs=[vmem] * 4 + [anywhere] * 4,
        out_specs=[vmem] * 10,
        scratch_shapes=[
            pltpu.VMEM((D, QW), BF),
            pltpu.VMEM((D, FH), BF),
            pltpu.VMEM((D, FH), BF),
            pltpu.VMEM((D, FH), BF),
            pltpu.VMEM((tokens, D), F32),
            pltpu.VMEM((2, 2, tokens, D // 2), F32),
            pltpu.VMEM((2, 2, tokens, D // 2), F32),
            pltpu.VMEM((tokens, D), F32),
            pltpu.VMEM((TOK, D), F32),
            pltpu.SemaphoreType.DMA((4,)),
            pltpu.SemaphoreType.DMA((5, 2)),
        ],
        compiler_params=pltpu.CompilerParams(
            collective_id=cid, has_side_effects=True, vmem_limit_bytes=62 * 1024 * 1024
        ),
        name="feed",
    )(attn, x, dy, gains, w_out, w_gate, w_up, w_down)


def body(layer_input, w_qkv, w_out, w_gate_up, w_down, norm_gains, span_map, cotangent):
    at = here()
    core, low = at["core"], at["l"]
    w_q = w_qkv[:, : HQ * HD].reshape(16, 2, QW).transpose(1, 0, 2)
    w_k = w_qkv[:, HQ * HD : (HQ + HK) * HD].reshape(16, 2, HH, HD)
    w_v = w_qkv[:, (HQ + HK) * HD :].reshape(16, 2, HH, HD)
    w_kv = jnp.concatenate([w_k, w_v], axis=3).reshape(16, 2, KVW).transpose(1, 0, 2)
    shard_one = jnp.concatenate([w_q, w_kv], axis=2)
    share = norm_gains.shape[0]
    device = lax.axis_index(("ctx", "fsdp"))
    own_gain = lax.dynamic_update_slice_in_dim(jnp.zeros((40 * 128,), F32), norm_gains.astype(F32), device * share, 0)

    ctx_index = lax.axis_index("ctx")
    maps = lax.dynamic_slice_in_dim(span_map, low * 2, 2, 0)
    own_span = lax.dynamic_slice_in_dim(maps, ctx_index, 1, 1)
    spans = jnp.concatenate([own_span, 2 * N_CTX - 1 - own_span], axis=1)
    positions = (spans[:, :, None] * SPAN + jnp.arange(SPAN, dtype=jnp.int32)).reshape(2 * TOK)
    match = maps[:, None, :] == jnp.arange(N_CTX, dtype=jnp.int32)[None, :, None]
    inverse_map = jnp.sum(jnp.where(match, jnp.arange(N_CTX, dtype=jnp.int32), 0), axis=2)
    holder = jnp.concatenate([inverse_map, inverse_map[:, ::-1]], axis=1)
    upper = (jnp.arange(2 * N_CTX, dtype=jnp.int32) >= N_CTX).astype(jnp.int32)[None, :] + jnp.zeros_like(holder)
    low_block = own_span // SPANS_STEP
    low_limit = own_span % SPANS_STEP * SPAN
    three = jnp.arange(3, dtype=jnp.int32)[None, :]
    step_half = (three >= low_block).astype(jnp.int32)
    tab = jnp.concatenate(
        [
            holder // 16,
            holder // 4 % 4,
            holder % 4,
            upper,
            step_half,
            jnp.where(step_half == 0, three, 6 - three),
            (jnp.arange(4, dtype=jnp.int32)[None, :] == low_block).astype(jnp.int32),
            low_block,
            KEY_BLOCKS - 1 - low_block,
            low_limit,
            KEYS - SPAN - low_limit,
            maps,
            2 * N_CTX - 1 - maps,
        ],
        axis=1,
    )
    half_dim = HD // 2
    frequencies = ROPE_BASE ** (-(jnp.arange(half_dim, dtype=F32) * 2.0 / HD))
    angles = positions.astype(F32)[:, None] * frequencies[None, :]
    cosine, sine = jnp.cos(angles), jnp.sin(angles)
    cosine = jnp.concatenate([cosine] * 4, axis=1)
    sine = jnp.concatenate([-sine, sine] * 2, axis=1)

    weights = [shard_one, w_gate_up, w_down, w_out]
    (w_one, w_gate, w_up, w_back, w_proj, x_pair, dy_pair, gains, joined, normed_one, query, keys, attn_f32, attn_low, log_sum) = front(
        tab, weights, layer_input[0], cotangent[0], own_gain.reshape(40, 128), cosine, sine, 1
    )
    w_gate, w_up, w_back, w_proj = (w.reshape(D, -1) for w in (w_gate, w_up, w_back, w_proj))
    dy = dy_pair.reshape(2 * TOK, D)

    result, grad_middle, grad_attn, normed_two, hidden, grad_gate, grad_up, grad_branch, stats, gain_two_terms = feed(
        attn_low, x_pair.reshape(2 * TOK, D), dy, gains, w_proj, w_gate, w_up, w_back, 2
    )
    operands = (tab, query, grad_attn, attn_f32, attn_low, log_sum, keys, normed_two, dy, grad_branch, hidden)
    operands += (grad_gate, grad_up, joined, normed_one, w_one, gains, cosine, sine, grad_middle, layer_input[0])
    grad_input, gain_one_terms, head_terms, grads, begun = attend_back(operands, 4)
    sums = jnp.concatenate(
        [
            gain_one_terms[0],
            gain_two_terms[0],
            head_terms[0],
            stats[:, 0],
        ]
    )
    sums = jnp.pad(sums, (0, 40 * 128 - sums.shape[0])).reshape(40, 128)
    grad_mlp, grad_down, grad_proj, own_qkv, sums = sum_weights(
        grads, sums, begun, SUMS, 5, 62 * 1024 * 1024
    )
    sums = sums.reshape(-1)
    own_qkv = own_qkv.reshape(16, 2, QW + KVW)
    kv_cols = own_qkv[:, :, QW:].reshape(16, 2, HH, 2, HD)
    grad_qkv = jnp.concatenate(
        [own_qkv[:, 0, :QW], own_qkv[:, 1, :QW]]
        + [kv_cols[:, half, :, kind].reshape(16, HH * HD) for kind in range(2) for half in range(2)],
        axis=1,
    )
    own_gains = lax.dynamic_slice_in_dim(sums, device * share, share, 0)
    stream_rms = sums[4224:4228] / (TOK * N_CTX * 4)
    return (
        result[None],
        grad_input[None],
        grad_qkv,
        grad_proj,
        grad_mlp,
        grad_down,
        own_gains,
        stream_rms,
    )


def solution(mesh):
    rows = P(("ctx", "fsdp"), None)
    tokens = P("fsdp", "ctx", None)
    return jax.shard_map(
        body,
        mesh=mesh,
        in_specs=(tokens, rows, rows, rows, rows, P(("ctx", "fsdp")), P(), tokens),
        out_specs=(tokens, tokens, rows, rows, rows, rows, P(("ctx", "fsdp")), P()),
        check_vma=False,
    )
```

```python
import functools

import jax
import jax.numpy as jnp
from jax import lax
from jax.experimental import pallas as pl
from jax.experimental.pallas import tpu as pltpu
from jax.sharding import PartitionSpec as P

D = 2048
HQ = 24
HK = 6
HD = 64
FF = 4352
TOK = 128
SPAN = 64
N_CTX = 32

HH = HK // 2
GROUP = HQ // HK
QH = HQ // 2
QW = QH * HD
KVW = HH * 2 * HD
FH = FF // 2
KEYS = 512
SPANS_STEP = KEYS // SPAN
KEY_BLOCKS = 8
QROWS = GROUP * SPAN

EPSILON = 1e-06
ROPE_BASE = 10000.0
LOG2E = 1.4426950408889634
AT_H, AT_X, AT_Y, AT_HALF = 0, 64, 128, 192
AT_STEP_HALF, AT_STEP_BLOCK, AT_MARK, AT_EDGE, AT_LIMIT, AT_MAP = 256, 259, 262, 266, 268, 270
MESH = pl.DeviceIdType.MESH
BF = jnp.bfloat16
F32 = jnp.float32
NT = (((1,), (1,)), ((), ()))
NN = (((1,), (0,)), ((), ()))
TN = (((0,), (0,)), ((), ()))
W_DIMS = ("h", "x", "y", "l")
KV_DIMS = ("h", "x", "y")
ORDERS = (("x", "y", "z"), ("y", "z", "x"), ("z", "x", "y"))
KV_ORDERS = (("h", "x", "y"), ("x", "y", "h"), ("y", "h", "x"))
KV_PARTS = ((0, 96, ("y", "x", "h")), (96, 96, ("x", "y", "h")), (192, 64, ("h", "x", "y")))
SUMS = (
    (0, 0, 1152, ORDERS[0]),
    (1, 0, 1152, ORDERS[1]),
    (2, 0, 1152, ORDERS[2]),
    (0, 1152, 1024, ORDERS[0]),
    (1, 1152, 1024, ORDERS[1]),
    (2, 1152, 1024, ORDERS[2]),
    (3, 0, 256, ORDERS[0]),
    (3, 256, 256, ORDERS[1]),
    (3, 512, 256, ORDERS[2]),
    (4, 0, 384, ORDERS[0]),
    (4, 384, 384, ORDERS[1]),
    (4, 768, 384, ORDERS[2]),
)
N_EARLY = 9
ADVANCE = (0, 4, 0, 6, 0, 2)
SIZES = {"x": 4, "y": 4, "z": 4, "h": 2}


def here():
    c = lax.axis_index("ctx")
    f = lax.axis_index("fsdp")
    return {
        "x": lax.rem(lax.div(c, 4), 4),
        "y": lax.rem(c, 4),
        "z": lax.div(c, 16) * 2 + lax.div(f, 2),
        "h": lax.div(c, 16),
        "l": lax.div(f, 2),
        "core": lax.rem(f, 2),
    }


def device_of(x, y, z, core):
    return (lax.div(z, 2) * 16 + x * 4 + y, lax.rem(z, 2) * 2 + core)


def moved(at, axis, by):
    if axis == "core":
        return device_of(at["x"], at["y"], at["z"], 1 - at["core"])
    place = {k: at[k] for k in ("x", "y", "z")}
    if axis == "h":
        place["z"] = lax.rem(at["z"] + 2, 4)
    else:
        place[axis] = lax.rem(at[axis] + by + 4, 4)
    return device_of(place["x"], place["y"], place["z"], at["core"])


def labels(axis, value):
    if axis == "z":
        return {"h": lax.div(value, 2), "l": lax.rem(value, 2)}
    return {axis: value}


def pick(ref, dims, values, tail):
    return ref.at[tuple(values[d] if d in values else slice(None) for d in dims) + tail]


def greet(devices):
    barrier = pltpu.get_barrier_semaphore()
    for d in devices:
        pl.semaphore_signal(barrier, inc=1, device_id=d, device_id_type=MESH)
    pl.semaphore_wait(barrier, len(devices))


def send(src, dst, ssem, rsem, device):
    copy = pltpu.make_async_remote_copy(
        src_ref=src, dst_ref=dst, send_sem=ssem, recv_sem=rsem, device_id=device, device_id_type=MESH
    )
    copy.start()
    return copy


class Gathering:
    def __init__(self, ref, dims, at, order, rows, cols, ssem, rsem):
        self.ref, self.dims, self.at, self.order, self.rows, self.cols = ref, dims, at, order, rows, cols
        self.ssem, self.rsem, self.phase, self.sent = ssem, rsem, 0, []

    def block(self, coordinate, rows):
        later = {}
        for a in self.order[self.phase + 1 :]:
            later.update(labels(a, self.at[a]))
        return pick(self.ref, self.dims, {**later, **labels(self.axis, coordinate)}, (rows, self.cols))

    def send(self, n, ref, by):
        c = send(ref, ref, self.ssem.at[self.phase, n], self.rsem.at[self.phase, n], moved(self.at, self.axis, by))
        self.sent.append(c)
        return c

    def start(self):
        self.axis = self.order[self.phase]
        mine = self.block(self.at[self.axis], slice(None))
        self.first = [self.send(0, mine, 1)]
        if SIZES[self.axis] == 4:
            self.first.append(self.send(1, mine, 3))

    def pass_on(self):
        for c in self.first:
            c.wait_recv()
        self.second = []
        if SIZES[self.axis] == 4:
            half = self.rows // 2
            me = self.at[self.axis]
            self.second.append(self.send(2, self.block(lax.rem(me + 3, 4), pl.ds(0, half)), 1))
            self.second.append(self.send(3, self.block(lax.rem(me + 1, 4), pl.ds(half, half)), 3))

    def finish(self):
        for c in self.second:
            c.wait_recv()
        self.phase += 1

    def wait_sent(self):
        for c in self.sent:
            c.wait_send()


def neighbours(at, axes):
    out = []
    for a in axes:
        if a in ("core", "h"):
            out.append(moved(at, a, 1))
        else:
            out.append(moved(at, a, 1))
            out.append(moved(at, a, 3))
    return out


GATHER = (
    (0, 0, 1152, ORDERS[0]),
    (1, 0, 1152, ORDERS[1]),
    (2, 0, 1152, ORDERS[2]),
    (0, 1152, 1024, ORDERS[0]),
    (1, 1152, 1024, ORDERS[1]),
    (2, 1152, 1024, ORDERS[2]),
    (3, 0, 256, ORDERS[0]),
    (3, 256, 256, ORDERS[1]),
    (3, 512, 256, ORDERS[2]),
)


def lane_of(shape):
    return lax.broadcasted_iota(jnp.int32, shape, len(shape) - 1)


def swap_halves(v):
    return jnp.where(lax.rem(lane_of(v.shape), HD) < HD // 2, pltpu.roll(v, 96, 1), pltpu.roll(v, 32, 1))


def head_sums(v):
    low = lane_of(v.shape) < HD
    a = jnp.sum(jnp.where(low, v, 0.0), axis=1, keepdims=True)
    b = jnp.sum(jnp.where(low, 0.0, v), axis=1, keepdims=True)
    return jnp.where(low, a, b)


def tile_gain(row, is_key):
    low = lane_of(row.shape) < HD
    turned = pltpu.roll(row, HD, 1)
    return jnp.where(low, turned, 1.0) if is_key else jnp.where(low, row, turned)


def front_kernel(
    tab, shard_one, gate_up, down, out, x, dy, gains, cosine, sine,
    w_one, w_gate, w_up, w_down, w_out, x_pair, dy_pair, gain_all, joined, normed, query, kv_out, o_ref, low_ref, l_ref,
    one, kv_src, kvg, kvs, q_ref, acc, sum_ref, small_buf, psem, lsem, tssem, trsem, ossem, orsem, gssem, grsem, kssem, krsem, ksem,
):
    at = here()
    core = at["core"]
    sibling = moved(at, "core", 1)
    greet([sibling] + sum_peers(at, ("x", "y", "z")))
    own = {d: at[d] for d in W_DIMS}
    total = Total(gains[...], at, small_buf, tssem, trsem)
    remote, local = [], []

    def half_of(src, start, width, which):
        return src.at[:, pl.ds(pl.multiple_of(start + which * width, 128), width)]

    pairs = [
        (lambda c: shard_one.at[c], one),
        (lambda c: half_of(gate_up, 0, FH, c), w_gate),
        (lambda c: half_of(gate_up, FF, FH, c), w_up),
        (lambda c: half_of(down, 0, FH, c), w_down),
        (lambda c: half_of(out, 0, QW, c), w_out),
    ]
    for i, (src, ref) in enumerate(pairs):
        dst = pick(ref, W_DIMS, own, (pl.ds(core * 16, 16), slice(None)))
        remote.append(send(src(1 - core), dst, psem.at[i, 0], psem.at[i, 1], sibling))
        local.append(pltpu.make_async_copy(src(core), dst, lsem.at[i]))
        local[-1].start()
    for i, (src, ref) in ((5, (x, x_pair)), (6, (dy, dy_pair))):
        remote.append(send(src, ref.at[core], psem.at[i, 0], psem.at[i, 1], sibling))
        local.append(pltpu.make_async_copy(src, ref.at[core], lsem.at[i]))
        local[-1].start()

    def arrived(i):
        remote[i].wait_recv()
        local[i].wait()

    ones = [
        Gathering(one, W_DIMS, at, ORDERS[k], 32, pl.ds(k * 384, 384), ossem.at[k], orsem.at[k]) for k in range(3)
    ]
    rest = [
        Gathering(pairs[1 + a][1], W_DIMS, at, order, 32, pl.ds(start, width), gssem.at[k], grsem.at[k])
        for k, (a, start, width, order) in enumerate(GATHER)
    ]
    keys = [
        Gathering(kvg.at[h], KV_DIMS, at, KV_ORDERS[h], 4, slice(None), kssem.at[h], krsem.at[h]) for h in range(HH)
    ]

    def every(streams, *steps):
        for s in streams:
            for step in steps:
                getattr(s, step)()

    arrived(0)
    every(ones, "start")
    for i in range(1, 5):
        arrived(i)
    every(rest, "start")
    total.step()
    every(ones, "pass_on")
    every(rest, "pass_on")
    total.step()
    every(ones, "finish", "start")
    every(rest, "finish")
    total.step()
    every(ones, "pass_on")
    total.step()
    gain_all[...] = total.value
    every(ones, "finish", "start")
    every(rest, "start")
    arrived(5)
    gain_row = jnp.concatenate([total.value[j : j + 1] for j in range(D // 128)], axis=1)

    def norm(r, carry):
        rows = pl.ds(pl.multiple_of(r * 32, 32), 32)
        for s in range(2):
            v = x_pair[s, rows, :].astype(F32)
            inverse = lax.rsqrt(jnp.sum(v * v, axis=1, keepdims=True) * (1.0 / D) + EPSILON)
            normed[pl.ds(pl.multiple_of(s * TOK + r * 32, 32), 32), :] = (v * inverse * gain_row).astype(BF)
        return carry

    lax.fori_loop(0, TOK // 32, norm, 0)
    every(ones, "pass_on")
    every(ones, "finish")
    keep = pltpu.make_async_copy(one, w_one, lsem.at[7])
    keep.start()
    head_gains = total.value[32:33]

    def product(start, width):
        w = one[:, :, :, :, :, start : start + width].reshape(D, width)
        joined[:, start : start + width] = jnp.dot(normed[...], w, preferred_element_type=F32)

    def rope(tile, is_key):
        v = joined[:, tile * 128 : (tile + 1) * 128]
        low = lane_of(v.shape) < HD
        c, n = cosine[...], sine[...]
        inverse = lax.rsqrt(head_sums(v * v) * (1.0 / HD) + EPSILON)
        if is_key:
            inverse = jnp.where(low, inverse, 1.0)
            c, n = jnp.where(low, c, 1.0), jnp.where(low, n, 0.0)
        v = v * inverse * tile_gain(head_gains, is_key)
        return (v * c + swap_halves(v) * n).astype(BF)

    product(QW, KVW)
    for h in range(HH):
        kv_src[h] = rope(QW // 128 + h, True).reshape(4, SPAN, 2 * HD)
    kv_own = {d: at[d] for d in KV_DIMS}
    puts = [pltpu.make_async_copy(kv_src.at[h], pick(kvg.at[h], KV_DIMS, kv_own, ()), ksem.at[h]) for h in range(HH)]
    for c in puts:
        c.start()
    for c in puts:
        c.wait()
    every(keys, "start")
    every(rest, "pass_on")
    product(0, 384)
    every(keys, "pass_on")
    every(rest[:3], "finish", "start")
    every(keys, "finish", "start")
    product(384, 384)
    every(keys, "pass_on")
    for t in range(QW // 128):
        query[:, t * 128 : (t + 1) * 128] = rope(t, False)
    every(keys, "finish", "start")
    every(rest[3:], "finish")
    blank = jnp.zeros((QROWS, HD), BF)
    for s in range(2):
        for h in range(HH):
            for half in range(2):
                q_ref[s, h, half] = jnp.concatenate([heads_at(query, s, h, half), blank], axis=1)
    every(keys, "pass_on")
    every(rest[3:], "start")
    every(keys, "finish")

    def sort(p, carry):
        for s in range(2):
            place = tuple(tab[s, column + p] for column in (AT_H, AT_X, AT_Y))
            half = tab[s, AT_HALF + p]
            for h in range(HH):
                kvs[s, h, lax.div(p, SPANS_STEP), lax.rem(p, SPANS_STEP)] = kvg[(h,) + place + (s * 2 + half,)]
        return carry

    lax.fori_loop(0, 2 * N_CTX, sort, 0)
    keep_keys = pltpu.make_async_copy(kvs, kv_out, ksem.at[HH])
    keep_keys.start()
    attend_heads(tab, 0, q_ref, kvs, o_ref, low_ref, l_ref, acc, sum_ref)
    every(rest[:3], "pass_on")
    attend_heads(tab, 1, q_ref, kvs, o_ref, low_ref, l_ref, acc, sum_ref)
    every(rest[3:], "pass_on")
    every(rest, "finish")
    keep_keys.wait()
    arrived(6)
    keep.wait()
    for c in remote + total.sent:
        c.wait_send()
    for s in ones + rest + keys:
        s.wait_sent()


def front(tab, shards, x, dy, gains, cosine, sine, cid):
    anywhere = pl.BlockSpec(memory_space=pl.ANY)
    vmem = pl.BlockSpec(memory_space=pltpu.VMEM)
    full = [jax.ShapeDtypeStruct((2, 4, 4, 2, 32, w), BF) for w in (QW + KVW, FH, FH, FH, QW)]
    n = len(GATHER)
    return pl.pallas_call(
        front_kernel,
        out_shape=full
        + [
            jax.ShapeDtypeStruct((2,) + x.shape, BF),
            jax.ShapeDtypeStruct((2,) + dy.shape, BF),
            jax.ShapeDtypeStruct(gains.shape, F32),
            jax.ShapeDtypeStruct((2 * TOK, QW + KVW), F32),
            jax.ShapeDtypeStruct((2 * TOK, D), BF),
            jax.ShapeDtypeStruct((2 * TOK, QW), BF),
            jax.ShapeDtypeStruct((2, HH, KEY_BLOCKS, SPANS_STEP, SPAN, 2 * HD), BF),
            jax.ShapeDtypeStruct((2 * TOK, QW), F32),
            jax.ShapeDtypeStruct((2 * TOK, QW), BF),
            jax.ShapeDtypeStruct((2, HH, 2, 1, QROWS), F32),
        ],
        in_specs=[pl.BlockSpec(memory_space=pltpu.SMEM)] + [anywhere] * 6 + [vmem] * 3,
        out_specs=[anywhere] * 5 + [vmem, anywhere] + [vmem] * 4 + [anywhere] + [vmem] * 3,
        scratch_shapes=[
            pltpu.VMEM((2, 4, 4, 2, 32, QW + KVW), BF),
            pltpu.VMEM((HH, 4, SPAN, 2 * HD), BF),
            pltpu.VMEM((HH, 2, 4, 4, 4, SPAN, 2 * HD), BF),
            pltpu.VMEM((2, HH, KEY_BLOCKS, SPANS_STEP, SPAN, 2 * HD), BF),
            pltpu.VMEM((2, HH, 2, QROWS, 2 * HD), BF),
            pltpu.VMEM((2, 2 * HD, QROWS), F32),
            pltpu.VMEM((2, 1, QROWS), F32),
            pltpu.VMEM((4, 4) + gains.shape, F32),
            pltpu.SemaphoreType.DMA((7, 2)),
            pltpu.SemaphoreType.DMA((8,)),
            pltpu.SemaphoreType.DMA((4, 4)),
            pltpu.SemaphoreType.DMA((4, 4)),
            pltpu.SemaphoreType.DMA((3, 3, 4)),
            pltpu.SemaphoreType.DMA((3, 3, 4)),
            pltpu.SemaphoreType.DMA((n, 3, 4)),
            pltpu.SemaphoreType.DMA((n, 3, 4)),
            pltpu.SemaphoreType.DMA((HH, 3, 4)),
            pltpu.SemaphoreType.DMA((HH, 3, 4)),
            pltpu.SemaphoreType.DMA((HH + 1,)),
        ],
        compiler_params=pltpu.CompilerParams(
            collective_id=cid, has_side_effects=True, vmem_limit_bytes=60 * 1024 * 1024
        ),
        name="front",
    )(tab, *shards, x, dy, gains, cosine, sine)


def lead_shape(dims):
    full = {"h": 2, "x": 4, "y": 4, "l": 2}
    return tuple(full[d] for d in dims)


def without(dims, axis):
    gone = ("h", "l") if axis == "z" else (axis,)
    return tuple(d for d in dims if d not in gone)


class Summing:
    def __init__(self, source, dims, at, order, rows, cols, buffers, ssem, rsem, lsem, begun=None, base=None):
        self.ref, self.dims, self.at, self.order, self.begun = source, dims, at, order, begun
        self.cols, self.buffers, self.rows = cols, buffers, rows
        self.ssem, self.rsem, self.lsem = ssem, rsem, lsem
        self.phase, self.sent, self.base = 0, [], base
        self.resident = base is not None

    def part(self, coordinate, start, length):
        rows = pl.ds(start + (self.base or 0), length)
        return pick(self.ref, self.dims, labels(self.axis, coordinate), (rows, self.cols))

    def send(self, n, src, dst, by):
        c = send(src, dst, self.ssem.at[self.phase, n], self.rsem.at[self.phase, n], moved(self.at, self.axis, by))
        self.sent.append(c)
        return c

    def start(self):
        self.axis = self.order[self.phase]
        self.rest = without(self.dims, self.axis)
        self.lead = lead_shape(self.rest)
        half = self.rows // 2
        first, second, every = (0, half), (half, half), (0, self.rows)
        i = self.at[self.axis]
        buf = self.buffers[self.phase]
        self.local = []
        if SIZES[self.axis] == 2:
            self.direct = (self.send(0, self.part(1 - i, *every), buf["got"].at[0], 1),)
        else:
            up, down, far = lax.rem(i + 1, 4), lax.rem(i + 3, 4), lax.rem(i + 2, 4)
            self.near = (up, down)
        if self.phase == 0 and self.begun is not None:
            self.relay, self.direct = (), ()
        elif SIZES[self.axis] == 4:
            self.relay = (
                self.send(0, self.part(far, *first), buf["relay"].at[0], 1),
                self.send(1, self.part(far, *second), buf["relay"].at[1], 3),
            )
            self.direct = (
                self.send(2, self.part(up, *second), buf["got"].at[1, 1], 1),
                self.send(3, self.part(down, *first), buf["got"].at[0, 1], 3),
            )
        if self.phase == 0 and not self.resident:
            todo = [(self.part(i, *every), buf["mine"])]
            if self.begun is not None:
                passed, direct = self.begun[1], self.begun[0]
                todo += [(passed.at[n], buf["got"].at[n, 0]) for n in range(2)]
                todo += [(direct.at[n], buf["got"].at[n, 1]) for n in range(2)]
            elif SIZES[self.axis] == 4:
                todo.append((self.part(up, *first), buf["own"].at[0]))
                todo.append((self.part(down, *second), buf["own"].at[1]))
            for n, (src, dst) in enumerate(todo):
                c = pltpu.make_async_copy(src, dst, self.lsem.at[n])
                c.start()
                self.local.append(c)

    def over_lead(self, add):
        rest = self.lead[1:]
        spots = [()]
        for n in rest:
            spots = [s + (j,) for s in spots for j in range(n)]
        if not self.lead:
            add(())
            return

        def go(j, carry):
            for s in spots:
                add((j,) + s)
            return carry

        lax.fori_loop(0, self.lead[0], go, 0)

    def pass_on(self):
        if SIZES[self.axis] == 2 or (self.phase == 0 and self.begun is not None):
            return
        buf = self.buffers[self.phase]
        half = self.rows // 2
        for n, by in ((0, 1), (1, 3)):
            self.relay[n].wait_recv()
            if self.phase == 0 and not self.resident:
                self.local[1 + n].wait()
                own = buf["own"].at[n]
            else:
                own = self.part(self.near[n], n * half, half)

            def add(spot):
                here_ = spot + (slice(None), slice(None))
                both = buf["relay"][(n,) + here_].astype(F32) + own[here_].astype(F32)
                buf["relay"][(n,) + here_] = both.astype(BF)

            self.over_lead(add)
            c = self.send(4 + n, buf["relay"].at[n], buf["got"].at[n, 0], by)
            self.direct = self.direct + (c,)

    def finish(self):
        buf = self.buffers[self.phase]
        half = self.rows // 2
        if self.local:
            self.local[0].wait()
        if self.begun is not None:
            for c in self.local[1:]:
                c.wait()
        for c in self.direct:
            c.wait_recv()
        copied = self.phase == 0 and not self.resident
        own = buf["mine"] if copied else self.part(self.at[self.axis], 0, self.rows)
        out = buf["mine"] if copied else buf["sum"]

        def add(spot):
            if SIZES[self.axis] == 2:
                here_ = spot + (slice(None), slice(None))
                out[here_] = (own[here_].astype(F32) + buf["got"][(0,) + here_].astype(F32)).astype(out.dtype)
                return
            for n in range(2):
                rows = spot + (pl.ds(n * half, half), slice(None))
                all_ = spot + (slice(None), slice(None))
                total = own[rows].astype(F32) + buf["got"][(n, 0) + all_].astype(F32)
                total = total + buf["got"][(n, 1) + all_].astype(F32)
                out[rows] = total.astype(out.dtype)

        self.over_lead(add)
        self.ref, self.dims, self.cols = out, self.rest, slice(None)
        self.phase += 1
        self.base = 0


class Total:
    def __init__(self, value, at, buf, ssem, rsem):
        self.value, self.at, self.buf, self.ssem, self.rsem = value, at, buf, ssem, rsem
        self.phase, self.sent = 0, []
        self.start()

    def start(self):
        n, axis = self.phase, ("core", "z", "y", "x")[self.phase]
        self.buf[n, 0] = self.value
        self.copies = []
        for i in (1, 3, 2) if axis != "core" else (1,):
            self.copies.append(
                send(self.buf.at[n, 0], self.buf.at[n, i], self.ssem.at[n, i], self.rsem.at[n, i], moved(self.at, axis, i))
            )

    def step(self):
        n, buf = self.phase, self.buf
        if n == 4:
            return
        for c in self.copies:
            c.wait_recv()
            self.sent.append(c)
        if n == 0:
            self.value = buf[n, 0] + buf[n, 1]
        else:
            self.value = (buf[n, 0] + buf[n, 2]) + (buf[n, 1] + buf[n, 3])
        self.phase += 1
        if self.phase < 4:
            self.start()


def run_sums(streams, total):
    todo = []
    for s in streams:
        s.start()
        steps = [("pass_on",), ("finish", "start"), ("pass_on",), ("finish", "start"), ("pass_on",), ("finish",)]
        todo.append(steps[1:] if s.begun is not None else steps)
    while any(todo):
        for s, steps in zip(streams, todo):
            if steps:
                for name in steps.pop(0):
                    getattr(s, name)()
        total.step()
    for s in streams:
        for c in s.sent:
            c.wait_send()


def sum_scratch(order, dims, rows, width, begun=False, resident=False):
    buffers = []
    for phase, axis in enumerate(order):
        rest = without(dims, axis)
        lead = lead_shape(rest)
        buf = {}
        if SIZES[axis] == 2:
            buf["got"] = pltpu.VMEM((1,) + lead + (rows, width), BF)
        else:
            buf["got"] = pltpu.VMEM((2, 2) + lead + (rows // 2, width), BF)
            if phase or not begun:
                buf["relay"] = pltpu.VMEM((2,) + lead + (rows // 2, width), BF)
        if phase == 0 and not resident:
            buf["mine"] = pltpu.VMEM(lead + (rows, width), BF)
            if SIZES[axis] == 4 and not begun:
                buf["own"] = pltpu.VMEM((2,) + lead + (rows // 2, width), BF)
        else:
            buf["sum"] = pltpu.VMEM(lead + (rows, width), BF if phase < 2 else F32)
        buffers.append(buf)
        dims = rest
    return buffers


def weight_sum_kernel(pieces, n, *refs):
    ins, small, begun, refs = refs[:n], refs[n], refs[n + 1 : n + 1 + 2 * N_EARLY], refs[n + 1 + 2 * N_EARLY :]
    outs, small_out = refs[: n - 1], refs[n - 1]
    buffers, stages, swapped, halves, small_buf, ssem, rsem, lsem, csem, tssem, trsem = refs[n:]
    at = here()
    core = at["core"]
    sibling = moved(at, "core", 1)
    greet([sibling] + sum_peers(at, ("x", "y", "z")))
    streams = [
        Summing(
            ins[a], W_DIMS, at, order, 32, pl.ds(start, width), buffers[k], ssem.at[k], rsem.at[k], lsem.at[k],
            (begun[2 * k], begun[2 * k + 1]) if k < N_EARLY else None,
        )
        for k, (a, start, width, order) in enumerate(pieces)
    ]
    total = Total(small[...], at, small_buf, tssem, trsem)
    run_sums(streams, total)
    small_out[...] = total.value
    for k, (a, start, width, order) in enumerate(pieces):
        stages[a][:, start : start + width] = buffers[k][2]["sum"][...]
    other = pl.ds(pl.multiple_of((1 - core) * 16, 16), 16)
    own = pl.ds(pl.multiple_of(core * 16, 16), 16)
    copies = [send(stages[a].at[other], swapped[a], csem.at[a, 0], csem.at[a, 1], sibling) for a in range(n)]

    def put(a, half, value):
        width = value.shape[1]
        if a == 4:
            outs[3][:, pl.ds(pl.multiple_of(half * QW, 128), QW)] = value[:, :QW]
            halves[half] = value[:, QW:]
            return
        ref, start = ((outs[0], 0), (outs[0], FF), (outs[1], 0), (outs[2], 0))[a]
        ref[:, pl.ds(pl.multiple_of(start + half * width, 128), width)] = value

    for a in range(n):
        put(a, core, stages[a][own, :])
    for a in range(n):
        copies[a].wait_recv()
        put(a, 1 - core, swapped[a][...])
    for kind in range(2):
        at_ = [half_kv[:, (2 * h + kind) * HD : (2 * h + kind + 1) * HD] for half_kv in (halves[0], halves[1]) for h in range(HH)]
        start = HQ * HD + kind * HK * HD
        outs[3][:, start : start + HK * HD] = jnp.concatenate(at_, axis=1)
    for c in copies + total.sent:
        c.wait_send()


def sum_weights(grads, small, begun, pieces, cid, limit):
    n, count = len(grads), len(pieces)
    anywhere = pl.BlockSpec(memory_space=pl.ANY)
    vmem = pl.BlockSpec(memory_space=pltpu.VMEM)
    widths = [g.shape[-1] for g in grads]
    return pl.pallas_call(
        functools.partial(weight_sum_kernel, pieces, n),
        out_shape=[jax.ShapeDtypeStruct((16, w), F32) for w in (2 * FF, FF, HQ * HD, (HQ + 2 * HK) * HD)]
        + [jax.ShapeDtypeStruct(small.shape, F32)],
        in_specs=[anywhere] * n + [vmem] + [anywhere] * len(begun),
        out_specs=[vmem] * n,
        scratch_shapes=[
            [sum_scratch(order, W_DIMS, 32, width, k < N_EARLY) for k, (a, start, width, order) in enumerate(pieces)],
            [pltpu.VMEM((32, w), F32) for w in widths],
            [pltpu.VMEM((16, w), F32) for w in widths],
            pltpu.VMEM((2, 16, KVW), F32),
            pltpu.VMEM((4, 4) + small.shape, F32),
            pltpu.SemaphoreType.DMA((count, 3, 6)),
            pltpu.SemaphoreType.DMA((count, 3, 6)),
            pltpu.SemaphoreType.DMA((count, 6)),
            pltpu.SemaphoreType.DMA((n, 2)),
            pltpu.SemaphoreType.DMA((4, 4)),
            pltpu.SemaphoreType.DMA((4, 4)),
        ],
        compiler_params=pltpu.CompilerParams(collective_id=cid, has_side_effects=True, vmem_limit_bytes=limit),
        name="sum_weights",
    )(*grads, small, *begun)


def sum_peers(at, axes):
    out = []
    for a in axes:
        for i in (1, 3, 2) if SIZES[a] == 4 else (1,):
            out.append(moved(at, a, i))
    return out


def heads_at(ref, s, h, half):
    rows = slice(s * TOK + half * SPAN, s * TOK + (half + 1) * SPAN)
    return jnp.concatenate([ref[rows, (h * GROUP + g) * HD : (h * GROUP + g + 1) * HD] for g in range(GROUP)], axis=0)


def put_heads(ref, s, h, half, value):
    rows = pl.ds(pl.multiple_of(s * TOK + half * SPAN, SPAN), SPAN)
    for g in range(0, GROUP, 2):
        both = jnp.concatenate([value[g * SPAN : (g + 1) * SPAN], value[(g + 1) * SPAN : (g + 2) * SPAN]], axis=1)
        ref[rows, pl.ds(pl.multiple_of((h * GROUP + g) * HD, 2 * HD), 2 * HD)] = both.astype(ref.dtype)


def masked(prob, limit):
    if limit is None:
        return prob
    row = lax.broadcasted_iota(jnp.int32, prob.shape, 0)
    col = lax.rem(lax.broadcasted_iota(jnp.int32, prob.shape, 1), SPAN)
    return jnp.where(row <= col + limit, prob, 0.0)


def attend_heads(tab, s, q_ref, kvs, o_ref, low_ref, l_ref, acc, total):
    rate = LOG2E * HD**-0.5

    def head(h, carry):
        acc[...] = jnp.zeros_like(acc)
        total[...] = jnp.zeros_like(total)

        def scored(half, block, limit):
            keys = kvs[s, h, block].reshape(KEYS, 2 * HD)
            scores = lax.dot_general(keys, q_ref[s, h, half], NT, preferred_element_type=F32)
            prob = masked(jnp.exp2(scores * rate), limit)
            return (
                jnp.sum(prob, axis=0, keepdims=True),
                lax.dot_general(keys, prob.astype(BF), TN, preferred_element_type=F32),
            )

        def high(k, c):
            t, o = scored(1, k, None)
            total[1] += t
            acc[1] += o
            return c

        def either(k, c):
            half = tab[s, AT_STEP_HALF + k]
            t, o = scored(half, tab[s, AT_STEP_BLOCK + k], None)
            up = half.astype(F32)
            total[0] += t * (1.0 - up)
            total[1] += t * up
            acc[0] += o * (1.0 - up)
            acc[1] += o * up
            return c

        lax.fori_loop(0, 4, high, 0)
        lax.fori_loop(0, 3, either, 0)
        for half in range(2):
            t, o = scored(half, tab[s, AT_EDGE + half], tab[s, AT_LIMIT + half])
            t, o = total[half] + t, acc[half] + o
            out = (o[HD:, :] / t).T
            put_heads(o_ref, s, h, half, out)
            put_heads(low_ref, s, h, half, out)
            l_ref[s, h, half] = jnp.log2(t)
        return carry

    lax.fori_loop(0, HH, head, 0)


class Early:
    def __init__(self, source, at, order, cols, width, relay, direct, passed, ssem, rsem):
        self.source, self.at, self.axis, self.cols, self.width = source, at, order[0], cols, width
        self.relay, self.passed, self.ssem, self.rsem, self.views = relay, passed, ssem, rsem, {}
        i = at[self.axis]
        self.near = (lax.rem(i + 1, 4), lax.rem(i + 3, 4))
        far = lax.rem(i + 2, 4)
        plan = (
            (far, 0, relay, 0, 1),
            (far, 1, relay, 1, 3),
            (self.near[0], 1, direct, 1, 1),
            (self.near[1], 0, direct, 0, 3),
        )
        self.copies = []
        for n, (coordinate, half, dst, slot, by) in enumerate(plan):
            self.copies.append(self.send(n, self.part(coordinate, half), dst.at[slot], by))

    def part(self, coordinate, half):
        return pick(self.source, W_DIMS, labels(self.axis, coordinate), (pl.ds(half * 16, 16), self.cols))

    def send(self, n, src, dst, by):
        return send(src, dst, self.ssem.at[n], self.rsem.at[n], moved(self.at, self.axis, by))

    def load(self, n, own, sem):
        lead = lead_shape(without(W_DIMS, self.axis))
        view = own.at[(slice(None),) * (len(lead) + 1) + (pl.ds(0, self.width),)]
        self.views[n] = view
        copy = pltpu.make_async_copy(self.part(self.near[n], n), view, sem)
        copy.start()
        return copy

    def add(self, n):
        self.copies[n].wait_recv()
        came, own = self.relay.at[n], self.views[n]
        lead = lead_shape(without(W_DIMS, self.axis))
        spots = [()]
        for size in lead[1:]:
            spots = [s + (j,) for s in spots for j in range(size)]

        def go(j, carry):
            for s in spots:
                at = (j,) + s + (slice(None), slice(None))
                came[at] = (came[at].astype(F32) + own[at].astype(F32)).astype(BF)
            return carry

        lax.fori_loop(0, lead[0], go, 0)
        self.copies.append(self.send(4 + n, came, self.passed.at[n], 1 if n == 0 else 3))

    def wait(self):
        for c in self.copies[2:]:
            c.wait_recv()


def early_shapes():
    shapes = []
    for a, start, width, order in SUMS[:N_EARLY]:
        lead = lead_shape(without(W_DIMS, order[0]))
        shapes += [jax.ShapeDtypeStruct((2,) + lead + (16, width), BF)] * 2
    return shapes


def attend_back_kernel(*refs):
    tab, qr, da, attn, attn_low, l_ref, kv_sorted, normed, dy, low_mid, hid, dgate, dup = refs[:13]
    joined, normed_one, w_one, gains, cosine, sine, grad_mid, own_x = refs[13:21]
    input_grad, terms, head_terms = refs[21:24]
    grads, refs = refs[24:29], refs[29:]
    begun, refs = refs[: 2 * N_EARLY], refs[2 * N_EARLY :]
    held, qd_ref, delta_ref, stage, acc, dq_acc, dq_ref, buffers, refs = refs[:8] + (refs[8:],)
    tiles, mix, mix_z, relays, w_ref, d_joined, part, got = refs[:8]
    essem, ersem, ssem, rsem, sems, tsem, msem, psem = refs[8:]
    at = here()
    core = at["core"]
    sibling = moved(at, "core", 1)
    def load_keys(h):
        return [pltpu.make_async_copy(kv_sorted.at[s, h], held[h % 2].at[s], sems.at[s, h]) for s in range(2)]

    for c in load_keys(0):
        c.start()

    def load_w(start, width):
        src = w_one.at[:, :, :, :, :, pl.ds(start, width)]
        return pltpu.make_async_copy(src, w_ref.at[:, :, :, :, :, pl.ds(0, width)], psem.at[0])

    load_w(0, QW).start()
    greet([sibling] + neighbours(at, ("x", "y", "z", "h")))
    sides = ((normed, dgate), (normed, dup), (dy, hid), (low_mid, attn_low), (normed_one, d_joined))

    def tile_copy(n, i, slot, parity):
        a, start, width = n
        half = lax.rem(i, 2)
        return pltpu.make_async_copy(
            tiles.at[parity, slot, :, :, :, :, pl.ds(0, width)],
            grads[a].at[lax.div(i, 2), pl.ds(half * 2, 2), :, :, :, pl.ds(start, width)],
            tsem.at[parity, slot],
        )

    def outer(n, parity):
        a, start, width = n
        left, right = sides[a]

        def go(i, carry):
            slot = lax.rem(i, 2)

            @pl.when(i > 1)
            def _():
                tile_copy(n, i, slot, parity).wait()

            rows = pl.ds(pl.multiple_of(i * 512, 512), 512)
            value = lax.dot_general(left[:, rows], right[:, start : start + width], TN, preferred_element_type=F32)
            tiles[parity, slot, :, :, :, :, :width] = value.astype(BF).reshape(2, 4, 2, 32, width)
            tile_copy(n, i, slot, parity).start()
            return carry

        lax.fori_loop(0, 4, go, 0)

    def drain(n, parity):
        for slot in range(2):
            tile_copy(n, slot, slot, parity).wait()

    early = []

    def begin(k):
        a, start, width, order = SUMS[k]
        drain((a, start, width), k % 2)
        early.append(
            Early(
                grads[a], at, order, pl.ds(start, width), width, relays[k], begun[2 * k], begun[2 * k + 1],
                essem.at[k], ersem.at[k],
            )
        )

    for k in range(N_EARLY):
        outer(SUMS[k][:3], k % 2)
        if k:
            begin(k - 1)
    rate = LOG2E * HD**-0.5
    factor = jnp.where(lax.broadcasted_iota(jnp.int32, (1, 2 * HD), 1) < HD, HD**-0.5, 1.0)
    blank = jnp.zeros((QROWS, HD), BF)
    for s in range(2):
        for h in range(HH):
            for half in range(2):
                up = heads_at(da, s, h, half)
                qd_ref[s, h, half, :QROWS] = jnp.concatenate([heads_at(qr, s, h, half), blank], axis=1)
                qd_ref[s, h, half, QROWS:] = jnp.concatenate([blank, up], axis=1)
                inner = (up.astype(F32) * heads_at(attn, s, h, half)).T
                delta_ref[s, h, half] = jnp.sum(inner, axis=0, keepdims=True)
    begin(N_EARLY - 1)
    streams = [
        [
            Summing(
                stage.at[h], KV_DIMS, at, order, rows, slice(None), buffers[h][j],
                ssem.at[h, j], rsem.at[h, j], None, None, start,
            )
            for j, (start, rows, order) in enumerate(KV_PARTS)
        ]
        for h in range(HH)
    ]
    todo = [[("pass_on",), ("finish", "start"), ("pass_on",), ("finish", "start"), ("pass_on",), ("finish",)] for h in range(HH)]

    def move(h):
        for name_of in todo[h].pop(0) if todo[h] else ():
            for st in streams[h]:
                getattr(st, name_of)()

    units = [(k, n) for k in range(N_EARLY) for n in range(2)]
    used, flying, ahead = {}, [], [0]

    def fetch():
        k, n = units[ahead[0]]
        pool, slots, first = (mix_z, 2, 2) if early[k].axis == "z" else (mix, 2, 0)
        slot = used.get(first, 0) % slots
        used[first] = used.get(first, 0) + 1
        flying.append((k, n, early[k].load(n, pool.at[slot], msem.at[first + slot])))
        ahead[0] += 1

    def advance(count):
        for _ in range(count):
            while ahead[0] < len(units) and len(flying) < 2:
                fetch()
            if flying:
                k, n, copy = flying.pop(0)
                copy.wait()
                early[k].add(n)

    for h in range(HH):
        for c in load_keys(h):
            c.wait()
        if h + 1 < HH:
            for c in load_keys(h + 1):
                c.start()
        kvs = held[h % 2]

        def sequence(s, carry, h=h, kvs=kvs):
            dq_acc[...] = jnp.zeros_like(dq_acc)
            acc[...] = jnp.zeros_like(acc)

            def backward(half, block, limit):
                keys = kvs[s, block].reshape(KEYS, 2 * HD)
                both = lax.dot_general(keys, qd_ref[s, h, half], NT, preferred_element_type=F32)
                prob = masked(jnp.exp2(both[:, :QROWS] * rate - l_ref[s, h, half]), limit)
                grad = (prob * (both[:, QROWS:] - delta_ref[s, h, half])).astype(BF)
                pair = jnp.concatenate([grad, prob.astype(BF)], axis=1)
                kv = lax.dot_general(pair, qd_ref[s, h, half], NN, preferred_element_type=F32)
                return (
                    kv.reshape(SPANS_STEP, SPAN, 2 * HD),
                    lax.dot_general(keys, grad, TN, preferred_element_type=F32),
                )

            def spans(block):
                return pl.ds(block * SPANS_STEP, SPANS_STEP)

            def high(k, c):
                kv, q = backward(1, k, None)
                acc[spans(k)] += kv
                dq_acc[1] += q
                return c

            def either(k, c):
                half = tab[s, AT_STEP_HALF + k]
                kv, q = backward(half, tab[s, AT_STEP_BLOCK + k], None)
                up = half.astype(F32)
                acc[spans(k)] += kv * (1.0 - up)
                acc[spans(6 - k)] += kv * up
                dq_acc[0] += q * (1.0 - up)
                dq_acc[1] += q * up
                return c

            lax.fori_loop(0, 4, high, 0)
            lax.fori_loop(0, 3, either, 0)
            for half in range(2):
                kv, q = backward(half, tab[s, AT_EDGE + half], tab[s, AT_LIMIT + half])
                for k in range(4):
                    acc[spans(k if half == 0 else 7 - k)] += kv * tab[s, AT_MARK + k].astype(F32)
                q = dq_acc[half] + q
                put_heads(dq_ref, s, h, half, (q[:HD, :] * HD**-0.5).T)

            def put(j, c):
                for half in range(2):
                    v = acc[tab[s, AT_MAP + half * N_CTX + j]] * factor
                    rows = pl.ds(pl.multiple_of(s * TOK + half * SPAN, SPAN), SPAN)
                    stage[h, lax.div(j, 16), lax.rem(lax.div(j, 4), 4), lax.rem(j, 4), rows, :] = v.astype(BF)
                return c

            lax.fori_loop(0, N_CTX, put, 0)
            return carry

        for s in range(2):
            sequence(s, 0)
            if s == 1:
                for k in range(h):
                    move(k)
                for st in streams[h]:
                    st.start()
            advance(ADVANCE[2 * h + s])

    head_gains = gains[32:33]

    def tile(t, is_key, grad):
        v = joined[:, t * 128 : (t + 1) * 128]
        low = lane_of(v.shape) < HD
        back = grad * cosine[...] - swap_halves(grad) * sine[...]
        inverse = lax.rsqrt(head_sums(v * v) * (1.0 / HD) + EPSILON)
        scaled = back * tile_gain(head_gains, is_key)
        inner = head_sums(scaled * v) * (1.0 / HD)
        result = inverse * scaled - v * (inverse * inverse * inverse) * inner
        if is_key:
            result = jnp.where(low, result, grad)
        d_joined[:, t * 128 : (t + 1) * 128] = result.astype(BF)
        return jnp.sum(back * v * inverse, axis=0, keepdims=True)

    def undo_queries():
        return sum(tile(t, False, dq_ref[:, t * 128 : (t + 1) * 128]) for t in range(QW // 128))

    def back_part(c, start, width):
        w = w_ref[c, :, :, :, :, :width].reshape(D // 2, width)
        return lax.dot_general(d_joined[:, start : start + width], w, NT, preferred_element_type=F32)

    def queries_back():
        load_w(0, QW).wait()
        for c in range(2):
            part[c] = back_part(c, 0, QW)
        load_w(QW, KVW).start()

    q_terms = undo_queries()
    tasks = [queries_back, lambda: outer((4, 0, QW), 0)]
    while any(todo):
        for h in range(HH):
            move(h)
        if tasks:
            tasks.pop(0)()
        advance(1)
    k_terms = 0.0
    for h in range(HH):
        grad = jnp.concatenate([buffers[h][j][2]["sum"][...] for j in range(len(KV_PARTS))], axis=0)
        k_terms = k_terms + tile(QW // 128 + h, True, grad)
    q_terms = q_terms + pltpu.roll(q_terms, HD, 1)
    head_terms[...] = jnp.where(lane_of(q_terms.shape) < HD, q_terms, pltpu.roll(k_terms, HD, 1))
    other = pl.ds(pl.multiple_of((1 - core) * TOK, TOK), TOK)
    load_w(QW, KVW).wait()
    swaps = []
    for c in range(2):
        part[c] += back_part(c, QW, KVW)
        swaps.append(send(part.at[c, other], got.at[c], psem.at[1 + c], psem.at[3 + c], sibling))
    advance(2)
    outer((4, QW, KVW), 1)
    advance(2)
    gain_row = jnp.concatenate([gains[j : j + 1] for j in range(D // 128)], axis=1)
    for c in swaps:
        c.wait_recv()

    def last(r, carry):
        rows = rows_at(r)
        own = pl.ds(pl.multiple_of(core * TOK + r * 32, 32), 32)
        e = jnp.concatenate([part[c, own, :] + got[c, rows, :] for c in range(2)], axis=1)
        v = own_x[rows, :].astype(F32)
        inverse = lax.rsqrt(jnp.sum(v * v, axis=1, keepdims=True) * (1.0 / D) + EPSILON)
        scaled = e * gain_row
        inner = jnp.sum(scaled * v, axis=1, keepdims=True) * (1.0 / D)
        total = grad_mid[rows, :] + inverse * scaled - v * (inverse * inverse * inverse) * inner
        input_grad[rows, :] = total.astype(BF)
        return carry + jnp.sum(e * v * inverse, axis=0, keepdims=True)

    terms[...] = lax.fori_loop(0, TOK // 32, last, jnp.zeros((1, D), F32))
    advance(len(units))
    drain((4, 0, QW), 0)
    drain((4, QW, KVW), 1)
    for e in early:
        e.wait()
    pending = [c for e in early for c in e.copies] + swaps + [c for group in streams for st in group for c in st.sent]
    for c in pending:
        c.wait_send()


def attend_back(operands, cid):
    vmem = pl.BlockSpec(memory_space=pltpu.VMEM)
    anywhere = pl.BlockSpec(memory_space=pl.ANY)
    tokens = 2 * TOK
    widths = (FH, FH, FH, QW, QW + KVW)
    out = pl.pallas_call(
        attend_back_kernel,
        out_shape=[
            jax.ShapeDtypeStruct((TOK, D), BF),
            jax.ShapeDtypeStruct((1, D), F32),
            jax.ShapeDtypeStruct((1, 128), F32),
        ]
        + [jax.ShapeDtypeStruct((2, 4, 4, 2, 32, w), BF) for w in widths]
        + early_shapes(),
        in_specs=[pl.BlockSpec(memory_space=pltpu.SMEM)]
        + [vmem] * 5
        + [anywhere]
        + [vmem] * 8
        + [anywhere]
        + [vmem] * 5,
        out_specs=[vmem] * 3 + [anywhere] * (5 + 2 * N_EARLY),
        scratch_shapes=[
            [pltpu.VMEM((2, KEY_BLOCKS, SPANS_STEP, SPAN, 2 * HD), BF)] * 2,
            pltpu.VMEM((2, HH, 2, 2 * QROWS, 2 * HD), BF),
            pltpu.VMEM((2, HH, 2, 1, QROWS), F32),
            pltpu.VMEM((HH, 2, 4, 4, tokens, 2 * HD), BF),
            pltpu.VMEM((2 * N_CTX, SPAN, 2 * HD), F32),
            pltpu.VMEM((2, 2 * HD, QROWS), F32),
            pltpu.VMEM((tokens, QW), F32),
            [
                [sum_scratch(order, KV_DIMS, rows, 2 * HD, False, True) for start, rows, order in KV_PARTS]
                for h in range(HH)
            ],
            pltpu.VMEM((2, 2, 2, 4, 2, 32, 1152), BF),
            pltpu.VMEM((2, 2, 4, 2, 16, 1152), BF),
            pltpu.VMEM((2, 4, 4, 16, 1152), BF),
            [
                pltpu.VMEM((2,) + lead_shape(without(W_DIMS, order[0])) + (16, width), BF)
                for a, start, width, order in SUMS[:N_EARLY]
            ],
            pltpu.VMEM((2, 4, 4, 2, 32, QW), BF),
            pltpu.VMEM((tokens, QW + KVW), BF),
            pltpu.VMEM((2, tokens, D // 2), F32),
            pltpu.VMEM((2, TOK, D // 2), F32),
            pltpu.SemaphoreType.DMA((N_EARLY, 6)),
            pltpu.SemaphoreType.DMA((N_EARLY, 6)),
            pltpu.SemaphoreType.DMA((HH, 3, 3, 6)),
            pltpu.SemaphoreType.DMA((HH, 3, 3, 6)),
            pltpu.SemaphoreType.DMA((2, HH)),
            pltpu.SemaphoreType.DMA((2, 2)),
            pltpu.SemaphoreType.DMA((5,)),
            pltpu.SemaphoreType.DMA((5,)),
        ],
        compiler_params=pltpu.CompilerParams(
            collective_id=cid, has_side_effects=True, vmem_limit_bytes=63 * 1024 * 1024
        ),
        name="attend_back",
    )(*operands)
    return out[0], out[1], out[2], out[3:8], out[8:]


CHUNKS = ((0, 768), (768, 768), (1536, 640))


def rows_at(r, n=32):
    return pl.ds(pl.multiple_of(r * n, n), n)


def feed_kernel(
    attn, x, dy, gains, wo_h, wg_h, wu_h, wd_h,
    result, grad_mid, grad_attn, normed, hid, dgate, dup, low_mid, stats, terms,
    wo, wg, wu, wd, mid, part, got, part_f, got_f, back_ref, wsem, psem,
):
    at = here()
    core = at["core"]
    sibling = moved(at, "core", 1)
    loads = []
    for i, (src, dst) in enumerate(((wo_h, wo), (wd_h, wd), (wg_h, wg), (wu_h, wu))):
        loads.append(pltpu.make_async_copy(src, dst, wsem.at[i]))
        loads[-1].start()
    greet([sibling])
    gain_row = jnp.concatenate([gains[16 + j : 17 + j] for j in range(D // 128)], axis=1)
    sent = []
    loads[0].wait()
    for c in range(2):
        cols = slice(c * 1024, (c + 1) * 1024)
        part[0, c] = lax.dot_general(attn[...], wo[cols, :], NT, preferred_element_type=F32)
        sent.append(send(part.at[0, c], got.at[0, c], psem.at[c, 0], psem.at[c, 1], sibling))
    loads[1].wait()
    for start, width in CHUNKS:
        cols = slice(start, start + width)
        back_ref[:, cols] = jnp.dot(dy[...], wd[:, cols], preferred_element_type=F32)
    for c in sent:
        c.wait_recv()

    def root(v):
        return jnp.sum(jnp.sqrt(jnp.sum(v * v, axis=1, keepdims=True) * (1.0 / D)), axis=0, keepdims=True)

    def middle(r, carry):
        rows = rows_at(r)
        branch = jnp.concatenate([part[0, c, rows, :] + got[0, c, rows, :] for c in range(2)], axis=1)
        v = x[rows, :].astype(F32)
        m = v + branch
        mid[rows, :] = m
        inverse = lax.rsqrt(jnp.sum(m * m, axis=1, keepdims=True) * (1.0 / D) + EPSILON)
        normed[rows, :] = (m * inverse * gain_row).astype(BF)
        own = jnp.where(lax.div(r, TOK // 32) == core, 1.0, 0.0)
        return tuple(t + own * root(u) for t, u in zip(carry, (v, branch, m)))

    zero = jnp.zeros((1, 1), F32)
    roots = lax.fori_loop(0, 2 * TOK // 32, middle, (zero, zero, zero))
    for c in loads[2:]:
        c.wait()
    for start, width in CHUNKS:
        cols = slice(start, start + width)
        gate = jnp.dot(normed[...], wg[:, cols], preferred_element_type=F32)
        up = jnp.dot(normed[...], wu[:, cols], preferred_element_type=F32)
        back = back_ref[:, cols]
        sigmoid = lax.logistic(gate)
        silu = gate * sigmoid
        hid[:, cols] = (silu * up).astype(BF)
        dup[:, cols] = (back * silu).astype(BF)
        dgate[:, cols] = (back * up * sigmoid * (1.0 + gate * (1.0 - sigmoid))).astype(BF)
    late = []
    for c in range(2):
        cols = slice(c * 1024, (c + 1) * 1024)
        one = lax.dot_general(dgate[...], wg[cols, :], NT, preferred_element_type=F32)
        part[1, c] = one + lax.dot_general(dup[...], wu[cols, :], NT, preferred_element_type=F32)
        late.append(send(part.at[1, c], got.at[1, c], psem.at[2 + c, 0], psem.at[2 + c, 1], sibling))
    part_f[...] = lax.dot_general(hid[...], wd[...], NT, preferred_element_type=F32)
    other = pl.ds(pl.multiple_of((1 - core) * TOK, TOK), TOK)
    last = send(part_f.at[other], got_f, psem.at[4, 0], psem.at[4, 1], sibling)

    for c in late:
        c.wait_recv()

    def backward(r, carry):
        rows = rows_at(r)
        e = jnp.concatenate([part[1, c, rows, :] + got[1, c, rows, :] for c in range(2)], axis=1)
        v = mid[rows, :]
        inverse = lax.rsqrt(jnp.sum(v * v, axis=1, keepdims=True) * (1.0 / D) + EPSILON)
        scaled = e * gain_row
        inner = jnp.sum(scaled * v, axis=1, keepdims=True) * (1.0 / D)
        total = dy[rows, :].astype(F32) + inverse * scaled - v * (inverse * inverse * inverse) * inner
        low_mid[rows, :] = total.astype(BF)
        mid[rows, :] = total
        own = jnp.where(lax.div(r, TOK // 32) == core, 1.0, 0.0)
        return carry + own * jnp.sum(e * v * inverse, axis=0, keepdims=True)

    def finish(r, carry):
        rows = rows_at(r)
        own = pl.ds(pl.multiple_of(core * TOK + r * 32, 32), 32)
        branch = part_f[own, :] + got_f[rows, :]
        result[rows, :] = (mid[own, :] + branch).astype(BF)
        return carry + root(branch)

    last.wait_recv()
    final = lax.fori_loop(0, TOK // 32, finish, zero)
    terms[...] = lax.fori_loop(0, 2 * TOK // 32, backward, jnp.zeros((1, D), F32))
    for i, v in enumerate(roots + (final,)):
        stats[i : i + 1, :] = jnp.broadcast_to(v, (1, 128))
    grad_attn[...] = jnp.dot(low_mid[...], wo[...], preferred_element_type=F32).astype(BF)
    grad_mid[...] = mid[pl.ds(pl.multiple_of(core * TOK, TOK), TOK), :]
    for c in sent + late + [last]:
        c.wait_send()


def feed(attn, x, dy, gains, w_out, w_gate, w_up, w_down, cid):
    vmem = pl.BlockSpec(memory_space=pltpu.VMEM)
    anywhere = pl.BlockSpec(memory_space=pl.ANY)
    tokens = 2 * TOK
    return pl.pallas_call(
        feed_kernel,
        out_shape=[
            jax.ShapeDtypeStruct((TOK, D), BF),
            jax.ShapeDtypeStruct((TOK, D), F32),
            jax.ShapeDtypeStruct((tokens, QW), BF),
            jax.ShapeDtypeStruct((tokens, D), BF),
            jax.ShapeDtypeStruct((tokens, FH), BF),
            jax.ShapeDtypeStruct((tokens, FH), BF),
            jax.ShapeDtypeStruct((tokens, FH), BF),
            jax.ShapeDtypeStruct((tokens, D), BF),
            jax.ShapeDtypeStruct((4, 128), F32),
            jax.ShapeDtypeStruct((1, D), F32),
        ],
        in_specs=[vmem] * 4 + [anywhere] * 4,
        out_specs=[vmem] * 10,
        scratch_shapes=[
            pltpu.VMEM((D, QW), BF),
            pltpu.VMEM((D, FH), BF),
            pltpu.VMEM((D, FH), BF),
            pltpu.VMEM((D, FH), BF),
            pltpu.VMEM((tokens, D), F32),
            pltpu.VMEM((2, 2, tokens, D // 2), F32),
            pltpu.VMEM((2, 2, tokens, D // 2), F32),
            pltpu.VMEM((tokens, D), F32),
            pltpu.VMEM((TOK, D), F32),
            pltpu.VMEM((tokens, FH), F32),
            pltpu.SemaphoreType.DMA((4,)),
            pltpu.SemaphoreType.DMA((5, 2)),
        ],
        compiler_params=pltpu.CompilerParams(
            collective_id=cid, has_side_effects=True, vmem_limit_bytes=62 * 1024 * 1024
        ),
        name="feed",
    )(attn, x, dy, gains, w_out, w_gate, w_up, w_down)


def body(layer_input, w_qkv, w_out, w_gate_up, w_down, norm_gains, span_map, cotangent):
    at = here()
    core, low = at["core"], at["l"]
    w_q = w_qkv[:, : HQ * HD].reshape(16, 2, QW).transpose(1, 0, 2)
    w_k = w_qkv[:, HQ * HD : (HQ + HK) * HD].reshape(16, 2, HH, HD)
    w_v = w_qkv[:, (HQ + HK) * HD :].reshape(16, 2, HH, HD)
    w_kv = jnp.concatenate([w_k, w_v], axis=3).reshape(16, 2, KVW).transpose(1, 0, 2)
    shard_one = jnp.concatenate([w_q, w_kv], axis=2)
    share = norm_gains.shape[0]
    device = lax.axis_index(("ctx", "fsdp"))
    own_gain = lax.dynamic_update_slice_in_dim(jnp.zeros((40 * 128,), F32), norm_gains.astype(F32), device * share, 0)

    ctx_index = lax.axis_index("ctx")
    maps = lax.dynamic_slice_in_dim(span_map, low * 2, 2, 0)
    own_span = lax.dynamic_slice_in_dim(maps, ctx_index, 1, 1)
    spans = jnp.concatenate([own_span, 2 * N_CTX - 1 - own_span], axis=1)
    positions = (spans[:, :, None] * SPAN + jnp.arange(SPAN, dtype=jnp.int32)).reshape(2 * TOK)
    match = maps[:, None, :] == jnp.arange(N_CTX, dtype=jnp.int32)[None, :, None]
    inverse_map = jnp.sum(jnp.where(match, jnp.arange(N_CTX, dtype=jnp.int32), 0), axis=2)
    holder = jnp.concatenate([inverse_map, inverse_map[:, ::-1]], axis=1)
    upper = (jnp.arange(2 * N_CTX, dtype=jnp.int32) >= N_CTX).astype(jnp.int32)[None, :] + jnp.zeros_like(holder)
    low_block = own_span // SPANS_STEP
    low_limit = own_span % SPANS_STEP * SPAN
    three = jnp.arange(3, dtype=jnp.int32)[None, :]
    step_half = (three >= low_block).astype(jnp.int32)
    tab = jnp.concatenate(
        [
            holder // 16,
            holder // 4 % 4,
            holder % 4,
            upper,
            step_half,
            jnp.where(step_half == 0, three, 6 - three),
            (jnp.arange(4, dtype=jnp.int32)[None, :] == low_block).astype(jnp.int32),
            low_block,
            KEY_BLOCKS - 1 - low_block,
            low_limit,
            KEYS - SPAN - low_limit,
            maps,
            2 * N_CTX - 1 - maps,
        ],
        axis=1,
    )
    half_dim = HD // 2
    frequencies = ROPE_BASE ** (-(jnp.arange(half_dim, dtype=F32) * 2.0 / HD))
    angles = positions.astype(F32)[:, None] * frequencies[None, :]
    cosine, sine = jnp.cos(angles), jnp.sin(angles)
    cosine = jnp.concatenate([cosine] * 4, axis=1)
    sine = jnp.concatenate([-sine, sine] * 2, axis=1)

    weights = [shard_one, w_gate_up, w_down, w_out]
    (w_one, w_gate, w_up, w_back, w_proj, x_pair, dy_pair, gains, joined, normed_one, query, keys, attn_f32, attn_low, log_sum) = front(
        tab, weights, layer_input[0], cotangent[0], own_gain.reshape(40, 128), cosine, sine, 1
    )
    w_gate, w_up, w_back, w_proj = (w.reshape(D, -1) for w in (w_gate, w_up, w_back, w_proj))
    dy = dy_pair.reshape(2 * TOK, D)

    result, grad_middle, grad_attn, normed_two, hidden, grad_gate, grad_up, grad_branch, stats, gain_two_terms = feed(
        attn_low, x_pair.reshape(2 * TOK, D), dy, gains, w_proj, w_gate, w_up, w_back, 2
    )
    operands = (tab, query, grad_attn, attn_f32, attn_low, log_sum, keys, normed_two, dy, grad_branch, hidden)
    operands += (grad_gate, grad_up, joined, normed_one, w_one, gains, cosine, sine, grad_middle, layer_input[0])
    grad_input, gain_one_terms, head_terms, grads, begun = attend_back(operands, 4)
    sums = jnp.concatenate(
        [
            gain_one_terms[0],
            gain_two_terms[0],
            head_terms[0],
            stats[:, 0],
        ]
    )
    sums = jnp.pad(sums, (0, 40 * 128 - sums.shape[0])).reshape(40, 128)
    grad_mlp, grad_down, grad_proj, grad_qkv, sums = sum_weights(
        grads, sums, begun, SUMS, 5, 62 * 1024 * 1024
    )
    sums = sums.reshape(-1)
    own_gains = lax.dynamic_slice_in_dim(sums, device * share, share, 0)
    stream_rms = sums[4224:4228] / (TOK * N_CTX * 4)
    arrays = [result[None], grad_input[None], grad_qkv, grad_proj, grad_mlp, grad_down]
    result, grad_input, grad_qkv, grad_proj, grad_mlp, grad_down = publish(arrays)
    return (
        result,
        grad_input,
        grad_qkv,
        grad_proj,
        grad_mlp,
        grad_down,
        own_gains,
        stream_rms,
    )


def publish_kernel(n, *refs):
    copies = [pltpu.make_async_copy(refs[i], refs[n + i], refs[2 * n].at[i]) for i in range(n)]
    for c in copies:
        c.start()
    for c in copies:
        c.wait()


def publish(arrays):
    n = len(arrays)
    anywhere = pl.BlockSpec(memory_space=pl.ANY)
    return pl.pallas_call(
        functools.partial(publish_kernel, n),
        out_shape=[jax.ShapeDtypeStruct(a.shape, a.dtype) for a in arrays],
        in_specs=[pl.BlockSpec(memory_space=pltpu.VMEM)] * n,
        out_specs=[anywhere] * n,
        scratch_shapes=[pltpu.SemaphoreType.DMA((n,))],
        name="publish",
    )(*arrays)


def solution(mesh):
    rows = P(("ctx", "fsdp"), None)
    tokens = P("fsdp", "ctx", None)
    return jax.shard_map(
        body,
        mesh=mesh,
        in_specs=(tokens, rows, rows, rows, rows, P(("ctx", "fsdp")), P(), tokens),
        out_specs=(tokens, tokens, rows, rows, rows, rows, P(("ctx", "fsdp")), P()),
        check_vma=False,
    )
```

```python
import functools

import jax
import jax.numpy as jnp
from jax import lax
from jax.experimental import pallas as pl
from jax.experimental.pallas import tpu as pltpu
from jax.sharding import PartitionSpec as P

D = 2048
HQ = 24
HK = 6
HD = 64
FF = 4352
TOK = 128
SPAN = 64
N_CTX = 32

HH = HK // 2
GROUP = HQ // HK
QH = HQ // 2
QW = QH * HD
KVW = HH * 2 * HD
FH = FF // 2
KEYS = 512
SPANS_STEP = KEYS // SPAN
KEY_BLOCKS = 8
QROWS = GROUP * SPAN

EPSILON = 1e-06
ROPE_BASE = 10000.0
LOG2E = 1.4426950408889634
AT_H, AT_X, AT_Y, AT_HALF = 0, 64, 128, 192
AT_STEP_HALF, AT_STEP_BLOCK, AT_MARK, AT_EDGE, AT_LIMIT, AT_MAP = 256, 259, 262, 266, 268, 270
MESH = pl.DeviceIdType.MESH
BF = jnp.bfloat16
F32 = jnp.float32
NT = (((1,), (1,)), ((), ()))
NN = (((1,), (0,)), ((), ()))
TN = (((0,), (0,)), ((), ()))
W_DIMS = ("h", "x", "y", "l")
KV_DIMS = ("h", "x", "y")
ORDERS = (("x", "y", "z"), ("y", "z", "x"), ("z", "x", "y"))
KV_ORDERS = (("h", "x", "y"), ("x", "y", "h"), ("y", "h", "x"))
KV_PARTS = ((0, 96, ("y", "x", "h")), (96, 96, ("x", "y", "h")), (192, 64, ("h", "x", "y")))
SUMS = (
    (0, 0, 1152, ORDERS[0]),
    (1, 0, 1152, ORDERS[1]),
    (2, 0, 1152, ORDERS[2]),
    (0, 1152, 1024, ORDERS[0]),
    (1, 1152, 1024, ORDERS[1]),
    (2, 1152, 1024, ORDERS[2]),
    (3, 0, 256, ORDERS[0]),
    (3, 256, 256, ORDERS[1]),
    (3, 512, 256, ORDERS[2]),
    (4, 0, 384, ORDERS[0]),
    (4, 384, 384, ORDERS[1]),
    (4, 768, 384, ORDERS[2]),
)
N_EARLY = 9
ADVANCE = (0, 4, 0, 6, 0, 2)
SIZES = {"x": 4, "y": 4, "z": 4, "h": 2}


def here():
    c = lax.axis_index("ctx")
    f = lax.axis_index("fsdp")
    return {
        "x": lax.rem(lax.div(c, 4), 4),
        "y": lax.rem(c, 4),
        "z": lax.div(c, 16) * 2 + lax.div(f, 2),
        "h": lax.div(c, 16),
        "l": lax.div(f, 2),
        "core": lax.rem(f, 2),
    }


def device_of(x, y, z, core):
    return (lax.div(z, 2) * 16 + x * 4 + y, lax.rem(z, 2) * 2 + core)


def moved(at, axis, by):
    if axis == "core":
        return device_of(at["x"], at["y"], at["z"], 1 - at["core"])
    place = {k: at[k] for k in ("x", "y", "z")}
    if axis == "h":
        place["z"] = lax.rem(at["z"] + 2, 4)
    else:
        place[axis] = lax.rem(at[axis] + by + 4, 4)
    return device_of(place["x"], place["y"], place["z"], at["core"])


def labels(axis, value):
    if axis == "z":
        return {"h": lax.div(value, 2), "l": lax.rem(value, 2)}
    return {axis: value}


def pick(ref, dims, values, tail):
    return ref.at[tuple(values[d] if d in values else slice(None) for d in dims) + tail]


def greet(devices):
    barrier = pltpu.get_barrier_semaphore()
    for d in devices:
        pl.semaphore_signal(barrier, inc=1, device_id=d, device_id_type=MESH)
    pl.semaphore_wait(barrier, len(devices))


def send(src, dst, ssem, rsem, device):
    copy = pltpu.make_async_remote_copy(
        src_ref=src, dst_ref=dst, send_sem=ssem, recv_sem=rsem, device_id=device, device_id_type=MESH
    )
    copy.start()
    return copy


class Gathering:
    def __init__(self, ref, dims, at, order, rows, cols, ssem, rsem):
        self.ref, self.dims, self.at, self.order, self.rows, self.cols = ref, dims, at, order, rows, cols
        self.ssem, self.rsem, self.phase, self.sent = ssem, rsem, 0, []

    def block(self, coordinate, rows):
        later = {}
        for a in self.order[self.phase + 1 :]:
            later.update(labels(a, self.at[a]))
        return pick(self.ref, self.dims, {**later, **labels(self.axis, coordinate)}, (rows, self.cols))

    def send(self, n, ref, by):
        c = send(ref, ref, self.ssem.at[self.phase, n], self.rsem.at[self.phase, n], moved(self.at, self.axis, by))
        self.sent.append(c)
        return c

    def start(self):
        self.axis = self.order[self.phase]
        mine = self.block(self.at[self.axis], slice(None))
        self.first = [self.send(0, mine, 1)]
        if SIZES[self.axis] == 4:
            self.first.append(self.send(1, mine, 3))

    def pass_on(self):
        for c in self.first:
            c.wait_recv()
        self.second = []
        if SIZES[self.axis] == 4:
            half = self.rows // 2
            me = self.at[self.axis]
            self.second.append(self.send(2, self.block(lax.rem(me + 3, 4), pl.ds(0, half)), 1))
            self.second.append(self.send(3, self.block(lax.rem(me + 1, 4), pl.ds(half, half)), 3))

    def finish(self):
        for c in self.second:
            c.wait_recv()
        self.phase += 1

    def wait_sent(self):
        for c in self.sent:
            c.wait_send()


def neighbours(at, axes):
    out = []
    for a in axes:
        if a in ("core", "h"):
            out.append(moved(at, a, 1))
        else:
            out.append(moved(at, a, 1))
            out.append(moved(at, a, 3))
    return out


GATHER = (
    (0, 0, 1152, ORDERS[0]),
    (1, 0, 1152, ORDERS[1]),
    (2, 0, 1152, ORDERS[2]),
    (0, 1152, 1024, ORDERS[0]),
    (1, 1152, 1024, ORDERS[1]),
    (2, 1152, 1024, ORDERS[2]),
    (3, 0, 256, ORDERS[0]),
    (3, 256, 256, ORDERS[1]),
    (3, 512, 256, ORDERS[2]),
)


def lane_of(shape):
    return lax.broadcasted_iota(jnp.int32, shape, len(shape) - 1)


def swap_halves(v):
    return jnp.where(lax.rem(lane_of(v.shape), HD) < HD // 2, pltpu.roll(v, 96, 1), pltpu.roll(v, 32, 1))


def head_sums(v):
    low = lane_of(v.shape) < HD
    a = jnp.sum(jnp.where(low, v, 0.0), axis=1, keepdims=True)
    b = jnp.sum(jnp.where(low, 0.0, v), axis=1, keepdims=True)
    return jnp.where(low, a, b)


def tile_gain(row, is_key):
    low = lane_of(row.shape) < HD
    turned = pltpu.roll(row, HD, 1)
    return jnp.where(low, turned, 1.0) if is_key else jnp.where(low, row, turned)


def front_kernel(
    tab, shard_one, gate_up, down, out, x, dy, gains, cosine, sine,
    w_one, w_gate, w_up, w_down, w_out, x_pair, dy_pair, gain_all, joined, normed, query, kv_out, o_ref, low_ref, l_ref,
    one, kv_src, kvg, kvs, q_ref, acc, sum_ref, small_buf, psem, lsem, tssem, trsem, ossem, orsem, gssem, grsem, kssem, krsem, ksem,
):
    at = here()
    core = at["core"]
    sibling = moved(at, "core", 1)
    greet([sibling] + sum_peers(at, ("x", "y", "z")))
    own = {d: at[d] for d in W_DIMS}
    total = Total(gains[...], at, small_buf, tssem, trsem)
    remote, local = [], []

    def half_of(src, start, width, which):
        return src.at[:, pl.ds(pl.multiple_of(start + which * width, 128), width)]

    pairs = [
        (lambda c: shard_one.at[c], one),
        (lambda c: half_of(gate_up, 0, FH, c), w_gate),
        (lambda c: half_of(gate_up, FF, FH, c), w_up),
        (lambda c: half_of(down, 0, FH, c), w_down),
        (lambda c: half_of(out, 0, QW, c), w_out),
    ]
    for i, (src, ref) in enumerate(pairs):
        dst = pick(ref, W_DIMS, own, (pl.ds(core * 16, 16), slice(None)))
        remote.append(send(src(1 - core), dst, psem.at[i, 0], psem.at[i, 1], sibling))
        local.append(pltpu.make_async_copy(src(core), dst, lsem.at[i]))
        local[-1].start()
    for i, (src, ref) in ((5, (x, x_pair)), (6, (dy, dy_pair))):
        remote.append(send(src, ref.at[core], psem.at[i, 0], psem.at[i, 1], sibling))
        local.append(pltpu.make_async_copy(src, ref.at[core], lsem.at[i]))
        local[-1].start()

    def arrived(i):
        remote[i].wait_recv()
        local[i].wait()

    ones = [
        Gathering(one, W_DIMS, at, ORDERS[k], 32, pl.ds(k * 384, 384), ossem.at[k], orsem.at[k]) for k in range(3)
    ]
    rest = [
        Gathering(pairs[1 + a][1], W_DIMS, at, order, 32, pl.ds(start, width), gssem.at[k], grsem.at[k])
        for k, (a, start, width, order) in enumerate(GATHER)
    ]
    keys = [
        Gathering(kvg.at[h], KV_DIMS, at, KV_ORDERS[h], 4, slice(None), kssem.at[h], krsem.at[h]) for h in range(HH)
    ]

    def every(streams, *steps):
        for s in streams:
            for step in steps:
                getattr(s, step)()

    arrived(0)
    every(ones, "start")
    for i in range(1, 5):
        arrived(i)
    every(rest, "start")
    total.step()
    every(ones, "pass_on")
    every(rest, "pass_on")
    total.step()
    every(ones, "finish", "start")
    every(rest, "finish")
    total.step()
    every(ones, "pass_on")
    total.step()
    gain_all[...] = total.value
    every(ones, "finish", "start")
    every(rest, "start")
    arrived(5)
    gain_row = jnp.concatenate([total.value[j : j + 1] for j in range(D // 128)], axis=1)

    def norm(r, carry):
        rows = pl.ds(pl.multiple_of(r * 32, 32), 32)
        for s in range(2):
            v = x_pair[s, rows, :].astype(F32)
            inverse = lax.rsqrt(jnp.sum(v * v, axis=1, keepdims=True) * (1.0 / D) + EPSILON)
            normed[pl.ds(pl.multiple_of(s * TOK + r * 32, 32), 32), :] = (v * inverse * gain_row).astype(BF)
        return carry

    lax.fori_loop(0, TOK // 32, norm, 0)
    every(ones, "pass_on")
    every(ones, "finish")
    keep = pltpu.make_async_copy(one, w_one, lsem.at[7])
    keep.start()
    head_gains = total.value[32:33]

    def product(start, width):
        w = one[:, :, :, :, :, start : start + width].reshape(D, width)
        joined[:, start : start + width] = jnp.dot(normed[...], w, preferred_element_type=F32)

    def rope(tile, is_key):
        v = joined[:, tile * 128 : (tile + 1) * 128]
        low = lane_of(v.shape) < HD
        c, n = cosine[...], sine[...]
        inverse = lax.rsqrt(head_sums(v * v) * (1.0 / HD) + EPSILON)
        if is_key:
            inverse = jnp.where(low, inverse, 1.0)
            c, n = jnp.where(low, c, 1.0), jnp.where(low, n, 0.0)
        v = v * inverse * tile_gain(head_gains, is_key)
        return (v * c + swap_halves(v) * n).astype(BF)

    product(QW, KVW)
    for h in range(HH):
        kv_src[h] = rope(QW // 128 + h, True).reshape(4, SPAN, 2 * HD)
    kv_own = {d: at[d] for d in KV_DIMS}
    puts = [pltpu.make_async_copy(kv_src.at[h], pick(kvg.at[h], KV_DIMS, kv_own, ()), ksem.at[h]) for h in range(HH)]
    for c in puts:
        c.start()
    for c in puts:
        c.wait()
    every(keys, "start")
    every(rest, "pass_on")
    product(0, 384)
    every(keys, "pass_on")
    every(keys, "finish", "start")
    product(384, 384)
    every(keys, "pass_on")
    for t in range(QW // 128):
        query[:, t * 128 : (t + 1) * 128] = rope(t, False)
    every(keys, "finish", "start")
    blank = jnp.zeros((QROWS, HD), BF)
    for s in range(2):
        for h in range(HH):
            for half in range(2):
                q_ref[s, h, half] = jnp.concatenate([heads_at(query, s, h, half), blank], axis=1)
    every(keys, "pass_on")
    every(keys, "finish")
    every(rest[:3] + rest[6:], "finish", "start")
    every(rest[3:6], "finish")

    def sort(p, carry):
        for s in range(2):
            place = tuple(tab[s, column + p] for column in (AT_H, AT_X, AT_Y))
            half = tab[s, AT_HALF + p]
            for h in range(HH):
                kvs[s, h, lax.div(p, SPANS_STEP), lax.rem(p, SPANS_STEP)] = kvg[(h,) + place + (s * 2 + half,)]
        return carry

    lax.fori_loop(0, 2 * N_CTX, sort, 0)
    keep_keys = pltpu.make_async_copy(kvs, kv_out, ksem.at[HH])
    keep_keys.start()
    attend_heads(tab, 0, q_ref, kvs, o_ref, low_ref, l_ref, acc, sum_ref)
    every(rest[:3], "pass_on")
    attend_heads(tab, 1, q_ref, kvs, o_ref, low_ref, l_ref, acc, sum_ref)
    every(rest[6:], "pass_on")
    every(rest[:3] + rest[6:], "finish")
    keep_keys.wait()
    arrived(6)
    keep.wait()
    for c in remote + total.sent:
        c.wait_send()
    for s in ones + rest + keys:
        s.wait_sent()


def front(tab, shards, x, dy, gains, cosine, sine, cid):
    anywhere = pl.BlockSpec(memory_space=pl.ANY)
    vmem = pl.BlockSpec(memory_space=pltpu.VMEM)
    full = [jax.ShapeDtypeStruct((2, 4, 4, 2, 32, w), BF) for w in (QW + KVW, FH, FH, FH, QW)]
    n = len(GATHER)
    return pl.pallas_call(
        front_kernel,
        out_shape=full
        + [
            jax.ShapeDtypeStruct((2,) + x.shape, BF),
            jax.ShapeDtypeStruct((2,) + dy.shape, BF),
            jax.ShapeDtypeStruct(gains.shape, F32),
            jax.ShapeDtypeStruct((2 * TOK, QW + KVW), F32),
            jax.ShapeDtypeStruct((2 * TOK, D), BF),
            jax.ShapeDtypeStruct((2 * TOK, QW), BF),
            jax.ShapeDtypeStruct((2, HH, KEY_BLOCKS, SPANS_STEP, SPAN, 2 * HD), BF),
            jax.ShapeDtypeStruct((2 * TOK, QW), F32),
            jax.ShapeDtypeStruct((2 * TOK, QW), BF),
            jax.ShapeDtypeStruct((2, HH, 2, 1, QROWS), F32),
        ],
        in_specs=[pl.BlockSpec(memory_space=pltpu.SMEM)] + [anywhere] * 6 + [vmem] * 3,
        out_specs=[anywhere] * 5 + [vmem, anywhere] + [vmem] * 4 + [anywhere] + [vmem] * 3,
        scratch_shapes=[
            pltpu.VMEM((2, 4, 4, 2, 32, QW + KVW), BF),
            pltpu.VMEM((HH, 4, SPAN, 2 * HD), BF),
            pltpu.VMEM((HH, 2, 4, 4, 4, SPAN, 2 * HD), BF),
            pltpu.VMEM((2, HH, KEY_BLOCKS, SPANS_STEP, SPAN, 2 * HD), BF),
            pltpu.VMEM((2, HH, 2, QROWS, 2 * HD), BF),
            pltpu.VMEM((2, 2 * HD, QROWS), F32),
            pltpu.VMEM((2, 1, QROWS), F32),
            pltpu.VMEM((4, 4) + gains.shape, F32),
            pltpu.SemaphoreType.DMA((7, 2)),
            pltpu.SemaphoreType.DMA((8,)),
            pltpu.SemaphoreType.DMA((4, 4)),
            pltpu.SemaphoreType.DMA((4, 4)),
            pltpu.SemaphoreType.DMA((3, 3, 4)),
            pltpu.SemaphoreType.DMA((3, 3, 4)),
            pltpu.SemaphoreType.DMA((n, 3, 4)),
            pltpu.SemaphoreType.DMA((n, 3, 4)),
            pltpu.SemaphoreType.DMA((HH, 3, 4)),
            pltpu.SemaphoreType.DMA((HH, 3, 4)),
            pltpu.SemaphoreType.DMA((HH + 1,)),
        ],
        compiler_params=pltpu.CompilerParams(
            collective_id=cid, has_side_effects=True, vmem_limit_bytes=60 * 1024 * 1024
        ),
        name="front",
    )(tab, *shards, x, dy, gains, cosine, sine)


def lead_shape(dims):
    full = {"h": 2, "x": 4, "y": 4, "l": 2}
    return tuple(full[d] for d in dims)


def without(dims, axis):
    gone = ("h", "l") if axis == "z" else (axis,)
    return tuple(d for d in dims if d not in gone)


class Summing:
    def __init__(self, source, dims, at, order, rows, cols, buffers, ssem, rsem, lsem, begun=None, base=None):
        self.ref, self.dims, self.at, self.order, self.begun = source, dims, at, order, begun
        self.cols, self.buffers, self.rows = cols, buffers, rows
        self.ssem, self.rsem, self.lsem = ssem, rsem, lsem
        self.phase, self.sent, self.base = 0, [], base
        self.resident = base is not None

    def part(self, coordinate, start, length):
        rows = pl.ds(start + (self.base or 0), length)
        return pick(self.ref, self.dims, labels(self.axis, coordinate), (rows, self.cols))

    def send(self, n, src, dst, by):
        c = send(src, dst, self.ssem.at[self.phase, n], self.rsem.at[self.phase, n], moved(self.at, self.axis, by))
        self.sent.append(c)
        return c

    def start(self):
        self.axis = self.order[self.phase]
        self.rest = without(self.dims, self.axis)
        self.lead = lead_shape(self.rest)
        half = self.rows // 2
        first, second, every = (0, half), (half, half), (0, self.rows)
        i = self.at[self.axis]
        buf = self.buffers[self.phase]
        self.local = []
        if SIZES[self.axis] == 2:
            self.direct = (self.send(0, self.part(1 - i, *every), buf["got"].at[0], 1),)
        else:
            up, down, far = lax.rem(i + 1, 4), lax.rem(i + 3, 4), lax.rem(i + 2, 4)
            self.near = (up, down)
        if self.phase == 0 and self.begun is not None:
            self.relay, self.direct = (), ()
        elif SIZES[self.axis] == 4:
            self.relay = (
                self.send(0, self.part(far, *first), buf["relay"].at[0], 1),
                self.send(1, self.part(far, *second), buf["relay"].at[1], 3),
            )
            self.direct = (
                self.send(2, self.part(up, *second), buf["got"].at[1, 1], 1),
                self.send(3, self.part(down, *first), buf["got"].at[0, 1], 3),
            )
        if self.phase == 0 and not self.resident:
            todo = [(self.part(i, *every), buf["mine"])]
            if self.begun is not None:
                passed, direct = self.begun[1], self.begun[0]
                todo += [(passed.at[n], buf["got"].at[n, 0]) for n in range(2)]
                todo += [(direct.at[n], buf["got"].at[n, 1]) for n in range(2)]
            elif SIZES[self.axis] == 4:
                todo.append((self.part(up, *first), buf["own"].at[0]))
                todo.append((self.part(down, *second), buf["own"].at[1]))
            for n, (src, dst) in enumerate(todo):
                c = pltpu.make_async_copy(src, dst, self.lsem.at[n])
                c.start()
                self.local.append(c)

    def over_lead(self, add):
        rest = self.lead[1:]
        spots = [()]
        for n in rest:
            spots = [s + (j,) for s in spots for j in range(n)]
        if not self.lead:
            add(())
            return

        def go(j, carry):
            for s in spots:
                add((j,) + s)
            return carry

        lax.fori_loop(0, self.lead[0], go, 0)

    def pass_on(self):
        if SIZES[self.axis] == 2 or (self.phase == 0 and self.begun is not None):
            return
        buf = self.buffers[self.phase]
        half = self.rows // 2
        for n, by in ((0, 1), (1, 3)):
            self.relay[n].wait_recv()
            if self.phase == 0 and not self.resident:
                self.local[1 + n].wait()
                own = buf["own"].at[n]
            else:
                own = self.part(self.near[n], n * half, half)

            def add(spot):
                here_ = spot + (slice(None), slice(None))
                both = buf["relay"][(n,) + here_].astype(F32) + own[here_].astype(F32)
                buf["relay"][(n,) + here_] = both.astype(BF)

            self.over_lead(add)
            c = self.send(4 + n, buf["relay"].at[n], buf["got"].at[n, 0], by)
            self.direct = self.direct + (c,)

    def finish(self):
        buf = self.buffers[self.phase]
        half = self.rows // 2
        if self.local:
            self.local[0].wait()
        if self.begun is not None:
            for c in self.local[1:]:
                c.wait()
        for c in self.direct:
            c.wait_recv()
        copied = self.phase == 0 and not self.resident
        own = buf["mine"] if copied else self.part(self.at[self.axis], 0, self.rows)
        out = buf["mine"] if copied else buf["sum"]

        def add(spot):
            if SIZES[self.axis] == 2:
                here_ = spot + (slice(None), slice(None))
                out[here_] = (own[here_].astype(F32) + buf["got"][(0,) + here_].astype(F32)).astype(out.dtype)
                return
            for n in range(2):
                rows = spot + (pl.ds(n * half, half), slice(None))
                all_ = spot + (slice(None), slice(None))
                total = own[rows].astype(F32) + buf["got"][(n, 0) + all_].astype(F32)
                total = total + buf["got"][(n, 1) + all_].astype(F32)
                out[rows] = total.astype(out.dtype)

        self.over_lead(add)
        self.ref, self.dims, self.cols = out, self.rest, slice(None)
        self.phase += 1
        self.base = 0


class Total:
    def __init__(self, value, at, buf, ssem, rsem):
        self.value, self.at, self.buf, self.ssem, self.rsem = value, at, buf, ssem, rsem
        self.phase, self.sent = 0, []
        self.start()

    def start(self):
        n, axis = self.phase, ("core", "z", "y", "x")[self.phase]
        self.buf[n, 0] = self.value
        self.copies = []
        for i in (1, 3, 2) if axis != "core" else (1,):
            self.copies.append(
                send(self.buf.at[n, 0], self.buf.at[n, i], self.ssem.at[n, i], self.rsem.at[n, i], moved(self.at, axis, i))
            )

    def step(self):
        n, buf = self.phase, self.buf
        if n == 4:
            return
        for c in self.copies:
            c.wait_recv()
            self.sent.append(c)
        if n == 0:
            self.value = buf[n, 0] + buf[n, 1]
        else:
            self.value = (buf[n, 0] + buf[n, 2]) + (buf[n, 1] + buf[n, 3])
        self.phase += 1
        if self.phase < 4:
            self.start()


def run_sums(streams, total):
    todo = []
    for s in streams:
        if s.begun is None:
            s.start()
    for s in streams:
        if s.begun is not None:
            s.start()
        steps = [("pass_on",), ("finish", "start"), ("pass_on",), ("finish", "start"), ("pass_on",), ("finish",)]
        todo.append(steps[1:] if s.begun is not None else steps)
    while any(todo):
        for s, steps in zip(streams, todo):
            if steps:
                for name in steps.pop(0):
                    getattr(s, name)()
        total.step()
    for s in streams:
        for c in s.sent:
            c.wait_send()


def sum_scratch(order, dims, rows, width, begun=False, resident=False):
    buffers = []
    for phase, axis in enumerate(order):
        rest = without(dims, axis)
        lead = lead_shape(rest)
        buf = {}
        if SIZES[axis] == 2:
            buf["got"] = pltpu.VMEM((1,) + lead + (rows, width), BF)
        else:
            buf["got"] = pltpu.VMEM((2, 2) + lead + (rows // 2, width), BF)
            if phase or not begun:
                buf["relay"] = pltpu.VMEM((2,) + lead + (rows // 2, width), BF)
        if phase == 0 and not resident:
            buf["mine"] = pltpu.VMEM(lead + (rows, width), BF)
            if SIZES[axis] == 4 and not begun:
                buf["own"] = pltpu.VMEM((2,) + lead + (rows // 2, width), BF)
        else:
            buf["sum"] = pltpu.VMEM(lead + (rows, width), BF if phase < 2 else F32)
        buffers.append(buf)
        dims = rest
    return buffers


def weight_sum_kernel(pieces, n, *refs):
    ins, small, begun, refs = refs[:n], refs[n], refs[n + 1 : n + 1 + 2 * N_EARLY], refs[n + 1 + 2 * N_EARLY :]
    outs, small_out = refs[: n - 1], refs[n - 1]
    buffers, stages, swapped, halves, small_buf, ssem, rsem, lsem, csem, tssem, trsem = refs[n:]
    at = here()
    core = at["core"]
    sibling = moved(at, "core", 1)
    greet([sibling] + sum_peers(at, ("x", "y", "z")))
    streams = [
        Summing(
            ins[a], W_DIMS, at, order, 32, pl.ds(start, width), buffers[k], ssem.at[k], rsem.at[k], lsem.at[k],
            (begun[2 * k], begun[2 * k + 1]) if k < N_EARLY else None,
        )
        for k, (a, start, width, order) in enumerate(pieces)
    ]
    total = Total(small[...], at, small_buf, tssem, trsem)
    run_sums(streams, total)
    small_out[...] = total.value
    for k, (a, start, width, order) in enumerate(pieces):
        stages[a][:, start : start + width] = buffers[k][2]["sum"][...]
    other = pl.ds(pl.multiple_of((1 - core) * 16, 16), 16)
    own = pl.ds(pl.multiple_of(core * 16, 16), 16)
    copies = [send(stages[a].at[other], swapped[a], csem.at[a, 0], csem.at[a, 1], sibling) for a in range(n)]

    def put(a, half, value):
        width = value.shape[1]
        if a == 4:
            outs[3][:, pl.ds(pl.multiple_of(half * QW, 128), QW)] = value[:, :QW]
            halves[half] = value[:, QW:]
            return
        ref, start = ((outs[0], 0), (outs[0], FF), (outs[1], 0), (outs[2], 0))[a]
        ref[:, pl.ds(pl.multiple_of(start + half * width, 128), width)] = value

    for a in range(n):
        put(a, core, stages[a][own, :])
    for a in range(n):
        copies[a].wait_recv()
        put(a, 1 - core, swapped[a][...])
    for kind in range(2):
        at_ = [half_kv[:, (2 * h + kind) * HD : (2 * h + kind + 1) * HD] for half_kv in (halves[0], halves[1]) for h in range(HH)]
        start = HQ * HD + kind * HK * HD
        outs[3][:, start : start + HK * HD] = jnp.concatenate(at_, axis=1)
    for c in copies + total.sent:
        c.wait_send()


def sum_weights(grads, small, begun, pieces, cid, limit):
    n, count = len(grads), len(pieces)
    anywhere = pl.BlockSpec(memory_space=pl.ANY)
    vmem = pl.BlockSpec(memory_space=pltpu.VMEM)
    widths = [g.shape[-1] for g in grads]
    return pl.pallas_call(
        functools.partial(weight_sum_kernel, pieces, n),
        out_shape=[jax.ShapeDtypeStruct((16, w), F32) for w in (2 * FF, FF, HQ * HD, (HQ + 2 * HK) * HD)]
        + [jax.ShapeDtypeStruct(small.shape, F32)],
        in_specs=[anywhere] * n + [vmem] + [anywhere] * len(begun),
        out_specs=[vmem] * n,
        scratch_shapes=[
            [sum_scratch(order, W_DIMS, 32, width, k < N_EARLY) for k, (a, start, width, order) in enumerate(pieces)],
            [pltpu.VMEM((32, w), F32) for w in widths],
            [pltpu.VMEM((16, w), F32) for w in widths],
            pltpu.VMEM((2, 16, KVW), F32),
            pltpu.VMEM((4, 4) + small.shape, F32),
            pltpu.SemaphoreType.DMA((count, 3, 6)),
            pltpu.SemaphoreType.DMA((count, 3, 6)),
            pltpu.SemaphoreType.DMA((count, 6)),
            pltpu.SemaphoreType.DMA((n, 2)),
            pltpu.SemaphoreType.DMA((4, 4)),
            pltpu.SemaphoreType.DMA((4, 4)),
        ],
        compiler_params=pltpu.CompilerParams(collective_id=cid, has_side_effects=True, vmem_limit_bytes=limit),
        name="sum_weights",
    )(*grads, small, *begun)


def sum_peers(at, axes):
    out = []
    for a in axes:
        for i in (1, 3, 2) if SIZES[a] == 4 else (1,):
            out.append(moved(at, a, i))
    return out


def heads_at(ref, s, h, half):
    rows = slice(s * TOK + half * SPAN, s * TOK + (half + 1) * SPAN)
    return jnp.concatenate([ref[rows, (h * GROUP + g) * HD : (h * GROUP + g + 1) * HD] for g in range(GROUP)], axis=0)


def put_heads(ref, s, h, half, value):
    rows = pl.ds(pl.multiple_of(s * TOK + half * SPAN, SPAN), SPAN)
    for g in range(0, GROUP, 2):
        both = jnp.concatenate([value[g * SPAN : (g + 1) * SPAN], value[(g + 1) * SPAN : (g + 2) * SPAN]], axis=1)
        ref[rows, pl.ds(pl.multiple_of((h * GROUP + g) * HD, 2 * HD), 2 * HD)] = both.astype(ref.dtype)


def masked(prob, limit):
    if limit is None:
        return prob
    row = lax.broadcasted_iota(jnp.int32, prob.shape, 0)
    col = lax.rem(lax.broadcasted_iota(jnp.int32, prob.shape, 1), SPAN)
    return jnp.where(row <= col + limit, prob, 0.0)


def attend_heads(tab, s, q_ref, kvs, o_ref, low_ref, l_ref, acc, total):
    rate = LOG2E * HD**-0.5

    def head(h, carry):
        acc[...] = jnp.zeros_like(acc)
        total[...] = jnp.zeros_like(total)

        def scored(half, block, limit):
            keys = kvs[s, h, block].reshape(KEYS, 2 * HD)
            scores = lax.dot_general(keys, q_ref[s, h, half], NT, preferred_element_type=F32)
            prob = masked(jnp.exp2(scores * rate), limit)
            return (
                jnp.sum(prob, axis=0, keepdims=True),
                lax.dot_general(keys, prob.astype(BF), TN, preferred_element_type=F32),
            )

        def high(k, c):
            t, o = scored(1, k, None)
            total[1] += t
            acc[1] += o
            return c

        def either(k, c):
            half = tab[s, AT_STEP_HALF + k]
            t, o = scored(half, tab[s, AT_STEP_BLOCK + k], None)
            up = half.astype(F32)
            total[0] += t * (1.0 - up)
            total[1] += t * up
            acc[0] += o * (1.0 - up)
            acc[1] += o * up
            return c

        lax.fori_loop(0, 4, high, 0)
        lax.fori_loop(0, 3, either, 0)
        for half in range(2):
            t, o = scored(half, tab[s, AT_EDGE + half], tab[s, AT_LIMIT + half])
            t, o = total[half] + t, acc[half] + o
            out = (o[HD:, :] / t).T
            put_heads(o_ref, s, h, half, out)
            put_heads(low_ref, s, h, half, out)
            l_ref[s, h, half] = jnp.log2(t)
        return carry

    lax.fori_loop(0, HH, head, 0)


class Early:
    def __init__(self, source, at, order, cols, width, relay, direct, passed, ssem, rsem):
        self.source, self.at, self.axis, self.cols, self.width = source, at, order[0], cols, width
        self.relay, self.passed, self.ssem, self.rsem, self.views = relay, passed, ssem, rsem, {}
        i = at[self.axis]
        self.near = (lax.rem(i + 1, 4), lax.rem(i + 3, 4))
        far = lax.rem(i + 2, 4)
        plan = (
            (far, 0, relay, 0, 1),
            (far, 1, relay, 1, 3),
            (self.near[0], 1, direct, 1, 1),
            (self.near[1], 0, direct, 0, 3),
        )
        self.copies = []
        for n, (coordinate, half, dst, slot, by) in enumerate(plan):
            self.copies.append(self.send(n, self.part(coordinate, half), dst.at[slot], by))

    def part(self, coordinate, half):
        return pick(self.source, W_DIMS, labels(self.axis, coordinate), (pl.ds(half * 16, 16), self.cols))

    def send(self, n, src, dst, by):
        return send(src, dst, self.ssem.at[n], self.rsem.at[n], moved(self.at, self.axis, by))

    def load(self, n, own, sem):
        lead = lead_shape(without(W_DIMS, self.axis))
        view = own.at[(slice(None),) * (len(lead) + 1) + (pl.ds(0, self.width),)]
        self.views[n] = view
        copy = pltpu.make_async_copy(self.part(self.near[n], n), view, sem)
        copy.start()
        return copy

    def add(self, n):
        self.copies[n].wait_recv()
        came, own = self.relay.at[n], self.views[n]
        lead = lead_shape(without(W_DIMS, self.axis))
        spots = [()]
        for size in lead[1:]:
            spots = [s + (j,) for s in spots for j in range(size)]

        def go(j, carry):
            for s in spots:
                at = (j,) + s + (slice(None), slice(None))
                came[at] = (came[at].astype(F32) + own[at].astype(F32)).astype(BF)
            return carry

        lax.fori_loop(0, lead[0], go, 0)
        self.copies.append(self.send(4 + n, came, self.passed.at[n], 1 if n == 0 else 3))

    def wait(self):
        for c in self.copies[2:]:
            c.wait_recv()


def early_shapes():
    shapes = []
    for a, start, width, order in SUMS[:N_EARLY]:
        lead = lead_shape(without(W_DIMS, order[0]))
        shapes += [jax.ShapeDtypeStruct((2,) + lead + (16, width), BF)] * 2
    return shapes


def attend_back_kernel(*refs):
    tab, qr, da, attn, attn_low, l_ref, kv_sorted, normed, dy, low_mid, hid, dgate, dup = refs[:13]
    joined, normed_one, w_one, gains, cosine, sine, grad_mid, own_x = refs[13:21]
    input_grad, terms, head_terms = refs[21:24]
    grads, refs = refs[24:29], refs[29:]
    begun, refs = refs[: 2 * N_EARLY], refs[2 * N_EARLY :]
    held, qd_ref, delta_ref, stage, acc, dq_acc, dq_ref, buffers, refs = refs[:8] + (refs[8:],)
    tiles, mix, mix_z, relays, w_ref, d_joined, part, got = refs[:8]
    essem, ersem, ssem, rsem, sems, tsem, msem, psem = refs[8:]
    at = here()
    core = at["core"]
    sibling = moved(at, "core", 1)
    def load_keys(h):
        return [pltpu.make_async_copy(kv_sorted.at[s, h], held[h % 2].at[s], sems.at[s, h]) for s in range(2)]

    for c in load_keys(0):
        c.start()

    def load_w(start, width):
        src = w_one.at[:, :, :, :, :, pl.ds(start, width)]
        return pltpu.make_async_copy(src, w_ref.at[:, :, :, :, :, pl.ds(0, width)], psem.at[0])

    load_w(0, QW).start()
    greet([sibling] + neighbours(at, ("x", "y", "z", "h")))
    sides = ((normed, dgate), (normed, dup), (dy, hid), (low_mid, attn_low), (normed_one, d_joined))

    def tile_copy(n, i, slot, parity):
        a, start, width = n
        half = lax.rem(i, 2)
        return pltpu.make_async_copy(
            tiles.at[parity, slot, :, :, :, :, pl.ds(0, width)],
            grads[a].at[lax.div(i, 2), pl.ds(half * 2, 2), :, :, :, pl.ds(start, width)],
            tsem.at[parity, slot],
        )

    def outer(n, parity):
        a, start, width = n
        left, right = sides[a]

        def go(i, carry):
            slot = lax.rem(i, 2)

            @pl.when(i > 1)
            def _():
                tile_copy(n, i, slot, parity).wait()

            rows = pl.ds(pl.multiple_of(i * 512, 512), 512)
            value = lax.dot_general(left[:, rows], right[:, start : start + width], TN, preferred_element_type=F32)
            tiles[parity, slot, :, :, :, :, :width] = value.astype(BF).reshape(2, 4, 2, 32, width)
            tile_copy(n, i, slot, parity).start()
            return carry

        lax.fori_loop(0, 4, go, 0)

    def drain(n, parity):
        for slot in range(2):
            tile_copy(n, slot, slot, parity).wait()

    early = []

    def begin(k):
        a, start, width, order = SUMS[k]
        drain((a, start, width), k % 2)
        early.append(
            Early(
                grads[a], at, order, pl.ds(start, width), width, relays[k], begun[2 * k], begun[2 * k + 1],
                essem.at[k], ersem.at[k],
            )
        )

    for k in range(N_EARLY):
        outer(SUMS[k][:3], k % 2)
        if k:
            begin(k - 1)
    rate = LOG2E * HD**-0.5
    factor = jnp.where(lax.broadcasted_iota(jnp.int32, (1, 2 * HD), 1) < HD, HD**-0.5, 1.0)
    blank = jnp.zeros((QROWS, HD), BF)
    for s in range(2):
        for h in range(HH):
            for half in range(2):
                up = heads_at(da, s, h, half)
                qd_ref[s, h, half, :QROWS] = jnp.concatenate([heads_at(qr, s, h, half), blank], axis=1)
                qd_ref[s, h, half, QROWS:] = jnp.concatenate([blank, up], axis=1)
                inner = (up.astype(F32) * heads_at(attn, s, h, half)).T
                delta_ref[s, h, half] = jnp.sum(inner, axis=0, keepdims=True)
    begin(N_EARLY - 1)
    streams = [
        [
            Summing(
                stage.at[h], KV_DIMS, at, order, rows, slice(None), buffers[h][j],
                ssem.at[h, j], rsem.at[h, j], None, None, start,
            )
            for j, (start, rows, order) in enumerate(KV_PARTS)
        ]
        for h in range(HH)
    ]
    todo = [[("pass_on",), ("finish", "start"), ("pass_on",), ("finish", "start"), ("pass_on",), ("finish",)] for h in range(HH)]

    def move(h):
        for name_of in todo[h].pop(0) if todo[h] else ():
            for st in streams[h]:
                getattr(st, name_of)()

    units = [(k, n) for k in range(N_EARLY) for n in range(2)]
    used, flying, ahead = {}, [], [0]

    def fetch():
        k, n = units[ahead[0]]
        pool, slots, first = (mix_z, 2, 2) if early[k].axis == "z" else (mix, 2, 0)
        slot = used.get(first, 0) % slots
        used[first] = used.get(first, 0) + 1
        flying.append((k, n, early[k].load(n, pool.at[slot], msem.at[first + slot])))
        ahead[0] += 1

    def advance(count):
        for _ in range(count):
            while ahead[0] < len(units) and len(flying) < 2:
                fetch()
            if flying:
                k, n, copy = flying.pop(0)
                copy.wait()
                early[k].add(n)

    for h in range(HH):
        for c in load_keys(h):
            c.wait()
        if h + 1 < HH:
            for c in load_keys(h + 1):
                c.start()
        kvs = held[h % 2]

        def sequence(s, carry, h=h, kvs=kvs):
            dq_acc[...] = jnp.zeros_like(dq_acc)
            acc[...] = jnp.zeros_like(acc)

            def backward(half, block, limit):
                keys = kvs[s, block].reshape(KEYS, 2 * HD)
                both = lax.dot_general(keys, qd_ref[s, h, half], NT, preferred_element_type=F32)
                prob = masked(jnp.exp2(both[:, :QROWS] * rate - l_ref[s, h, half]), limit)
                grad = (prob * (both[:, QROWS:] - delta_ref[s, h, half])).astype(BF)
                pair = jnp.concatenate([grad, prob.astype(BF)], axis=1)
                kv = lax.dot_general(pair, qd_ref[s, h, half], NN, preferred_element_type=F32)
                return (
                    kv.reshape(SPANS_STEP, SPAN, 2 * HD),
                    lax.dot_general(keys, grad, TN, preferred_element_type=F32),
                )

            def spans(block):
                return pl.ds(block * SPANS_STEP, SPANS_STEP)

            def high(k, c):
                kv, q = backward(1, k, None)
                acc[spans(k)] += kv
                dq_acc[1] += q
                return c

            def either(k, c):
                half = tab[s, AT_STEP_HALF + k]
                kv, q = backward(half, tab[s, AT_STEP_BLOCK + k], None)
                up = half.astype(F32)
                acc[spans(k)] += kv * (1.0 - up)
                acc[spans(6 - k)] += kv * up
                dq_acc[0] += q * (1.0 - up)
                dq_acc[1] += q * up
                return c

            lax.fori_loop(0, 4, high, 0)
            lax.fori_loop(0, 3, either, 0)
            for half in range(2):
                kv, q = backward(half, tab[s, AT_EDGE + half], tab[s, AT_LIMIT + half])
                for k in range(4):
                    acc[spans(k if half == 0 else 7 - k)] += kv * tab[s, AT_MARK + k].astype(F32)
                q = dq_acc[half] + q
                put_heads(dq_ref, s, h, half, (q[:HD, :] * HD**-0.5).T)

            def put(j, c):
                for half in range(2):
                    v = acc[tab[s, AT_MAP + half * N_CTX + j]] * factor
                    rows = pl.ds(pl.multiple_of(s * TOK + half * SPAN, SPAN), SPAN)
                    stage[h, lax.div(j, 16), lax.rem(lax.div(j, 4), 4), lax.rem(j, 4), rows, :] = v.astype(BF)
                return c

            lax.fori_loop(0, N_CTX, put, 0)
            return carry

        for s in range(2):
            sequence(s, 0)
            if s == 1:
                for k in range(h):
                    move(k)
                for st in streams[h]:
                    st.start()
            advance(ADVANCE[2 * h + s])

    head_gains = gains[32:33]

    def tile(t, is_key, grad):
        v = joined[:, t * 128 : (t + 1) * 128]
        low = lane_of(v.shape) < HD
        back = grad * cosine[...] - swap_halves(grad) * sine[...]
        inverse = lax.rsqrt(head_sums(v * v) * (1.0 / HD) + EPSILON)
        scaled = back * tile_gain(head_gains, is_key)
        inner = head_sums(scaled * v) * (1.0 / HD)
        result = inverse * scaled - v * (inverse * inverse * inverse) * inner
        if is_key:
            result = jnp.where(low, result, grad)
        d_joined[:, t * 128 : (t + 1) * 128] = result.astype(BF)
        return jnp.sum(back * v * inverse, axis=0, keepdims=True)

    def undo_queries():
        return sum(tile(t, False, dq_ref[:, t * 128 : (t + 1) * 128]) for t in range(QW // 128))

    def back_part(c, start, width):
        w = w_ref[c, :, :, :, :, :width].reshape(D // 2, width)
        return lax.dot_general(d_joined[:, start : start + width], w, NT, preferred_element_type=F32)

    def queries_back():
        load_w(0, QW).wait()
        for c in range(2):
            part[c] = back_part(c, 0, QW)
        load_w(QW, KVW).start()

    q_terms = undo_queries()
    tasks = [queries_back, lambda: outer((4, 0, QW), 0)]
    while any(todo):
        for h in range(HH):
            move(h)
        if tasks:
            tasks.pop(0)()
        advance(1)
    k_terms = 0.0
    for h in range(HH):
        grad = jnp.concatenate([buffers[h][j][2]["sum"][...] for j in range(len(KV_PARTS))], axis=0)
        k_terms = k_terms + tile(QW // 128 + h, True, grad)
    q_terms = q_terms + pltpu.roll(q_terms, HD, 1)
    head_terms[...] = jnp.where(lane_of(q_terms.shape) < HD, q_terms, pltpu.roll(k_terms, HD, 1))
    other = pl.ds(pl.multiple_of((1 - core) * TOK, TOK), TOK)
    load_w(QW, KVW).wait()
    swaps = []
    for c in range(2):
        part[c] += back_part(c, QW, KVW)
        swaps.append(send(part.at[c, other], got.at[c], psem.at[1 + c], psem.at[3 + c], sibling))
    advance(2)
    outer((4, QW, KVW), 1)
    advance(2)
    gain_row = jnp.concatenate([gains[j : j + 1] for j in range(D // 128)], axis=1)
    for c in swaps:
        c.wait_recv()

    def last(r, carry):
        rows = rows_at(r)
        own = pl.ds(pl.multiple_of(core * TOK + r * 32, 32), 32)
        e = jnp.concatenate([part[c, own, :] + got[c, rows, :] for c in range(2)], axis=1)
        v = own_x[rows, :].astype(F32)
        inverse = lax.rsqrt(jnp.sum(v * v, axis=1, keepdims=True) * (1.0 / D) + EPSILON)
        scaled = e * gain_row
        inner = jnp.sum(scaled * v, axis=1, keepdims=True) * (1.0 / D)
        total = grad_mid[rows, :] + inverse * scaled - v * (inverse * inverse * inverse) * inner
        input_grad[rows, :] = total.astype(BF)
        return carry + jnp.sum(e * v * inverse, axis=0, keepdims=True)

    terms[...] = lax.fori_loop(0, TOK // 32, last, jnp.zeros((1, D), F32))
    advance(len(units))
    drain((4, 0, QW), 0)
    drain((4, QW, KVW), 1)
    for e in early:
        e.wait()
    pending = [c for e in early for c in e.copies] + swaps + [c for group in streams for st in group for c in st.sent]
    for c in pending:
        c.wait_send()


def attend_back(operands, cid):
    vmem = pl.BlockSpec(memory_space=pltpu.VMEM)
    anywhere = pl.BlockSpec(memory_space=pl.ANY)
    tokens = 2 * TOK
    widths = (FH, FH, FH, QW, QW + KVW)
    out = pl.pallas_call(
        attend_back_kernel,
        out_shape=[
            jax.ShapeDtypeStruct((TOK, D), BF),
            jax.ShapeDtypeStruct((1, D), F32),
            jax.ShapeDtypeStruct((1, 128), F32),
        ]
        + [jax.ShapeDtypeStruct((2, 4, 4, 2, 32, w), BF) for w in widths]
        + early_shapes(),
        in_specs=[pl.BlockSpec(memory_space=pltpu.SMEM)]
        + [vmem] * 5
        + [anywhere]
        + [vmem] * 8
        + [anywhere]
        + [vmem] * 5,
        out_specs=[vmem] * 3 + [anywhere] * (5 + 2 * N_EARLY),
        scratch_shapes=[
            [pltpu.VMEM((2, KEY_BLOCKS, SPANS_STEP, SPAN, 2 * HD), BF)] * 2,
            pltpu.VMEM((2, HH, 2, 2 * QROWS, 2 * HD), BF),
            pltpu.VMEM((2, HH, 2, 1, QROWS), F32),
            pltpu.VMEM((HH, 2, 4, 4, tokens, 2 * HD), BF),
            pltpu.VMEM((2 * N_CTX, SPAN, 2 * HD), F32),
            pltpu.VMEM((2, 2 * HD, QROWS), F32),
            pltpu.VMEM((tokens, QW), F32),
            [
                [sum_scratch(order, KV_DIMS, rows, 2 * HD, False, True) for start, rows, order in KV_PARTS]
                for h in range(HH)
            ],
            pltpu.VMEM((2, 2, 2, 4, 2, 32, 1152), BF),
            pltpu.VMEM((2, 2, 4, 2, 16, 1152), BF),
            pltpu.VMEM((2, 4, 4, 16, 1152), BF),
            [
                pltpu.VMEM((2,) + lead_shape(without(W_DIMS, order[0])) + (16, width), BF)
                for a, start, width, order in SUMS[:N_EARLY]
            ],
            pltpu.VMEM((2, 4, 4, 2, 32, QW), BF),
            pltpu.VMEM((tokens, QW + KVW), BF),
            pltpu.VMEM((2, tokens, D // 2), F32),
            pltpu.VMEM((2, TOK, D // 2), F32),
            pltpu.SemaphoreType.DMA((N_EARLY, 6)),
            pltpu.SemaphoreType.DMA((N_EARLY, 6)),
            pltpu.SemaphoreType.DMA((HH, 3, 3, 6)),
            pltpu.SemaphoreType.DMA((HH, 3, 3, 6)),
            pltpu.SemaphoreType.DMA((2, HH)),
            pltpu.SemaphoreType.DMA((2, 2)),
            pltpu.SemaphoreType.DMA((5,)),
            pltpu.SemaphoreType.DMA((5,)),
        ],
        compiler_params=pltpu.CompilerParams(
            collective_id=cid, has_side_effects=True, vmem_limit_bytes=63 * 1024 * 1024
        ),
        name="attend_back",
    )(*operands)
    return out[0], out[1], out[2], out[3:8], out[8:]


FIRST = ((0, 768), (768, 384))
SECOND = ((1152, 1024),)


def rows_at(r, n=32):
    return pl.ds(pl.multiple_of(r * n, n), n)


def feed_kernel(
    attn, x, dy, gains, wo_h, wg_h, wu_h, wd_h,
    result, grad_mid, grad_attn, normed, hid, dgate, dup, low_mid, stats, terms,
    wo, wg, wu, wd, mid, part, got, part_f, got_f, back_ref, wsem, psem, gssem, grsem,
):
    at = here()
    core = at["core"]
    sibling = moved(at, "core", 1)
    late_cols = pl.ds(1152, 1024)
    weights = ((wg_h, wg), (wu_h, wu), (wd_h, wd))
    quarters, loads = [], []
    for k, (src, dst) in enumerate(weights):
        held = labels(ORDERS[k][2], at[ORDERS[k][2]])
        tail = (slice(None), late_cols)
        quarters.append(
            pltpu.make_async_copy(pick(src, W_DIMS, held, tail), pick(dst, W_DIMS, held, tail), wsem.at[4 + k])
        )
        quarters[-1].start()
    whole = (slice(None),) * 5
    for i, (src, dst) in enumerate(((wo_h, wo), (wd_h, wd), (wg_h, wg), (wu_h, wu))):
        cols = whole + (pl.ds(0, QW if i == 0 else 1152),)
        loads.append(pltpu.make_async_copy(src.at[cols], dst.at[cols], wsem.at[i]))
        loads[-1].start()
    greet([sibling] + neighbours(at, ("x", "y", "z")))
    gathers = []
    for k, (src, dst) in enumerate(weights):
        quarters[k].wait()
        g = Gathering(dst, W_DIMS, at, ORDERS[k], 32, late_cols, gssem.at[k], grsem.at[k])
        g.phase = 2
        g.start()
        gathers.append(g)

    def columns(ref, start, width):
        return ref[:, :, :, :, :, start : start + width].reshape(D, width)

    def half_rows(ref, c, start, width):
        return ref[c, :, :, :, :, start : start + width].reshape(D // 2, width)

    gain_row = jnp.concatenate([gains[16 + j : 17 + j] for j in range(D // 128)], axis=1)
    sent = []
    loads[0].wait()
    for c in range(2):
        part[0, c] = lax.dot_general(attn[...], half_rows(wo, c, 0, QW), NT, preferred_element_type=F32)
        sent.append(send(part.at[0, c], got.at[0, c], psem.at[c, 0], psem.at[c, 1], sibling))
    loads[1].wait()

    def product(out, left, right, pieces):
        for start, width in pieces:
            out[:, start : start + width] = jnp.dot(left[...], columns(right, start, width), preferred_element_type=F32)

    product(back_ref, dy, wd, FIRST)
    for c in sent:
        c.wait_recv()

    def root(v):
        return jnp.sum(jnp.sqrt(jnp.sum(v * v, axis=1, keepdims=True) * (1.0 / D)), axis=0, keepdims=True)

    def middle(r, carry):
        rows = rows_at(r)
        branch = jnp.concatenate([part[0, c, rows, :] + got[0, c, rows, :] for c in range(2)], axis=1)
        v = x[rows, :].astype(F32)
        m = v + branch
        mid[rows, :] = m
        inverse = lax.rsqrt(jnp.sum(m * m, axis=1, keepdims=True) * (1.0 / D) + EPSILON)
        normed[rows, :] = (m * inverse * gain_row).astype(BF)
        own = jnp.where(lax.div(r, TOK // 32) == core, 1.0, 0.0)
        return tuple(t + own * root(u) for t, u in zip(carry, (v, branch, m)))

    zero = jnp.zeros((1, 1), F32)
    roots = lax.fori_loop(0, 2 * TOK // 32, middle, (zero, zero, zero))
    for c in loads[2:]:
        c.wait()

    def hidden(pieces):
        for start, width in pieces:
            cols = slice(start, start + width)
            gate = jnp.dot(normed[...], columns(wg, start, width), preferred_element_type=F32)
            up = jnp.dot(normed[...], columns(wu, start, width), preferred_element_type=F32)
            back = back_ref[:, cols]
            sigmoid = lax.logistic(gate)
            silu = gate * sigmoid
            hid[:, cols] = (silu * up).astype(BF)
            dup[:, cols] = (back * silu).astype(BF)
            dgate[:, cols] = (back * up * sigmoid * (1.0 + gate * (1.0 - sigmoid))).astype(BF)

    def back_half(c, start, width):
        cols = slice(start, start + width)
        one = lax.dot_general(dgate[:, cols], half_rows(wg, c, start, width), NT, preferred_element_type=F32)
        return one + lax.dot_general(dup[:, cols], half_rows(wu, c, start, width), NT, preferred_element_type=F32)

    def forward_half(c, start, width):
        cols = slice(start, start + width)
        return lax.dot_general(hid[:, cols], half_rows(wd, c, start, width), NT, preferred_element_type=F32)

    hidden(FIRST)
    for g in gathers:
        g.pass_on()
    for c in range(2):
        part[1, c] = back_half(c, 0, 1152)
        part_f[:, c * 1024 : (c + 1) * 1024] = forward_half(c, 0, 1152)
    for g in gathers:
        g.finish()
    product(back_ref, dy, wd, SECOND)
    hidden(SECOND)
    late = []
    for c in range(2):
        part[1, c] += back_half(c, 1152, 1024)
        late.append(send(part.at[1, c], got.at[1, c], psem.at[2 + c, 0], psem.at[2 + c, 1], sibling))
    for c in range(2):
        part_f[:, c * 1024 : (c + 1) * 1024] += forward_half(c, 1152, 1024)
    other = pl.ds(pl.multiple_of((1 - core) * TOK, TOK), TOK)
    last = send(part_f.at[other], got_f, psem.at[4, 0], psem.at[4, 1], sibling)

    for c in late:
        c.wait_recv()

    def backward(r, carry):
        rows = rows_at(r)
        e = jnp.concatenate([part[1, c, rows, :] + got[1, c, rows, :] for c in range(2)], axis=1)
        v = mid[rows, :]
        inverse = lax.rsqrt(jnp.sum(v * v, axis=1, keepdims=True) * (1.0 / D) + EPSILON)
        scaled = e * gain_row
        inner = jnp.sum(scaled * v, axis=1, keepdims=True) * (1.0 / D)
        total = dy[rows, :].astype(F32) + inverse * scaled - v * (inverse * inverse * inverse) * inner
        low_mid[rows, :] = total.astype(BF)
        mid[rows, :] = total
        own = jnp.where(lax.div(r, TOK // 32) == core, 1.0, 0.0)
        return carry + own * jnp.sum(e * v * inverse, axis=0, keepdims=True)

    def finish(r, carry):
        rows = rows_at(r)
        own = pl.ds(pl.multiple_of(core * TOK + r * 32, 32), 32)
        branch = part_f[own, :] + got_f[rows, :]
        result[rows, :] = (mid[own, :] + branch).astype(BF)
        return carry + root(branch)

    last.wait_recv()
    final = lax.fori_loop(0, TOK // 32, finish, zero)
    terms[...] = lax.fori_loop(0, 2 * TOK // 32, backward, jnp.zeros((1, D), F32))
    for i, v in enumerate(roots + (final,)):
        stats[i : i + 1, :] = jnp.broadcast_to(v, (1, 128))
    grad_attn[...] = jnp.dot(low_mid[...], columns(wo, 0, QW), preferred_element_type=F32).astype(BF)
    grad_mid[...] = mid[pl.ds(pl.multiple_of(core * TOK, TOK), TOK), :]
    for c in sent + late + [last]:
        c.wait_send()
    for g in gathers:
        g.wait_sent()


def feed(attn, x, dy, gains, w_out, w_gate, w_up, w_down, cid):
    vmem = pl.BlockSpec(memory_space=pltpu.VMEM)
    anywhere = pl.BlockSpec(memory_space=pl.ANY)
    tokens = 2 * TOK
    return pl.pallas_call(
        feed_kernel,
        out_shape=[
            jax.ShapeDtypeStruct((TOK, D), BF),
            jax.ShapeDtypeStruct((TOK, D), F32),
            jax.ShapeDtypeStruct((tokens, QW), BF),
            jax.ShapeDtypeStruct((tokens, D), BF),
            jax.ShapeDtypeStruct((tokens, FH), BF),
            jax.ShapeDtypeStruct((tokens, FH), BF),
            jax.ShapeDtypeStruct((tokens, FH), BF),
            jax.ShapeDtypeStruct((tokens, D), BF),
            jax.ShapeDtypeStruct((4, 128), F32),
            jax.ShapeDtypeStruct((1, D), F32),
        ],
        in_specs=[vmem] * 4 + [anywhere] * 4,
        out_specs=[vmem] * 10,
        scratch_shapes=[
            pltpu.VMEM((2, 4, 4, 2, 32, QW), BF),
            pltpu.VMEM((2, 4, 4, 2, 32, FH), BF),
            pltpu.VMEM((2, 4, 4, 2, 32, FH), BF),
            pltpu.VMEM((2, 4, 4, 2, 32, FH), BF),
            pltpu.VMEM((tokens, D), F32),
            pltpu.VMEM((2, 2, tokens, D // 2), F32),
            pltpu.VMEM((2, 2, tokens, D // 2), F32),
            pltpu.VMEM((tokens, D), F32),
            pltpu.VMEM((TOK, D), F32),
            pltpu.VMEM((tokens, FH), F32),
            pltpu.SemaphoreType.DMA((7,)),
            pltpu.SemaphoreType.DMA((5, 2)),
            pltpu.SemaphoreType.DMA((3, 3, 4)),
            pltpu.SemaphoreType.DMA((3, 3, 4)),
        ],
        compiler_params=pltpu.CompilerParams(
            collective_id=cid, has_side_effects=True, vmem_limit_bytes=62 * 1024 * 1024
        ),
        name="feed",
    )(attn, x, dy, gains, w_out, w_gate, w_up, w_down)


def body(layer_input, w_qkv, w_out, w_gate_up, w_down, norm_gains, span_map, cotangent):
    at = here()
    core, low = at["core"], at["l"]
    w_q = w_qkv[:, : HQ * HD].reshape(16, 2, QW).transpose(1, 0, 2)
    w_k = w_qkv[:, HQ * HD : (HQ + HK) * HD].reshape(16, 2, HH, HD)
    w_v = w_qkv[:, (HQ + HK) * HD :].reshape(16, 2, HH, HD)
    w_kv = jnp.concatenate([w_k, w_v], axis=3).reshape(16, 2, KVW).transpose(1, 0, 2)
    shard_one = jnp.concatenate([w_q, w_kv], axis=2)
    share = norm_gains.shape[0]
    device = lax.axis_index(("ctx", "fsdp"))
    own_gain = lax.dynamic_update_slice_in_dim(jnp.zeros((40 * 128,), F32), norm_gains.astype(F32), device * share, 0)

    ctx_index = lax.axis_index("ctx")
    maps = lax.dynamic_slice_in_dim(span_map, low * 2, 2, 0)
    own_span = lax.dynamic_slice_in_dim(maps, ctx_index, 1, 1)
    spans = jnp.concatenate([own_span, 2 * N_CTX - 1 - own_span], axis=1)
    positions = (spans[:, :, None] * SPAN + jnp.arange(SPAN, dtype=jnp.int32)).reshape(2 * TOK)
    match = maps[:, None, :] == jnp.arange(N_CTX, dtype=jnp.int32)[None, :, None]
    inverse_map = jnp.sum(jnp.where(match, jnp.arange(N_CTX, dtype=jnp.int32), 0), axis=2)
    holder = jnp.concatenate([inverse_map, inverse_map[:, ::-1]], axis=1)
    upper = (jnp.arange(2 * N_CTX, dtype=jnp.int32) >= N_CTX).astype(jnp.int32)[None, :] + jnp.zeros_like(holder)
    low_block = own_span // SPANS_STEP
    low_limit = own_span % SPANS_STEP * SPAN
    three = jnp.arange(3, dtype=jnp.int32)[None, :]
    step_half = (three >= low_block).astype(jnp.int32)
    tab = jnp.concatenate(
        [
            holder // 16,
            holder // 4 % 4,
            holder % 4,
            upper,
            step_half,
            jnp.where(step_half == 0, three, 6 - three),
            (jnp.arange(4, dtype=jnp.int32)[None, :] == low_block).astype(jnp.int32),
            low_block,
            KEY_BLOCKS - 1 - low_block,
            low_limit,
            KEYS - SPAN - low_limit,
            maps,
            2 * N_CTX - 1 - maps,
        ],
        axis=1,
    )
    half_dim = HD // 2
    frequencies = ROPE_BASE ** (-(jnp.arange(half_dim, dtype=F32) * 2.0 / HD))
    angles = positions.astype(F32)[:, None] * frequencies[None, :]
    cosine, sine = jnp.cos(angles), jnp.sin(angles)
    cosine = jnp.concatenate([cosine] * 4, axis=1)
    sine = jnp.concatenate([-sine, sine] * 2, axis=1)

    weights = [shard_one, w_gate_up, w_down, w_out]
    (w_one, w_gate, w_up, w_back, w_proj, x_pair, dy_pair, gains, joined, normed_one, query, keys, attn_f32, attn_low, log_sum) = front(
        tab, weights, layer_input[0], cotangent[0], own_gain.reshape(40, 128), cosine, sine, 1
    )
    dy = dy_pair.reshape(2 * TOK, D)

    result, grad_middle, grad_attn, normed_two, hidden, grad_gate, grad_up, grad_branch, stats, gain_two_terms = feed(
        attn_low, x_pair.reshape(2 * TOK, D), dy, gains, w_proj, w_gate, w_up, w_back, 2
    )
    operands = (tab, query, grad_attn, attn_f32, attn_low, log_sum, keys, normed_two, dy, grad_branch, hidden)
    operands += (grad_gate, grad_up, joined, normed_one, w_one, gains, cosine, sine, grad_middle, layer_input[0])
    grad_input, gain_one_terms, head_terms, grads, begun = attend_back(operands, 4)
    sums = jnp.concatenate(
        [
            gain_one_terms[0],
            gain_two_terms[0],
            head_terms[0],
            stats[:, 0],
        ]
    )
    sums = jnp.pad(sums, (0, 40 * 128 - sums.shape[0])).reshape(40, 128)
    grad_mlp, grad_down, grad_proj, grad_qkv, sums = sum_weights(
        grads, sums, begun, SUMS, 5, 62 * 1024 * 1024
    )
    sums = sums.reshape(-1)
    own_gains = lax.dynamic_slice_in_dim(sums, device * share, share, 0)
    stream_rms = sums[4224:4228] / (TOK * N_CTX * 4)
    arrays = [result[None], grad_input[None], grad_qkv, grad_proj, grad_mlp, grad_down]
    result, grad_input, grad_qkv, grad_proj, grad_mlp, grad_down = publish(arrays)
    return (
        result,
        grad_input,
        grad_qkv,
        grad_proj,
        grad_mlp,
        grad_down,
        own_gains,
        stream_rms,
    )


def publish_kernel(n, *refs):
    copies = [pltpu.make_async_copy(refs[i], refs[n + i], refs[2 * n].at[i]) for i in range(n)]
    for c in copies:
        c.start()
    for c in copies:
        c.wait()


def publish(arrays):
    n = len(arrays)
    anywhere = pl.BlockSpec(memory_space=pl.ANY)
    return pl.pallas_call(
        functools.partial(publish_kernel, n),
        out_shape=[jax.ShapeDtypeStruct(a.shape, a.dtype) for a in arrays],
        in_specs=[pl.BlockSpec(memory_space=pltpu.VMEM)] * n,
        out_specs=[anywhere] * n,
        scratch_shapes=[pltpu.SemaphoreType.DMA((n,))],
        name="publish",
    )(*arrays)


def solution(mesh):
    rows = P(("ctx", "fsdp"), None)
    tokens = P("fsdp", "ctx", None)
    return jax.shard_map(
        body,
        mesh=mesh,
        in_specs=(tokens, rows, rows, rows, rows, P(("ctx", "fsdp")), P(), tokens),
        out_specs=(tokens, tokens, rows, rows, rows, rows, P(("ctx", "fsdp")), P()),
        check_vma=False,
    )
```

```python
import functools

import jax
import jax.numpy as jnp
from jax import lax
from jax.experimental import pallas as pl
from jax.experimental.pallas import tpu as pltpu
from jax.sharding import PartitionSpec as P

D = 2048
HQ = 24
HK = 6
HD = 64
FF = 4352
TOK = 128
SPAN = 64
N_CTX = 32

HH = HK // 2
GROUP = HQ // HK
QH = HQ // 2
QW = QH * HD
KVW = HH * 2 * HD
FH = FF // 2
KEYS = 512
SPANS_STEP = KEYS // SPAN
KEY_BLOCKS = 8
QROWS = GROUP * SPAN

EPSILON = 1e-06
ROPE_BASE = 10000.0
LOG2E = 1.4426950408889634
AT_H, AT_X, AT_Y, AT_HALF = 0, 64, 128, 192
AT_STEP_HALF, AT_STEP_BLOCK, AT_MARK, AT_EDGE, AT_LIMIT, AT_MAP = 256, 259, 262, 266, 268, 270
MESH = pl.DeviceIdType.MESH
BF = jnp.bfloat16
F32 = jnp.float32
NT = (((1,), (1,)), ((), ()))
NN = (((1,), (0,)), ((), ()))
TN = (((0,), (0,)), ((), ()))
W_DIMS = ("h", "x", "y", "l")
KV_DIMS = ("h", "x", "y")
ORDERS = (("x", "y", "z"), ("y", "z", "x"), ("z", "x", "y"))
KV_ORDERS = (("h", "x", "y"), ("x", "y", "h"), ("y", "h", "x"))
KV_PARTS = ((0, 96, ("y", "x", "h")), (96, 96, ("x", "y", "h")), (192, 64, ("h", "x", "y")))
SUMS = (
    (0, 0, 1152, ORDERS[0]),
    (1, 0, 1152, ORDERS[1]),
    (2, 0, 1152, ORDERS[2]),
    (0, 1152, 1024, ORDERS[0]),
    (1, 1152, 1024, ORDERS[1]),
    (2, 1152, 1024, ORDERS[2]),
    (3, 0, 256, ORDERS[0]),
    (3, 256, 256, ORDERS[1]),
    (3, 512, 256, ORDERS[2]),
    (4, 0, 384, ORDERS[0]),
    (4, 384, 384, ORDERS[1]),
    (4, 768, 384, ORDERS[2]),
)
N_EARLY = 9
ADVANCE = (0, 4, 0, 6, 0, 2)
SIZES = {"x": 4, "y": 4, "z": 4, "h": 2}


def here():
    c = lax.axis_index("ctx")
    f = lax.axis_index("fsdp")
    return {
        "x": lax.rem(lax.div(c, 4), 4),
        "y": lax.rem(c, 4),
        "z": lax.div(c, 16) * 2 + lax.div(f, 2),
        "h": lax.div(c, 16),
        "l": lax.div(f, 2),
        "core": lax.rem(f, 2),
    }


def device_of(x, y, z, core):
    return (lax.div(z, 2) * 16 + x * 4 + y, lax.rem(z, 2) * 2 + core)


def moved(at, axis, by):
    if axis == "core":
        return device_of(at["x"], at["y"], at["z"], 1 - at["core"])
    place = {k: at[k] for k in ("x", "y", "z")}
    if axis == "h":
        place["z"] = lax.rem(at["z"] + 2, 4)
    else:
        place[axis] = lax.rem(at[axis] + by + 4, 4)
    return device_of(place["x"], place["y"], place["z"], at["core"])


def labels(axis, value):
    if axis == "z":
        return {"h": lax.div(value, 2), "l": lax.rem(value, 2)}
    return {axis: value}


def pick(ref, dims, values, tail):
    return ref.at[tuple(values[d] if d in values else slice(None) for d in dims) + tail]


def greet(devices):
    barrier = pltpu.get_barrier_semaphore()
    for d in devices:
        pl.semaphore_signal(barrier, inc=1, device_id=d, device_id_type=MESH)
    pl.semaphore_wait(barrier, len(devices))


def send(src, dst, ssem, rsem, device):
    copy = pltpu.make_async_remote_copy(
        src_ref=src, dst_ref=dst, send_sem=ssem, recv_sem=rsem, device_id=device, device_id_type=MESH
    )
    copy.start()
    return copy


class Gathering:
    def __init__(self, ref, dims, at, order, rows, cols, ssem, rsem):
        self.ref, self.dims, self.at, self.order, self.rows, self.cols = ref, dims, at, order, rows, cols
        self.ssem, self.rsem, self.phase, self.sent = ssem, rsem, 0, []

    def block(self, coordinate, rows):
        later = {}
        for a in self.order[self.phase + 1 :]:
            later.update(labels(a, self.at[a]))
        return pick(self.ref, self.dims, {**later, **labels(self.axis, coordinate)}, (rows, self.cols))

    def send(self, n, ref, by):
        c = send(ref, ref, self.ssem.at[self.phase, n], self.rsem.at[self.phase, n], moved(self.at, self.axis, by))
        self.sent.append(c)
        return c

    def start(self):
        self.axis = self.order[self.phase]
        mine = self.block(self.at[self.axis], slice(None))
        self.first = [self.send(0, mine, 1)]
        if SIZES[self.axis] == 4:
            self.first.append(self.send(1, mine, 3))

    def pass_on(self):
        for c in self.first:
            c.wait_recv()
        self.second = []
        if SIZES[self.axis] == 4:
            half = self.rows // 2
            me = self.at[self.axis]
            self.second.append(self.send(2, self.block(lax.rem(me + 3, 4), pl.ds(0, half)), 1))
            self.second.append(self.send(3, self.block(lax.rem(me + 1, 4), pl.ds(half, half)), 3))

    def finish(self):
        for c in self.second:
            c.wait_recv()
        self.phase += 1

    def wait_sent(self):
        for c in self.sent:
            c.wait_send()


def neighbours(at, axes):
    out = []
    for a in axes:
        if a in ("core", "h"):
            out.append(moved(at, a, 1))
        else:
            out.append(moved(at, a, 1))
            out.append(moved(at, a, 3))
    return out


SPLIT = 1664
GATHER = (
    (0, 0, SPLIT, ORDERS[0]),
    (1, 0, SPLIT, ORDERS[1]),
    (2, 0, SPLIT, ORDERS[2]),
    (0, SPLIT, FH - SPLIT, ORDERS[0]),
    (1, SPLIT, FH - SPLIT, ORDERS[1]),
    (2, SPLIT, FH - SPLIT, ORDERS[2]),
    (3, 0, 256, ORDERS[0]),
    (3, 256, 256, ORDERS[1]),
    (3, 512, 256, ORDERS[2]),
)


def lane_of(shape):
    return lax.broadcasted_iota(jnp.int32, shape, len(shape) - 1)


def swap_halves(v):
    return jnp.where(lax.rem(lane_of(v.shape), HD) < HD // 2, pltpu.roll(v, 96, 1), pltpu.roll(v, 32, 1))


def head_sums(v):
    low = lane_of(v.shape) < HD
    a = jnp.sum(jnp.where(low, v, 0.0), axis=1, keepdims=True)
    b = jnp.sum(jnp.where(low, 0.0, v), axis=1, keepdims=True)
    return jnp.where(low, a, b)


def tile_gain(row, is_key):
    low = lane_of(row.shape) < HD
    turned = pltpu.roll(row, HD, 1)
    return jnp.where(low, turned, 1.0) if is_key else jnp.where(low, row, turned)


def front_kernel(
    tab, shard_one, gate_up, down, out, x, dy, gains, cosine, sine,
    w_one, w_gate, w_up, w_down, w_out, x_pair, dy_pair, gain_all, joined, normed, query, kv_out, o_ref, low_ref, l_ref,
    one, kv_src, kvg, kvs, q_ref, acc, sum_ref, small_buf, psem, lsem, tssem, trsem, ossem, orsem, gssem, grsem, kssem, krsem, ksem,
):
    at = here()
    core = at["core"]
    sibling = moved(at, "core", 1)
    greet([sibling] + sum_peers(at, ("x", "y", "z")))
    own = {d: at[d] for d in W_DIMS}
    total = Total(gains[...], at, small_buf, tssem, trsem)
    remote, local = [], []

    def half_of(src, start, width, which):
        return src.at[:, pl.ds(pl.multiple_of(start + which * width, 128), width)]

    pairs = [
        (lambda c: shard_one.at[c], one),
        (lambda c: half_of(gate_up, 0, FH, c), w_gate),
        (lambda c: half_of(gate_up, FF, FH, c), w_up),
        (lambda c: half_of(down, 0, FH, c), w_down),
        (lambda c: half_of(out, 0, QW, c), w_out),
    ]
    for i, (src, ref) in enumerate(pairs):
        dst = pick(ref, W_DIMS, own, (pl.ds(core * 16, 16), slice(None)))
        remote.append(send(src(1 - core), dst, psem.at[i, 0], psem.at[i, 1], sibling))
        local.append(pltpu.make_async_copy(src(core), dst, lsem.at[i]))
        local[-1].start()
    for i, (src, ref) in ((5, (x, x_pair)), (6, (dy, dy_pair))):
        remote.append(send(src, ref.at[core], psem.at[i, 0], psem.at[i, 1], sibling))
        local.append(pltpu.make_async_copy(src, ref.at[core], lsem.at[i]))
        local[-1].start()

    def arrived(i):
        remote[i].wait_recv()
        local[i].wait()

    ones = [
        Gathering(one, W_DIMS, at, ORDERS[k], 32, pl.ds(k * 384, 384), ossem.at[k], orsem.at[k]) for k in range(3)
    ]
    rest = [
        Gathering(pairs[1 + a][1], W_DIMS, at, order, 32, pl.ds(start, width), gssem.at[k], grsem.at[k])
        for k, (a, start, width, order) in enumerate(GATHER)
    ]
    keys = [
        Gathering(kvg.at[h], KV_DIMS, at, KV_ORDERS[h], 4, slice(None), kssem.at[h], krsem.at[h]) for h in range(HH)
    ]

    def every(streams, *steps):
        for s in streams:
            for step in steps:
                getattr(s, step)()

    arrived(0)
    every(ones, "start")
    for i in range(1, 5):
        arrived(i)
    every(rest, "start")
    total.step()
    every(ones, "pass_on")
    every(rest, "pass_on")
    total.step()
    every(ones, "finish", "start")
    every(rest, "finish")
    total.step()
    every(ones, "pass_on")
    total.step()
    gain_all[...] = total.value
    every(ones, "finish", "start")
    every(rest, "start")
    arrived(5)
    gain_row = jnp.concatenate([total.value[j : j + 1] for j in range(D // 128)], axis=1)

    def norm(r, carry):
        rows = pl.ds(pl.multiple_of(r * 32, 32), 32)
        for s in range(2):
            v = x_pair[s, rows, :].astype(F32)
            inverse = lax.rsqrt(jnp.sum(v * v, axis=1, keepdims=True) * (1.0 / D) + EPSILON)
            normed[pl.ds(pl.multiple_of(s * TOK + r * 32, 32), 32), :] = (v * inverse * gain_row).astype(BF)
        return carry

    lax.fori_loop(0, TOK // 32, norm, 0)
    every(ones, "pass_on")
    every(ones, "finish")
    keep = pltpu.make_async_copy(one, w_one, lsem.at[7])
    keep.start()
    head_gains = total.value[32:33]

    def product(start, width):
        w = one[:, :, :, :, :, start : start + width].reshape(D, width)
        joined[:, start : start + width] = jnp.dot(normed[...], w, preferred_element_type=F32)

    def rope(tile, is_key):
        v = joined[:, tile * 128 : (tile + 1) * 128]
        low = lane_of(v.shape) < HD
        c, n = cosine[...], sine[...]
        inverse = lax.rsqrt(head_sums(v * v) * (1.0 / HD) + EPSILON)
        if is_key:
            inverse = jnp.where(low, inverse, 1.0)
            c, n = jnp.where(low, c, 1.0), jnp.where(low, n, 0.0)
        v = v * inverse * tile_gain(head_gains, is_key)
        return (v * c + swap_halves(v) * n).astype(BF)

    product(QW, KVW)
    for h in range(HH):
        kv_src[h] = rope(QW // 128 + h, True).reshape(4, SPAN, 2 * HD)
    kv_own = {d: at[d] for d in KV_DIMS}
    puts = [pltpu.make_async_copy(kv_src.at[h], pick(kvg.at[h], KV_DIMS, kv_own, ()), ksem.at[h]) for h in range(HH)]
    for c in puts:
        c.start()
    for c in puts:
        c.wait()
    every(keys, "start")
    every(rest, "pass_on")
    product(0, 384)
    every(keys, "pass_on")
    every(keys, "finish", "start")
    product(384, 384)
    every(keys, "pass_on")
    for t in range(QW // 128):
        query[:, t * 128 : (t + 1) * 128] = rope(t, False)
    every(keys, "finish", "start")
    blank = jnp.zeros((QROWS, HD), BF)
    for s in range(2):
        for h in range(HH):
            for half in range(2):
                q_ref[s, h, half] = jnp.concatenate([heads_at(query, s, h, half), blank], axis=1)
    every(keys, "pass_on")
    every(keys, "finish")
    every(rest[:3] + rest[6:], "finish", "start")
    every(rest[3:6], "finish")

    def sort(p, carry):
        for s in range(2):
            place = tuple(tab[s, column + p] for column in (AT_H, AT_X, AT_Y))
            half = tab[s, AT_HALF + p]
            for h in range(HH):
                kvs[s, h, lax.div(p, SPANS_STEP), lax.rem(p, SPANS_STEP)] = kvg[(h,) + place + (s * 2 + half,)]
        return carry

    lax.fori_loop(0, 2 * N_CTX, sort, 0)
    keep_keys = pltpu.make_async_copy(kvs, kv_out, ksem.at[HH])
    keep_keys.start()
    attend_heads(tab, 0, q_ref, kvs, o_ref, low_ref, l_ref, acc, sum_ref)
    every(rest[:3], "pass_on")
    attend_heads(tab, 1, q_ref, kvs, o_ref, low_ref, l_ref, acc, sum_ref)
    every(rest[6:], "pass_on")
    every(rest[:3] + rest[6:], "finish")
    keep_keys.wait()
    arrived(6)
    keep.wait()
    for c in remote + total.sent:
        c.wait_send()
    for s in ones + rest + keys:
        s.wait_sent()


def front(tab, shards, x, dy, gains, cosine, sine, cid):
    anywhere = pl.BlockSpec(memory_space=pl.ANY)
    vmem = pl.BlockSpec(memory_space=pltpu.VMEM)
    full = [jax.ShapeDtypeStruct((2, 4, 4, 2, 32, w), BF) for w in (QW + KVW, FH, FH, FH, QW)]
    n = len(GATHER)
    return pl.pallas_call(
        front_kernel,
        out_shape=full
        + [
            jax.ShapeDtypeStruct((2,) + x.shape, BF),
            jax.ShapeDtypeStruct((2,) + dy.shape, BF),
            jax.ShapeDtypeStruct(gains.shape, F32),
            jax.ShapeDtypeStruct((2 * TOK, QW + KVW), F32),
            jax.ShapeDtypeStruct((2 * TOK, D), BF),
            jax.ShapeDtypeStruct((2 * TOK, QW), BF),
            jax.ShapeDtypeStruct((2, HH, KEY_BLOCKS, SPANS_STEP, SPAN, 2 * HD), BF),
            jax.ShapeDtypeStruct((2 * TOK, QW), F32),
            jax.ShapeDtypeStruct((2 * TOK, QW), BF),
            jax.ShapeDtypeStruct((2, HH, 2, 1, QROWS), F32),
        ],
        in_specs=[pl.BlockSpec(memory_space=pltpu.SMEM)] + [anywhere] * 6 + [vmem] * 3,
        out_specs=[anywhere] * 5 + [vmem, anywhere] + [vmem] * 4 + [anywhere] + [vmem] * 3,
        scratch_shapes=[
            pltpu.VMEM((2, 4, 4, 2, 32, QW + KVW), BF),
            pltpu.VMEM((HH, 4, SPAN, 2 * HD), BF),
            pltpu.VMEM((HH, 2, 4, 4, 4, SPAN, 2 * HD), BF),
            pltpu.VMEM((2, HH, KEY_BLOCKS, SPANS_STEP, SPAN, 2 * HD), BF),
            pltpu.VMEM((2, HH, 2, QROWS, 2 * HD), BF),
            pltpu.VMEM((2, 2 * HD, QROWS), F32),
            pltpu.VMEM((2, 1, QROWS), F32),
            pltpu.VMEM((4, 4) + gains.shape, F32),
            pltpu.SemaphoreType.DMA((7, 2)),
            pltpu.SemaphoreType.DMA((8,)),
            pltpu.SemaphoreType.DMA((4, 4)),
            pltpu.SemaphoreType.DMA((4, 4)),
            pltpu.SemaphoreType.DMA((3, 3, 4)),
            pltpu.SemaphoreType.DMA((3, 3, 4)),
            pltpu.SemaphoreType.DMA((n, 3, 4)),
            pltpu.SemaphoreType.DMA((n, 3, 4)),
            pltpu.SemaphoreType.DMA((HH, 3, 4)),
            pltpu.SemaphoreType.DMA((HH, 3, 4)),
            pltpu.SemaphoreType.DMA((HH + 1,)),
        ],
        compiler_params=pltpu.CompilerParams(
            collective_id=cid, has_side_effects=True, vmem_limit_bytes=60 * 1024 * 1024
        ),
        name="front",
    )(tab, *shards, x, dy, gains, cosine, sine)


def lead_shape(dims):
    full = {"h": 2, "x": 4, "y": 4, "l": 2}
    return tuple(full[d] for d in dims)


def without(dims, axis):
    gone = ("h", "l") if axis == "z" else (axis,)
    return tuple(d for d in dims if d not in gone)


class Summing:
    def __init__(self, source, dims, at, order, rows, cols, buffers, ssem, rsem, lsem, begun=None, base=None):
        self.ref, self.dims, self.at, self.order, self.begun = source, dims, at, order, begun
        self.cols, self.buffers, self.rows = cols, buffers, rows
        self.ssem, self.rsem, self.lsem = ssem, rsem, lsem
        self.phase, self.sent, self.base = 0, [], base
        self.resident = base is not None

    def part(self, coordinate, start, length):
        rows = pl.ds(start + (self.base or 0), length)
        return pick(self.ref, self.dims, labels(self.axis, coordinate), (rows, self.cols))

    def send(self, n, src, dst, by):
        c = send(src, dst, self.ssem.at[self.phase, n], self.rsem.at[self.phase, n], moved(self.at, self.axis, by))
        self.sent.append(c)
        return c

    def start(self):
        self.axis = self.order[self.phase]
        self.rest = without(self.dims, self.axis)
        self.lead = lead_shape(self.rest)
        half = self.rows // 2
        first, second, every = (0, half), (half, half), (0, self.rows)
        i = self.at[self.axis]
        buf = self.buffers[self.phase]
        self.local = []
        if SIZES[self.axis] == 2:
            self.direct = (self.send(0, self.part(1 - i, *every), buf["got"].at[0], 1),)
        else:
            up, down, far = lax.rem(i + 1, 4), lax.rem(i + 3, 4), lax.rem(i + 2, 4)
            self.near = (up, down)
        if self.phase == 0 and self.begun is not None:
            self.relay, self.direct = (), ()
        elif SIZES[self.axis] == 4:
            self.relay = (
                self.send(0, self.part(far, *first), buf["relay"].at[0], 1),
                self.send(1, self.part(far, *second), buf["relay"].at[1], 3),
            )
            self.direct = (
                self.send(2, self.part(up, *second), buf["got"].at[1, 1], 1),
                self.send(3, self.part(down, *first), buf["got"].at[0, 1], 3),
            )
        if self.phase == 0 and not self.resident:
            todo = [(self.part(i, *every), buf["mine"])]
            if self.begun is not None:
                passed, direct = self.begun[1], self.begun[0]
                todo += [(passed.at[n], buf["got"].at[n, 0]) for n in range(2)]
                todo += [(direct.at[n], buf["got"].at[n, 1]) for n in range(2)]
            elif SIZES[self.axis] == 4:
                todo.append((self.part(up, *first), buf["own"].at[0]))
                todo.append((self.part(down, *second), buf["own"].at[1]))
            for n, (src, dst) in enumerate(todo):
                c = pltpu.make_async_copy(src, dst, self.lsem.at[n])
                c.start()
                self.local.append(c)

    def over_lead(self, add):
        rest = self.lead[1:]
        spots = [()]
        for n in rest:
            spots = [s + (j,) for s in spots for j in range(n)]
        if not self.lead:
            add(())
            return

        def go(j, carry):
            for s in spots:
                add((j,) + s)
            return carry

        lax.fori_loop(0, self.lead[0], go, 0)

    def pass_on(self):
        if SIZES[self.axis] == 2 or (self.phase == 0 and self.begun is not None):
            return
        buf = self.buffers[self.phase]
        half = self.rows // 2
        for n, by in ((0, 1), (1, 3)):
            self.relay[n].wait_recv()
            if self.phase == 0 and not self.resident:
                self.local[1 + n].wait()
                own = buf["own"].at[n]
            else:
                own = self.part(self.near[n], n * half, half)

            def add(spot):
                here_ = spot + (slice(None), slice(None))
                both = buf["relay"][(n,) + here_].astype(F32) + own[here_].astype(F32)
                buf["relay"][(n,) + here_] = both.astype(BF)

            self.over_lead(add)
            c = self.send(4 + n, buf["relay"].at[n], buf["got"].at[n, 0], by)
            self.direct = self.direct + (c,)

    def finish(self):
        buf = self.buffers[self.phase]
        half = self.rows // 2
        if self.local:
            self.local[0].wait()
        if self.begun is not None:
            for c in self.local[1:]:
                c.wait()
        for c in self.direct:
            c.wait_recv()
        copied = self.phase == 0 and not self.resident
        own = buf["mine"] if copied else self.part(self.at[self.axis], 0, self.rows)
        out = buf["mine"] if copied else buf["sum"]

        def add(spot):
            if SIZES[self.axis] == 2:
                here_ = spot + (slice(None), slice(None))
                out[here_] = (own[here_].astype(F32) + buf["got"][(0,) + here_].astype(F32)).astype(out.dtype)
                return
            for n in range(2):
                rows = spot + (pl.ds(n * half, half), slice(None))
                all_ = spot + (slice(None), slice(None))
                total = own[rows].astype(F32) + buf["got"][(n, 0) + all_].astype(F32)
                total = total + buf["got"][(n, 1) + all_].astype(F32)
                out[rows] = total.astype(out.dtype)

        self.over_lead(add)
        self.ref, self.dims, self.cols = out, self.rest, slice(None)
        self.phase += 1
        self.base = 0


class Total:
    def __init__(self, value, at, buf, ssem, rsem):
        self.value, self.at, self.buf, self.ssem, self.rsem = value, at, buf, ssem, rsem
        self.phase, self.sent = 0, []
        self.start()

    def start(self):
        n, axis = self.phase, ("core", "z", "y", "x")[self.phase]
        self.buf[n, 0] = self.value
        self.copies = []
        for i in (1, 3, 2) if axis != "core" else (1,):
            self.copies.append(
                send(self.buf.at[n, 0], self.buf.at[n, i], self.ssem.at[n, i], self.rsem.at[n, i], moved(self.at, axis, i))
            )

    def step(self):
        n, buf = self.phase, self.buf
        if n == 4:
            return
        for c in self.copies:
            c.wait_recv()
            self.sent.append(c)
        if n == 0:
            self.value = buf[n, 0] + buf[n, 1]
        else:
            self.value = (buf[n, 0] + buf[n, 2]) + (buf[n, 1] + buf[n, 3])
        self.phase += 1
        if self.phase < 4:
            self.start()


def run_sums(streams, total):
    todo = []
    for s in streams:
        if s.begun is None:
            s.start()
    for s in streams:
        if s.begun is not None:
            s.start()
        steps = [("pass_on",), ("finish", "start"), ("pass_on",), ("finish", "start"), ("pass_on",), ("finish",)]
        todo.append(steps[1:] if s.begun is not None else steps)
    while any(todo):
        for s, steps in zip(streams, todo):
            if steps:
                for name in steps.pop(0):
                    getattr(s, name)()
        total.step()
    for s in streams:
        for c in s.sent:
            c.wait_send()


def sum_scratch(order, dims, rows, width, begun=False, resident=False):
    buffers = []
    for phase, axis in enumerate(order):
        rest = without(dims, axis)
        lead = lead_shape(rest)
        buf = {}
        if SIZES[axis] == 2:
            buf["got"] = pltpu.VMEM((1,) + lead + (rows, width), BF)
        else:
            buf["got"] = pltpu.VMEM((2, 2) + lead + (rows // 2, width), BF)
            if phase or not begun:
                buf["relay"] = pltpu.VMEM((2,) + lead + (rows // 2, width), BF)
        if phase == 0 and not resident:
            buf["mine"] = pltpu.VMEM(lead + (rows, width), BF)
            if SIZES[axis] == 4 and not begun:
                buf["own"] = pltpu.VMEM((2,) + lead + (rows // 2, width), BF)
        else:
            buf["sum"] = pltpu.VMEM(lead + (rows, width), BF if phase < 2 else F32)
        buffers.append(buf)
        dims = rest
    return buffers


def weight_sum_kernel(pieces, n, *refs):
    ins, small, begun, refs = refs[:n], refs[n], refs[n + 1 : n + 1 + 2 * N_EARLY], refs[n + 1 + 2 * N_EARLY :]
    outs, small_out = refs[: n - 1], refs[n - 1]
    buffers, stages, swapped, halves, small_buf, ssem, rsem, lsem, csem, tssem, trsem = refs[n:]
    at = here()
    core = at["core"]
    sibling = moved(at, "core", 1)
    greet([sibling] + sum_peers(at, ("x", "y", "z")))
    streams = [
        Summing(
            ins[a], W_DIMS, at, order, 32, pl.ds(start, width), buffers[k], ssem.at[k], rsem.at[k], lsem.at[k],
            (begun[2 * k], begun[2 * k + 1]) if k < N_EARLY else None,
        )
        for k, (a, start, width, order) in enumerate(pieces)
    ]
    total = Total(small[...], at, small_buf, tssem, trsem)
    run_sums(streams, total)
    small_out[...] = total.value
    for k, (a, start, width, order) in enumerate(pieces):
        stages[a][:, start : start + width] = buffers[k][2]["sum"][...]
    other = pl.ds(pl.multiple_of((1 - core) * 16, 16), 16)
    own = pl.ds(pl.multiple_of(core * 16, 16), 16)
    copies = [send(stages[a].at[other], swapped[a], csem.at[a, 0], csem.at[a, 1], sibling) for a in range(n)]

    def put(a, half, value):
        width = value.shape[1]
        if a == 4:
            outs[3][:, pl.ds(pl.multiple_of(half * QW, 128), QW)] = value[:, :QW]
            halves[half] = value[:, QW:]
            return
        ref, start = ((outs[0], 0), (outs[0], FF), (outs[1], 0), (outs[2], 0))[a]
        ref[:, pl.ds(pl.multiple_of(start + half * width, 128), width)] = value

    for a in range(n):
        put(a, core, stages[a][own, :])
    for a in range(n):
        copies[a].wait_recv()
        put(a, 1 - core, swapped[a][...])
    for kind in range(2):
        at_ = [half_kv[:, (2 * h + kind) * HD : (2 * h + kind + 1) * HD] for half_kv in (halves[0], halves[1]) for h in range(HH)]
        start = HQ * HD + kind * HK * HD
        outs[3][:, start : start + HK * HD] = jnp.concatenate(at_, axis=1)
    for c in copies + total.sent:
        c.wait_send()


def sum_weights(grads, small, begun, pieces, cid, limit):
    n, count = len(grads), len(pieces)
    anywhere = pl.BlockSpec(memory_space=pl.ANY)
    vmem = pl.BlockSpec(memory_space=pltpu.VMEM)
    widths = [g.shape[-1] for g in grads]
    return pl.pallas_call(
        functools.partial(weight_sum_kernel, pieces, n),
        out_shape=[jax.ShapeDtypeStruct((16, w), F32) for w in (2 * FF, FF, HQ * HD, (HQ + 2 * HK) * HD)]
        + [jax.ShapeDtypeStruct(small.shape, F32)],
        in_specs=[anywhere] * n + [vmem] + [anywhere] * len(begun),
        out_specs=[vmem] * n,
        scratch_shapes=[
            [sum_scratch(order, W_DIMS, 32, width, k < N_EARLY) for k, (a, start, width, order) in enumerate(pieces)],
            [pltpu.VMEM((32, w), F32) for w in widths],
            [pltpu.VMEM((16, w), F32) for w in widths],
            pltpu.VMEM((2, 16, KVW), F32),
            pltpu.VMEM((4, 4) + small.shape, F32),
            pltpu.SemaphoreType.DMA((count, 3, 6)),
            pltpu.SemaphoreType.DMA((count, 3, 6)),
            pltpu.SemaphoreType.DMA((count, 6)),
            pltpu.SemaphoreType.DMA((n, 2)),
            pltpu.SemaphoreType.DMA((4, 4)),
            pltpu.SemaphoreType.DMA((4, 4)),
        ],
        compiler_params=pltpu.CompilerParams(collective_id=cid, has_side_effects=True, vmem_limit_bytes=limit),
        name="sum_weights",
    )(*grads, small, *begun)


def sum_peers(at, axes):
    out = []
    for a in axes:
        for i in (1, 3, 2) if SIZES[a] == 4 else (1,):
            out.append(moved(at, a, i))
    return out


def heads_at(ref, s, h, half):
    rows = slice(s * TOK + half * SPAN, s * TOK + (half + 1) * SPAN)
    return jnp.concatenate([ref[rows, (h * GROUP + g) * HD : (h * GROUP + g + 1) * HD] for g in range(GROUP)], axis=0)


def put_heads(ref, s, h, half, value):
    rows = pl.ds(pl.multiple_of(s * TOK + half * SPAN, SPAN), SPAN)
    for g in range(0, GROUP, 2):
        both = jnp.concatenate([value[g * SPAN : (g + 1) * SPAN], value[(g + 1) * SPAN : (g + 2) * SPAN]], axis=1)
        ref[rows, pl.ds(pl.multiple_of((h * GROUP + g) * HD, 2 * HD), 2 * HD)] = both.astype(ref.dtype)


def masked(prob, limit):
    if limit is None:
        return prob
    row = lax.broadcasted_iota(jnp.int32, prob.shape, 0)
    col = lax.rem(lax.broadcasted_iota(jnp.int32, prob.shape, 1), SPAN)
    return jnp.where(row <= col + limit, prob, 0.0)


def attend_heads(tab, s, q_ref, kvs, o_ref, low_ref, l_ref, acc, total):
    rate = LOG2E * HD**-0.5

    def head(h, carry):
        acc[...] = jnp.zeros_like(acc)
        total[...] = jnp.zeros_like(total)

        def scored(half, block, limit):
            keys = kvs[s, h, block].reshape(KEYS, 2 * HD)
            scores = lax.dot_general(keys, q_ref[s, h, half], NT, preferred_element_type=F32)
            prob = masked(jnp.exp2(scores * rate), limit)
            return (
                jnp.sum(prob, axis=0, keepdims=True),
                lax.dot_general(keys, prob.astype(BF), TN, preferred_element_type=F32),
            )

        def high(k, c):
            t, o = scored(1, k, None)
            total[1] += t
            acc[1] += o
            return c

        def either(k, c):
            half = tab[s, AT_STEP_HALF + k]
            t, o = scored(half, tab[s, AT_STEP_BLOCK + k], None)
            up = half.astype(F32)
            total[0] += t * (1.0 - up)
            total[1] += t * up
            acc[0] += o * (1.0 - up)
            acc[1] += o * up
            return c

        lax.fori_loop(0, 4, high, 0)
        lax.fori_loop(0, 3, either, 0)
        for half in range(2):
            t, o = scored(half, tab[s, AT_EDGE + half], tab[s, AT_LIMIT + half])
            t, o = total[half] + t, acc[half] + o
            out = (o[HD:, :] / t).T
            put_heads(o_ref, s, h, half, out)
            put_heads(low_ref, s, h, half, out)
            l_ref[s, h, half] = jnp.log2(t)
        return carry

    lax.fori_loop(0, HH, head, 0)


class Early:
    def __init__(self, source, at, order, cols, width, relay, direct, passed, ssem, rsem):
        self.source, self.at, self.axis, self.cols, self.width = source, at, order[0], cols, width
        self.relay, self.passed, self.ssem, self.rsem, self.views = relay, passed, ssem, rsem, {}
        i = at[self.axis]
        self.near = (lax.rem(i + 1, 4), lax.rem(i + 3, 4))
        far = lax.rem(i + 2, 4)
        plan = (
            (far, 0, relay, 0, 1),
            (far, 1, relay, 1, 3),
            (self.near[0], 1, direct, 1, 1),
            (self.near[1], 0, direct, 0, 3),
        )
        self.copies = []
        for n, (coordinate, half, dst, slot, by) in enumerate(plan):
            self.copies.append(self.send(n, self.part(coordinate, half), dst.at[slot], by))

    def part(self, coordinate, half):
        return pick(self.source, W_DIMS, labels(self.axis, coordinate), (pl.ds(half * 16, 16), self.cols))

    def send(self, n, src, dst, by):
        return send(src, dst, self.ssem.at[n], self.rsem.at[n], moved(self.at, self.axis, by))

    def load(self, n, own, sem):
        lead = lead_shape(without(W_DIMS, self.axis))
        view = own.at[(slice(None),) * (len(lead) + 1) + (pl.ds(0, self.width),)]
        self.views[n] = view
        copy = pltpu.make_async_copy(self.part(self.near[n], n), view, sem)
        copy.start()
        return copy

    def add(self, n):
        self.copies[n].wait_recv()
        came, own = self.relay.at[n], self.views[n]
        lead = lead_shape(without(W_DIMS, self.axis))
        spots = [()]
        for size in lead[1:]:
            spots = [s + (j,) for s in spots for j in range(size)]

        def go(j, carry):
            for s in spots:
                at = (j,) + s + (slice(None), slice(None))
                came[at] = (came[at].astype(F32) + own[at].astype(F32)).astype(BF)
            return carry

        lax.fori_loop(0, lead[0], go, 0)
        self.copies.append(self.send(4 + n, came, self.passed.at[n], 1 if n == 0 else 3))

    def wait(self):
        for c in self.copies[2:]:
            c.wait_recv()


def early_shapes():
    shapes = []
    for a, start, width, order in SUMS[:N_EARLY]:
        lead = lead_shape(without(W_DIMS, order[0]))
        shapes += [jax.ShapeDtypeStruct((2,) + lead + (16, width), BF)] * 2
    return shapes


def attend_back_kernel(*refs):
    tab, qr, da, attn, attn_low, l_ref, kv_sorted, normed, dy, low_mid, hid, dgate, dup = refs[:13]
    joined, normed_one, w_one, gains, cosine, sine, grad_mid, own_x = refs[13:21]
    input_grad, terms, head_terms = refs[21:24]
    grads, refs = refs[24:29], refs[29:]
    begun, refs = refs[: 2 * N_EARLY], refs[2 * N_EARLY :]
    held, qd_ref, delta_ref, stage, acc, dq_acc, dq_ref, buffers, refs = refs[:8] + (refs[8:],)
    tiles, mix, mix_z, relays, w_ref, d_joined, part, got = refs[:8]
    essem, ersem, ssem, rsem, sems, tsem, msem, psem = refs[8:]
    at = here()
    core = at["core"]
    sibling = moved(at, "core", 1)
    def load_keys(h):
        return [pltpu.make_async_copy(kv_sorted.at[s, h], held[h % 2].at[s], sems.at[s, h]) for s in range(2)]

    for c in load_keys(0):
        c.start()

    def load_w(start, width):
        src = w_one.at[:, :, :, :, :, pl.ds(start, width)]
        return pltpu.make_async_copy(src, w_ref.at[:, :, :, :, :, pl.ds(0, width)], psem.at[0])

    load_w(0, QW).start()
    greet([sibling] + neighbours(at, ("x", "y", "z", "h")))
    sides = ((normed, dgate), (normed, dup), (dy, hid), (low_mid, attn_low), (normed_one, d_joined))

    def tile_copy(n, i, slot, parity):
        a, start, width = n
        half = lax.rem(i, 2)
        return pltpu.make_async_copy(
            tiles.at[parity, slot, :, :, :, :, pl.ds(0, width)],
            grads[a].at[lax.div(i, 2), pl.ds(half * 2, 2), :, :, :, pl.ds(start, width)],
            tsem.at[parity, slot],
        )

    def outer(n, parity):
        a, start, width = n
        left, right = sides[a]

        def go(i, carry):
            slot = lax.rem(i, 2)

            @pl.when(i > 1)
            def _():
                tile_copy(n, i, slot, parity).wait()

            rows = pl.ds(pl.multiple_of(i * 512, 512), 512)
            value = lax.dot_general(left[:, rows], right[:, start : start + width], TN, preferred_element_type=F32)
            tiles[parity, slot, :, :, :, :, :width] = value.astype(BF).reshape(2, 4, 2, 32, width)
            tile_copy(n, i, slot, parity).start()
            return carry

        lax.fori_loop(0, 4, go, 0)

    def drain(n, parity):
        for slot in range(2):
            tile_copy(n, slot, slot, parity).wait()

    early = []

    def begin(k):
        a, start, width, order = SUMS[k]
        drain((a, start, width), k % 2)
        early.append(
            Early(
                grads[a], at, order, pl.ds(start, width), width, relays[k], begun[2 * k], begun[2 * k + 1],
                essem.at[k], ersem.at[k],
            )
        )

    for k in range(N_EARLY):
        outer(SUMS[k][:3], k % 2)
        if k:
            begin(k - 1)
    rate = LOG2E * HD**-0.5
    factor = jnp.where(lax.broadcasted_iota(jnp.int32, (1, 2 * HD), 1) < HD, HD**-0.5, 1.0)
    blank = jnp.zeros((QROWS, HD), BF)
    for s in range(2):
        for h in range(HH):
            for half in range(2):
                up = heads_at(da, s, h, half)
                qd_ref[s, h, half, :QROWS] = jnp.concatenate([heads_at(qr, s, h, half), blank], axis=1)
                qd_ref[s, h, half, QROWS:] = jnp.concatenate([blank, up], axis=1)
                inner = (up.astype(F32) * heads_at(attn, s, h, half)).T
                delta_ref[s, h, half] = jnp.sum(inner, axis=0, keepdims=True)
    begin(N_EARLY - 1)
    streams = [
        [
            Summing(
                stage.at[h], KV_DIMS, at, order, rows, slice(None), buffers[h][j],
                ssem.at[h, j], rsem.at[h, j], None, None, start,
            )
            for j, (start, rows, order) in enumerate(KV_PARTS)
        ]
        for h in range(HH)
    ]
    todo = [[("pass_on",), ("finish", "start"), ("pass_on",), ("finish", "start"), ("pass_on",), ("finish",)] for h in range(HH)]

    def move(h):
        for name_of in todo[h].pop(0) if todo[h] else ():
            for st in streams[h]:
                getattr(st, name_of)()

    units = [(k, n) for k in range(N_EARLY) for n in range(2)]
    used, flying, ahead = {}, [], [0]

    def fetch():
        k, n = units[ahead[0]]
        pool, slots, first = (mix_z, 2, 2) if early[k].axis == "z" else (mix, 2, 0)
        slot = used.get(first, 0) % slots
        used[first] = used.get(first, 0) + 1
        flying.append((k, n, early[k].load(n, pool.at[slot], msem.at[first + slot])))
        ahead[0] += 1

    def advance(count):
        for _ in range(count):
            while ahead[0] < len(units) and len(flying) < 2:
                fetch()
            if flying:
                k, n, copy = flying.pop(0)
                copy.wait()
                early[k].add(n)

    for h in range(HH):
        for c in load_keys(h):
            c.wait()
        if h + 1 < HH:
            for c in load_keys(h + 1):
                c.start()
        kvs = held[h % 2]

        def sequence(s, carry, h=h, kvs=kvs):
            dq_acc[...] = jnp.zeros_like(dq_acc)
            acc[...] = jnp.zeros_like(acc)

            def backward(half, block, limit):
                keys = kvs[s, block].reshape(KEYS, 2 * HD)
                both = lax.dot_general(keys, qd_ref[s, h, half], NT, preferred_element_type=F32)
                prob = masked(jnp.exp2(both[:, :QROWS] * rate - l_ref[s, h, half]), limit)
                grad = (prob * (both[:, QROWS:] - delta_ref[s, h, half])).astype(BF)
                pair = jnp.concatenate([grad, prob.astype(BF)], axis=1)
                kv = lax.dot_general(pair, qd_ref[s, h, half], NN, preferred_element_type=F32)
                return (
                    kv.reshape(SPANS_STEP, SPAN, 2 * HD),
                    lax.dot_general(keys, grad, TN, preferred_element_type=F32),
                )

            def spans(block):
                return pl.ds(block * SPANS_STEP, SPANS_STEP)

            def high(k, c):
                kv, q = backward(1, k, None)
                acc[spans(k)] += kv
                dq_acc[1] += q
                return c

            def either(k, c):
                half = tab[s, AT_STEP_HALF + k]
                kv, q = backward(half, tab[s, AT_STEP_BLOCK + k], None)
                up = half.astype(F32)
                acc[spans(k)] += kv * (1.0 - up)
                acc[spans(6 - k)] += kv * up
                dq_acc[0] += q * (1.0 - up)
                dq_acc[1] += q * up
                return c

            lax.fori_loop(0, 4, high, 0)
            lax.fori_loop(0, 3, either, 0)
            for half in range(2):
                kv, q = backward(half, tab[s, AT_EDGE + half], tab[s, AT_LIMIT + half])
                for k in range(4):
                    acc[spans(k if half == 0 else 7 - k)] += kv * tab[s, AT_MARK + k].astype(F32)
                q = dq_acc[half] + q
                put_heads(dq_ref, s, h, half, (q[:HD, :] * HD**-0.5).T)

            def put(j, c):
                for half in range(2):
                    v = acc[tab[s, AT_MAP + half * N_CTX + j]] * factor
                    rows = pl.ds(pl.multiple_of(s * TOK + half * SPAN, SPAN), SPAN)
                    stage[h, lax.div(j, 16), lax.rem(lax.div(j, 4), 4), lax.rem(j, 4), rows, :] = v.astype(BF)
                return c

            lax.fori_loop(0, N_CTX, put, 0)
            return carry

        for s in range(2):
            sequence(s, 0)
            if s == 1:
                for k in range(h):
                    move(k)
                for st in streams[h]:
                    st.start()
            advance(ADVANCE[2 * h + s])

    head_gains = gains[32:33]

    def tile(t, is_key, grad):
        v = joined[:, t * 128 : (t + 1) * 128]
        low = lane_of(v.shape) < HD
        back = grad * cosine[...] - swap_halves(grad) * sine[...]
        inverse = lax.rsqrt(head_sums(v * v) * (1.0 / HD) + EPSILON)
        scaled = back * tile_gain(head_gains, is_key)
        inner = head_sums(scaled * v) * (1.0 / HD)
        result = inverse * scaled - v * (inverse * inverse * inverse) * inner
        if is_key:
            result = jnp.where(low, result, grad)
        d_joined[:, t * 128 : (t + 1) * 128] = result.astype(BF)
        return jnp.sum(back * v * inverse, axis=0, keepdims=True)

    def undo_queries():
        return sum(tile(t, False, dq_ref[:, t * 128 : (t + 1) * 128]) for t in range(QW // 128))

    def back_part(c, start, width):
        w = w_ref[c, :, :, :, :, :width].reshape(D // 2, width)
        return lax.dot_general(d_joined[:, start : start + width], w, NT, preferred_element_type=F32)

    def queries_back():
        load_w(0, QW).wait()
        for c in range(2):
            part[c] = back_part(c, 0, QW)
        load_w(QW, KVW).start()

    q_terms = undo_queries()
    tasks = [queries_back, lambda: outer((4, 0, QW), 0)]
    while any(todo):
        for h in range(HH):
            move(h)
        if tasks:
            tasks.pop(0)()
        advance(1)
    k_terms = 0.0
    for h in range(HH):
        grad = jnp.concatenate([buffers[h][j][2]["sum"][...] for j in range(len(KV_PARTS))], axis=0)
        k_terms = k_terms + tile(QW // 128 + h, True, grad)
    q_terms = q_terms + pltpu.roll(q_terms, HD, 1)
    head_terms[...] = jnp.where(lane_of(q_terms.shape) < HD, q_terms, pltpu.roll(k_terms, HD, 1))
    other = pl.ds(pl.multiple_of((1 - core) * TOK, TOK), TOK)
    load_w(QW, KVW).wait()
    swaps = []
    for c in range(2):
        part[c] += back_part(c, QW, KVW)
        swaps.append(send(part.at[c, other], got.at[c], psem.at[1 + c], psem.at[3 + c], sibling))
    advance(2)
    outer((4, QW, KVW), 1)
    advance(2)
    gain_row = jnp.concatenate([gains[j : j + 1] for j in range(D // 128)], axis=1)
    for c in swaps:
        c.wait_recv()

    def last(r, carry):
        rows = rows_at(r)
        own = pl.ds(pl.multiple_of(core * TOK + r * 32, 32), 32)
        e = jnp.concatenate([part[c, own, :] + got[c, rows, :] for c in range(2)], axis=1)
        v = own_x[rows, :].astype(F32)
        inverse = lax.rsqrt(jnp.sum(v * v, axis=1, keepdims=True) * (1.0 / D) + EPSILON)
        scaled = e * gain_row
        inner = jnp.sum(scaled * v, axis=1, keepdims=True) * (1.0 / D)
        total = grad_mid[rows, :] + inverse * scaled - v * (inverse * inverse * inverse) * inner
        input_grad[rows, :] = total.astype(BF)
        return carry + jnp.sum(e * v * inverse, axis=0, keepdims=True)

    terms[...] = lax.fori_loop(0, TOK // 32, last, jnp.zeros((1, D), F32))
    advance(len(units))
    drain((4, 0, QW), 0)
    drain((4, QW, KVW), 1)
    for e in early:
        e.wait()
    pending = [c for e in early for c in e.copies] + swaps + [c for group in streams for st in group for c in st.sent]
    for c in pending:
        c.wait_send()


def attend_back(operands, cid):
    vmem = pl.BlockSpec(memory_space=pltpu.VMEM)
    anywhere = pl.BlockSpec(memory_space=pl.ANY)
    tokens = 2 * TOK
    widths = (FH, FH, FH, QW, QW + KVW)
    out = pl.pallas_call(
        attend_back_kernel,
        out_shape=[
            jax.ShapeDtypeStruct((TOK, D), BF),
            jax.ShapeDtypeStruct((1, D), F32),
            jax.ShapeDtypeStruct((1, 128), F32),
        ]
        + [jax.ShapeDtypeStruct((2, 4, 4, 2, 32, w), BF) for w in widths]
        + early_shapes(),
        in_specs=[pl.BlockSpec(memory_space=pltpu.SMEM)]
        + [vmem] * 5
        + [anywhere]
        + [vmem] * 8
        + [anywhere]
        + [vmem] * 5,
        out_specs=[vmem] * 3 + [anywhere] * (5 + 2 * N_EARLY),
        scratch_shapes=[
            [pltpu.VMEM((2, KEY_BLOCKS, SPANS_STEP, SPAN, 2 * HD), BF)] * 2,
            pltpu.VMEM((2, HH, 2, 2 * QROWS, 2 * HD), BF),
            pltpu.VMEM((2, HH, 2, 1, QROWS), F32),
            pltpu.VMEM((HH, 2, 4, 4, tokens, 2 * HD), BF),
            pltpu.VMEM((2 * N_CTX, SPAN, 2 * HD), F32),
            pltpu.VMEM((2, 2 * HD, QROWS), F32),
            pltpu.VMEM((tokens, QW), F32),
            [
                [sum_scratch(order, KV_DIMS, rows, 2 * HD, False, True) for start, rows, order in KV_PARTS]
                for h in range(HH)
            ],
            pltpu.VMEM((2, 2, 2, 4, 2, 32, 1152), BF),
            pltpu.VMEM((2, 2, 4, 2, 16, 1152), BF),
            pltpu.VMEM((2, 4, 4, 16, 1152), BF),
            [
                pltpu.VMEM((2,) + lead_shape(without(W_DIMS, order[0])) + (16, width), BF)
                for a, start, width, order in SUMS[:N_EARLY]
            ],
            pltpu.VMEM((2, 4, 4, 2, 32, QW), BF),
            pltpu.VMEM((tokens, QW + KVW), BF),
            pltpu.VMEM((2, tokens, D // 2), F32),
            pltpu.VMEM((2, TOK, D // 2), F32),
            pltpu.SemaphoreType.DMA((N_EARLY, 6)),
            pltpu.SemaphoreType.DMA((N_EARLY, 6)),
            pltpu.SemaphoreType.DMA((HH, 3, 3, 6)),
            pltpu.SemaphoreType.DMA((HH, 3, 3, 6)),
            pltpu.SemaphoreType.DMA((2, HH)),
            pltpu.SemaphoreType.DMA((2, 2)),
            pltpu.SemaphoreType.DMA((5,)),
            pltpu.SemaphoreType.DMA((5,)),
        ],
        compiler_params=pltpu.CompilerParams(
            collective_id=cid, has_side_effects=True, vmem_limit_bytes=63 * 1024 * 1024
        ),
        name="attend_back",
    )(*operands)
    return out[0], out[1], out[2], out[3:8], out[8:]


FIRST = ((0, 768), (768, SPLIT - 768))
SECOND = ((SPLIT, FH - SPLIT),)


def rows_at(r, n=32):
    return pl.ds(pl.multiple_of(r * n, n), n)


def feed_kernel(
    attn, x, dy, gains, wo_h, wg_h, wu_h, wd_h,
    result, grad_mid, grad_attn, normed, hid, dgate, dup, low_mid, stats, terms,
    wo, wg, wu, wd, mid, part, got, part_f, got_f, back_ref, wsem, psem, gssem, grsem,
):
    at = here()
    core = at["core"]
    sibling = moved(at, "core", 1)
    late_cols = pl.ds(SPLIT, FH - SPLIT)
    weights = ((wg_h, wg), (wu_h, wu), (wd_h, wd))
    quarters, loads = [], []
    for k, (src, dst) in enumerate(weights):
        held = labels(ORDERS[k][2], at[ORDERS[k][2]])
        tail = (slice(None), late_cols)
        quarters.append(
            pltpu.make_async_copy(pick(src, W_DIMS, held, tail), pick(dst, W_DIMS, held, tail), wsem.at[4 + k])
        )
        quarters[-1].start()
    whole = (slice(None),) * 5
    for i, (src, dst) in enumerate(((wo_h, wo), (wd_h, wd), (wg_h, wg), (wu_h, wu))):
        cols = whole + (pl.ds(0, QW if i == 0 else SPLIT),)
        loads.append(pltpu.make_async_copy(src.at[cols], dst.at[cols], wsem.at[i]))
        loads[-1].start()
    greet([sibling] + neighbours(at, ("x", "y", "z")))
    gathers = []
    for k, (src, dst) in enumerate(weights):
        quarters[k].wait()
        g = Gathering(dst, W_DIMS, at, ORDERS[k], 32, late_cols, gssem.at[k], grsem.at[k])
        g.phase = 2
        g.start()
        gathers.append(g)

    def columns(ref, start, width):
        return ref[:, :, :, :, :, start : start + width].reshape(D, width)

    def half_rows(ref, c, start, width):
        return ref[c, :, :, :, :, start : start + width].reshape(D // 2, width)

    gain_row = jnp.concatenate([gains[16 + j : 17 + j] for j in range(D // 128)], axis=1)
    sent = []
    loads[0].wait()
    for c in range(2):
        part[0, c] = lax.dot_general(attn[...], half_rows(wo, c, 0, QW), NT, preferred_element_type=F32)
        sent.append(send(part.at[0, c], got.at[0, c], psem.at[c, 0], psem.at[c, 1], sibling))
    loads[1].wait()

    def product(out, left, right, pieces):
        for start, width in pieces:
            out[:, start : start + width] = jnp.dot(left[...], columns(right, start, width), preferred_element_type=F32)

    product(back_ref, dy, wd, FIRST)
    for c in sent:
        c.wait_recv()

    def root(v):
        return jnp.sum(jnp.sqrt(jnp.sum(v * v, axis=1, keepdims=True) * (1.0 / D)), axis=0, keepdims=True)

    def middle(r, carry):
        rows = rows_at(r)
        branch = jnp.concatenate([part[0, c, rows, :] + got[0, c, rows, :] for c in range(2)], axis=1)
        v = x[rows, :].astype(F32)
        m = v + branch
        mid[rows, :] = m
        inverse = lax.rsqrt(jnp.sum(m * m, axis=1, keepdims=True) * (1.0 / D) + EPSILON)
        normed[rows, :] = (m * inverse * gain_row).astype(BF)
        own = jnp.where(lax.div(r, TOK // 32) == core, 1.0, 0.0)
        return tuple(t + own * root(u) for t, u in zip(carry, (v, branch, m)))

    zero = jnp.zeros((1, 1), F32)
    roots = lax.fori_loop(0, 2 * TOK // 32, middle, (zero, zero, zero))
    for c in loads[2:]:
        c.wait()

    def hidden(pieces):
        for start, width in pieces:
            cols = slice(start, start + width)
            gate = jnp.dot(normed[...], columns(wg, start, width), preferred_element_type=F32)
            up = jnp.dot(normed[...], columns(wu, start, width), preferred_element_type=F32)
            back = back_ref[:, cols]
            sigmoid = lax.logistic(gate)
            silu = gate * sigmoid
            hid[:, cols] = (silu * up).astype(BF)
            dup[:, cols] = (back * silu).astype(BF)
            dgate[:, cols] = (back * up * sigmoid * (1.0 + gate * (1.0 - sigmoid))).astype(BF)

    def back_half(c, start, width):
        cols = slice(start, start + width)
        one = lax.dot_general(dgate[:, cols], half_rows(wg, c, start, width), NT, preferred_element_type=F32)
        return one + lax.dot_general(dup[:, cols], half_rows(wu, c, start, width), NT, preferred_element_type=F32)

    def forward_half(c, start, width):
        cols = slice(start, start + width)
        return lax.dot_general(hid[:, cols], half_rows(wd, c, start, width), NT, preferred_element_type=F32)

    hidden(FIRST)
    for g in gathers:
        g.pass_on()
    for c in range(2):
        part[1, c] = back_half(c, 0, SPLIT)
        part_f[:, c * 1024 : (c + 1) * 1024] = forward_half(c, 0, SPLIT)
    for g in gathers:
        g.finish()
    product(back_ref, dy, wd, SECOND)
    hidden(SECOND)
    late = []
    for c in range(2):
        part[1, c] += back_half(c, SPLIT, FH - SPLIT)
        late.append(send(part.at[1, c], got.at[1, c], psem.at[2 + c, 0], psem.at[2 + c, 1], sibling))
    for c in range(2):
        part_f[:, c * 1024 : (c + 1) * 1024] += forward_half(c, SPLIT, FH - SPLIT)
    other = pl.ds(pl.multiple_of((1 - core) * TOK, TOK), TOK)
    last = send(part_f.at[other], got_f, psem.at[4, 0], psem.at[4, 1], sibling)

    for c in late:
        c.wait_recv()

    def backward(r, carry):
        rows = rows_at(r)
        e = jnp.concatenate([part[1, c, rows, :] + got[1, c, rows, :] for c in range(2)], axis=1)
        v = mid[rows, :]
        inverse = lax.rsqrt(jnp.sum(v * v, axis=1, keepdims=True) * (1.0 / D) + EPSILON)
        scaled = e * gain_row
        inner = jnp.sum(scaled * v, axis=1, keepdims=True) * (1.0 / D)
        total = dy[rows, :].astype(F32) + inverse * scaled - v * (inverse * inverse * inverse) * inner
        low_mid[rows, :] = total.astype(BF)
        mid[rows, :] = total
        own = jnp.where(lax.div(r, TOK // 32) == core, 1.0, 0.0)
        return carry + own * jnp.sum(e * v * inverse, axis=0, keepdims=True)

    def finish(r, carry):
        rows = rows_at(r)
        own = pl.ds(pl.multiple_of(core * TOK + r * 32, 32), 32)
        branch = part_f[own, :] + got_f[rows, :]
        result[rows, :] = (mid[own, :] + branch).astype(BF)
        return carry + root(branch)

    last.wait_recv()
    final = lax.fori_loop(0, TOK // 32, finish, zero)
    terms[...] = lax.fori_loop(0, 2 * TOK // 32, backward, jnp.zeros((1, D), F32))
    for i, v in enumerate(roots + (final,)):
        stats[i : i + 1, :] = jnp.broadcast_to(v, (1, 128))
    grad_attn[...] = jnp.dot(low_mid[...], columns(wo, 0, QW), preferred_element_type=F32).astype(BF)
    grad_mid[...] = mid[pl.ds(pl.multiple_of(core * TOK, TOK), TOK), :]
    for c in sent + late + [last]:
        c.wait_send()
    for g in gathers:
        g.wait_sent()


def feed(attn, x, dy, gains, w_out, w_gate, w_up, w_down, cid):
    vmem = pl.BlockSpec(memory_space=pltpu.VMEM)
    anywhere = pl.BlockSpec(memory_space=pl.ANY)
    tokens = 2 * TOK
    return pl.pallas_call(
        feed_kernel,
        out_shape=[
            jax.ShapeDtypeStruct((TOK, D), BF),
            jax.ShapeDtypeStruct((TOK, D), F32),
            jax.ShapeDtypeStruct((tokens, QW), BF),
            jax.ShapeDtypeStruct((tokens, D), BF),
            jax.ShapeDtypeStruct((tokens, FH), BF),
            jax.ShapeDtypeStruct((tokens, FH), BF),
            jax.ShapeDtypeStruct((tokens, FH), BF),
            jax.ShapeDtypeStruct((tokens, D), BF),
            jax.ShapeDtypeStruct((4, 128), F32),
            jax.ShapeDtypeStruct((1, D), F32),
        ],
        in_specs=[vmem] * 4 + [anywhere] * 4,
        out_specs=[vmem] * 10,
        scratch_shapes=[
            pltpu.VMEM((2, 4, 4, 2, 32, QW), BF),
            pltpu.VMEM((2, 4, 4, 2, 32, FH), BF),
            pltpu.VMEM((2, 4, 4, 2, 32, FH), BF),
            pltpu.VMEM((2, 4, 4, 2, 32, FH), BF),
            pltpu.VMEM((tokens, D), F32),
            pltpu.VMEM((2, 2, tokens, D // 2), F32),
            pltpu.VMEM((2, 2, tokens, D // 2), F32),
            pltpu.VMEM((tokens, D), F32),
            pltpu.VMEM((TOK, D), F32),
            pltpu.VMEM((tokens, FH), F32),
            pltpu.SemaphoreType.DMA((7,)),
            pltpu.SemaphoreType.DMA((5, 2)),
            pltpu.SemaphoreType.DMA((3, 3, 4)),
            pltpu.SemaphoreType.DMA((3, 3, 4)),
        ],
        compiler_params=pltpu.CompilerParams(
            collective_id=cid, has_side_effects=True, vmem_limit_bytes=62 * 1024 * 1024
        ),
        name="feed",
    )(attn, x, dy, gains, w_out, w_gate, w_up, w_down)


def body(layer_input, w_qkv, w_out, w_gate_up, w_down, norm_gains, span_map, cotangent):
    at = here()
    core, low = at["core"], at["l"]
    w_q = w_qkv[:, : HQ * HD].reshape(16, 2, QW).transpose(1, 0, 2)
    w_k = w_qkv[:, HQ * HD : (HQ + HK) * HD].reshape(16, 2, HH, HD)
    w_v = w_qkv[:, (HQ + HK) * HD :].reshape(16, 2, HH, HD)
    w_kv = jnp.concatenate([w_k, w_v], axis=3).reshape(16, 2, KVW).transpose(1, 0, 2)
    shard_one = jnp.concatenate([w_q, w_kv], axis=2)
    share = norm_gains.shape[0]
    device = lax.axis_index(("ctx", "fsdp"))
    own_gain = lax.dynamic_update_slice_in_dim(jnp.zeros((40 * 128,), F32), norm_gains.astype(F32), device * share, 0)

    ctx_index = lax.axis_index("ctx")
    maps = lax.dynamic_slice_in_dim(span_map, low * 2, 2, 0)
    own_span = lax.dynamic_slice_in_dim(maps, ctx_index, 1, 1)
    spans = jnp.concatenate([own_span, 2 * N_CTX - 1 - own_span], axis=1)
    positions = (spans[:, :, None] * SPAN + jnp.arange(SPAN, dtype=jnp.int32)).reshape(2 * TOK)
    match = maps[:, None, :] == jnp.arange(N_CTX, dtype=jnp.int32)[None, :, None]
    inverse_map = jnp.sum(jnp.where(match, jnp.arange(N_CTX, dtype=jnp.int32), 0), axis=2)
    holder = jnp.concatenate([inverse_map, inverse_map[:, ::-1]], axis=1)
    upper = (jnp.arange(2 * N_CTX, dtype=jnp.int32) >= N_CTX).astype(jnp.int32)[None, :] + jnp.zeros_like(holder)
    low_block = own_span // SPANS_STEP
    low_limit = own_span % SPANS_STEP * SPAN
    three = jnp.arange(3, dtype=jnp.int32)[None, :]
    step_half = (three >= low_block).astype(jnp.int32)
    tab = jnp.concatenate(
        [
            holder // 16,
            holder // 4 % 4,
            holder % 4,
            upper,
            step_half,
            jnp.where(step_half == 0, three, 6 - three),
            (jnp.arange(4, dtype=jnp.int32)[None, :] == low_block).astype(jnp.int32),
            low_block,
            KEY_BLOCKS - 1 - low_block,
            low_limit,
            KEYS - SPAN - low_limit,
            maps,
            2 * N_CTX - 1 - maps,
        ],
        axis=1,
    )
    half_dim = HD // 2
    frequencies = ROPE_BASE ** (-(jnp.arange(half_dim, dtype=F32) * 2.0 / HD))
    angles = positions.astype(F32)[:, None] * frequencies[None, :]
    cosine, sine = jnp.cos(angles), jnp.sin(angles)
    cosine = jnp.concatenate([cosine] * 4, axis=1)
    sine = jnp.concatenate([-sine, sine] * 2, axis=1)

    weights = [shard_one, w_gate_up, w_down, w_out]
    (w_one, w_gate, w_up, w_back, w_proj, x_pair, dy_pair, gains, joined, normed_one, query, keys, attn_f32, attn_low, log_sum) = front(
        tab, weights, layer_input[0], cotangent[0], own_gain.reshape(40, 128), cosine, sine, 1
    )
    dy = dy_pair.reshape(2 * TOK, D)

    result, grad_middle, grad_attn, normed_two, hidden, grad_gate, grad_up, grad_branch, stats, gain_two_terms = feed(
        attn_low, x_pair.reshape(2 * TOK, D), dy, gains, w_proj, w_gate, w_up, w_back, 2
    )
    operands = (tab, query, grad_attn, attn_f32, attn_low, log_sum, keys, normed_two, dy, grad_branch, hidden)
    operands += (grad_gate, grad_up, joined, normed_one, w_one, gains, cosine, sine, grad_middle, layer_input[0])
    grad_input, gain_one_terms, head_terms, grads, begun = attend_back(operands, 4)
    sums = jnp.concatenate(
        [
            gain_one_terms[0],
            gain_two_terms[0],
            head_terms[0],
            stats[:, 0],
        ]
    )
    sums = jnp.pad(sums, (0, 40 * 128 - sums.shape[0])).reshape(40, 128)
    grad_mlp, grad_down, grad_proj, grad_qkv, sums = sum_weights(
        grads, sums, begun, SUMS, 5, 62 * 1024 * 1024
    )
    sums = sums.reshape(-1)
    own_gains = lax.dynamic_slice_in_dim(sums, device * share, share, 0)
    stream_rms = sums[4224:4228] / (TOK * N_CTX * 4)
    arrays = [result[None], grad_input[None], grad_qkv, grad_proj, grad_mlp, grad_down]
    result, grad_input, grad_qkv, grad_proj, grad_mlp, grad_down = publish(arrays)
    return (
        result,
        grad_input,
        grad_qkv,
        grad_proj,
        grad_mlp,
        grad_down,
        own_gains,
        stream_rms,
    )


def publish_kernel(n, *refs):
    copies = [pltpu.make_async_copy(refs[i], refs[n + i], refs[2 * n].at[i]) for i in range(n)]
    for c in copies:
        c.start()
    for c in copies:
        c.wait()


def publish(arrays):
    n = len(arrays)
    anywhere = pl.BlockSpec(memory_space=pl.ANY)
    return pl.pallas_call(
        functools.partial(publish_kernel, n),
        out_shape=[jax.ShapeDtypeStruct(a.shape, a.dtype) for a in arrays],
        in_specs=[pl.BlockSpec(memory_space=pltpu.VMEM)] * n,
        out_specs=[anywhere] * n,
        scratch_shapes=[pltpu.SemaphoreType.DMA((n,))],
        name="publish",
    )(*arrays)


def solution(mesh):
    rows = P(("ctx", "fsdp"), None)
    tokens = P("fsdp", "ctx", None)
    return jax.shard_map(
        body,
        mesh=mesh,
        in_specs=(tokens, rows, rows, rows, rows, P(("ctx", "fsdp")), P(), tokens),
        out_specs=(tokens, tokens, rows, rows, rows, rows, P(("ctx", "fsdp")), P()),
        check_vma=False,
    )
```

```python
import functools

import jax
import jax.numpy as jnp
from jax import lax
from jax.experimental import pallas as pl
from jax.experimental.pallas import tpu as pltpu
from jax.sharding import PartitionSpec as P

D = 2048
HQ = 24
HK = 6
HD = 64
FF = 4352
TOK = 128
SPAN = 64
N_CTX = 32

HH = HK // 2
GROUP = HQ // HK
QH = HQ // 2
QW = QH * HD
KVW = HH * 2 * HD
FH = FF // 2
KEYS = 512
SPANS_STEP = KEYS // SPAN
KEY_BLOCKS = 8
QROWS = GROUP * SPAN

EPSILON = 1e-06
ROPE_BASE = 10000.0
LOG2E = 1.4426950408889634
AT_H, AT_X, AT_Y, AT_HALF = 0, 64, 128, 192
AT_STEP_HALF, AT_STEP_BLOCK, AT_MARK, AT_EDGE, AT_LIMIT, AT_MAP = 256, 259, 262, 266, 268, 270
MESH = pl.DeviceIdType.MESH
BF = jnp.bfloat16
F32 = jnp.float32
NT = (((1,), (1,)), ((), ()))
NN = (((1,), (0,)), ((), ()))
TN = (((0,), (0,)), ((), ()))
W_DIMS = ("h", "x", "y", "l")
KV_DIMS = ("h", "x", "y")
ORDERS = (("x", "y", "z"), ("y", "z", "x"), ("z", "x", "y"))
KV_ORDERS = (("h", "x", "y"), ("x", "y", "h"), ("y", "h", "x"))
KV_PARTS = ((0, 96, ("y", "x", "h")), (96, 96, ("x", "y", "h")), (192, 64, ("h", "x", "y")))
SUMS = (
    (0, 0, 1152, ORDERS[0]),
    (1, 0, 1152, ORDERS[1]),
    (2, 0, 1152, ORDERS[2]),
    (0, 1152, 1024, ORDERS[0]),
    (1, 1152, 1024, ORDERS[1]),
    (2, 1152, 1024, ORDERS[2]),
    (3, 0, 256, ORDERS[0]),
    (3, 256, 256, ORDERS[1]),
    (3, 512, 256, ORDERS[2]),
    (4, 0, 384, ORDERS[0]),
    (4, 384, 384, ORDERS[1]),
    (4, 768, 384, ORDERS[2]),
)
N_EARLY = 9
ADVANCE = (0, 4, 0, 8, 0, 4)
SIZES = {"x": 4, "y": 4, "z": 4, "h": 2}


def here():
    c = lax.axis_index("ctx")
    f = lax.axis_index("fsdp")
    return {
        "x": lax.rem(lax.div(c, 4), 4),
        "y": lax.rem(c, 4),
        "z": lax.div(c, 16) * 2 + lax.div(f, 2),
        "h": lax.div(c, 16),
        "l": lax.div(f, 2),
        "core": lax.rem(f, 2),
    }


def device_of(x, y, z, core):
    return (lax.div(z, 2) * 16 + x * 4 + y, lax.rem(z, 2) * 2 + core)


def moved(at, axis, by):
    if axis == "core":
        return device_of(at["x"], at["y"], at["z"], 1 - at["core"])
    place = {k: at[k] for k in ("x", "y", "z")}
    if axis == "h":
        place["z"] = lax.rem(at["z"] + 2, 4)
    else:
        place[axis] = lax.rem(at[axis] + by + 4, 4)
    return device_of(place["x"], place["y"], place["z"], at["core"])


def labels(axis, value):
    if axis == "z":
        return {"h": lax.div(value, 2), "l": lax.rem(value, 2)}
    return {axis: value}


def pick(ref, dims, values, tail):
    return ref.at[tuple(values[d] if d in values else slice(None) for d in dims) + tail]


def greet(devices):
    barrier = pltpu.get_barrier_semaphore()
    for d in devices:
        pl.semaphore_signal(barrier, inc=1, device_id=d, device_id_type=MESH)
    pl.semaphore_wait(barrier, len(devices))


def send(src, dst, ssem, rsem, device):
    copy = pltpu.make_async_remote_copy(
        src_ref=src, dst_ref=dst, send_sem=ssem, recv_sem=rsem, device_id=device, device_id_type=MESH
    )
    copy.start()
    return copy


class Gathering:
    def __init__(self, ref, dims, at, order, rows, cols, ssem, rsem):
        self.ref, self.dims, self.at, self.order, self.rows, self.cols = ref, dims, at, order, rows, cols
        self.ssem, self.rsem, self.phase, self.sent = ssem, rsem, 0, []

    def block(self, coordinate, rows):
        later = {}
        for a in self.order[self.phase + 1 :]:
            later.update(labels(a, self.at[a]))
        return pick(self.ref, self.dims, {**later, **labels(self.axis, coordinate)}, (rows, self.cols))

    def send(self, n, ref, by):
        c = send(ref, ref, self.ssem.at[self.phase, n], self.rsem.at[self.phase, n], moved(self.at, self.axis, by))
        self.sent.append(c)
        return c

    def start(self):
        self.axis = self.order[self.phase]
        mine = self.block(self.at[self.axis], slice(None))
        self.first = [self.send(0, mine, 1)]
        if SIZES[self.axis] == 4:
            self.first.append(self.send(1, mine, 3))

    def pass_on(self):
        for c in self.first:
            c.wait_recv()
        self.second = []
        if SIZES[self.axis] == 4:
            half = self.rows // 2
            me = self.at[self.axis]
            self.second.append(self.send(2, self.block(lax.rem(me + 3, 4), pl.ds(0, half)), 1))
            self.second.append(self.send(3, self.block(lax.rem(me + 1, 4), pl.ds(half, half)), 3))

    def finish(self):
        for c in self.second:
            c.wait_recv()
        self.phase += 1

    def wait_sent(self):
        for c in self.sent:
            c.wait_send()


def neighbours(at, axes):
    out = []
    for a in axes:
        if a in ("core", "h"):
            out.append(moved(at, a, 1))
        else:
            out.append(moved(at, a, 1))
            out.append(moved(at, a, 3))
    return out


SPLIT = 1664
GATHER = (
    (0, 0, SPLIT, ORDERS[0]),
    (1, 0, SPLIT, ORDERS[1]),
    (2, 0, SPLIT, ORDERS[2]),
    (0, SPLIT, FH - SPLIT, ORDERS[0]),
    (1, SPLIT, FH - SPLIT, ORDERS[1]),
    (2, SPLIT, FH - SPLIT, ORDERS[2]),
    (3, 0, 256, ORDERS[0]),
    (3, 256, 256, ORDERS[1]),
    (3, 512, 256, ORDERS[2]),
)


def lane_of(shape):
    return lax.broadcasted_iota(jnp.int32, shape, len(shape) - 1)


def swap_halves(v):
    return jnp.where(lax.rem(lane_of(v.shape), HD) < HD // 2, pltpu.roll(v, 96, 1), pltpu.roll(v, 32, 1))


def head_sums(v):
    low = lane_of(v.shape) < HD
    a = jnp.sum(jnp.where(low, v, 0.0), axis=1, keepdims=True)
    b = jnp.sum(jnp.where(low, 0.0, v), axis=1, keepdims=True)
    return jnp.where(low, a, b)


def tile_gain(row, is_key):
    low = lane_of(row.shape) < HD
    turned = pltpu.roll(row, HD, 1)
    return jnp.where(low, turned, 1.0) if is_key else jnp.where(low, row, turned)


def front_kernel(
    tab, shard_one, gate_up, down, out, x, dy, gains, cosine, sine,
    w_one, w_gate, w_up, w_down, w_out, x_pair, dy_pair, gain_all, joined, normed, query, kv_out, o_ref, low_ref, l_ref,
    one, kv_src, kvg, kvs, q_ref, acc, sum_ref, small_buf, psem, lsem, tssem, trsem, ossem, orsem, gssem, grsem, kssem, krsem, ksem,
):
    at = here()
    core = at["core"]
    sibling = moved(at, "core", 1)
    greet([sibling] + sum_peers(at, ("x", "y", "z")))
    own = {d: at[d] for d in W_DIMS}
    total = Total(gains[...], at, small_buf, tssem, trsem)
    remote, local = [], []

    def half_of(src, start, width, which):
        return src.at[:, pl.ds(pl.multiple_of(start + which * width, 128), width)]

    pairs = [
        (lambda c: shard_one.at[c], one),
        (lambda c: half_of(gate_up, 0, FH, c), w_gate),
        (lambda c: half_of(gate_up, FF, FH, c), w_up),
        (lambda c: half_of(down, 0, FH, c), w_down),
        (lambda c: half_of(out, 0, QW, c), w_out),
    ]
    for i, (src, ref) in enumerate(pairs):
        dst = pick(ref, W_DIMS, own, (pl.ds(core * 16, 16), slice(None)))
        remote.append(send(src(1 - core), dst, psem.at[i, 0], psem.at[i, 1], sibling))
        local.append(pltpu.make_async_copy(src(core), dst, lsem.at[i]))
        local[-1].start()
    for i, (src, ref) in ((5, (x, x_pair)), (6, (dy, dy_pair))):
        remote.append(send(src, ref.at[core], psem.at[i, 0], psem.at[i, 1], sibling))
        local.append(pltpu.make_async_copy(src, ref.at[core], lsem.at[i]))
        local[-1].start()

    def arrived(i):
        remote[i].wait_recv()
        local[i].wait()

    ones = [
        Gathering(one, W_DIMS, at, ORDERS[k], 32, pl.ds(k * 384, 384), ossem.at[k], orsem.at[k]) for k in range(3)
    ]
    rest = [
        Gathering(pairs[1 + a][1], W_DIMS, at, order, 32, pl.ds(start, width), gssem.at[k], grsem.at[k])
        for k, (a, start, width, order) in enumerate(GATHER)
    ]
    keys = [
        Gathering(kvg.at[h], KV_DIMS, at, KV_ORDERS[h], 4, slice(None), kssem.at[h], krsem.at[h]) for h in range(HH)
    ]

    def every(streams, *steps):
        for s in streams:
            for step in steps:
                getattr(s, step)()

    arrived(0)
    every(ones, "start")
    for i in range(1, 5):
        arrived(i)
    every(rest, "start")
    total.step()
    every(ones, "pass_on")
    every(rest, "pass_on")
    total.step()
    every(ones, "finish", "start")
    every(rest, "finish")
    total.step()
    every(ones, "pass_on")
    total.step()
    gain_all[...] = total.value
    every(ones, "finish", "start")
    every(rest, "start")
    arrived(5)
    gain_row = jnp.concatenate([total.value[j : j + 1] for j in range(D // 128)], axis=1)

    def norm(r, carry):
        rows = pl.ds(pl.multiple_of(r * 32, 32), 32)
        for s in range(2):
            v = x_pair[s, rows, :].astype(F32)
            inverse = lax.rsqrt(jnp.sum(v * v, axis=1, keepdims=True) * (1.0 / D) + EPSILON)
            normed[pl.ds(pl.multiple_of(s * TOK + r * 32, 32), 32), :] = (v * inverse * gain_row).astype(BF)
        return carry

    lax.fori_loop(0, TOK // 32, norm, 0)
    every(ones, "pass_on")
    every(ones, "finish")
    keep = pltpu.make_async_copy(one, w_one, lsem.at[7])
    keep.start()
    head_gains = total.value[32:33]

    def product(start, width):
        w = one[:, :, :, :, :, start : start + width].reshape(D, width)
        joined[:, start : start + width] = jnp.dot(normed[...], w, preferred_element_type=F32)

    def rope(tile, is_key):
        v = joined[:, tile * 128 : (tile + 1) * 128]
        low = lane_of(v.shape) < HD
        c, n = cosine[...], sine[...]
        inverse = lax.rsqrt(head_sums(v * v) * (1.0 / HD) + EPSILON)
        if is_key:
            inverse = jnp.where(low, inverse, 1.0)
            c, n = jnp.where(low, c, 1.0), jnp.where(low, n, 0.0)
        v = v * inverse * tile_gain(head_gains, is_key)
        return (v * c + swap_halves(v) * n).astype(BF)

    product(QW, KVW)
    for h in range(HH):
        kv_src[h] = rope(QW // 128 + h, True).reshape(4, SPAN, 2 * HD)
    kv_own = {d: at[d] for d in KV_DIMS}
    puts = [pltpu.make_async_copy(kv_src.at[h], pick(kvg.at[h], KV_DIMS, kv_own, ()), ksem.at[h]) for h in range(HH)]
    for c in puts:
        c.start()
    for c in puts:
        c.wait()
    every(keys, "start")
    every(rest, "pass_on")
    product(0, 384)
    every(keys, "pass_on")
    every(keys, "finish", "start")
    product(384, 384)
    every(keys, "pass_on")
    for t in range(QW // 128):
        query[:, t * 128 : (t + 1) * 128] = rope(t, False)
    every(keys, "finish", "start")
    blank = jnp.zeros((QROWS, HD), BF)
    for s in range(2):
        for h in range(HH):
            for half in range(2):
                q_ref[s, h, half] = jnp.concatenate([heads_at(query, s, h, half), blank], axis=1)
    every(keys, "pass_on")
    every(keys, "finish")
    every(rest[:3] + rest[6:], "finish", "start")
    every(rest[3:6], "finish")

    def sort(p, carry):
        for s in range(2):
            place = tuple(tab[s, column + p] for column in (AT_H, AT_X, AT_Y))
            half = tab[s, AT_HALF + p]
            for h in range(HH):
                kvs[s, h, lax.div(p, SPANS_STEP), lax.rem(p, SPANS_STEP)] = kvg[(h,) + place + (s * 2 + half,)]
        return carry

    lax.fori_loop(0, 2 * N_CTX, sort, 0)
    keep_keys = pltpu.make_async_copy(kvs, kv_out, ksem.at[HH])
    keep_keys.start()
    attend_heads(tab, 0, q_ref, kvs, o_ref, low_ref, l_ref, acc, sum_ref)
    every(rest[:3], "pass_on")
    attend_heads(tab, 1, q_ref, kvs, o_ref, low_ref, l_ref, acc, sum_ref)
    every(rest[6:], "pass_on")
    every(rest[:3] + rest[6:], "finish")
    keep_keys.wait()
    arrived(6)
    keep.wait()
    for c in remote + total.sent:
        c.wait_send()
    for s in ones + rest + keys:
        s.wait_sent()


def front(tab, shards, x, dy, gains, cosine, sine, cid):
    anywhere = pl.BlockSpec(memory_space=pl.ANY)
    vmem = pl.BlockSpec(memory_space=pltpu.VMEM)
    full = [jax.ShapeDtypeStruct((2, 4, 4, 2, 32, w), BF) for w in (QW + KVW, FH, FH, FH, QW)]
    n = len(GATHER)
    return pl.pallas_call(
        front_kernel,
        out_shape=full
        + [
            jax.ShapeDtypeStruct((2,) + x.shape, BF),
            jax.ShapeDtypeStruct((2,) + dy.shape, BF),
            jax.ShapeDtypeStruct(gains.shape, F32),
            jax.ShapeDtypeStruct((2 * TOK, QW + KVW), F32),
            jax.ShapeDtypeStruct((2 * TOK, D), BF),
            jax.ShapeDtypeStruct((2 * TOK, QW), BF),
            jax.ShapeDtypeStruct((2, HH, KEY_BLOCKS, SPANS_STEP, SPAN, 2 * HD), BF),
            jax.ShapeDtypeStruct((2 * TOK, QW), F32),
            jax.ShapeDtypeStruct((2 * TOK, QW), BF),
            jax.ShapeDtypeStruct((2, HH, 2, 1, QROWS), F32),
        ],
        in_specs=[pl.BlockSpec(memory_space=pltpu.SMEM)] + [anywhere] * 6 + [vmem] * 3,
        out_specs=[anywhere] * 5 + [vmem, anywhere] + [vmem] * 4 + [anywhere] + [vmem] * 3,
        scratch_shapes=[
            pltpu.VMEM((2, 4, 4, 2, 32, QW + KVW), BF),
            pltpu.VMEM((HH, 4, SPAN, 2 * HD), BF),
            pltpu.VMEM((HH, 2, 4, 4, 4, SPAN, 2 * HD), BF),
            pltpu.VMEM((2, HH, KEY_BLOCKS, SPANS_STEP, SPAN, 2 * HD), BF),
            pltpu.VMEM((2, HH, 2, QROWS, 2 * HD), BF),
            pltpu.VMEM((2, 2 * HD, QROWS), F32),
            pltpu.VMEM((2, 1, QROWS), F32),
            pltpu.VMEM((4, 4) + gains.shape, F32),
            pltpu.SemaphoreType.DMA((7, 2)),
            pltpu.SemaphoreType.DMA((8,)),
            pltpu.SemaphoreType.DMA((4, 4)),
            pltpu.SemaphoreType.DMA((4, 4)),
            pltpu.SemaphoreType.DMA((3, 3, 4)),
            pltpu.SemaphoreType.DMA((3, 3, 4)),
            pltpu.SemaphoreType.DMA((n, 3, 4)),
            pltpu.SemaphoreType.DMA((n, 3, 4)),
            pltpu.SemaphoreType.DMA((HH, 3, 4)),
            pltpu.SemaphoreType.DMA((HH, 3, 4)),
            pltpu.SemaphoreType.DMA((HH + 1,)),
        ],
        compiler_params=pltpu.CompilerParams(
            collective_id=cid, has_side_effects=True, vmem_limit_bytes=60 * 1024 * 1024
        ),
        name="front",
    )(tab, *shards, x, dy, gains, cosine, sine)


def lead_shape(dims):
    full = {"h": 2, "x": 4, "y": 4, "l": 2}
    return tuple(full[d] for d in dims)


def without(dims, axis):
    gone = ("h", "l") if axis == "z" else (axis,)
    return tuple(d for d in dims if d not in gone)


class Summing:
    def __init__(self, source, dims, at, order, rows, cols, buffers, ssem, rsem, lsem, begun=None, base=None):
        self.ref, self.dims, self.at, self.order, self.begun = source, dims, at, order, begun
        self.cols, self.buffers, self.rows = cols, buffers, rows
        self.ssem, self.rsem, self.lsem = ssem, rsem, lsem
        self.phase, self.sent, self.base = 0, [], base
        self.resident = base is not None

    def part(self, coordinate, start, length):
        rows = pl.ds(start + (self.base or 0), length)
        return pick(self.ref, self.dims, labels(self.axis, coordinate), (rows, self.cols))

    def send(self, n, src, dst, by):
        c = send(src, dst, self.ssem.at[self.phase, n], self.rsem.at[self.phase, n], moved(self.at, self.axis, by))
        self.sent.append(c)
        return c

    def start(self):
        self.axis = self.order[self.phase]
        self.rest = without(self.dims, self.axis)
        self.lead = lead_shape(self.rest)
        half = self.rows // 2
        first, second, every = (0, half), (half, half), (0, self.rows)
        i = self.at[self.axis]
        buf = self.buffers[self.phase]
        self.local = []
        if SIZES[self.axis] == 2:
            self.direct = (self.send(0, self.part(1 - i, *every), buf["got"].at[0], 1),)
        else:
            up, down, far = lax.rem(i + 1, 4), lax.rem(i + 3, 4), lax.rem(i + 2, 4)
            self.near = (up, down)
        if self.phase == 0 and self.begun is not None:
            self.relay, self.direct = (), ()
        elif SIZES[self.axis] == 4:
            self.relay = (
                self.send(0, self.part(far, *first), buf["relay"].at[0], 1),
                self.send(1, self.part(far, *second), buf["relay"].at[1], 3),
            )
            self.direct = (
                self.send(2, self.part(up, *second), buf["got"].at[1, 1], 1),
                self.send(3, self.part(down, *first), buf["got"].at[0, 1], 3),
            )
        if self.phase == 0 and not self.resident:
            todo = [(self.part(i, *every), buf["mine"])]
            if self.begun is not None:
                passed, direct = self.begun[1], self.begun[0]
                todo += [(passed.at[n], buf["got"].at[n, 0]) for n in range(2)]
                todo += [(direct.at[n], buf["got"].at[n, 1]) for n in range(2)]
            elif SIZES[self.axis] == 4:
                todo.append((self.part(up, *first), buf["own"].at[0]))
                todo.append((self.part(down, *second), buf["own"].at[1]))
            for n, (src, dst) in enumerate(todo):
                c = pltpu.make_async_copy(src, dst, self.lsem.at[n])
                c.start()
                self.local.append(c)

    def over_lead(self, add):
        rest = self.lead[1:]
        spots = [()]
        for n in rest:
            spots = [s + (j,) for s in spots for j in range(n)]
        if not self.lead:
            add(())
            return

        def go(j, carry):
            for s in spots:
                add((j,) + s)
            return carry

        lax.fori_loop(0, self.lead[0], go, 0)

    def pass_on(self):
        if SIZES[self.axis] == 2 or (self.phase == 0 and self.begun is not None):
            return
        buf = self.buffers[self.phase]
        half = self.rows // 2
        for n, by in ((0, 1), (1, 3)):
            self.relay[n].wait_recv()
            if self.phase == 0 and not self.resident:
                self.local[1 + n].wait()
                own = buf["own"].at[n]
            else:
                own = self.part(self.near[n], n * half, half)

            def add(spot):
                here_ = spot + (slice(None), slice(None))
                both = buf["relay"][(n,) + here_].astype(F32) + own[here_].astype(F32)
                buf["relay"][(n,) + here_] = both.astype(BF)

            self.over_lead(add)
            c = self.send(4 + n, buf["relay"].at[n], buf["got"].at[n, 0], by)
            self.direct = self.direct + (c,)

    def finish(self):
        buf = self.buffers[self.phase]
        half = self.rows // 2
        if self.local:
            self.local[0].wait()
        if self.begun is not None:
            for c in self.local[1:]:
                c.wait()
        for c in self.direct:
            c.wait_recv()
        copied = self.phase == 0 and not self.resident
        own = buf["mine"] if copied else self.part(self.at[self.axis], 0, self.rows)
        out = buf["mine"] if copied else buf["sum"]

        def add(spot):
            if SIZES[self.axis] == 2:
                here_ = spot + (slice(None), slice(None))
                out[here_] = (own[here_].astype(F32) + buf["got"][(0,) + here_].astype(F32)).astype(out.dtype)
                return
            for n in range(2):
                rows = spot + (pl.ds(n * half, half), slice(None))
                all_ = spot + (slice(None), slice(None))
                total = own[rows].astype(F32) + buf["got"][(n, 0) + all_].astype(F32)
                total = total + buf["got"][(n, 1) + all_].astype(F32)
                out[rows] = total.astype(out.dtype)

        self.over_lead(add)
        self.ref, self.dims, self.cols = out, self.rest, slice(None)
        self.phase += 1
        self.base = 0


class Total:
    def __init__(self, value, at, buf, ssem, rsem):
        self.value, self.at, self.buf, self.ssem, self.rsem = value, at, buf, ssem, rsem
        self.phase, self.sent = 0, []
        self.start()

    def start(self):
        n, axis = self.phase, ("core", "z", "y", "x")[self.phase]
        self.buf[n, 0] = self.value
        self.copies = []
        for i in (1, 3, 2) if axis != "core" else (1,):
            self.copies.append(
                send(self.buf.at[n, 0], self.buf.at[n, i], self.ssem.at[n, i], self.rsem.at[n, i], moved(self.at, axis, i))
            )

    def step(self):
        n, buf = self.phase, self.buf
        if n == 4:
            return
        for c in self.copies:
            c.wait_recv()
            self.sent.append(c)
        if n == 0:
            self.value = buf[n, 0] + buf[n, 1]
        else:
            self.value = (buf[n, 0] + buf[n, 2]) + (buf[n, 1] + buf[n, 3])
        self.phase += 1
        if self.phase < 4:
            self.start()


def run_sums(streams, total):
    todo = []
    for s in streams:
        if s.begun is None:
            s.start()
    for s in streams:
        if s.begun is not None:
            s.start()
        steps = [("pass_on",), ("finish", "start"), ("pass_on",), ("finish", "start"), ("pass_on",), ("finish",)]
        todo.append(steps[1:] if s.begun is not None else steps)
    while any(todo):
        for s, steps in zip(streams, todo):
            if steps:
                for name in steps.pop(0):
                    getattr(s, name)()
        total.step()
    for s in streams:
        for c in s.sent:
            c.wait_send()


def sum_scratch(order, dims, rows, width, begun=False, resident=False):
    buffers = []
    for phase, axis in enumerate(order):
        rest = without(dims, axis)
        lead = lead_shape(rest)
        buf = {}
        if SIZES[axis] == 2:
            buf["got"] = pltpu.VMEM((1,) + lead + (rows, width), BF)
        else:
            buf["got"] = pltpu.VMEM((2, 2) + lead + (rows // 2, width), BF)
            if phase or not begun:
                buf["relay"] = pltpu.VMEM((2,) + lead + (rows // 2, width), BF)
        if phase == 0 and not resident:
            buf["mine"] = pltpu.VMEM(lead + (rows, width), BF)
            if SIZES[axis] == 4 and not begun:
                buf["own"] = pltpu.VMEM((2,) + lead + (rows // 2, width), BF)
        else:
            buf["sum"] = pltpu.VMEM(lead + (rows, width), BF if phase < 2 else F32)
        buffers.append(buf)
        dims = rest
    return buffers


def weight_sum_kernel(pieces, n, *refs):
    ins, small, begun, refs = refs[:n], refs[n], refs[n + 1 : n + 1 + 2 * N_EARLY], refs[n + 1 + 2 * N_EARLY :]
    outs, small_out = refs[: n - 1], refs[n - 1]
    buffers, stages, swapped, halves, small_buf, ssem, rsem, lsem, csem, tssem, trsem = refs[n:]
    at = here()
    core = at["core"]
    sibling = moved(at, "core", 1)
    greet([sibling] + sum_peers(at, ("x", "y", "z")))
    streams = [
        Summing(
            ins[a], W_DIMS, at, order, 32, pl.ds(start, width), buffers[k], ssem.at[k], rsem.at[k], lsem.at[k],
            (begun[2 * k], begun[2 * k + 1]) if k < N_EARLY else None,
        )
        for k, (a, start, width, order) in enumerate(pieces)
    ]
    total = Total(small[...], at, small_buf, tssem, trsem)
    run_sums(streams, total)
    small_out[...] = total.value
    for k, (a, start, width, order) in enumerate(pieces):
        stages[a][:, start : start + width] = buffers[k][2]["sum"][...]
    other = pl.ds(pl.multiple_of((1 - core) * 16, 16), 16)
    own = pl.ds(pl.multiple_of(core * 16, 16), 16)
    copies = [send(stages[a].at[other], swapped[a], csem.at[a, 0], csem.at[a, 1], sibling) for a in range(n)]

    def put(a, half, value):
        width = value.shape[1]
        if a == 4:
            outs[3][:, pl.ds(pl.multiple_of(half * QW, 128), QW)] = value[:, :QW]
            halves[half] = value[:, QW:]
            return
        ref, start = ((outs[0], 0), (outs[0], FF), (outs[1], 0), (outs[2], 0))[a]
        ref[:, pl.ds(pl.multiple_of(start + half * width, 128), width)] = value

    for a in range(n):
        put(a, core, stages[a][own, :])
    for a in range(n):
        copies[a].wait_recv()
        put(a, 1 - core, swapped[a][...])
    for kind in range(2):
        at_ = [half_kv[:, (2 * h + kind) * HD : (2 * h + kind + 1) * HD] for half_kv in (halves[0], halves[1]) for h in range(HH)]
        start = HQ * HD + kind * HK * HD
        outs[3][:, start : start + HK * HD] = jnp.concatenate(at_, axis=1)
    for c in copies + total.sent:
        c.wait_send()


def sum_weights(grads, small, begun, pieces, cid, limit):
    n, count = len(grads), len(pieces)
    anywhere = pl.BlockSpec(memory_space=pl.ANY)
    vmem = pl.BlockSpec(memory_space=pltpu.VMEM)
    widths = [g.shape[-1] for g in grads]
    return pl.pallas_call(
        functools.partial(weight_sum_kernel, pieces, n),
        out_shape=[jax.ShapeDtypeStruct((16, w), F32) for w in (2 * FF, FF, HQ * HD, (HQ + 2 * HK) * HD)]
        + [jax.ShapeDtypeStruct(small.shape, F32)],
        in_specs=[anywhere] * n + [vmem] + [anywhere] * len(begun),
        out_specs=[vmem] * n,
        scratch_shapes=[
            [sum_scratch(order, W_DIMS, 32, width, k < N_EARLY) for k, (a, start, width, order) in enumerate(pieces)],
            [pltpu.VMEM((32, w), F32) for w in widths],
            [pltpu.VMEM((16, w), F32) for w in widths],
            pltpu.VMEM((2, 16, KVW), F32),
            pltpu.VMEM((4, 4) + small.shape, F32),
            pltpu.SemaphoreType.DMA((count, 3, 6)),
            pltpu.SemaphoreType.DMA((count, 3, 6)),
            pltpu.SemaphoreType.DMA((count, 6)),
            pltpu.SemaphoreType.DMA((n, 2)),
            pltpu.SemaphoreType.DMA((4, 4)),
            pltpu.SemaphoreType.DMA((4, 4)),
        ],
        compiler_params=pltpu.CompilerParams(collective_id=cid, has_side_effects=True, vmem_limit_bytes=limit),
        name="sum_weights",
    )(*grads, small, *begun)


def sum_peers(at, axes):
    out = []
    for a in axes:
        for i in (1, 3, 2) if SIZES[a] == 4 else (1,):
            out.append(moved(at, a, i))
    return out


def heads_at(ref, s, h, half):
    rows = slice(s * TOK + half * SPAN, s * TOK + (half + 1) * SPAN)
    return jnp.concatenate([ref[rows, (h * GROUP + g) * HD : (h * GROUP + g + 1) * HD] for g in range(GROUP)], axis=0)


def put_heads(ref, s, h, half, value):
    rows = pl.ds(pl.multiple_of(s * TOK + half * SPAN, SPAN), SPAN)
    for g in range(0, GROUP, 2):
        both = jnp.concatenate([value[g * SPAN : (g + 1) * SPAN], value[(g + 1) * SPAN : (g + 2) * SPAN]], axis=1)
        ref[rows, pl.ds(pl.multiple_of((h * GROUP + g) * HD, 2 * HD), 2 * HD)] = both.astype(ref.dtype)


def masked(prob, limit):
    if limit is None:
        return prob
    row = lax.broadcasted_iota(jnp.int32, prob.shape, 0)
    col = lax.rem(lax.broadcasted_iota(jnp.int32, prob.shape, 1), SPAN)
    return jnp.where(row <= col + limit, prob, 0.0)


def attend_heads(tab, s, q_ref, kvs, o_ref, low_ref, l_ref, acc, total):
    rate = LOG2E * HD**-0.5

    def head(h, carry):
        acc[...] = jnp.zeros_like(acc)
        total[...] = jnp.zeros_like(total)

        def scored(half, block, limit):
            keys = kvs[s, h, block].reshape(KEYS, 2 * HD)
            scores = lax.dot_general(keys, q_ref[s, h, half], NT, preferred_element_type=F32)
            prob = masked(jnp.exp2(scores * rate), limit)
            return (
                jnp.sum(prob, axis=0, keepdims=True),
                lax.dot_general(keys, prob.astype(BF), TN, preferred_element_type=F32),
            )

        def high(k, c):
            t, o = scored(1, k, None)
            total[1] += t
            acc[1] += o
            return c

        def either(k, c):
            half = tab[s, AT_STEP_HALF + k]
            t, o = scored(half, tab[s, AT_STEP_BLOCK + k], None)
            up = half.astype(F32)
            total[0] += t * (1.0 - up)
            total[1] += t * up
            acc[0] += o * (1.0 - up)
            acc[1] += o * up
            return c

        lax.fori_loop(0, 4, high, 0)
        lax.fori_loop(0, 3, either, 0)
        for half in range(2):
            t, o = scored(half, tab[s, AT_EDGE + half], tab[s, AT_LIMIT + half])
            t, o = total[half] + t, acc[half] + o
            out = (o[HD:, :] / t).T
            put_heads(o_ref, s, h, half, out)
            put_heads(low_ref, s, h, half, out)
            l_ref[s, h, half] = jnp.log2(t)
        return carry

    lax.fori_loop(0, HH, head, 0)


class Early:
    def __init__(self, source, at, order, cols, width, relay, direct, passed, ssem, rsem):
        self.source, self.at, self.axis, self.cols, self.width = source, at, order[0], cols, width
        self.relay, self.passed, self.ssem, self.rsem, self.views = relay, passed, ssem, rsem, {}
        i = at[self.axis]
        self.near = (lax.rem(i + 1, 4), lax.rem(i + 3, 4))
        far = lax.rem(i + 2, 4)
        plan = (
            (far, 0, relay, 0, 1),
            (far, 1, relay, 1, 3),
            (self.near[0], 1, direct, 1, 1),
            (self.near[1], 0, direct, 0, 3),
        )
        self.copies = []
        for n, (coordinate, half, dst, slot, by) in enumerate(plan):
            self.copies.append(self.send(n, self.part(coordinate, half), dst.at[slot], by))

    def part(self, coordinate, half):
        return pick(self.source, W_DIMS, labels(self.axis, coordinate), (pl.ds(half * 16, 16), self.cols))

    def send(self, n, src, dst, by):
        return send(src, dst, self.ssem.at[n], self.rsem.at[n], moved(self.at, self.axis, by))

    def load(self, n, own, sem):
        lead = lead_shape(without(W_DIMS, self.axis))
        view = own.at[(slice(None),) * (len(lead) + 1) + (pl.ds(0, self.width),)]
        self.views[n] = view
        copy = pltpu.make_async_copy(self.part(self.near[n], n), view, sem)
        copy.start()
        return copy

    def add(self, n):
        self.copies[n].wait_recv()
        came, own = self.relay.at[n], self.views[n]
        lead = lead_shape(without(W_DIMS, self.axis))
        spots = [()]
        for size in lead[1:]:
            spots = [s + (j,) for s in spots for j in range(size)]

        def go(j, carry):
            for s in spots:
                at = (j,) + s + (slice(None), slice(None))
                came[at] = (came[at].astype(F32) + own[at].astype(F32)).astype(BF)
            return carry

        lax.fori_loop(0, lead[0], go, 0)
        self.copies.append(self.send(4 + n, came, self.passed.at[n], 1 if n == 0 else 3))

    def wait(self):
        for c in self.copies[2:]:
            c.wait_recv()


def early_shapes():
    shapes = []
    for a, start, width, order in SUMS[:N_EARLY]:
        lead = lead_shape(without(W_DIMS, order[0]))
        shapes += [jax.ShapeDtypeStruct((2,) + lead + (16, width), BF)] * 2
    return shapes


def attend_back_kernel(*refs):
    tab, qr, da, attn, attn_low, l_ref, kv_sorted, normed, dy, low_mid, hid, dgate, dup = refs[:13]
    joined, normed_one, w_one, gains, cosine, sine, grad_mid, own_x = refs[13:21]
    input_grad, terms, head_terms = refs[21:24]
    grads, refs = refs[24:29], refs[29:]
    begun, refs = refs[: 2 * N_EARLY], refs[2 * N_EARLY :]
    held, qd_ref, delta_ref, stage, acc, dq_acc, dq_ref, buffers, refs = refs[:8] + (refs[8:],)
    tiles, mix, mix_z, relays, w_ref, d_joined, part, got = refs[:8]
    essem, ersem, ssem, rsem, sems, tsem, msem, psem = refs[8:]
    at = here()
    core = at["core"]
    sibling = moved(at, "core", 1)
    def load_keys(h):
        return [pltpu.make_async_copy(kv_sorted.at[s, h], held[h % 2].at[s], sems.at[s, h]) for s in range(2)]

    for c in load_keys(0):
        c.start()

    def load_w(start, width):
        src = w_one.at[:, :, :, :, :, pl.ds(start, width)]
        return pltpu.make_async_copy(src, w_ref.at[:, :, :, :, :, pl.ds(0, width)], psem.at[0])

    load_w(0, QW).start()
    greet([sibling] + neighbours(at, ("x", "y", "z", "h")))
    sides = ((normed, dgate), (normed, dup), (dy, hid), (low_mid, attn_low), (normed_one, d_joined))

    def tile_copy(n, i, slot, parity):
        a, start, width = n
        half = lax.rem(i, 2)
        return pltpu.make_async_copy(
            tiles.at[parity, slot, :, :, :, :, pl.ds(0, width)],
            grads[a].at[lax.div(i, 2), pl.ds(half * 2, 2), :, :, :, pl.ds(start, width)],
            tsem.at[parity, slot],
        )

    def outer(n, parity):
        a, start, width = n
        left, right = sides[a]

        def go(i, carry):
            slot = lax.rem(i, 2)

            @pl.when(i > 1)
            def _():
                tile_copy(n, i, slot, parity).wait()

            rows = pl.ds(pl.multiple_of(i * 512, 512), 512)
            value = lax.dot_general(left[:, rows], right[:, start : start + width], TN, preferred_element_type=F32)
            tiles[parity, slot, :, :, :, :, :width] = value.astype(BF).reshape(2, 4, 2, 32, width)
            tile_copy(n, i, slot, parity).start()
            return carry

        lax.fori_loop(0, 4, go, 0)

    def drain(n, parity):
        for slot in range(2):
            tile_copy(n, slot, slot, parity).wait()

    early = []

    def begin(k):
        a, start, width, order = SUMS[k]
        drain((a, start, width), k % 2)
        early.append(
            Early(
                grads[a], at, order, pl.ds(start, width), width, relays[k], begun[2 * k], begun[2 * k + 1],
                essem.at[k], ersem.at[k],
            )
        )

    for k in range(N_EARLY):
        outer(SUMS[k][:3], k % 2)
        if k:
            begin(k - 1)
    rate = LOG2E * HD**-0.5
    factor = jnp.where(lax.broadcasted_iota(jnp.int32, (1, 2 * HD), 1) < HD, HD**-0.5, 1.0)
    blank = jnp.zeros((QROWS, HD), BF)
    for s in range(2):
        for h in range(HH):
            for half in range(2):
                up = heads_at(da, s, h, half)
                qd_ref[s, h, half, :QROWS] = jnp.concatenate([heads_at(qr, s, h, half), blank], axis=1)
                qd_ref[s, h, half, QROWS:] = jnp.concatenate([blank, up], axis=1)
                inner = (up.astype(F32) * heads_at(attn, s, h, half)).T
                delta_ref[s, h, half] = jnp.sum(inner, axis=0, keepdims=True)
    begin(N_EARLY - 1)
    streams = [
        [
            Summing(
                stage.at[h], KV_DIMS, at, order, rows, slice(None), buffers[h][j],
                ssem.at[h, j], rsem.at[h, j], None, None, start,
            )
            for j, (start, rows, order) in enumerate(KV_PARTS)
        ]
        for h in range(HH)
    ]
    todo = [[("pass_on",), ("finish", "start"), ("pass_on",), ("finish", "start"), ("pass_on",), ("finish",)] for h in range(HH)]

    def move(h):
        for name_of in todo[h].pop(0) if todo[h] else ():
            for st in streams[h]:
                getattr(st, name_of)()

    units = [(k, n) for k in range(N_EARLY) for n in range(2)]
    used, flying, ahead = {}, [], [0]

    def fetch():
        k, n = units[ahead[0]]
        pool, slots, first = (mix_z, 2, 2) if early[k].axis == "z" else (mix, 2, 0)
        slot = used.get(first, 0) % slots
        used[first] = used.get(first, 0) + 1
        flying.append((k, n, early[k].load(n, pool.at[slot], msem.at[first + slot])))
        ahead[0] += 1

    def advance(count):
        for _ in range(count):
            while ahead[0] < len(units) and len(flying) < 2:
                fetch()
            if flying:
                k, n, copy = flying.pop(0)
                copy.wait()
                early[k].add(n)

    for h in range(HH):
        for c in load_keys(h):
            c.wait()
        if h + 1 < HH:
            for c in load_keys(h + 1):
                c.start()
        kvs = held[h % 2]

        def sequence(s, carry, h=h, kvs=kvs):
            dq_acc[...] = jnp.zeros_like(dq_acc)
            acc[...] = jnp.zeros_like(acc)

            def backward(half, block, limit):
                keys = kvs[s, block].reshape(KEYS, 2 * HD)
                both = lax.dot_general(keys, qd_ref[s, h, half], NT, preferred_element_type=F32)
                prob = masked(jnp.exp2(both[:, :QROWS] * rate - l_ref[s, h, half]), limit)
                grad = (prob * (both[:, QROWS:] - delta_ref[s, h, half])).astype(BF)
                pair = jnp.concatenate([grad, prob.astype(BF)], axis=1)
                kv = lax.dot_general(pair, qd_ref[s, h, half], NN, preferred_element_type=F32)
                return (
                    kv.reshape(SPANS_STEP, SPAN, 2 * HD),
                    lax.dot_general(keys, grad, TN, preferred_element_type=F32),
                )

            def spans(block):
                return pl.ds(block * SPANS_STEP, SPANS_STEP)

            def high(k, c):
                kv, q = backward(1, k, None)
                acc[spans(k)] += kv
                dq_acc[1] += q
                return c

            def either(k, c):
                half = tab[s, AT_STEP_HALF + k]
                kv, q = backward(half, tab[s, AT_STEP_BLOCK + k], None)
                up = half.astype(F32)
                acc[spans(k)] += kv * (1.0 - up)
                acc[spans(6 - k)] += kv * up
                dq_acc[0] += q * (1.0 - up)
                dq_acc[1] += q * up
                return c

            lax.fori_loop(0, 4, high, 0)
            lax.fori_loop(0, 3, either, 0)
            for half in range(2):
                kv, q = backward(half, tab[s, AT_EDGE + half], tab[s, AT_LIMIT + half])
                for k in range(4):
                    acc[spans(k if half == 0 else 7 - k)] += kv * tab[s, AT_MARK + k].astype(F32)
                q = dq_acc[half] + q
                put_heads(dq_ref, s, h, half, (q[:HD, :] * HD**-0.5).T)

            def put(j, c):
                for half in range(2):
                    v = acc[tab[s, AT_MAP + half * N_CTX + j]] * factor
                    rows = pl.ds(pl.multiple_of(s * TOK + half * SPAN, SPAN), SPAN)
                    stage[h, lax.div(j, 16), lax.rem(lax.div(j, 4), 4), lax.rem(j, 4), rows, :] = v.astype(BF)
                return c

            lax.fori_loop(0, N_CTX, put, 0)
            return carry

        for s in range(2):
            sequence(s, 0)
            if s == 1:
                for k in range(h):
                    move(k)
                for st in streams[h]:
                    st.start()
            advance(ADVANCE[2 * h + s])

    head_gains = gains[32:33]

    def tile(t, is_key, grad):
        v = joined[:, t * 128 : (t + 1) * 128]
        low = lane_of(v.shape) < HD
        back = grad * cosine[...] - swap_halves(grad) * sine[...]
        inverse = lax.rsqrt(head_sums(v * v) * (1.0 / HD) + EPSILON)
        scaled = back * tile_gain(head_gains, is_key)
        inner = head_sums(scaled * v) * (1.0 / HD)
        result = inverse * scaled - v * (inverse * inverse * inverse) * inner
        if is_key:
            result = jnp.where(low, result, grad)
        d_joined[:, t * 128 : (t + 1) * 128] = result.astype(BF)
        return jnp.sum(back * v * inverse, axis=0, keepdims=True)

    def undo_queries():
        return sum(tile(t, False, dq_ref[:, t * 128 : (t + 1) * 128]) for t in range(QW // 128))

    def back_part(c, start, width):
        w = w_ref[c, :, :, :, :, :width].reshape(D // 2, width)
        return lax.dot_general(d_joined[:, start : start + width], w, NT, preferred_element_type=F32)

    def queries_back():
        load_w(0, QW).wait()
        for c in range(2):
            part[c] = back_part(c, 0, QW)
        load_w(QW, KVW).start()

    q_terms = undo_queries()
    tasks = [queries_back, lambda: outer((4, 0, QW), 0)]
    while any(todo):
        for h in range(HH):
            move(h)
        if tasks:
            tasks.pop(0)()
        advance(1)
    k_terms = 0.0
    for h in range(HH):
        grad = jnp.concatenate([buffers[h][j][2]["sum"][...] for j in range(len(KV_PARTS))], axis=0)
        k_terms = k_terms + tile(QW // 128 + h, True, grad)
    q_terms = q_terms + pltpu.roll(q_terms, HD, 1)
    head_terms[...] = jnp.where(lane_of(q_terms.shape) < HD, q_terms, pltpu.roll(k_terms, HD, 1))
    other = pl.ds(pl.multiple_of((1 - core) * TOK, TOK), TOK)
    load_w(QW, KVW).wait()
    swaps = []
    for c in range(2):
        part[c] += back_part(c, QW, KVW)
        swaps.append(send(part.at[c, other], got.at[c], psem.at[1 + c], psem.at[3 + c], sibling))
    advance(2)
    outer((4, QW, KVW), 1)
    advance(2)
    gain_row = jnp.concatenate([gains[j : j + 1] for j in range(D // 128)], axis=1)
    for c in swaps:
        c.wait_recv()

    def last(r, carry):
        rows = rows_at(r)
        own = pl.ds(pl.multiple_of(core * TOK + r * 32, 32), 32)
        e = jnp.concatenate([part[c, own, :] + got[c, rows, :] for c in range(2)], axis=1)
        v = own_x[rows, :].astype(F32)
        inverse = lax.rsqrt(jnp.sum(v * v, axis=1, keepdims=True) * (1.0 / D) + EPSILON)
        scaled = e * gain_row
        inner = jnp.sum(scaled * v, axis=1, keepdims=True) * (1.0 / D)
        total = grad_mid[rows, :] + inverse * scaled - v * (inverse * inverse * inverse) * inner
        input_grad[rows, :] = total.astype(BF)
        return carry + jnp.sum(e * v * inverse, axis=0, keepdims=True)

    terms[...] = lax.fori_loop(0, TOK // 32, last, jnp.zeros((1, D), F32))
    advance(len(units))
    drain((4, 0, QW), 0)
    drain((4, QW, KVW), 1)
    for e in early:
        e.wait()
    pending = [c for e in early for c in e.copies] + swaps + [c for group in streams for st in group for c in st.sent]
    for c in pending:
        c.wait_send()


def attend_back(operands, cid):
    vmem = pl.BlockSpec(memory_space=pltpu.VMEM)
    anywhere = pl.BlockSpec(memory_space=pl.ANY)
    tokens = 2 * TOK
    widths = (FH, FH, FH, QW, QW + KVW)
    out = pl.pallas_call(
        attend_back_kernel,
        out_shape=[
            jax.ShapeDtypeStruct((TOK, D), BF),
            jax.ShapeDtypeStruct((1, D), F32),
            jax.ShapeDtypeStruct((1, 128), F32),
        ]
        + [jax.ShapeDtypeStruct((2, 4, 4, 2, 32, w), BF) for w in widths]
        + early_shapes(),
        in_specs=[pl.BlockSpec(memory_space=pltpu.SMEM)]
        + [vmem] * 5
        + [anywhere]
        + [vmem] * 8
        + [anywhere]
        + [vmem] * 5,
        out_specs=[vmem] * 3 + [anywhere] * (5 + 2 * N_EARLY),
        scratch_shapes=[
            [pltpu.VMEM((2, KEY_BLOCKS, SPANS_STEP, SPAN, 2 * HD), BF)] * 2,
            pltpu.VMEM((2, HH, 2, 2 * QROWS, 2 * HD), BF),
            pltpu.VMEM((2, HH, 2, 1, QROWS), F32),
            pltpu.VMEM((HH, 2, 4, 4, tokens, 2 * HD), BF),
            pltpu.VMEM((2 * N_CTX, SPAN, 2 * HD), F32),
            pltpu.VMEM((2, 2 * HD, QROWS), F32),
            pltpu.VMEM((tokens, QW), F32),
            [
                [sum_scratch(order, KV_DIMS, rows, 2 * HD, False, True) for start, rows, order in KV_PARTS]
                for h in range(HH)
            ],
            pltpu.VMEM((2, 2, 2, 4, 2, 32, 1152), BF),
            pltpu.VMEM((2, 2, 4, 2, 16, 1152), BF),
            pltpu.VMEM((2, 4, 4, 16, 1152), BF),
            [
                pltpu.VMEM((2,) + lead_shape(without(W_DIMS, order[0])) + (16, width), BF)
                for a, start, width, order in SUMS[:N_EARLY]
            ],
            pltpu.VMEM((2, 4, 4, 2, 32, QW), BF),
            pltpu.VMEM((tokens, QW + KVW), BF),
            pltpu.VMEM((2, tokens, D // 2), F32),
            pltpu.VMEM((2, TOK, D // 2), F32),
            pltpu.SemaphoreType.DMA((N_EARLY, 6)),
            pltpu.SemaphoreType.DMA((N_EARLY, 6)),
            pltpu.SemaphoreType.DMA((HH, 3, 3, 6)),
            pltpu.SemaphoreType.DMA((HH, 3, 3, 6)),
            pltpu.SemaphoreType.DMA((2, HH)),
            pltpu.SemaphoreType.DMA((2, 2)),
            pltpu.SemaphoreType.DMA((5,)),
            pltpu.SemaphoreType.DMA((5,)),
        ],
        compiler_params=pltpu.CompilerParams(
            collective_id=cid, has_side_effects=True, vmem_limit_bytes=63 * 1024 * 1024
        ),
        name="attend_back",
    )(*operands)
    return out[0], out[1], out[2], out[3:8], out[8:]


FIRST = ((0, 768), (768, SPLIT - 768))
SECOND = ((SPLIT, FH - SPLIT),)


def rows_at(r, n=32):
    return pl.ds(pl.multiple_of(r * n, n), n)


def feed_kernel(
    attn, x, dy, gains, wo_h, wg_h, wu_h, wd_h,
    result, grad_mid, grad_attn, normed, hid, dgate, dup, low_mid, stats, terms,
    wo, wg, wu, wd, mid, part, got, part_f, got_f, back_ref, wsem, psem, gssem, grsem,
):
    at = here()
    core = at["core"]
    sibling = moved(at, "core", 1)
    late_cols = pl.ds(SPLIT, FH - SPLIT)
    weights = ((wg_h, wg), (wu_h, wu), (wd_h, wd))
    quarters, loads = [], []
    for k, (src, dst) in enumerate(weights):
        held = labels(ORDERS[k][2], at[ORDERS[k][2]])
        tail = (slice(None), late_cols)
        quarters.append(
            pltpu.make_async_copy(pick(src, W_DIMS, held, tail), pick(dst, W_DIMS, held, tail), wsem.at[4 + k])
        )
        quarters[-1].start()
    whole = (slice(None),) * 5
    for i, (src, dst) in enumerate(((wo_h, wo), (wd_h, wd), (wg_h, wg), (wu_h, wu))):
        cols = whole + (pl.ds(0, QW if i == 0 else SPLIT),)
        loads.append(pltpu.make_async_copy(src.at[cols], dst.at[cols], wsem.at[i]))
        loads[-1].start()
    greet([sibling] + neighbours(at, ("x", "y", "z")))
    gathers = []
    for k, (src, dst) in enumerate(weights):
        quarters[k].wait()
        g = Gathering(dst, W_DIMS, at, ORDERS[k], 32, late_cols, gssem.at[k], grsem.at[k])
        g.phase = 2
        g.start()
        gathers.append(g)

    def columns(ref, start, width):
        return ref[:, :, :, :, :, start : start + width].reshape(D, width)

    def half_rows(ref, c, start, width):
        return ref[c, :, :, :, :, start : start + width].reshape(D // 2, width)

    gain_row = jnp.concatenate([gains[16 + j : 17 + j] for j in range(D // 128)], axis=1)
    sent = []
    loads[0].wait()
    for c in range(2):
        part[0, c] = lax.dot_general(attn[...], half_rows(wo, c, 0, QW), NT, preferred_element_type=F32)
        sent.append(send(part.at[0, c], got.at[0, c], psem.at[c, 0], psem.at[c, 1], sibling))
    loads[1].wait()

    def product(out, left, right, pieces):
        for start, width in pieces:
            out[:, start : start + width] = jnp.dot(left[...], columns(right, start, width), preferred_element_type=F32)

    product(back_ref, dy, wd, FIRST)
    for c in sent:
        c.wait_recv()

    def root(v):
        return jnp.sum(jnp.sqrt(jnp.sum(v * v, axis=1, keepdims=True) * (1.0 / D)), axis=0, keepdims=True)

    def middle(r, carry):
        rows = rows_at(r)
        branch = jnp.concatenate([part[0, c, rows, :] + got[0, c, rows, :] for c in range(2)], axis=1)
        v = x[rows, :].astype(F32)
        m = v + branch
        mid[rows, :] = m
        inverse = lax.rsqrt(jnp.sum(m * m, axis=1, keepdims=True) * (1.0 / D) + EPSILON)
        normed[rows, :] = (m * inverse * gain_row).astype(BF)
        own = jnp.where(lax.div(r, TOK // 32) == core, 1.0, 0.0)
        return tuple(t + own * root(u) for t, u in zip(carry, (v, branch, m)))

    zero = jnp.zeros((1, 1), F32)
    roots = lax.fori_loop(0, 2 * TOK // 32, middle, (zero, zero, zero))
    for c in loads[2:]:
        c.wait()

    def hidden(pieces):
        for start, width in pieces:
            cols = slice(start, start + width)
            gate = jnp.dot(normed[...], columns(wg, start, width), preferred_element_type=F32)
            up = jnp.dot(normed[...], columns(wu, start, width), preferred_element_type=F32)
            back = back_ref[:, cols]
            sigmoid = lax.logistic(gate)
            silu = gate * sigmoid
            hid[:, cols] = (silu * up).astype(BF)
            dup[:, cols] = (back * silu).astype(BF)
            dgate[:, cols] = (back * up * sigmoid * (1.0 + gate * (1.0 - sigmoid))).astype(BF)

    def back_half(c, start, width):
        cols = slice(start, start + width)
        one = lax.dot_general(dgate[:, cols], half_rows(wg, c, start, width), NT, preferred_element_type=F32)
        return one + lax.dot_general(dup[:, cols], half_rows(wu, c, start, width), NT, preferred_element_type=F32)

    def forward_half(c, start, width):
        cols = slice(start, start + width)
        return lax.dot_general(hid[:, cols], half_rows(wd, c, start, width), NT, preferred_element_type=F32)

    hidden(FIRST)
    for g in gathers:
        g.pass_on()
    for c in range(2):
        part[1, c] = back_half(c, 0, SPLIT)
        part_f[:, c * 1024 : (c + 1) * 1024] = forward_half(c, 0, SPLIT)
    for g in gathers:
        g.finish()
    product(back_ref, dy, wd, SECOND)
    hidden(SECOND)
    late = []
    for c in range(2):
        part[1, c] += back_half(c, SPLIT, FH - SPLIT)
        late.append(send(part.at[1, c], got.at[1, c], psem.at[2 + c, 0], psem.at[2 + c, 1], sibling))
    for c in range(2):
        part_f[:, c * 1024 : (c + 1) * 1024] += forward_half(c, SPLIT, FH - SPLIT)
    other = pl.ds(pl.multiple_of((1 - core) * TOK, TOK), TOK)
    last = send(part_f.at[other], got_f, psem.at[4, 0], psem.at[4, 1], sibling)

    for c in late:
        c.wait_recv()

    def backward(r, carry):
        rows = rows_at(r)
        e = jnp.concatenate([part[1, c, rows, :] + got[1, c, rows, :] for c in range(2)], axis=1)
        v = mid[rows, :]
        inverse = lax.rsqrt(jnp.sum(v * v, axis=1, keepdims=True) * (1.0 / D) + EPSILON)
        scaled = e * gain_row
        inner = jnp.sum(scaled * v, axis=1, keepdims=True) * (1.0 / D)
        total = dy[rows, :].astype(F32) + inverse * scaled - v * (inverse * inverse * inverse) * inner
        low_mid[rows, :] = total.astype(BF)
        mid[rows, :] = total
        own = jnp.where(lax.div(r, TOK // 32) == core, 1.0, 0.0)
        return carry + own * jnp.sum(e * v * inverse, axis=0, keepdims=True)

    def finish(r, carry):
        rows = rows_at(r)
        own = pl.ds(pl.multiple_of(core * TOK + r * 32, 32), 32)
        branch = part_f[own, :] + got_f[rows, :]
        result[rows, :] = (mid[own, :] + branch).astype(BF)
        return carry + root(branch)

    last.wait_recv()
    final = lax.fori_loop(0, TOK // 32, finish, zero)
    terms[...] = lax.fori_loop(0, 2 * TOK // 32, backward, jnp.zeros((1, D), F32))
    for i, v in enumerate(roots + (final,)):
        stats[i : i + 1, :] = jnp.broadcast_to(v, (1, 128))
    grad_attn[...] = jnp.dot(low_mid[...], columns(wo, 0, QW), preferred_element_type=F32).astype(BF)
    grad_mid[...] = mid[pl.ds(pl.multiple_of(core * TOK, TOK), TOK), :]
    for c in sent + late + [last]:
        c.wait_send()
    for g in gathers:
        g.wait_sent()


def feed(attn, x, dy, gains, w_out, w_gate, w_up, w_down, cid):
    vmem = pl.BlockSpec(memory_space=pltpu.VMEM)
    anywhere = pl.BlockSpec(memory_space=pl.ANY)
    tokens = 2 * TOK
    return pl.pallas_call(
        feed_kernel,
        out_shape=[
            jax.ShapeDtypeStruct((TOK, D), BF),
            jax.ShapeDtypeStruct((TOK, D), F32),
            jax.ShapeDtypeStruct((tokens, QW), BF),
            jax.ShapeDtypeStruct((tokens, D), BF),
            jax.ShapeDtypeStruct((tokens, FH), BF),
            jax.ShapeDtypeStruct((tokens, FH), BF),
            jax.ShapeDtypeStruct((tokens, FH), BF),
            jax.ShapeDtypeStruct((tokens, D), BF),
            jax.ShapeDtypeStruct((4, 128), F32),
            jax.ShapeDtypeStruct((1, D), F32),
        ],
        in_specs=[vmem] * 4 + [anywhere] * 4,
        out_specs=[vmem] * 10,
        scratch_shapes=[
            pltpu.VMEM((2, 4, 4, 2, 32, QW), BF),
            pltpu.VMEM((2, 4, 4, 2, 32, FH), BF),
            pltpu.VMEM((2, 4, 4, 2, 32, FH), BF),
            pltpu.VMEM((2, 4, 4, 2, 32, FH), BF),
            pltpu.VMEM((tokens, D), F32),
            pltpu.VMEM((2, 2, tokens, D // 2), F32),
            pltpu.VMEM((2, 2, tokens, D // 2), F32),
            pltpu.VMEM((tokens, D), F32),
            pltpu.VMEM((TOK, D), F32),
            pltpu.VMEM((tokens, FH), F32),
            pltpu.SemaphoreType.DMA((7,)),
            pltpu.SemaphoreType.DMA((5, 2)),
            pltpu.SemaphoreType.DMA((3, 3, 4)),
            pltpu.SemaphoreType.DMA((3, 3, 4)),
        ],
        compiler_params=pltpu.CompilerParams(
            collective_id=cid, has_side_effects=True, vmem_limit_bytes=62 * 1024 * 1024
        ),
        name="feed",
    )(attn, x, dy, gains, w_out, w_gate, w_up, w_down)


def body(layer_input, w_qkv, w_out, w_gate_up, w_down, norm_gains, span_map, cotangent):
    at = here()
    core, low = at["core"], at["l"]
    w_q = w_qkv[:, : HQ * HD].reshape(16, 2, QW).transpose(1, 0, 2)
    w_k = w_qkv[:, HQ * HD : (HQ + HK) * HD].reshape(16, 2, HH, HD)
    w_v = w_qkv[:, (HQ + HK) * HD :].reshape(16, 2, HH, HD)
    w_kv = jnp.concatenate([w_k, w_v], axis=3).reshape(16, 2, KVW).transpose(1, 0, 2)
    shard_one = jnp.concatenate([w_q, w_kv], axis=2)
    share = norm_gains.shape[0]
    device = lax.axis_index(("ctx", "fsdp"))
    own_gain = lax.dynamic_update_slice_in_dim(jnp.zeros((40 * 128,), F32), norm_gains.astype(F32), device * share, 0)

    ctx_index = lax.axis_index("ctx")
    maps = lax.dynamic_slice_in_dim(span_map, low * 2, 2, 0)
    own_span = lax.dynamic_slice_in_dim(maps, ctx_index, 1, 1)
    spans = jnp.concatenate([own_span, 2 * N_CTX - 1 - own_span], axis=1)
    positions = (spans[:, :, None] * SPAN + jnp.arange(SPAN, dtype=jnp.int32)).reshape(2 * TOK)
    match = maps[:, None, :] == jnp.arange(N_CTX, dtype=jnp.int32)[None, :, None]
    inverse_map = jnp.sum(jnp.where(match, jnp.arange(N_CTX, dtype=jnp.int32), 0), axis=2)
    holder = jnp.concatenate([inverse_map, inverse_map[:, ::-1]], axis=1)
    upper = (jnp.arange(2 * N_CTX, dtype=jnp.int32) >= N_CTX).astype(jnp.int32)[None, :] + jnp.zeros_like(holder)
    low_block = own_span // SPANS_STEP
    low_limit = own_span % SPANS_STEP * SPAN
    three = jnp.arange(3, dtype=jnp.int32)[None, :]
    step_half = (three >= low_block).astype(jnp.int32)
    tab = jnp.concatenate(
        [
            holder // 16,
            holder // 4 % 4,
            holder % 4,
            upper,
            step_half,
            jnp.where(step_half == 0, three, 6 - three),
            (jnp.arange(4, dtype=jnp.int32)[None, :] == low_block).astype(jnp.int32),
            low_block,
            KEY_BLOCKS - 1 - low_block,
            low_limit,
            KEYS - SPAN - low_limit,
            maps,
            2 * N_CTX - 1 - maps,
        ],
        axis=1,
    )
    half_dim = HD // 2
    frequencies = ROPE_BASE ** (-(jnp.arange(half_dim, dtype=F32) * 2.0 / HD))
    angles = positions.astype(F32)[:, None] * frequencies[None, :]
    cosine, sine = jnp.cos(angles), jnp.sin(angles)
    cosine = jnp.concatenate([cosine] * 4, axis=1)
    sine = jnp.concatenate([-sine, sine] * 2, axis=1)

    weights = [shard_one, w_gate_up, w_down, w_out]
    (w_one, w_gate, w_up, w_back, w_proj, x_pair, dy_pair, gains, joined, normed_one, query, keys, attn_f32, attn_low, log_sum) = front(
        tab, weights, layer_input[0], cotangent[0], own_gain.reshape(40, 128), cosine, sine, 1
    )
    dy = dy_pair.reshape(2 * TOK, D)

    result, grad_middle, grad_attn, normed_two, hidden, grad_gate, grad_up, grad_branch, stats, gain_two_terms = feed(
        attn_low, x_pair.reshape(2 * TOK, D), dy, gains, w_proj, w_gate, w_up, w_back, 2
    )
    operands = (tab, query, grad_attn, attn_f32, attn_low, log_sum, keys, normed_two, dy, grad_branch, hidden)
    operands += (grad_gate, grad_up, joined, normed_one, w_one, gains, cosine, sine, grad_middle, layer_input[0])
    grad_input, gain_one_terms, head_terms, grads, begun = attend_back(operands, 4)
    sums = jnp.concatenate(
        [
            gain_one_terms[0],
            gain_two_terms[0],
            head_terms[0],
            stats[:, 0] / (TOK * N_CTX * 4),
        ]
    )
    sums = jnp.pad(sums, (0, 40 * 128 - sums.shape[0])).reshape(40, 128)
    grad_mlp, grad_down, grad_proj, grad_qkv, sums = sum_weights(
        grads, sums, begun, SUMS, 5, 62 * 1024 * 1024
    )
    sums = sums.reshape(-1)
    own_gains = lax.dynamic_slice_in_dim(sums, device * share, share, 0)
    stream_rms = sums[4224:4228]
    arrays = [result[None], grad_input[None], grad_qkv, grad_proj, grad_mlp, grad_down]
    result, grad_input, grad_qkv, grad_proj, grad_mlp, grad_down = publish(arrays)
    return (
        result,
        grad_input,
        grad_qkv,
        grad_proj,
        grad_mlp,
        grad_down,
        own_gains,
        stream_rms,
    )


def publish_kernel(n, *refs):
    copies = [pltpu.make_async_copy(refs[i], refs[n + i], refs[2 * n].at[i]) for i in range(n)]
    for c in copies:
        c.start()
    for c in copies:
        c.wait()


def publish(arrays):
    n = len(arrays)
    anywhere = pl.BlockSpec(memory_space=pl.ANY)
    return pl.pallas_call(
        functools.partial(publish_kernel, n),
        out_shape=[jax.ShapeDtypeStruct(a.shape, a.dtype) for a in arrays],
        in_specs=[pl.BlockSpec(memory_space=pltpu.VMEM)] * n,
        out_specs=[anywhere] * n,
        scratch_shapes=[pltpu.SemaphoreType.DMA((n,))],
        name="publish",
    )(*arrays)


def solution(mesh):
    rows = P(("ctx", "fsdp"), None)
    tokens = P("fsdp", "ctx", None)
    return jax.shard_map(
        body,
        mesh=mesh,
        in_specs=(tokens, rows, rows, rows, rows, P(("ctx", "fsdp")), P(), tokens),
        out_specs=(tokens, tokens, rows, rows, rows, rows, P(("ctx", "fsdp")), P()),
        check_vma=False,
    )
```
